32 devices in a mesh: gx: 4 (over z), gy: 8 (over y, x, core).
Axes of the slice: x: 2, y: 2, z: 4, core: 2. Of those that a mesh axis runs over, the one named last changes fastest.
Arguments:
- thickness: float32 [2048, 1024], P('gy', 'gx'), may hold values from 0.5 to 2
- driving: float32 [2, 2048, 1024], P(None, 'gy', 'gx'), may hold values from -6 to 6
- observed: float32 [2, 2048, 1024], P(None, 'gy', 'gx'), may hold values from -2 to 2
- control: float32 [32, 4096], P('gy'), may hold values from 0.5 to 1.5
- ice_mask: int32 [8, 4], replicated, may hold values 0 or 1
- tile_block: int32 [8, 4, 1], replicated, may hold values from 0 to 31
Outputs:
- vel_u: float32 [2048, 1024], P('gy', 'gx')
- vel_v: float32 [2048, 1024], P('gy', 'gx')
- grad_control: float32 [32, 4096], P('gy')
The draws below stay inside these ranges and needn't reach their ends.
Inputs may be any that keep to these rules, and one draw needn't show every extreme that they name: `tile_block`: every one of the 32 control blocks is named by at least one tile.
All inputs are finite; a program needn't handle non-finite values.
Results may differ from the reference program's by a relative error of at most 0.00015.
Values sent between devices are 32-bit elements; how exact they have to be, the bound alone decides.
No kernel may reach another device: no remote copies, remote signals or barrier semaphores. Data moves between devices by JAX's collectives and lax.ppermute only.
A program may use at most 64 MiB of HBM per device.

```python
import math
import jax
import jax.numpy as jnp
from jax import lax

TILE = 256
CPC = 4
PIC = 4
SW = 2
ADJ = 6
CT = 64
COARSE = 4096
TY = 8
TX = 4
NY = 2048
NX = 1024
K = 32


def place_ends(array, rng, least, top_value):
    index_at = [jax.random.randint(jax.random.fold_in(rng, axis), (), 0, length) for axis, length in enumerate(array.shape)]
    main_axis = array.shape.index(max(array.shape))
    neighbour = index_at[:main_axis] + [(index_at[main_axis] + 1) % array.shape[main_axis]] + index_at[main_axis + 1:]
    return array.at[tuple(index_at)].set(least).at[tuple(neighbour)].set(top_value)


def levels(rng, extent, cuts, least, largest):
    factor_of = 1.0
    for dim, blocks in cuts:
        heights = jax.random.uniform(jax.random.fold_in(jax.random.fold_in(rng, 6), dim), (blocks,), jnp.float32, least / len(cuts), largest / len(cuts))
        factor_of = factor_of * jnp.repeat(jnp.exp(heights), extent[dim] // blocks).reshape((-1,) + (1,) * (len(extent) - 1 - dim))
    return factor_of


def choose_distinct(rng, rows, count, top, lift):
    order = jax.random.permutation(jax.random.fold_in(rng, 1), count)
    favour = order
    for power in range(3):
        favour = favour * favour // count
    favour = favour * lift // count
    lots = jax.random.randint(jax.random.fold_in(rng, 2), (rows, count), 0, 4096) + favour
    sure = jax.random.permutation(jax.random.fold_in(rng, 3), rows)[jnp.arange(count) % rows]
    lots = jnp.where(jnp.arange(rows)[:, None] == sure[None, :], 1 << 14, lots)
    score = lots * count + jnp.arange(count)
    return lax.top_k(score.astype(jnp.int32), top)[1].astype(jnp.int32)


def gaussian(stream_key, shape, width, limit, cuts=(), dtype=jnp.bfloat16):
    values = jax.random.normal(stream_key, shape, jnp.float32) * width
    if len(cuts) > 0:
        values = levels(stream_key, shape, cuts, -0.22, 0.18) * values
    return jnp.clip(values, min=-limit, max=limit).astype(dtype)


def setup_inputs(seed: int = 0) -> dict:
    streams_of = jax.random.split(jax.random.key(seed), 7)
    thickness = jnp.clip(jnp.exp(math.log(2.0) - 1.3862944 * jax.random.uniform(streams_of[0], (NY, NX), jnp.float32) ** levels(streams_of[0], (NY, NX), ((0, 8), (1, 4)), -0.2, 0.2)), 0.5, 2.0)
    driving = gaussian(streams_of[1], (2, NY, NX), 1.0, 6.0, ((1, 8), (2, 4)), jnp.float32)
    observed = gaussian(streams_of[2], (2, NY, NX), 0.3, 2.0, ((1, 8), (2, 4)), jnp.float32)
    control = jnp.clip(0.5 + 1.0 * jax.random.uniform(streams_of[3], (K, COARSE), jnp.float32) ** levels(streams_of[3], (K, COARSE), ((0, 8),), -0.2, 0.2), 0.5, 1.5)
    ice_mask = place_ends((jax.random.randint(streams_of[4], (TY, TX), 0, 4) < 3).astype(jnp.int32), jax.random.fold_in(streams_of[4], 1), 0, 1)
    tile_block = choose_distinct(streams_of[5], TY * TX, K, 1, 512).reshape((TY, TX, 1))
    return dict(thickness=thickness, driving=driving, observed=observed, control=control, ice_mask=ice_mask, tile_block=tile_block)


visc_scale = 0.1
strain_floor = 0.05


def viscosity(vel_pad, thick):
    speed_x = vel_pad[0]
    speed_y = vel_pad[1]
    dudx = 0.5 * (speed_x[1:-1, 2:] - speed_x[1:-1, :-2])
    dudy = 0.5 * (speed_x[2:, 1:-1] - speed_x[:-2, 1:-1])
    dvdx = 0.5 * (speed_y[1:-1, 2:] - speed_y[1:-1, :-2])
    dvdy = 0.5 * (speed_y[2:, 1:-1] - speed_y[:-2, 1:-1])
    shear = dudy + dvdx
    strain = dudx * dudx + dvdy * dvdy + dudx * dvdy + 0.25 * shear * shear + strain_floor
    return visc_scale * thick * jnp.power(strain, -1.0 / 3.0)


def coefficients(visc_pad, friction):
    center = visc_pad[1:-1, 1:-1]
    east_w = 0.5 * (center + visc_pad[1:-1, 2:])
    west_w = 0.5 * (center + visc_pad[1:-1, :-2])
    south_w = 0.5 * (center + visc_pad[2:, 1:-1])
    north_w = 0.5 * (center + visc_pad[:-2, 1:-1])
    diag_u = friction + 4.0 * (east_w + west_w) + south_w + north_w
    diag_v = friction + east_w + west_w + 4.0 * (south_w + north_w)
    return (visc_pad, east_w, west_w, south_w, north_w, diag_u, diag_v)


def relaxation(vel_pad, stencil_coef, forcing, ice_cells):
    visc_pad, east_w, west_w, south_w, north_w, diag_u, diag_v = stencil_coef
    speed_x = vel_pad[0]
    speed_y = vel_pad[1]
    flux_p = 2.0 * visc_pad[1:-1, :] * (0.5 * (speed_y[2:, :] - speed_y[:-2, :]))
    flux_q = visc_pad[:, 1:-1] * (0.5 * (speed_y[:, 2:] - speed_y[:, :-2]))
    cross_u = 0.5 * (flux_p[:, 2:] - flux_p[:, :-2]) + 0.5 * (flux_q[2:, :] - flux_q[:-2, :])
    flux_r = 2.0 * visc_pad[:, 1:-1] * (0.5 * (speed_x[:, 2:] - speed_x[:, :-2]))
    flux_s = visc_pad[1:-1, :] * (0.5 * (speed_x[2:, :] - speed_x[:-2, :]))
    cross_v = 0.5 * (flux_r[2:, :] - flux_r[:-2, :]) + 0.5 * (flux_s[:, 2:] - flux_s[:, :-2])
    near_u = 4.0 * (east_w * speed_x[1:-1, 2:] + west_w * speed_x[1:-1, :-2]) + south_w * speed_x[2:, 1:-1] + north_w * speed_x[:-2, 1:-1]
    near_v = east_w * speed_y[1:-1, 2:] + west_w * speed_y[1:-1, :-2] + 4.0 * (south_w * speed_y[2:, 1:-1] + north_w * speed_y[:-2, 1:-1])
    new_u = ice_cells * (forcing[0] + near_u + cross_u) / diag_u
    new_v = ice_cells * (forcing[1] + near_v + cross_v) / diag_v
    return jnp.stack([new_u, new_v])


def pad_cells(field):
    return jnp.pad(field, ((0, 0), (1, 1), (1, 1)))


def reference(thickness, driving, observed, control, ice_mask, tile_block):
    blocks = tile_block[:, :, 0].astype(jnp.int32)
    rates = jnp.exp(control)[blocks]
    friction = jnp.broadcast_to(rates.reshape(TY, TX, CT, 1, CT, 1), (TY, TX, CT, CPC, CT, CPC))
    friction = friction.reshape(TY, TX, TILE, TILE).transpose(0, 2, 1, 3).reshape(NY, NX)
    ice_cells = jnp.broadcast_to(ice_mask.astype(jnp.float32)[:, None, :, None], (TY, TILE, TX, TILE)).reshape(NY, NX)
    velocity = jnp.zeros((2, NY, NX), jnp.float32)
    stencil_coef = None
    for picard in range(PIC):
        visc_cells = viscosity(pad_cells(velocity), thickness)
        stencil_coef = coefficients(jnp.pad(visc_cells, 1), friction)
        for sweep in range(SW):
            velocity = relaxation(pad_cells(velocity), stencil_coef, driving, ice_cells)
    misfit = ice_cells * (velocity - observed)
    adjoint = jnp.zeros((2, NY, NX), jnp.float32)
    for sweep in range(ADJ):
        adjoint = relaxation(pad_cells(adjoint), stencil_coef, misfit, ice_cells)
    cell_grad = -friction * (velocity[0] * adjoint[0] + velocity[1] * adjoint[1])
    tile_grad = cell_grad.reshape(TY, CT, CPC, TX, CT, CPC).sum(axis=(2, 5))
    tile_grad = tile_grad.transpose(0, 2, 1, 3).reshape(TY * TX, COARSE)
    gradient = jax.ops.segment_sum(tile_grad, blocks.reshape(-1), num_segments=K)
    return velocity[0], velocity[1], gradient
```

```python
import jax
import jax.numpy as jnp
from jax import lax
from jax.experimental import pallas as pl
from jax.experimental.pallas import tpu as pltpu
from jax.sharding import PartitionSpec as P

TILE = 256
PIC = 4
SW = 2
ADJ = 6
CT = 64
COARSE = 4096

LANES = 128
HALO = 16
OBS = 8
MARGIN = 8
TOP = MARGIN + HALO
ROWS = TILE + 2 * TOP
STEP = 16
PACK = COARSE // LANES
VMEM_LIMIT = 40 * 1024 * 1024

STRIP = ((0, HALO), (HALO, HALO), (2 * HALO, HALO), (3 * HALO, OBS), (3 * HALO + OBS, OBS))

visc_scale = 0.1
strain_floor = 0.05


def lanes_of(rows):
    return lax.broadcasted_iota(jnp.int32, (rows, LANES), 1)


def pack_kernel(thick, drive, obs, top, bottom, left, right, corners):
    fields = (thick, drive.at[0], drive.at[1], obs.at[0], obs.at[1])
    for field, (first, count) in zip(fields, STRIP):
        top[first : first + count, :] = field[0:count, :]
        bottom[first : first + count, :] = field[TILE - count : TILE, :]
    half = TILE // 2
    lane = lanes_of(half)
    for out, col, end in ((left, 0, False), (right, LANES, True)):
        packed = jnp.zeros((half, LANES), jnp.float32)
        for part in range(2):
            for field, (first, count) in zip(fields, STRIP):
                cells = field[part * half : (part + 1) * half, col : col + LANES]
                start = part * 64 + first
                source = LANES - count if end else 0
                moved = pltpu.roll(cells, (start - source) % LANES, 1)
                packed = jnp.where((lane >= start) & (lane < start + count), moved, packed)
        out[...] = packed
    lane = lanes_of(8)
    places = ((top, 0, 0), (top, LANES, LANES - HALO), (bottom, 0, 0), (bottom, LANES, LANES - HALO))
    for k, (strip, col, source) in enumerate(places):
        packed = jnp.zeros((8, LANES), jnp.float32)
        for g in range(8):
            cells = strip[8 * g : 8 * g + 8, col : col + LANES]
            moved = pltpu.roll(cells, (HALO * g - source) % LANES, 1)
            packed = jnp.where((lane >= HALO * g) & (lane < HALO * g + HALO), moved, packed)
        corners[k] = packed


def shift_east(tiles, lane):
    rolled = [pltpu.roll(t, LANES - 1, 1) for t in tiles]
    return [jnp.where(lane == LANES - 1, rolled[(c + 1) % 3], rolled[c]) for c in range(3)]


def shift_west(tiles, lane):
    rolled = [pltpu.roll(t, 1, 1) for t in tiles]
    return [jnp.where(lane == 0, rolled[(c + 2) % 3], rolled[c]) for c in range(3)]


def row_range(reach):
    wide = -(-reach // 8) * 8
    return TOP - wide, TILE + 2 * wide


def over_rows(reach, body):
    start, count = row_range(reach)

    def step(i, carry):
        body(pl.multiple_of(start + i * STEP, 8))
        return carry

    lax.fori_loop(0, count // STEP, step, 0)


def model_kernel(
    tile_block, ice_mask, gathered, thick, drive, obs, north, south, west, east, corner_nw, corner_ne, corner_sw, corner_se,
    vel_u, vel_v, sums,
    ext, fr, ice, visc, vel, coef, blocks, patch, small,
):
    tile_rows, tile_cols = ice_mask.shape
    owned = gathered.shape[1]
    row_tile = lax.axis_index("gy")
    col_tile = lax.axis_index("gx")

    fields = (thick, drive.at[0], drive.at[1], obs.at[0], obs.at[1])
    half = TILE // 2
    lane = lanes_of(half)
    lane8 = lanes_of(8)
    for f, (field, (first, count)) in enumerate(zip(fields, STRIP)):
        for c in range(2):
            cols = slice(c * LANES, (c + 1) * LANES)
            ext[f, c, TOP : TOP + TILE, :] = field[:, cols]
            ext[f, c, TOP - count : TOP, :] = north[first : first + count, cols]
            ext[f, c, TOP + TILE : TOP + TILE + count, :] = south[first : first + count, cols]
        for part in range(2):
            start = part * 64 + first
            from_east = pltpu.roll(east[...], (LANES - start) % LANES, 1)
            from_west = pltpu.roll(west[...], (2 * LANES - count - start) % LANES, 1)
            ext[f, 2, TOP + part * half : TOP + (part + 1) * half, :] = jnp.where(
                lane < count, from_east, jnp.where(lane >= LANES - count, from_west, 0.0)
            )
        for g in range(first // 8, (first + count) // 8):
            for at, lo, hi in (
                (TOP - count, corner_nw, corner_ne),
                (TOP + TILE, corner_sw, corner_se),
            ):
                from_east = pltpu.roll(hi[...], (LANES - HALO * g) % LANES, 1)
                from_west = pltpu.roll(lo[...], (2 * LANES - HALO - HALO * g) % LANES, 1)
                row = at + 8 * g - first
                ext[f, 2, row : row + 8, :] = jnp.where(
                    lane8 < HALO, from_east, jnp.where(lane8 >= LANES - HALO, from_west, 0.0)
                )

    masks = {}
    owner_row = lax.broadcasted_iota(jnp.int32, (owned, LANES), 0)
    for dr in (-1, 0, 1):
        for ds in (-1, 0, 1):
            row, col = row_tile + dr, col_tile + ds
            inside = (row >= 0) & (row < tile_rows) & (col >= 0) & (col < tile_cols)
            row = jnp.clip(row, 0, tile_rows - 1)
            col = jnp.clip(col, 0, tile_cols - 1)
            masks[dr, ds] = jnp.where(inside, ice_mask[row, col], 0).astype(jnp.float32)
            block = tile_block[row, col]
            holder = block // owned
            place = block - holder * owned
            spot = (dr + 1) * 3 + ds + 1
            for j in range(PACK) if dr == 0 else ((PACK - 2, PACK - 1) if dr < 0 else (0, 1)):
                held = gathered[holder, :, j * LANES : (j + 1) * LANES]
                blocks[spot, j : j + 1, :] = jnp.sum(jnp.where(owner_row == place, held, 0.0), axis=0, keepdims=True)
    for dr, first, count in ((-1, MARGIN, HALO), (0, TOP, TILE), (1, TOP + TILE, HALO)):
        rows_lane = lanes_of(count)
        for c in range(2):
            ice[c, first : first + count, :] = jnp.full((count, LANES), masks[dr, 0])
        ice[2, first : first + count, :] = jnp.where(
            rows_lane < HALO, masks[dr, 1], jnp.where(rows_lane >= LANES - HALO, masks[dr, -1], 0.0)
        )

    for dr, first, count, at in ((-1, PACK - 2, 2, 0), (0, 0, PACK, 4), (1, 0, 2, 68)):
        lo, mid, hi = (blocks[(dr + 1) * 3 + k, first : first + count, :] for k in range(3))
        wide = lanes_of(count)
        even = jnp.where(wide < 64, mid, jnp.where(wide < 96, pltpu.roll(hi, 64, 1), pltpu.roll(lo, 64, 1)))
        odd = jnp.where(wide < 64, pltpu.roll(mid, 64, 1), jnp.where(wide < 96, hi, lo))
        patch[pl.ds(at, count, stride=2), :] = jnp.exp(even)
        patch[pl.ds(at + 1, count, stride=2), :] = jnp.exp(odd)
    cells = patch[...]
    lane72 = lanes_of(72)
    for c in range(3):
        source = 32 * c + lane72 // 4
        if c == 2:
            source = jnp.where(lane72 < 64, source, source + 32)
        wide = jnp.take_along_axis(cells, source, axis=1)
        for j in range(4):
            fr[c, pl.ds(MARGIN + j, 72, stride=4), :] = wide

    lane = lanes_of(STEP)
    tiles = range(3)

    def load(ref, row, *lead):
        return [ref[(*lead, c, pl.ds(row, STEP), slice(None))] for c in tiles]

    def store(ref, row, values, *lead):
        for c in tiles:
            ref[(*lead, c, pl.ds(row, STEP), slice(None))] = values[c]

    def viscosity(reach, now):
        def body(row):
            thickness = load(ext, row, 0)
            if now is None:
                store(visc, row, [visc_scale * t * strain_floor ** (-1.0 / 3.0) for t in thickness])
                return
            u, v = load(vel, row, now, 0), load(vel, row, now, 1)
            u_n, v_n = load(vel, row - 1, now, 0), load(vel, row - 1, now, 1)
            u_s, v_s = load(vel, row + 1, now, 0), load(vel, row + 1, now, 1)
            u_e, u_w = shift_east(u, lane), shift_west(u, lane)
            v_e, v_w = shift_east(v, lane), shift_west(v, lane)
            result = []
            for c in tiles:
                ux, vx = u_e[c] - u_w[c], v_e[c] - v_w[c]
                uy, vy = u_s[c] - u_n[c], v_s[c] - v_n[c]
                shear = uy + vx
                strain = 0.25 * (ux * ux + vy * vy + ux * vy + 0.25 * (shear * shear)) + strain_floor
                result.append(visc_scale * thickness[c] * jnp.exp(jnp.log(strain) * (-1.0 / 3.0)))
            store(visc, row, result)

        over_rows(reach, body)

    def coefficients(row):
        m, m_n, m_s = load(visc, row), load(visc, row - 1), load(visc, row + 1)
        m_w = shift_west(m, lane)
        w = [0.5 * (m[c] + m_w[c]) for c in tiles]
        e = shift_east(w, lane)
        s = [0.5 * (m[c] + m_s[c]) for c in tiles]
        n = [0.5 * (m[c] + m_n[c]) for c in tiles]
        friction, mask = load(fr, row), load(ice, row)
        scale_u, scale_v = [], []
        for c in tiles:
            across, along = e[c] + w[c], s[c] + n[c]
            scale_u.append(mask[c] / (friction[c] + 4.0 * across + along))
            scale_v.append(mask[c] / (friction[c] + across + 4.0 * along))
        corners = []
        for shifted in (
            shift_west(m_s, lane), shift_west(m_n, lane), shift_east(m_s, lane), shift_east(m_n, lane),
        ):
            corners.append([0.5 * m[c] + 0.25 * shifted[c] for c in tiles])
            corners.append([0.25 * m[c] + 0.5 * shifted[c] for c in tiles])
        return [e, w, s, n, scale_u, scale_v] + corners

    def relaxed(row, now, k, forcing):
        e, w, s, n, scale_u, scale_v, sw_u, sw_v, nw_u, nw_v, se_u, se_v, ne_u, ne_v = k
        u, v = load(vel, row, now, 0), load(vel, row, now, 1)
        u_n, v_n = load(vel, row - 1, now, 0), load(vel, row - 1, now, 1)
        u_s, v_s = load(vel, row + 1, now, 0), load(vel, row + 1, now, 1)
        to_west_u, to_east_u, to_west_v, to_east_v = [], [], [], []
        for c in tiles:
            u4 = 4.0 * u[c]
            to_west_u.append(w[c] * u4 + (sw_u[c] * v_s[c] - nw_u[c] * v_n[c]))
            to_east_u.append(e[c] * u4 + (ne_u[c] * v_n[c] - se_u[c] * v_s[c]))
            to_west_v.append(w[c] * v[c] + (sw_v[c] * u_s[c] - nw_v[c] * u_n[c]))
            to_east_v.append(e[c] * v[c] + (ne_v[c] * u_n[c] - se_v[c] * u_s[c]))
        to_west_u, to_west_v = shift_east(to_west_u, lane), shift_east(to_west_v, lane)
        to_east_u, to_east_v = shift_west(to_east_u, lane), shift_west(to_east_v, lane)
        new_u, new_v = [], []
        for c in tiles:
            mid_u = s[c] * u_s[c] + n[c] * u_n[c]
            mid_v = 4.0 * (s[c] * v_s[c] + n[c] * v_n[c])
            new_u.append(scale_u[c] * (forcing[0][c] + mid_u + (to_west_u[c] + to_east_u[c])))
            new_v.append(scale_v[c] * (forcing[1][c] + mid_v + (to_west_v[c] + to_east_v[c])))
        return new_u, new_v

    def put(row, new, values):
        store(vel, row, values[0], new, 0)
        store(vel, row, values[1], new, 1)

    reach = HALO
    now = None
    for picard in range(PIC):
        if picard > 0:
            reach -= 1
        viscosity(reach, now)
        reach -= 1

        def first_sweep(row, now=now, new=0 if now is None else 1 - now):
            k = coefficients(row)
            for i, values in enumerate(k):
                store(coef, row, values, i)
            forcing = load(ext, row, 1), load(ext, row, 2)
            if now is None:
                put(row, new, [[k[4 + i][c] * forcing[i][c] for c in tiles] for i in range(2)])
            else:
                put(row, new, relaxed(row, now, k, forcing))

        over_rows(reach, first_sweep)
        now = 0 if now is None else 1 - now
        for sweep in range(1, SW):
            reach -= 1

            def next_sweep(row, now=now):
                k = [load(coef, row, i) for i in range(14)]
                put(row, 1 - now, relaxed(row, now, k, (load(ext, row, 1), load(ext, row, 2))))

            over_rows(reach, next_sweep)
            now = 1 - now

    final = now
    spare = (1 - now, 2)

    def first_adjoint(row):
        for i in range(2):
            u, seen, scale = load(vel, row, final, i), load(ext, row, 3 + i), load(coef, row, 4 + i)
            misfit = [u[c] - seen[c] for c in tiles]
            store(ext, row, misfit, 1 + i)
            store(vel, row, [scale[c] * misfit[c] for c in tiles], spare[0], i)

    over_rows(reach, first_adjoint)
    for i, out in enumerate((vel_u, vel_v)):
        for c in range(2):
            out[:, c * LANES : (c + 1) * LANES] = vel[final, i, c, TOP : TOP + TILE, :]
    for sweep in range(1, ADJ):
        reach -= 1

        def adjoint_sweep(row, now=spare[(sweep + 1) % 2], new=spare[sweep % 2]):
            k = [load(coef, row, i) for i in range(14)]
            put(row, new, relaxed(row, now, k, (load(ext, row, 1), load(ext, row, 2))))

        over_rows(reach, adjoint_sweep)
    last = spare[(ADJ - 1) % 2]

    def gradient(row):
        for c in range(2):
            at = (c, pl.ds(row, STEP), slice(None))
            dot = vel[(final, 0, *at)] * vel[(last, 0, *at)] + vel[(final, 1, *at)] * vel[(last, 1, *at)]
            visc[at] = -fr[at] * dot

    over_rows(0, gradient)
    down = [sum(visc[c, pl.ds(TOP + j, CT, stride=4), :] for j in range(4)) for c in range(2)]
    k = lax.broadcasted_iota(jnp.int32, (LANES, LANES), 0)
    l = lanes_of(LANES) % CT
    total = jnp.zeros((CT, LANES), jnp.float32)
    for c in range(2):
        total += jnp.dot(
            down[c],
            (k // 4 + 32 * c == l).astype(jnp.float32),
            precision=lax.Precision.HIGHEST,
            preferred_element_type=jnp.float32,
        )
    small[...] = total
    sums[...] = jnp.where(
        lanes_of(PACK) < CT, small[pl.ds(0, PACK, stride=2), :], small[pl.ds(1, PACK, stride=2), :]
    )


def collect_kernel(tile_block, gathered, out, total):
    owned = out.shape[0]
    first = lax.axis_index("gy") * owned
    tile_rows, tile_cols = tile_block.shape
    total[...] = jnp.zeros_like(total)

    def step(t, carry):
        col = t // tile_rows
        place = tile_block[t - col * tile_rows, col] - first

        @pl.when((place >= 0) & (place < owned))
        def _():
            total[place] += gathered[t]

        return carry

    lax.fori_loop(0, tile_rows * tile_cols, step, 0)
    for j in range(PACK):
        out[:, j * LANES : (j + 1) * LANES] = total[:, j, :]


def in_vmem(count):
    return [pl.BlockSpec(memory_space=pltpu.VMEM)] * count


def in_smem(count):
    return [pl.BlockSpec(memory_space=pltpu.SMEM)] * count


def per_device(thickness, driving, observed, control, ice_mask, tile_block):
    f32 = jnp.float32
    rows, cols = lax.axis_size("gy"), lax.axis_size("gx")
    tile_block = tile_block[:, :, 0]
    params = pltpu.CompilerParams(vmem_limit_bytes=VMEM_LIMIT)

    gathered = lax.all_gather(control, "gy", axis=0)
    top, bottom, left, right, corners = pl.pallas_call(
        pack_kernel,
        out_shape=(
            jax.ShapeDtypeStruct((64, TILE), f32),
            jax.ShapeDtypeStruct((64, TILE), f32),
            jax.ShapeDtypeStruct((TILE // 2, LANES), f32),
            jax.ShapeDtypeStruct((TILE // 2, LANES), f32),
            jax.ShapeDtypeStruct((4, 8, LANES), f32),
        ),
        in_specs=in_vmem(3),
        out_specs=in_vmem(5),
        compiler_params=params,
        name="pack",
    )(thickness, driving, observed)

    def moved(cells, dr, ds):
        pairs = []
        for r in range(rows):
            for s in range(cols):
                if 0 <= r + dr < rows and 0 <= s + ds < cols:
                    pairs.append((s * rows + r, (s + ds) * rows + r + dr))
        return lax.ppermute(cells, ("gx", "gy"), pairs)

    north, south = moved(bottom, 1, 0), moved(top, -1, 0)
    west, east = moved(right, 0, 1), moved(left, 0, -1)
    corner_se, corner_sw = moved(corners[0], -1, -1), moved(corners[1], -1, 1)
    corner_ne, corner_nw = moved(corners[2], 1, -1), moved(corners[3], 1, 1)

    vel_u, vel_v, sums = pl.pallas_call(
        model_kernel,
        out_shape=(
            jax.ShapeDtypeStruct((TILE, TILE), f32),
            jax.ShapeDtypeStruct((TILE, TILE), f32),
            jax.ShapeDtypeStruct((PACK, LANES), f32),
        ),
        in_specs=in_smem(2) + in_vmem(12),
        out_specs=in_vmem(3),
        scratch_shapes=[
            pltpu.VMEM((5, 3, ROWS, LANES), f32),
            pltpu.VMEM((3, ROWS, LANES), f32),
            pltpu.VMEM((3, ROWS, LANES), f32),
            pltpu.VMEM((3, ROWS, LANES), f32),
            pltpu.VMEM((3, 2, 3, ROWS, LANES), f32),
            pltpu.VMEM((14, 3, ROWS, LANES), f32),
            pltpu.VMEM((9, PACK, LANES), f32),
            pltpu.VMEM((72, LANES), f32),
            pltpu.VMEM((CT, LANES), f32),
        ],
        compiler_params=params,
        name="model",
    )(
        tile_block, ice_mask, gathered, thickness, driving, observed, north, south, west, east,
        corner_nw, corner_ne, corner_sw, corner_se,
    )

    tiles = lax.all_gather(sums, ("gx", "gy"), axis=0)
    gradient = pl.pallas_call(
        collect_kernel,
        out_shape=jax.ShapeDtypeStruct(control.shape, f32),
        in_specs=in_smem(1) + in_vmem(1),
        out_specs=pl.BlockSpec(memory_space=pltpu.VMEM),
        scratch_shapes=[pltpu.VMEM((control.shape[0], PACK, LANES), f32)],
        compiler_params=params,
        name="collect",
    )(tile_block, tiles)
    return vel_u, vel_v, gradient


def solution(mesh):
    return jax.shard_map(
        per_device,
        mesh=mesh,
        in_specs=(P("gy", "gx"), P(None, "gy", "gx"), P(None, "gy", "gx"), P("gy", None), P(), P()),
        out_specs=(P("gy", "gx"), P("gy", "gx"), P("gy", None)),
        check_vma=False,
    )
```

```python
import jax
import jax.numpy as jnp
from jax import lax
from jax.experimental import pallas as pl
from jax.experimental.pallas import tpu as pltpu
from jax.sharding import PartitionSpec as P

TILE = 256
PIC = 4
SW = 2
ADJ = 6
CT = 64
COARSE = 4096

LANES = 128
HALO = 16
OBS = 8
MARGIN = 8
TOP = MARGIN + HALO
ROWS = TILE + 2 * TOP
STEP = 32
PACK = COARSE // LANES
VMEM_LIMIT = 40 * 1024 * 1024

STRIP = ((0, HALO), (HALO, HALO), (2 * HALO, HALO), (3 * HALO, OBS), (3 * HALO + OBS, OBS))

PATCH_ROWS = ((-1, PACK - 2, 2, 0), (0, 0, PACK, 4), (1, 0, 2, CT + 4))
PATCH = CT + 8

visc_scale = 0.1
strain_floor = 0.05


def lanes_of(rows):
    return lax.broadcasted_iota(jnp.int32, (rows, LANES), 1)


def patch_lanes(count, ds):
    lane = lanes_of(count)
    return (lane < CT) if ds == 0 else ((lane >= CT) & (lane < 96) if ds > 0 else lane >= 96)


def pack_kernel(
    tile_block, control, thick, drive, obs, top, bottom, left, right, patches,
    held, owned_blocks, sems,
):
    copies = []
    for f, field in enumerate((thick, drive.at[0], drive.at[1], obs.at[0], obs.at[1])):
        copies.append(pltpu.make_async_copy(field, held.at[f], sems.at[f]))
        copies[-1].start()

    tile_rows, tile_cols = tile_block.shape
    owned = control.shape[0]
    mine = lax.axis_index("gy") * owned
    col_tile = lax.axis_index("gx")
    for j in range(PACK):
        owned_blocks[:, j, :] = control[:, j * LANES : (j + 1) * LANES]
    patches[...] = jnp.zeros_like(patches)

    def fill(target, carry):
        for dr, first, count, at in PATCH_ROWS:
            for ds in (-1, 0, 1):
                row = jnp.clip(target + dr, 0, tile_rows - 1)
                col = jnp.clip(col_tile + ds, 0, tile_cols - 1)
                place = tile_block[row, col] - mine

                @pl.when((place >= 0) & (place < owned))
                def _():
                    cells = owned_blocks[place, first : first + count, :]
                    turned = pltpu.roll(cells, CT, 1)
                    even, odd = (cells, turned) if ds == 0 else (turned, cells)
                    inside = patch_lanes(count, ds)
                    rows = pl.ds(at, count, stride=2)
                    patches[target, rows, :] += jnp.where(inside, even, 0.0)
                    rows = pl.ds(at + 1, count, stride=2)
                    patches[target, rows, :] += jnp.where(inside, odd, 0.0)

        return carry

    lax.fori_loop(0, tile_rows, fill, 0)

    for copy in copies:
        copy.wait()
    for f, (first, count) in enumerate(STRIP):
        for c in range(2):
            cols = slice(c * LANES, (c + 1) * LANES)
            top[c, first : first + count, :] = held[f, 0:count, cols]
            bottom[c, first : first + count, :] = held[f, TILE - count : TILE, cols]
    half = TILE // 2
    lane = lanes_of(half)
    for out, col, end in ((left, 0, False), (right, LANES, True)):
        packed = jnp.zeros((half, LANES), jnp.float32)
        for part in range(2):
            for f, (first, count) in enumerate(STRIP):
                cells = held[f, part * half : (part + 1) * half, col : col + LANES]
                start = part * 64 + first
                source = LANES - count if end else 0
                moved = pltpu.roll(cells, (start - source) % LANES, 1)
                packed = jnp.where((lane >= start) & (lane < start + count), moved, packed)
        out[...] = packed


def frame_cells(west, east, rows, start, count):
    from_east = pltpu.roll(east[rows, :], (LANES - start) % LANES, 1)
    from_west = pltpu.roll(west[rows, :], (2 * LANES - count - start) % LANES, 1)
    lane = lanes_of(from_east.shape[0])
    return jnp.where(lane < count, from_east, jnp.where(lane >= LANES - count, from_west, 0.0))


def corner_kernel(top, bottom, west, east, top_wide, bottom_wide):
    half = TILE // 2
    for narrow, wide, part in ((top, top_wide, 0), (bottom, bottom_wide, 1)):
        for c in range(2):
            wide[c] = narrow[c]
        for first, count in STRIP:
            rows = slice(half - count, half) if part else slice(0, count)
            wide[2, first : first + count, :] = frame_cells(west, east, rows, part * 64 + first, count)


def shift_east(tiles, lane):
    rolled = [pltpu.roll(t, LANES - 1, 1) for t in tiles]
    return [jnp.where(lane == LANES - 1, rolled[(c + 1) % 3], rolled[c]) for c in range(3)]


def shift_west(tiles, lane):
    rolled = [pltpu.roll(t, 1, 1) for t in tiles]
    return [jnp.where(lane == 0, rolled[(c + 2) % 3], rolled[c]) for c in range(3)]


def row_range(reach):
    wide = HALO if reach > 0 else 0
    return TOP - wide, TILE + 2 * wide


def over_rows(reach, body):
    start, count = row_range(reach)

    def step(i, carry):
        body(pl.multiple_of(start + i * STEP, 8))
        return carry

    lax.fori_loop(0, count // STEP, step, 0)


def model_kernel(
    ice_mask, patches, thick, drive, obs, north, south, west, east,
    vel_u, vel_v, sums,
    ext, fr, ice, visc, vel, coef, small,
):
    tile_rows, tile_cols = ice_mask.shape
    row_tile = lax.axis_index("gy")
    col_tile = lax.axis_index("gx")

    cells = jnp.exp(sum(patches[j] for j in range(tile_rows)))
    lane = lanes_of(PATCH)
    for c in range(3):
        source = 32 * c + lane // 4
        if c == 2:
            source = jnp.where(lane < CT, source, source + 32)
        wide = jnp.take_along_axis(cells, source, axis=1)
        for j in range(4):
            fr[c, pl.ds(MARGIN + j, PATCH, stride=4), :] = wide

    fields = (thick, drive.at[0], drive.at[1], obs.at[0], obs.at[1])
    half = TILE // 2
    for f, (field, (first, count)) in enumerate(zip(fields, STRIP)):
        for c in range(3):
            if c < 2:
                ext[f, c, TOP : TOP + TILE, :] = field[:, c * LANES : (c + 1) * LANES]
            ext[f, c, TOP - count : TOP, :] = north[c, first : first + count, :]
            ext[f, c, TOP + TILE : TOP + TILE + count, :] = south[c, first : first + count, :]
        for part in range(2):
            ext[f, 2, TOP + part * half : TOP + (part + 1) * half, :] = frame_cells(
                west, east, slice(None), part * 64 + first, count
            )

    for dr, first, count in ((-1, MARGIN, HALO), (0, TOP, TILE), (1, TOP + TILE, HALO)):
        masks = []
        for ds in (-1, 0, 1):
            row, col = row_tile + dr, col_tile + ds
            inside = (row >= 0) & (row < tile_rows) & (col >= 0) & (col < tile_cols)
            row = jnp.clip(row, 0, tile_rows - 1)
            col = jnp.clip(col, 0, tile_cols - 1)
            masks.append(jnp.where(inside, ice_mask[row, col], 0).astype(jnp.float32))
        lane = lanes_of(count)
        for c in range(2):
            ice[c, first : first + count, :] = jnp.full((count, LANES), masks[1])
        ice[2, first : first + count, :] = jnp.where(
            lane < HALO, masks[2], jnp.where(lane >= LANES - HALO, masks[0], 0.0)
        )

    lane = lanes_of(STEP)
    tiles = range(3)

    def load(ref, row, *lead):
        return [ref[(*lead, c, pl.ds(row, STEP), slice(None))] for c in tiles]

    def store(ref, row, values, *lead):
        for c in tiles:
            ref[(*lead, c, pl.ds(row, STEP), slice(None))] = values[c]

    def viscosity(reach, now):
        def body(row):
            thickness = load(ext, row, 0)
            if now is None:
                store(visc, row, [visc_scale * t * strain_floor ** (-1.0 / 3.0) for t in thickness])
                return
            u, v = load(vel, row, now, 0), load(vel, row, now, 1)
            u_n, v_n = load(vel, row - 1, now, 0), load(vel, row - 1, now, 1)
            u_s, v_s = load(vel, row + 1, now, 0), load(vel, row + 1, now, 1)
            u_e, u_w = shift_east(u, lane), shift_west(u, lane)
            v_e, v_w = shift_east(v, lane), shift_west(v, lane)
            result = []
            for c in tiles:
                ux, vx = u_e[c] - u_w[c], v_e[c] - v_w[c]
                uy, vy = u_s[c] - u_n[c], v_s[c] - v_n[c]
                shear = uy + vx
                strain = 0.25 * (ux * ux + vy * vy + ux * vy + 0.25 * (shear * shear)) + strain_floor
                result.append(visc_scale * thickness[c] * jnp.exp(jnp.log(strain) * (-1.0 / 3.0)))
            store(visc, row, result)

        over_rows(reach, body)

    def coefficients(row):
        m, m_n, m_s = load(visc, row), load(visc, row - 1), load(visc, row + 1)
        m_w = shift_west(m, lane)
        w = [0.5 * (m[c] + m_w[c]) for c in tiles]
        e = shift_east(w, lane)
        s = [0.5 * (m[c] + m_s[c]) for c in tiles]
        n = [0.5 * (m[c] + m_n[c]) for c in tiles]
        friction, mask = load(fr, row), load(ice, row)
        scale_u, scale_v = [], []
        for c in tiles:
            across, along = e[c] + w[c], s[c] + n[c]
            scale_u.append(mask[c] / (friction[c] + 4.0 * across + along))
            scale_v.append(mask[c] / (friction[c] + across + 4.0 * along))
        corners = []
        for shifted in (
            shift_west(m_s, lane), shift_west(m_n, lane), shift_east(m_s, lane), shift_east(m_n, lane),
        ):
            corners.append([0.5 * m[c] + 0.25 * shifted[c] for c in tiles])
            corners.append([0.25 * m[c] + 0.5 * shifted[c] for c in tiles])
        return [e, w, s, n, scale_u, scale_v] + corners

    def relaxed(row, now, k, forcing):
        e, w, s, n, scale_u, scale_v, sw_u, sw_v, nw_u, nw_v, se_u, se_v, ne_u, ne_v = k
        u, v = load(vel, row, now, 0), load(vel, row, now, 1)
        u_n, v_n = load(vel, row - 1, now, 0), load(vel, row - 1, now, 1)
        u_s, v_s = load(vel, row + 1, now, 0), load(vel, row + 1, now, 1)
        to_west_u, to_east_u, to_west_v, to_east_v = [], [], [], []
        for c in tiles:
            u4 = 4.0 * u[c]
            to_west_u.append(w[c] * u4 + (sw_u[c] * v_s[c] - nw_u[c] * v_n[c]))
            to_east_u.append(e[c] * u4 + (ne_u[c] * v_n[c] - se_u[c] * v_s[c]))
            to_west_v.append(w[c] * v[c] + (sw_v[c] * u_s[c] - nw_v[c] * u_n[c]))
            to_east_v.append(e[c] * v[c] + (ne_v[c] * u_n[c] - se_v[c] * u_s[c]))
        to_west_u, to_west_v = shift_east(to_west_u, lane), shift_east(to_west_v, lane)
        to_east_u, to_east_v = shift_west(to_east_u, lane), shift_west(to_east_v, lane)
        new_u, new_v = [], []
        for c in tiles:
            mid_u = s[c] * u_s[c] + n[c] * u_n[c]
            mid_v = 4.0 * (s[c] * v_s[c] + n[c] * v_n[c])
            new_u.append(scale_u[c] * (forcing[0][c] + mid_u + (to_west_u[c] + to_east_u[c])))
            new_v.append(scale_v[c] * (forcing[1][c] + mid_v + (to_west_v[c] + to_east_v[c])))
        return new_u, new_v

    def put(row, new, values):
        store(vel, row, values[0], new, 0)
        store(vel, row, values[1], new, 1)

    reach = HALO
    now = None
    for picard in range(PIC):
        if picard > 0:
            reach -= 1
        viscosity(reach, now)
        reach -= 1

        def first_sweep(row, now=now, new=0 if now is None else 1 - now):
            k = coefficients(row)
            for i, values in enumerate(k):
                store(coef, row, values, i)
            forcing = load(ext, row, 1), load(ext, row, 2)
            if now is None:
                put(row, new, [[k[4 + i][c] * forcing[i][c] for c in tiles] for i in range(2)])
            else:
                put(row, new, relaxed(row, now, k, forcing))

        over_rows(reach, first_sweep)
        now = 0 if now is None else 1 - now
        for sweep in range(1, SW):
            reach -= 1

            def next_sweep(row, now=now):
                k = [load(coef, row, i) for i in range(14)]
                put(row, 1 - now, relaxed(row, now, k, (load(ext, row, 1), load(ext, row, 2))))

            over_rows(reach, next_sweep)
            now = 1 - now

    final = now
    spare = (1 - now, 2)

    def first_adjoint(row):
        for i in range(2):
            u, seen, scale = load(vel, row, final, i), load(ext, row, 3 + i), load(coef, row, 4 + i)
            misfit = [u[c] - seen[c] for c in tiles]
            store(ext, row, misfit, 1 + i)
            store(vel, row, [scale[c] * misfit[c] for c in tiles], spare[0], i)

    over_rows(reach, first_adjoint)
    for i, out in enumerate((vel_u, vel_v)):
        for c in range(2):
            out[:, c * LANES : (c + 1) * LANES] = vel[final, i, c, TOP : TOP + TILE, :]
    for sweep in range(1, ADJ):
        reach -= 1

        def adjoint_sweep(row, now=spare[(sweep + 1) % 2], new=spare[sweep % 2]):
            k = [load(coef, row, i) for i in range(14)]
            put(row, new, relaxed(row, now, k, (load(ext, row, 1), load(ext, row, 2))))

        over_rows(reach, adjoint_sweep)
    last = spare[(ADJ - 1) % 2]

    def gradient(row):
        for c in range(2):
            at = (c, pl.ds(row, STEP), slice(None))
            dot = vel[(final, 0, *at)] * vel[(last, 0, *at)] + vel[(final, 1, *at)] * vel[(last, 1, *at)]
            visc[at] = -fr[at] * dot

    over_rows(0, gradient)
    down = [sum(visc[c, pl.ds(TOP + j, CT, stride=4), :] for j in range(4)) for c in range(2)]
    k = lax.broadcasted_iota(jnp.int32, (LANES, LANES), 0)
    l = lanes_of(LANES) % CT
    total = jnp.zeros((CT, LANES), jnp.float32)
    for c in range(2):
        total += jnp.dot(
            down[c],
            (k // 4 + 32 * c == l).astype(jnp.float32),
            precision=lax.Precision.HIGHEST,
            preferred_element_type=jnp.float32,
        )
    small[...] = total
    sums[...] = jnp.where(
        lanes_of(PACK) < CT, small[pl.ds(0, PACK, stride=2), :], small[pl.ds(1, PACK, stride=2), :]
    )


def pick_kernel(tile_block, gathered, out):
    owned = out.shape[0]
    first = lax.axis_index("gy") * owned
    col_tile = lax.axis_index("gx")
    out[...] = jnp.zeros_like(out)

    def step(row, carry):
        place = tile_block[row, col_tile] - first

        @pl.when((place >= 0) & (place < owned))
        def _():
            out[place] += gathered[row]

        return carry

    lax.fori_loop(0, tile_block.shape[0], step, 0)


def add_kernel(parts, out):
    total = sum(parts[i] for i in range(parts.shape[0]))
    for j in range(PACK):
        out[:, j * LANES : (j + 1) * LANES] = total[:, j, :]


def in_vmem(count):
    return [pl.BlockSpec(memory_space=pltpu.VMEM)] * count


def in_smem(count):
    return [pl.BlockSpec(memory_space=pltpu.SMEM)] * count


def per_device(thickness, driving, observed, control, ice_mask, tile_block):
    f32 = jnp.float32
    rows = lax.axis_size("gy")
    tile_block = tile_block[:, :, 0]
    params = pltpu.CompilerParams(vmem_limit_bytes=VMEM_LIMIT)

    def shape(*sizes):
        return jax.ShapeDtypeStruct(sizes, f32)

    top, bottom, left, right, patches = pl.pallas_call(
        pack_kernel,
        out_shape=(
            shape(2, 64, LANES), shape(2, 64, LANES), shape(TILE // 2, LANES), shape(TILE // 2, LANES),
            shape(rows, PATCH, LANES),
        ),
        in_specs=in_smem(1) + in_vmem(1) + [pl.BlockSpec(memory_space=pltpu.HBM)] * 3,
        out_specs=in_vmem(5),
        scratch_shapes=[
            pltpu.VMEM((5, TILE, TILE), f32),
            pltpu.VMEM((control.shape[0], PACK, LANES), f32),
            pltpu.SemaphoreType.DMA((5,)),
        ],
        compiler_params=params,
        name="pack",
    )(tile_block, control, thickness, driving, observed)

    def moved(cells, axis, step):
        count = lax.axis_size(axis)
        return lax.ppermute(cells, axis, [(i, i + step) for i in range(count) if 0 <= i + step < count])

    west, east = moved(right, "gx", 1), moved(left, "gx", -1)
    patches = lax.all_to_all(patches, "gy", 0, 0, tiled=True)
    top, bottom = pl.pallas_call(
        corner_kernel,
        out_shape=(shape(3, 64, LANES), shape(3, 64, LANES)),
        in_specs=in_vmem(4),
        out_specs=in_vmem(2),
        compiler_params=params,
        name="corners",
    )(top, bottom, west, east)
    north, south = moved(bottom, "gy", 1), moved(top, "gy", -1)

    vel_u, vel_v, sums = pl.pallas_call(
        model_kernel,
        out_shape=(shape(TILE, TILE), shape(TILE, TILE), shape(PACK, LANES)),
        in_specs=in_smem(1) + in_vmem(8),
        out_specs=in_vmem(3),
        scratch_shapes=[
            pltpu.VMEM((5, 3, ROWS, LANES), f32),
            pltpu.VMEM((3, ROWS, LANES), f32),
            pltpu.VMEM((3, ROWS, LANES), f32),
            pltpu.VMEM((3, ROWS, LANES), f32),
            pltpu.VMEM((3, 2, 3, ROWS, LANES), f32),
            pltpu.VMEM((14, 3, ROWS, LANES), f32),
            pltpu.VMEM((CT, LANES), f32),
        ],
        compiler_params=params,
        name="model",
    )(ice_mask, patches, thickness, driving, observed, north, south, west, east)

    owned = pl.pallas_call(
        pick_kernel,
        out_shape=shape(control.shape[0], PACK, LANES),
        in_specs=in_smem(1) + in_vmem(1),
        out_specs=pl.BlockSpec(memory_space=pltpu.VMEM),
        compiler_params=params,
        name="pick",
    )(tile_block, lax.all_gather(sums, "gy", axis=0))
    gradient = pl.pallas_call(
        add_kernel,
        out_shape=shape(*control.shape),
        in_specs=in_vmem(1),
        out_specs=pl.BlockSpec(memory_space=pltpu.VMEM),
        compiler_params=params,
        name="add",
    )(lax.all_gather(owned, "gx", axis=0))
    return vel_u, vel_v, gradient


def solution(mesh):
    return jax.shard_map(
        per_device,
        mesh=mesh,
        in_specs=(P("gy", "gx"), P(None, "gy", "gx"), P(None, "gy", "gx"), P("gy", None), P(), P()),
        out_specs=(P("gy", "gx"), P("gy", "gx"), P("gy", None)),
        check_vma=False,
    )
```

```python
import jax
import jax.numpy as jnp
from jax import lax
from jax.experimental import pallas as pl
from jax.experimental.pallas import tpu as pltpu
from jax.sharding import PartitionSpec as P

TILE = 256
PIC = 4
SW = 2
ADJ = 6
CT = 64
COARSE = 4096

LANES = 128
HALO = 16
OBS = 8
MARGIN = 8
TOP = MARGIN + HALO
ROWS = TILE + 2 * TOP
PACK = COARSE // LANES
VMEM_LIMIT = 40 * 1024 * 1024
PACK_VMEM_LIMIT = 62 * 1024 * 1024

STRIP = ((0, HALO), (HALO, HALO), (2 * HALO, HALO), (3 * HALO, OBS), (3 * HALO + OBS, OBS))

PATCH_ROWS = ((-1, PACK - 2, 2, 0), (0, 0, PACK, 4), (1, 0, 2, CT + 4))
PATCH = CT + 8

visc_scale = 0.1
strain_floor = 0.05


def lanes_of(rows):
    return lax.broadcasted_iota(jnp.int32, (rows, LANES), 1)


def patch_lanes(count, ds):
    lane = lanes_of(count)
    return (lane < CT) if ds == 0 else ((lane >= CT) & (lane < 96) if ds > 0 else lane >= 96)


def pack_kernel(
    tile_block, control, thick, drive, obs, top, bottom, left, right, patches,
    held, owned_blocks, sems,
):
    copies = []
    for f, field in enumerate((thick, drive.at[0], drive.at[1], obs.at[0], obs.at[1])):
        copies.append(pltpu.make_async_copy(field, held.at[f], sems.at[f]))
        copies[-1].start()

    tile_cols, tile_rows = tile_block.shape
    owned = control.shape[0]
    mine = lax.axis_index("gy") * owned
    col_tile = lax.axis_index("gx")
    for j in range(PACK):
        owned_blocks[:, j, :] = control[:, j * LANES : (j + 1) * LANES]
    patches[...] = jnp.zeros_like(patches)

    def fill(target, carry):
        for dr, first, count, at in PATCH_ROWS:
            for ds in (-1, 0, 1):
                row = jnp.clip(target + dr, 0, tile_rows - 1)
                col = jnp.clip(col_tile + ds, 0, tile_cols - 1)
                place = tile_block[col, row] - mine

                @pl.when((place >= 0) & (place < owned))
                def _():
                    cells = owned_blocks[place, first : first + count, :]
                    turned = pltpu.roll(cells, CT, 1)
                    even, odd = (cells, turned) if ds == 0 else (turned, cells)
                    inside = patch_lanes(count, ds)
                    rows = pl.ds(at, count, stride=2)
                    patches[target, rows, :] += jnp.where(inside, even, 0.0)
                    rows = pl.ds(at + 1, count, stride=2)
                    patches[target, rows, :] += jnp.where(inside, odd, 0.0)

        return carry

    lax.fori_loop(0, tile_rows, fill, 0)

    for copy in copies:
        copy.wait()
    for f, (first, count) in enumerate(STRIP):
        for c in range(2):
            cols = slice(c * LANES, (c + 1) * LANES)
            top[c, first : first + count, :] = held[f, 0:count, cols]
            bottom[c, first : first + count, :] = held[f, TILE - count : TILE, cols]
    half = TILE // 2
    lane = lanes_of(half)
    for out, col, end in ((left, 0, False), (right, LANES, True)):
        packed = jnp.zeros((half, LANES), jnp.float32)
        for part in range(2):
            for f, (first, count) in enumerate(STRIP):
                cells = held[f, part * half : (part + 1) * half, col : col + LANES]
                start = part * 64 + first
                source = LANES - count if end else 0
                moved = pltpu.roll(cells, (start - source) % LANES, 1)
                packed = jnp.where((lane >= start) & (lane < start + count), moved, packed)
        out[...] = packed


def frame_cells(west, east, rows, start, count):
    from_east = pltpu.roll(east[rows, :], (LANES - start) % LANES, 1)
    from_west = pltpu.roll(west[rows, :], (2 * LANES - count - start) % LANES, 1)
    lane = lanes_of(from_east.shape[0])
    return jnp.where(lane < count, from_east, jnp.where(lane >= LANES - count, from_west, 0.0))


def corner_kernel(top, bottom, west, east, top_wide, bottom_wide):
    half = TILE // 2
    for narrow, wide, part in ((top, top_wide, 0), (bottom, bottom_wide, 1)):
        for c in range(2):
            wide[c] = narrow[c]
        for first, count in STRIP:
            rows = slice(half - count, half) if part else slice(0, count)
            wide[2, first : first + count, :] = frame_cells(west, east, rows, part * 64 + first, count)


def shift_east(tiles, lane):
    rolled = [pltpu.roll(t, LANES - 1, 1) for t in tiles]
    return [jnp.where(lane == LANES - 1, rolled[(c + 1) % 3], rolled[c]) for c in range(3)]


def shift_west(tiles, lane):
    rolled = [pltpu.roll(t, 1, 1) for t in tiles]
    return [jnp.where(lane == 0, rolled[(c + 2) % 3], rolled[c]) for c in range(3)]


def over_rows(framed, body):
    start, count, step = (MARGIN, TILE + 2 * HALO, 48) if framed else (TOP, TILE, 64)

    def block(i, carry):
        body(pl.multiple_of(start + i * step, 8), step)
        return carry

    lax.fori_loop(0, count // step, block, 0)


def model_kernel(
    ice_mask, patches, thick, drive, obs, north, south, west, east,
    vel_u, vel_v, sums,
    ext, fr, ice, visc, vel, coef, small, sems,
):
    tile_cols, tile_rows = ice_mask.shape
    row_tile = lax.axis_index("gy")
    col_tile = lax.axis_index("gx")

    cells = jnp.exp(sum(patches[j] for j in range(tile_rows)))
    lane = lanes_of(PATCH)
    for c in range(3):
        source = 32 * c + lane // 4
        if c == 2:
            source = jnp.where(lane < CT, source, source + 32)
        wide = jnp.take_along_axis(cells, source, axis=1)
        for j in range(4):
            fr[c, pl.ds(MARGIN + j, PATCH, stride=4), :] = wide

    fields = (thick, drive.at[0], drive.at[1], obs.at[0], obs.at[1])
    half = TILE // 2
    for f, (field, (first, count)) in enumerate(zip(fields, STRIP)):
        for c in range(3):
            if c < 2:
                ext[f, c, TOP : TOP + TILE, :] = field[:, c * LANES : (c + 1) * LANES]
            ext[f, c, TOP - count : TOP, :] = north[c, first : first + count, :]
            ext[f, c, TOP + TILE : TOP + TILE + count, :] = south[c, first : first + count, :]
        for part in range(2):
            ext[f, 2, TOP + part * half : TOP + (part + 1) * half, :] = frame_cells(
                west, east, slice(None), part * 64 + first, count
            )

    for dr, first, count in ((-1, MARGIN, HALO), (0, TOP, TILE), (1, TOP + TILE, HALO)):
        masks = []
        for ds in (-1, 0, 1):
            row, col = row_tile + dr, col_tile + ds
            inside = (row >= 0) & (row < tile_rows) & (col >= 0) & (col < tile_cols)
            row = jnp.clip(row, 0, tile_rows - 1)
            col = jnp.clip(col, 0, tile_cols - 1)
            masks.append(jnp.where(inside, ice_mask[col, row], 0).astype(jnp.float32))
        lane = lanes_of(count)
        for c in range(2):
            ice[c, first : first + count, :] = jnp.full((count, LANES), masks[1])
        ice[2, first : first + count, :] = jnp.where(
            lane < HALO, masks[2], jnp.where(lane >= LANES - HALO, masks[0], 0.0)
        )

    tiles = range(3)

    def load(ref, at, *lead):
        return [ref[(*lead, c, at, slice(None))] for c in tiles]

    def store(ref, at, values, *lead):
        for c in tiles:
            ref[(*lead, c, at, slice(None))] = values[c]

    def load_around(row, step, now):
        rows = [pl.ds(row, step), pl.ds(row - 1, step), pl.ds(row + 1, step)]
        return [load(vel, at, now, i) for i in range(2) for at in rows]

    def first_viscosity(row, step):
        at = pl.ds(row, step)
        store(visc, at, [visc_scale * strain_floor ** (-1.0 / 3.0) * t for t in load(ext, at, 0)])

    def viscosity(row, step):
        at, lane = pl.ds(row, step), lanes_of(step)
        thickness = load(ext, at, 0)
        u, u_n, u_s, v, v_n, v_s = load_around(row, step, 1)
        u_e, u_w = shift_east(u, lane), shift_west(u, lane)
        v_e, v_w = shift_east(v, lane), shift_west(v, lane)
        result = []
        for c in tiles:
            ux, vx = u_e[c] - u_w[c], v_e[c] - v_w[c]
            uy, vy = u_s[c] - u_n[c], v_s[c] - v_n[c]
            shear = uy + vx
            strain = 0.25 * (ux * ux + vy * vy + ux * vy + 0.25 * (shear * shear)) + strain_floor
            result.append(visc_scale * thickness[c] * jnp.exp(jnp.log(strain) * (-1.0 / 3.0)))
        store(visc, at, result)

    def coefficients(row, step):
        at, lane = pl.ds(row, step), lanes_of(step)
        m, m_n, m_s = load(visc, at), load(visc, pl.ds(row - 1, step)), load(visc, pl.ds(row + 1, step))
        m_w = shift_west(m, lane)
        w = [0.5 * (m[c] + m_w[c]) for c in tiles]
        e = shift_east(w, lane)
        s = [0.5 * (m[c] + m_s[c]) for c in tiles]
        n = [0.5 * (m[c] + m_n[c]) for c in tiles]
        friction, mask = load(fr, at), load(ice, at)
        scale_u, scale_v = [], []
        for c in tiles:
            across, along = e[c] + w[c], s[c] + n[c]
            scale_u.append(mask[c] / (friction[c] + 4.0 * across + along))
            scale_v.append(mask[c] / (friction[c] + across + 4.0 * along))
        corners = []
        for shifted in (
            shift_west(m_s, lane), shift_west(m_n, lane), shift_east(m_s, lane), shift_east(m_n, lane),
        ):
            corners.append([0.5 * m[c] + 0.25 * shifted[c] for c in tiles])
            corners.append([0.25 * m[c] + 0.5 * shifted[c] for c in tiles])
        k = [e, w, s, n, scale_u, scale_v] + corners
        for i, values in enumerate(k):
            store(coef, at, values, i)
        return k

    def relax(row, step, k, now, new):
        at, lane = pl.ds(row, step), lanes_of(step)
        e, w, s, n, scale_u, scale_v, sw_u, sw_v, nw_u, nw_v, se_u, se_v, ne_u, ne_v = k
        u, u_n, u_s, v, v_n, v_s = load_around(row, step, now)
        to_west_u, to_east_u, to_west_v, to_east_v = [], [], [], []
        for c in tiles:
            u4 = 4.0 * u[c]
            to_west_u.append(w[c] * u4 + (sw_u[c] * v_s[c] - nw_u[c] * v_n[c]))
            to_east_u.append(e[c] * u4 + (ne_u[c] * v_n[c] - se_u[c] * v_s[c]))
            to_west_v.append(w[c] * v[c] + (sw_v[c] * u_s[c] - nw_v[c] * u_n[c]))
            to_east_v.append(e[c] * v[c] + (ne_v[c] * u_n[c] - se_v[c] * u_s[c]))
        to_west_u, to_west_v = shift_east(to_west_u, lane), shift_east(to_west_v, lane)
        to_east_u, to_east_v = shift_west(to_east_u, lane), shift_west(to_east_v, lane)
        right_u, right_v = load(ext, at, 1), load(ext, at, 2)
        new_u, new_v = [], []
        for c in tiles:
            mid_u = s[c] * u_s[c] + n[c] * u_n[c]
            mid_v = 4.0 * (s[c] * v_s[c] + n[c] * v_n[c])
            new_u.append(scale_u[c] * (right_u[c] + mid_u + (to_west_u[c] + to_east_u[c])))
            new_v.append(scale_v[c] * (right_v[c] + mid_v + (to_west_v[c] + to_east_v[c])))
        store(vel, at, new_u, new, 0)
        store(vel, at, new_v, new, 1)

    def sweep(framed, now, new):
        def body(row, step):
            at = pl.ds(row, step)
            relax(row, step, [load(coef, at, i) for i in range(14)], now, new)

        over_rows(framed, body)

    def first_start(row, step):
        k = coefficients(row, step)
        at = pl.ds(row, step)
        for i in range(2):
            right = load(ext, at, 1 + i)
            store(vel, at, [k[4 + i][c] * right[c] for c in tiles], 0, i)

    over_rows(True, first_viscosity)
    over_rows(True, first_start)
    sweep(True, 0, 1)

    def iteration(i, carry):
        over_rows(True, viscosity)
        over_rows(True, lambda row, step: relax(row, step, coefficients(row, step), 1, 0))
        sweep(True, 0, 1)
        return carry

    lax.fori_loop(1, PIC, iteration, 0)
    copies = []
    for i, out in enumerate((vel_u, vel_v)):
        for c in range(2):
            copies.append(
                pltpu.make_async_copy(
                    vel.at[1, i, c, TOP : TOP + TILE, :], out.at[:, c * LANES : (c + 1) * LANES], sems.at[2 * i + c]
                )
            )
            copies[-1].start()

    def first_adjoint(row, step):
        at = pl.ds(row, step)
        for i in range(2):
            u, seen, scale = load(vel, at, 1, i), load(ext, at, 3 + i), load(coef, at, 4 + i)
            misfit = [u[c] - seen[c] for c in tiles]
            store(ext, at, misfit, 1 + i)
            store(vel, at, [scale[c] * misfit[c] for c in tiles], 2, i)

    over_rows(True, first_adjoint)

    def two_sweeps(i, carry):
        sweep(True, 2, 0)
        sweep(True, 0, 2)
        return carry

    lax.fori_loop(0, (ADJ - 2) // 2, two_sweeps, 0)
    sweep(False, 2, 0)

    def gradient(row, step):
        for c in range(2):
            at = (c, pl.ds(row, step), slice(None))
            visc[at] = -fr[at] * (vel[(1, 0, *at)] * vel[(0, 0, *at)] + vel[(1, 1, *at)] * vel[(0, 1, *at)])

    over_rows(False, gradient)
    down = [sum(visc[c, pl.ds(TOP + j, CT, stride=4), :] for j in range(4)) for c in range(2)]
    k = lax.broadcasted_iota(jnp.int32, (LANES, LANES), 0)
    l = lanes_of(LANES) % CT
    total = jnp.zeros((CT, LANES), jnp.float32)
    for c in range(2):
        total += jnp.dot(
            down[c],
            (k // 4 + 32 * c == l).astype(jnp.float32),
            precision=lax.Precision.HIGHEST,
            preferred_element_type=jnp.float32,
        )
    small[...] = total
    packed = jnp.where(
        lanes_of(PACK) < CT, small[pl.ds(0, PACK, stride=2), :], small[pl.ds(1, PACK, stride=2), :]
    )
    for j in range(sums.shape[0]):
        sums[j] = packed
    for copy in copies:
        copy.wait()


def pick_kernel(tile_block, gathered, out, total):
    owned = total.shape[0]
    first = lax.axis_index("gy") * owned
    col_tile = lax.axis_index("gx")
    total[...] = jnp.zeros_like(total)

    def step(row, carry):
        place = tile_block[col_tile, row] - first

        @pl.when((place >= 0) & (place < owned))
        def _():
            total[place] += gathered[row]

        return carry

    lax.fori_loop(0, tile_block.shape[1], step, 0)
    for j in range(out.shape[0]):
        out[j] = total[...]


def add_kernel(parts, out):
    total = sum(parts[i] for i in range(parts.shape[0]))
    for j in range(PACK):
        out[:, j * LANES : (j + 1) * LANES] = total[:, j, :]


def in_vmem(count):
    return [pl.BlockSpec(memory_space=pltpu.VMEM)] * count


def in_smem(count):
    return [pl.BlockSpec(memory_space=pltpu.SMEM)] * count


def per_device(thickness, driving, observed, control, ice_mask, tile_block):
    f32 = jnp.float32
    rows, cols = lax.axis_size("gy"), lax.axis_size("gx")
    tile_block, ice_mask = tile_block[:, :, 0].T, ice_mask.T
    params = pltpu.CompilerParams(vmem_limit_bytes=VMEM_LIMIT)

    def shape(*sizes):
        return jax.ShapeDtypeStruct(sizes, f32)

    top, bottom, left, right, patches = pl.pallas_call(
        pack_kernel,
        out_shape=(
            shape(2, 64, LANES), shape(2, 64, LANES), shape(TILE // 2, LANES), shape(TILE // 2, LANES),
            shape(rows, PATCH, LANES),
        ),
        in_specs=in_smem(1) + in_vmem(1) + [pl.BlockSpec(memory_space=pltpu.HBM)] * 3,
        out_specs=in_vmem(5),
        scratch_shapes=[
            pltpu.VMEM((5, TILE, TILE), f32),
            pltpu.VMEM((control.shape[0], PACK, LANES), f32),
            pltpu.SemaphoreType.DMA((5,)),
        ],
        compiler_params=pltpu.CompilerParams(vmem_limit_bytes=PACK_VMEM_LIMIT),
        name="pack",
    )(tile_block, control, thickness, driving, observed)

    def moved(cells, axis, step):
        count = lax.axis_size(axis)
        return lax.ppermute(cells, axis, [(i, i + step) for i in range(count) if 0 <= i + step < count])

    west, east = moved(right, "gx", 1), moved(left, "gx", -1)
    patches = lax.all_to_all(patches, "gy", 0, 0, tiled=True)
    top, bottom = pl.pallas_call(
        corner_kernel,
        out_shape=(shape(3, 64, LANES), shape(3, 64, LANES)),
        in_specs=in_vmem(4),
        out_specs=in_vmem(2),
        compiler_params=params,
        name="corners",
    )(top, bottom, west, east)
    north, south = moved(bottom, "gy", 1), moved(top, "gy", -1)

    vel_u, vel_v, sums = pl.pallas_call(
        model_kernel,
        out_shape=(shape(TILE, TILE), shape(TILE, TILE), shape(rows, PACK, LANES)),
        in_specs=in_smem(1) + in_vmem(8),
        out_specs=[pl.BlockSpec(memory_space=pltpu.HBM)] * 2 + in_vmem(1),
        scratch_shapes=[
            pltpu.VMEM((5, 3, ROWS, LANES), f32),
            pltpu.VMEM((3, ROWS, LANES), f32),
            pltpu.VMEM((3, ROWS, LANES), f32),
            pltpu.VMEM((3, ROWS, LANES), f32),
            pltpu.VMEM((3, 2, 3, ROWS, LANES), f32),
            pltpu.VMEM((14, 3, ROWS, LANES), f32),
            pltpu.VMEM((CT, LANES), f32),
            pltpu.SemaphoreType.DMA((4,)),
        ],
        compiler_params=params,
        name="model",
    )(ice_mask, patches, thickness, driving, observed, north, south, west, east)

    owned = (control.shape[0], PACK, LANES)
    parts = pl.pallas_call(
        pick_kernel,
        out_shape=shape(cols, *owned),
        in_specs=in_smem(1) + in_vmem(1),
        out_specs=pl.BlockSpec(memory_space=pltpu.VMEM),
        scratch_shapes=[pltpu.VMEM(owned, f32)],
        compiler_params=params,
        name="pick",
    )(tile_block, lax.all_to_all(sums, "gy", 0, 0, tiled=True))
    gradient = pl.pallas_call(
        add_kernel,
        out_shape=shape(*control.shape),
        in_specs=in_vmem(1),
        out_specs=pl.BlockSpec(memory_space=pltpu.VMEM),
        compiler_params=params,
        name="add",
    )(lax.all_to_all(parts, "gx", 0, 0, tiled=True))
    return vel_u, vel_v, gradient


def solution(mesh):
    return jax.shard_map(
        per_device,
        mesh=mesh,
        in_specs=(P("gy", "gx"), P(None, "gy", "gx"), P(None, "gy", "gx"), P("gy", None), P(), P()),
        out_specs=(P("gy", "gx"), P("gy", "gx"), P("gy", None)),
        check_vma=False,
    )
```

```python
import jax
import jax.numpy as jnp
from jax import lax
from jax.experimental import pallas as pl
from jax.experimental.pallas import tpu as pltpu
from jax.sharding import PartitionSpec as P

TILE = 256
PIC = 4
SW = 2
ADJ = 6
CT = 64
COARSE = 4096

LANES = 128
HALO = 16
OBS = 8
MARGIN = 8
TOP = MARGIN + HALO
ROWS = TILE + 2 * TOP
PACK = COARSE // LANES
VMEM_LIMIT = 40 * 1024 * 1024
PACK_VMEM_LIMIT = 62 * 1024 * 1024

STRIP = ((0, HALO), (HALO, HALO), (2 * HALO, HALO), (3 * HALO, OBS), (3 * HALO + OBS, OBS))

PATCH_ROWS = ((-1, PACK - 2, 2, 0), (0, 0, PACK, 4), (1, 0, 2, CT + 4))
PATCH = CT + 8

visc_scale = 0.1
strain_floor = 0.05


def lanes_of(rows):
    return lax.broadcasted_iota(jnp.int32, (rows, LANES), 1)


def patch_lanes(count, ds):
    lane = lanes_of(count)
    return (lane < CT) if ds == 0 else ((lane >= CT) & (lane < 96) if ds > 0 else lane >= 96)


def is_even(axis):
    return lax.axis_index(axis) % 2 == 0


def columns_kernel(thick, drive, obs, first_pair, second_pair, held, sems):
    copies = []
    for f, field in enumerate((thick, drive.at[0], drive.at[1], obs.at[0], obs.at[1])):
        copies.append(pltpu.make_async_copy(field, held.at[f], sems.at[f]))
        copies[-1].start()
    half = TILE // 2
    lane = lanes_of(half)
    left = jnp.zeros((half, LANES), jnp.float32)
    right = jnp.zeros((half, LANES), jnp.float32)
    for f, (first, count) in enumerate(STRIP):
        copies[f].wait()
        for part in range(2):
            rows = slice(part * half, (part + 1) * half)
            start = part * 64 + first
            inside = (lane >= start) & (lane < start + count)
            left = jnp.where(inside, pltpu.roll(held[f, rows, :LANES], start, 1), left)
            right = jnp.where(inside, pltpu.roll(held[f, rows, LANES:], (start + count) % LANES, 1), right)
    even = is_even("gx")
    first_pair[...] = jnp.where(even, right, left)
    second_pair[...] = jnp.where(even, left, right)


def patches_kernel(tile_block, control, after, patches, owned_blocks):
    tile_cols, tile_rows = tile_block.shape
    owned = control.shape[0]
    mine = lax.axis_index("gy") * owned
    col_tile = lax.axis_index("gx")
    for j in range(PACK):
        owned_blocks[:, j, :] = control[:, j * LANES : (j + 1) * LANES]
    patches[...] = jnp.zeros_like(patches)

    def fill(target, carry):
        for dr, first, count, at in PATCH_ROWS:
            for ds in (-1, 0, 1):
                row = jnp.clip(target + dr, 0, tile_rows - 1)
                col = jnp.clip(col_tile + ds, 0, tile_cols - 1)
                place = tile_block[col, row] - mine

                @pl.when((place >= 0) & (place < owned))
                def _():
                    cells = owned_blocks[place, first : first + count, :]
                    turned = pltpu.roll(cells, CT, 1)
                    even, odd = (cells, turned) if ds == 0 else (turned, cells)
                    inside = patch_lanes(count, ds)
                    rows = pl.ds(at, count, stride=2)
                    patches[target, rows, :] += jnp.where(inside, even, 0.0)
                    rows = pl.ds(at + 1, count, stride=2)
                    patches[target, rows, :] += jnp.where(inside, odd, 0.0)

        return carry

    lax.fori_loop(0, tile_rows, fill, 0)


def sides(axis, first_pair, second_pair):
    even = is_even(axis)
    return jnp.where(even, second_pair, first_pair), jnp.where(even, first_pair, second_pair)


def frame_cells(west, east, start, count):
    from_east = pltpu.roll(east, (LANES - start) % LANES, 1)
    from_west = pltpu.roll(west, (2 * LANES - count - start) % LANES, 1)
    lane = lanes_of(from_east.shape[0])
    return jnp.where(lane < count, from_east, jnp.where(lane >= LANES - count, from_west, 0.0))


def rows_kernel(thick, drive, obs, first_col, second_col, first_pair, second_pair):
    half = TILE // 2
    west, east = sides("gx", first_col[...], second_col[...])
    even = is_even("gy")
    for field, (first, count) in zip((thick, drive.at[0], drive.at[1], obs.at[0], obs.at[1]), STRIP):
        for c in range(3):
            if c < 2:
                cols = slice(c * LANES, (c + 1) * LANES)
                top, bottom = field[0:count, cols], field[TILE - count : TILE, cols]
            else:
                top = frame_cells(west[:count], east[:count], first, count)
                bottom = frame_cells(west[half - count :], east[half - count :], 64 + first, count)
            first_pair[c, first : first + count, :] = jnp.where(even, bottom, top)
            second_pair[c, first : first + count, :] = jnp.where(even, top, bottom)


def shift_east(tiles, lane):
    rolled = [pltpu.roll(t, LANES - 1, 1) for t in tiles]
    return [jnp.where(lane == LANES - 1, rolled[(c + 1) % 3], rolled[c]) for c in range(3)]


def shift_west(tiles, lane):
    rolled = [pltpu.roll(t, 1, 1) for t in tiles]
    return [jnp.where(lane == 0, rolled[(c + 2) % 3], rolled[c]) for c in range(3)]


def over_rows(framed, body):
    start, count, step = (MARGIN, TILE + 2 * HALO, 48) if framed else (TOP, TILE, 64)

    def block(i, carry):
        body(pl.multiple_of(start + i * step, 8), step)
        return carry

    lax.fori_loop(0, count // step, block, 0)


def model_kernel(
    ice_mask, patches, thick, drive, obs, first_row, second_row, first_col, second_col,
    vel_u, vel_v, sums,
    ext, fr, ice, visc, vel, coef, small, sems,
):
    tile_cols, tile_rows = ice_mask.shape
    row_tile = lax.axis_index("gy")
    col_tile = lax.axis_index("gx")

    cells = jnp.exp(sum(patches[j] for j in range(tile_rows)))
    lane = lanes_of(PATCH)
    for c in range(3):
        source = 32 * c + lane // 4
        if c == 2:
            source = jnp.where(lane < CT, source, source + 32)
        wide = jnp.take_along_axis(cells, source, axis=1)
        for j in range(4):
            fr[c, pl.ds(MARGIN + j, PATCH, stride=4), :] = wide

    fields = (thick, drive.at[0], drive.at[1], obs.at[0], obs.at[1])
    half = TILE // 2
    west, east = sides("gx", first_col[...], second_col[...])
    even = is_even("gy")
    for f, (field, (first, count)) in enumerate(zip(fields, STRIP)):
        for c in range(3):
            if c < 2:
                ext[f, c, TOP : TOP + TILE, :] = field[:, c * LANES : (c + 1) * LANES]
            one, two = first_row[c, first : first + count, :], second_row[c, first : first + count, :]
            ext[f, c, TOP - count : TOP, :] = jnp.where(even, two, one)
            ext[f, c, TOP + TILE : TOP + TILE + count, :] = jnp.where(even, one, two)
        for part in range(2):
            ext[f, 2, TOP + part * half : TOP + (part + 1) * half, :] = frame_cells(
                west, east, part * 64 + first, count
            )

    for dr, first, count in ((-1, MARGIN, HALO), (0, TOP, TILE), (1, TOP + TILE, HALO)):
        masks = []
        for ds in (-1, 0, 1):
            row, col = row_tile + dr, col_tile + ds
            inside = (row >= 0) & (row < tile_rows) & (col >= 0) & (col < tile_cols)
            row = jnp.clip(row, 0, tile_rows - 1)
            col = jnp.clip(col, 0, tile_cols - 1)
            masks.append(jnp.where(inside, ice_mask[col, row], 0).astype(jnp.float32))
        lane = lanes_of(count)
        for c in range(2):
            ice[c, first : first + count, :] = jnp.full((count, LANES), masks[1])
        ice[2, first : first + count, :] = jnp.where(
            lane < HALO, masks[2], jnp.where(lane >= LANES - HALO, masks[0], 0.0)
        )

    tiles = range(3)

    def load(ref, at, *lead):
        return [ref[(*lead, c, at, slice(None))] for c in tiles]

    def store(ref, at, values, *lead):
        for c in tiles:
            ref[(*lead, c, at, slice(None))] = values[c]

    def load_around(row, step, now):
        rows = [pl.ds(row, step), pl.ds(row - 1, step), pl.ds(row + 1, step)]
        return [load(vel, at, now, i) for i in range(2) for at in rows]

    def first_viscosity(row, step):
        at = pl.ds(row, step)
        store(visc, at, [visc_scale * strain_floor ** (-1.0 / 3.0) * t for t in load(ext, at, 0)])

    def viscosity(row, step):
        at, lane = pl.ds(row, step), lanes_of(step)
        thickness = load(ext, at, 0)
        u, u_n, u_s, v, v_n, v_s = load_around(row, step, 1)
        u_e, u_w = shift_east(u, lane), shift_west(u, lane)
        v_e, v_w = shift_east(v, lane), shift_west(v, lane)
        result = []
        for c in tiles:
            ux, vx = u_e[c] - u_w[c], v_e[c] - v_w[c]
            uy, vy = u_s[c] - u_n[c], v_s[c] - v_n[c]
            shear = uy + vx
            strain = 0.25 * (ux * ux + vy * vy + ux * vy + 0.25 * (shear * shear)) + strain_floor
            result.append(visc_scale * thickness[c] * jnp.exp(jnp.log(strain) * (-1.0 / 3.0)))
        store(visc, at, result)

    def coefficients(row, step):
        at, lane = pl.ds(row, step), lanes_of(step)
        m, m_n, m_s = load(visc, at), load(visc, pl.ds(row - 1, step)), load(visc, pl.ds(row + 1, step))
        m_w = shift_west(m, lane)
        w = [0.5 * (m[c] + m_w[c]) for c in tiles]
        e = shift_east(w, lane)
        s = [0.5 * (m[c] + m_s[c]) for c in tiles]
        n = [0.5 * (m[c] + m_n[c]) for c in tiles]
        friction, mask = load(fr, at), load(ice, at)
        scale_u, scale_v = [], []
        for c in tiles:
            across, along = e[c] + w[c], s[c] + n[c]
            scale_u.append(mask[c] / (friction[c] + 4.0 * across + along))
            scale_v.append(mask[c] / (friction[c] + across + 4.0 * along))
        corners = []
        for shifted in (
            shift_west(m_s, lane), shift_west(m_n, lane), shift_east(m_s, lane), shift_east(m_n, lane),
        ):
            corners.append([0.5 * m[c] + 0.25 * shifted[c] for c in tiles])
            corners.append([0.25 * m[c] + 0.5 * shifted[c] for c in tiles])
        k = [e, w, s, n, scale_u, scale_v] + corners
        for i, values in enumerate(k):
            store(coef, at, values, i)
        return k

    def relax(row, step, k, now, new):
        at, lane = pl.ds(row, step), lanes_of(step)
        e, w, s, n, scale_u, scale_v, sw_u, sw_v, nw_u, nw_v, se_u, se_v, ne_u, ne_v = k
        u, u_n, u_s, v, v_n, v_s = load_around(row, step, now)
        to_west_u, to_east_u, to_west_v, to_east_v = [], [], [], []
        for c in tiles:
            u4 = 4.0 * u[c]
            to_west_u.append(w[c] * u4 + (sw_u[c] * v_s[c] - nw_u[c] * v_n[c]))
            to_east_u.append(e[c] * u4 + (ne_u[c] * v_n[c] - se_u[c] * v_s[c]))
            to_west_v.append(w[c] * v[c] + (sw_v[c] * u_s[c] - nw_v[c] * u_n[c]))
            to_east_v.append(e[c] * v[c] + (ne_v[c] * u_n[c] - se_v[c] * u_s[c]))
        to_west_u, to_west_v = shift_east(to_west_u, lane), shift_east(to_west_v, lane)
        to_east_u, to_east_v = shift_west(to_east_u, lane), shift_west(to_east_v, lane)
        right_u, right_v = load(ext, at, 1), load(ext, at, 2)
        new_u, new_v = [], []
        for c in tiles:
            mid_u = s[c] * u_s[c] + n[c] * u_n[c]
            mid_v = 4.0 * (s[c] * v_s[c] + n[c] * v_n[c])
            new_u.append(scale_u[c] * (right_u[c] + mid_u + (to_west_u[c] + to_east_u[c])))
            new_v.append(scale_v[c] * (right_v[c] + mid_v + (to_west_v[c] + to_east_v[c])))
        store(vel, at, new_u, new, 0)
        store(vel, at, new_v, new, 1)

    def sweep(framed, now, new):
        def body(row, step):
            at = pl.ds(row, step)
            relax(row, step, [load(coef, at, i) for i in range(14)], now, new)

        over_rows(framed, body)

    def first_start(row, step):
        k = coefficients(row, step)
        at = pl.ds(row, step)
        for i in range(2):
            right = load(ext, at, 1 + i)
            store(vel, at, [k[4 + i][c] * right[c] for c in tiles], 0, i)

    over_rows(True, first_viscosity)
    over_rows(True, first_start)
    sweep(True, 0, 1)

    def iteration(i, carry):
        over_rows(True, viscosity)
        over_rows(True, lambda row, step: relax(row, step, coefficients(row, step), 1, 0))
        sweep(True, 0, 1)
        return carry

    lax.fori_loop(1, PIC, iteration, 0)
    copies = []
    for i, out in enumerate((vel_u, vel_v)):
        for c in range(2):
            copies.append(
                pltpu.make_async_copy(
                    vel.at[1, i, c, TOP : TOP + TILE, :], out.at[:, c * LANES : (c + 1) * LANES], sems.at[2 * i + c]
                )
            )
            copies[-1].start()

    def first_adjoint(row, step):
        at = pl.ds(row, step)
        for i in range(2):
            u, seen, scale = load(vel, at, 1, i), load(ext, at, 3 + i), load(coef, at, 4 + i)
            misfit = [u[c] - seen[c] for c in tiles]
            store(ext, at, misfit, 1 + i)
            store(vel, at, [scale[c] * misfit[c] for c in tiles], 2, i)

    over_rows(True, first_adjoint)

    def two_sweeps(i, carry):
        sweep(True, 2, 0)
        sweep(True, 0, 2)
        return carry

    lax.fori_loop(0, (ADJ - 2) // 2, two_sweeps, 0)
    sweep(False, 2, 0)

    def gradient(row, step):
        for c in range(2):
            at = (c, pl.ds(row, step), slice(None))
            visc[at] = -fr[at] * (vel[(1, 0, *at)] * vel[(0, 0, *at)] + vel[(1, 1, *at)] * vel[(0, 1, *at)])

    over_rows(False, gradient)
    down = [sum(visc[c, pl.ds(TOP + j, CT, stride=4), :] for j in range(4)) for c in range(2)]
    k = lax.broadcasted_iota(jnp.int32, (LANES, LANES), 0)
    l = lanes_of(LANES) % CT
    total = jnp.zeros((CT, LANES), jnp.float32)
    for c in range(2):
        total += jnp.dot(
            down[c],
            (k // 4 + 32 * c == l).astype(jnp.float32),
            precision=lax.Precision.HIGHEST,
            preferred_element_type=jnp.float32,
        )
    small[...] = total
    packed = jnp.where(
        lanes_of(PACK) < CT, small[pl.ds(0, PACK, stride=2), :], small[pl.ds(1, PACK, stride=2), :]
    )
    part = PACK // sums.shape[0]
    for i in range(sums.shape[0]):
        for j in range(sums.shape[1]):
            sums[i, j] = packed[i * part : (i + 1) * part]
    for copy in copies:
        copy.wait()


def pick_kernel(tile_block, gathered, out, total):
    owned = total.shape[0]
    first = lax.axis_index("gy") * owned
    tile_cols, tile_rows = tile_block.shape
    total[...] = jnp.zeros_like(total)

    def step(t, carry):
        col = t // tile_rows
        place = tile_block[col, t - col * tile_rows] - first

        @pl.when((place >= 0) & (place < owned))
        def _():
            total[place] += gathered[t]

        return carry

    lax.fori_loop(0, tile_cols * tile_rows, step, 0)
    for j in range(out.shape[0]):
        out[j] = total[...]


def join_kernel(parts, out):
    share = parts.shape[2]
    for i in range(parts.shape[0]):
        for j in range(share):
            at = (i * share + j) * LANES
            out[:, at : at + LANES] = parts[i, :, j, :]


def in_vmem(count):
    return [pl.BlockSpec(memory_space=pltpu.VMEM)] * count


def in_smem(count):
    return [pl.BlockSpec(memory_space=pltpu.SMEM)] * count


def per_device(thickness, driving, observed, control, ice_mask, tile_block):
    f32 = jnp.float32
    rows, cols = lax.axis_size("gy"), lax.axis_size("gx")
    tile_block, ice_mask = tile_block[:, :, 0].T, ice_mask.T
    params = pltpu.CompilerParams(vmem_limit_bytes=VMEM_LIMIT)

    def shape(*sizes):
        return jax.ShapeDtypeStruct(sizes, f32)

    def swap(axis, cells_first, cells_second):
        count = lax.axis_size(axis)
        received = []
        for cells, low in ((cells_second, 1), (cells_first, 0)):
            pairs = [(i, i + 1) for i in range(low, count - 1, 2)]
            received.append(lax.ppermute(cells, axis, pairs + [(j, i) for i, j in pairs]))
        return received[1], received[0]

    fields = thickness, driving, observed
    columns = pl.pallas_call(
        columns_kernel,
        out_shape=[shape(TILE // 2, LANES)] * 2,
        in_specs=[pl.BlockSpec(memory_space=pltpu.HBM)] * 3,
        out_specs=in_vmem(2),
        scratch_shapes=[pltpu.VMEM((5, TILE, TILE), f32), pltpu.SemaphoreType.DMA((5,))],
        compiler_params=pltpu.CompilerParams(vmem_limit_bytes=PACK_VMEM_LIMIT),
        name="columns",
    )(*fields)
    columns_in = swap("gx", *columns)
    patches = pl.pallas_call(
        patches_kernel,
        out_shape=shape(rows, PATCH, LANES),
        in_specs=in_smem(1) + in_vmem(1) + [pl.BlockSpec(memory_space=pl.ANY)],
        out_specs=pl.BlockSpec(memory_space=pltpu.VMEM),
        scratch_shapes=[pltpu.VMEM((control.shape[0], PACK, LANES), f32)],
        compiler_params=params,
        cost_estimate=pl.CostEstimate(flops=10**7, bytes_accessed=10**7, transcendentals=0),
        name="patches",
    )(tile_block, control, columns[0])
    patches = lax.all_to_all(patches, "gy", 0, 0, tiled=True)
    strips = pl.pallas_call(
        rows_kernel,
        out_shape=[shape(3, 64, LANES)] * 2,
        in_specs=in_vmem(5),
        out_specs=in_vmem(2),
        compiler_params=params,
        name="rows",
    )(*fields, *columns_in)
    rows_in = swap("gy", *strips)

    vel_u, vel_v, sums = pl.pallas_call(
        model_kernel,
        out_shape=(shape(TILE, TILE), shape(TILE, TILE), shape(cols, rows, PACK // cols, LANES)),
        in_specs=in_smem(1) + in_vmem(8),
        out_specs=[pl.BlockSpec(memory_space=pltpu.HBM)] * 2 + in_vmem(1),
        scratch_shapes=[
            pltpu.VMEM((5, 3, ROWS, LANES), f32),
            pltpu.VMEM((3, ROWS, LANES), f32),
            pltpu.VMEM((3, ROWS, LANES), f32),
            pltpu.VMEM((3, ROWS, LANES), f32),
            pltpu.VMEM((3, 2, 3, ROWS, LANES), f32),
            pltpu.VMEM((14, 3, ROWS, LANES), f32),
            pltpu.VMEM((CT, LANES), f32),
            pltpu.SemaphoreType.DMA((4,)),
        ],
        compiler_params=params,
        name="model",
    )(ice_mask, patches, *fields, *rows_in, *columns_in)

    share = (control.shape[0], PACK // cols, LANES)
    sums = lax.all_to_all(sums.reshape(cols * rows, *share[1:]), ("gx", "gy"), 0, 0, tiled=True)
    parts = pl.pallas_call(
        pick_kernel,
        out_shape=shape(cols, *share),
        in_specs=in_smem(1) + in_vmem(1),
        out_specs=pl.BlockSpec(memory_space=pltpu.VMEM),
        scratch_shapes=[pltpu.VMEM(share, f32)],
        compiler_params=params,
        name="pick",
    )(tile_block, sums)
    gradient = pl.pallas_call(
        join_kernel,
        out_shape=shape(*control.shape),
        in_specs=in_vmem(1),
        out_specs=pl.BlockSpec(memory_space=pltpu.VMEM),
        compiler_params=params,
        name="join",
    )(lax.all_to_all(parts, "gx", 0, 0, tiled=True))
    return vel_u, vel_v, gradient


def solution(mesh):
    return jax.shard_map(
        per_device,
        mesh=mesh,
        in_specs=(P("gy", "gx"), P(None, "gy", "gx"), P(None, "gy", "gx"), P("gy", None), P(), P()),
        out_specs=(P("gy", "gx"), P("gy", "gx"), P("gy", None)),
        check_vma=False,
    )
```

```python
import jax
import jax.numpy as jnp
from jax import lax
from jax.experimental import pallas as pl
from jax.experimental.pallas import tpu as pltpu
from jax.sharding import PartitionSpec as P

TILE = 256
PIC = 4
SW = 2
ADJ = 6
CT = 64
COARSE = 4096

LANES = 128
HALO = 16
OBS = 8
MARGIN = 8
TOP = MARGIN + HALO
ROWS = TILE + 2 * TOP
HALF = TILE // 2
SIDE = 2 * ROWS
BAND = LANES // 2
ALL_ROWS = SIDE + HALF + 2 * TOP
MAIN = (0, ROWS)
SIDES = (SIDE,)
GROUP = 8
BLOCKS = 4
PACK = COARSE // LANES
VMEM_LIMIT = 40 * 1024 * 1024
PACK_VMEM_LIMIT = 62 * 1024 * 1024

STRIP = ((0, HALO), (HALO, HALO), (2 * HALO, HALO), (3 * HALO, OBS), (3 * HALO + OBS, OBS))

PATCH_ROWS = ((-1, PACK - 2, 2, 0), (0, 0, PACK, 4), (1, 0, 2, CT + 4))
PATCH = CT + 8

visc_scale = 0.1
strain_floor = 0.05


def lanes_of(rows):
    return lax.broadcasted_iota(jnp.int32, (rows, LANES), 1)


def patch_lanes(count, ds):
    lane = lanes_of(count)
    return (lane < CT) if ds == 0 else ((lane >= CT) & (lane < 96) if ds > 0 else lane >= 96)


def is_even(axis):
    return lax.axis_index(axis) % 2 == 0


def columns_kernel(thick, drive, obs, first_pair, second_pair, held, sems):
    copies = []
    for f, field in enumerate((thick, drive.at[0], drive.at[1], obs.at[0], obs.at[1])):
        copies.append(pltpu.make_async_copy(field, held.at[f], sems.at[f]))
        copies[-1].start()
    lane = lanes_of(HALF)
    left = jnp.zeros((HALF, LANES), jnp.float32)
    right = jnp.zeros((HALF, LANES), jnp.float32)
    for f, (first, count) in enumerate(STRIP):
        copies[f].wait()
        for part in range(2):
            rows = slice(part * HALF, (part + 1) * HALF)
            start = part * BAND + first
            inside = (lane >= start) & (lane < start + count)
            left = jnp.where(inside, pltpu.roll(held[f, rows, :LANES], start, 1), left)
            right = jnp.where(inside, pltpu.roll(held[f, rows, LANES:], (start + count) % LANES, 1), right)
    even = is_even("gx")
    first_pair[...] = jnp.where(even, right, left)
    second_pair[...] = jnp.where(even, left, right)


def patches_kernel(tile_block, control, patches, owned_blocks):
    tile_cols, tile_rows = tile_block.shape
    owned = control.shape[0]
    mine = lax.axis_index("gy") * owned
    col_tile = lax.axis_index("gx")
    for j in range(PACK):
        owned_blocks[:, j, :] = control[:, j * LANES : (j + 1) * LANES]
    patches[...] = jnp.zeros_like(patches)

    def spread(row, carry):
        for ds in (-1, 0, 1):
            col = col_tile + ds
            place = tile_block[jnp.clip(col, 0, tile_cols - 1), row] - mine

            @pl.when((col >= 0) & (col < tile_cols) & (place >= 0) & (place < owned))
            def _():
                for dr, first, count, at in PATCH_ROWS:
                    target = row - dr

                    @pl.when((target >= 0) & (target < tile_rows))
                    def _():
                        cells = owned_blocks[place, first : first + count, :]
                        turned = pltpu.roll(cells, CT, 1)
                        inside = patch_lanes(count, ds)
                        for j, new in enumerate((cells, turned) if ds == 0 else (turned, cells)):
                            rows = pl.ds(at + j, count, stride=2)
                            patches[target, rows, :] = jnp.where(inside, new, patches[target, rows, :])

        return carry

    lax.fori_loop(0, tile_rows, spread, 0)


def sides(axis, first_pair, second_pair):
    even = is_even(axis)
    return jnp.where(even, second_pair, first_pair), jnp.where(even, first_pair, second_pair)


def choose_side(lane, high, east, west, low):
    place = lane % BAND
    return jnp.where(
        place < HALO, high, jnp.where(place < 2 * HALO, east, jnp.where(place < 3 * HALO, west, low))
    )


def turn(cells, source, target):
    shift = (target - source) % LANES
    return pltpu.roll(cells, shift, 1) if shift else cells


def rows_kernel(thick, drive, obs, first_col, second_col, first_pair, second_pair):
    west, east = sides("gx", first_col[...], second_col[...])
    even = is_even("gy")
    for field, (first, count) in zip((thick, drive.at[0], drive.at[1], obs.at[0], obs.at[1]), STRIP):
        strips = []
        for rows, packed_rows, source, target in (
            (slice(0, count), slice(0, count), first, BAND),
            (slice(TILE - count, TILE), slice(HALF - count, HALF), BAND + first, 0),
        ):
            low, high = field[rows, :LANES], field[rows, LANES:]
            sides_row = choose_side(
                lanes_of(count),
                turn(high, LANES - HALO, target),
                turn(east[packed_rows], source, target + HALO),
                turn(west[packed_rows], source, target + 3 * HALO - count),
                turn(low, 0, target + 3 * HALO),
            )
            strips.append((low, high, sides_row))
        for c in range(3):
            top, bottom = strips[0][c], strips[1][c]
            first_pair[c, first : first + count, :] = jnp.where(even, bottom, top)
            second_pair[c, first : first + count, :] = jnp.where(even, top, bottom)


def shift_east(tiles, lane):
    rolled = [pltpu.roll(t, LANES - 1, 1) for t in tiles]
    if len(tiles) == 1:
        return rolled
    return [jnp.where(lane == LANES - 1, rolled[1 - c], rolled[c]) for c in range(2)]


def shift_west(tiles, lane):
    rolled = [pltpu.roll(t, 1, 1) for t in tiles]
    if len(tiles) == 1:
        return rolled
    return [jnp.where(lane == 0, rolled[1 - c], rolled[c]) for c in range(2)]


def over_rows(framed, body):
    start = MARGIN if framed else TOP
    wide = 2 * HALO if framed else 0
    main, side = (TILE + wide) // BLOCKS, (HALF + wide) // BLOCKS

    def block(i, carry):
        row = pl.multiple_of(start + i * main, 8)
        side_row = pl.multiple_of(start + i * side, 8)
        for g in range(0, main, GROUP):
            body(MAIN, row + g)
            if g < side:
                body(SIDES, side_row + g)
        return carry

    lax.fori_loop(0, BLOCKS, block, 0)


def join_parts(ref, leads, whole):
    edge = HALO // 2

    def join(row, upper, lower, count):
        lane = lanes_of(count)
        for lead in leads:
            def at(tile_row):
                return (*lead, pl.ds(tile_row, count), slice(None))

            mixed = ref[at(SIDE + row)]
            if whole:
                place = lane % BAND
                upper_lane = lane < BAND
                from_high = jnp.where(
                    upper_lane,
                    turn(ref[at(ROWS + row)], LANES - HALO, 0),
                    turn(ref[at(ROWS + row + HALF)], LANES - HALO, BAND),
                )
                from_low = jnp.where(
                    upper_lane,
                    turn(ref[at(row)], edge, BAND - edge),
                    turn(ref[at(row + HALF)], edge, LANES - edge),
                )
                ref[at(SIDE + row)] = jnp.where(
                    place < edge, from_high, jnp.where(place >= BAND - edge, from_low, mixed)
                )
            for wanted, band, main_row in ((upper, 0, row), (lower, BAND, row + HALF)):
                if wanted:
                    low = turn(mixed, band + 3 * HALO, 0)
                    high = turn(mixed, band + edge, LANES - edge)
                    ref[at(main_row)] = jnp.where(lane < edge, low, ref[at(main_row)])
                    ref[at(ROWS + main_row)] = jnp.where(lane >= LANES - edge, high, ref[at(ROWS + main_row)])

    step = 32

    def middle(i, carry):
        join(pl.multiple_of(TOP + i * step, 8), True, True, step)
        return carry

    lax.fori_loop(0, HALF // step, middle, 0)
    if whole:
        join(MARGIN, True, False, HALO)
        join(TOP + HALF, False, True, HALO)


def model_kernel(
    ice_mask, patches, thick, drive, obs, first_row, second_row, first_col, second_col,
    vel_u, vel_v, sums,
    ext, fr, ice, visc, vel, coef, small, sems,
):
    tile_cols, tile_rows = ice_mask.shape
    row_tile = lax.axis_index("gy")
    col_tile = lax.axis_index("gx")

    cells = 0.5 * jnp.exp(sum(patches[j] for j in range(tile_rows)))
    lane = lanes_of(PATCH)
    for c in range(2):
        wide = jnp.take_along_axis(cells, 32 * c + lane // 4, axis=1)
        for j in range(4):
            fr[pl.ds(MAIN[c] + MARGIN + j, PATCH, stride=4), :] = wide
    lane = lanes_of(40)
    place = lane % BAND // 4
    source = jnp.where(place < 8, 60 + place, (116 + place) % LANES)
    wide = jnp.where(
        lane < BAND,
        jnp.take_along_axis(cells[:40], source, axis=1),
        jnp.take_along_axis(cells[PATCH - 40 :], source, axis=1),
    )
    for j in range(4):
        fr[pl.ds(SIDE + MARGIN + j, 40, stride=4), :] = wide

    west, east = sides("gx", first_col[...], second_col[...])
    even = is_even("gy")
    lane = lanes_of(HALF)
    upper = lane < BAND
    for f, (field, (first, count)) in enumerate(zip((thick, drive.at[0], drive.at[1], obs.at[0], obs.at[1]), STRIP)):
        scale = 0.5 if f in (1, 2) else 1.0
        frames = []
        for c in range(3):
            one, two = scale * first_row[c, first : first + count, :], scale * second_row[c, first : first + count, :]
            frames.append((jnp.where(even, two, one), jnp.where(even, one, two)))
        for c in range(2):
            ext[f, MAIN[c] + TOP : MAIN[c] + TOP + TILE, :] = scale * field[:, c * LANES : (c + 1) * LANES]
            ext[f, MAIN[c] + TOP - count : MAIN[c] + TOP, :] = frames[c][0]
            ext[f, MAIN[c] + TOP + TILE : MAIN[c] + TOP + TILE + count, :] = frames[c][1]
        halves = (slice(0, HALF), slice(HALF, TILE))
        high = [turn(field[halves[b], LANES:], LANES - HALO, BAND * b) for b in range(2)]
        low = [turn(field[halves[b], :LANES], 0, BAND * b + 3 * HALO) for b in range(2)]
        here = SIDE + TOP
        ext[f, here : here + HALF, :] = scale * choose_side(
            lane,
            jnp.where(upper, high[0], high[1]),
            turn(east, first, HALO),
            turn(west, first, 3 * HALO - count),
            jnp.where(upper, low[0], low[1]),
        )
        upper_few = lanes_of(count) < BAND
        above = turn(ext[f, here + HALF - count : here + HALF, :], 0, BAND)
        below = turn(ext[f, here : here + count, :], 0, BAND)
        ext[f, here - count : here, :] = jnp.where(upper_few, frames[2][0], above)
        ext[f, here + HALF : here + HALF + count, :] = jnp.where(upper_few, below, frames[2][1])

    side_ice = []
    for dr, first, count in ((-1, MARGIN, HALO), (0, TOP, TILE), (1, TOP + TILE, HALO)):
        masks = []
        for ds in (-1, 0, 1):
            row, col = row_tile + dr, col_tile + ds
            inside = (row >= 0) & (row < tile_rows) & (col >= 0) & (col < tile_cols)
            row = jnp.clip(row, 0, tile_rows - 1)
            col = jnp.clip(col, 0, tile_cols - 1)
            masks.append(jnp.where(inside, ice_mask[col, row], 0).astype(jnp.float32))
        for c in range(2):
            ice[MAIN[c] + first : MAIN[c] + first + count, :] = jnp.full((count, LANES), masks[1])
        side_ice.append(choose_side(lanes_of(HALO), masks[1], masks[2], masks[0], masks[1]))
    upper = lanes_of(HALO) < BAND
    for i in range(HALF // HALO):
        ice[SIDE + TOP + i * HALO : SIDE + TOP + (i + 1) * HALO, :] = side_ice[1]
    ice[SIDE + MARGIN : SIDE + TOP, :] = jnp.where(upper, side_ice[0], side_ice[1])
    ice[SIDE + TOP + HALF : SIDE + TOP + HALF + HALO, :] = jnp.where(upper, side_ice[1], side_ice[2])

    lane = lanes_of(GROUP)

    def load(ref, part, row, *lead):
        return [ref[(*lead, pl.ds(row + tile, GROUP), slice(None))] for tile in part]

    def store(ref, part, row, values, *lead):
        for tile, value in zip(part, values):
            ref[(*lead, pl.ds(row + tile, GROUP), slice(None))] = value

    def load_around(part, row, now):
        return [load(vel, part, r, now, i) for i in range(2) for r in (row, row - 1, row + 1)]

    def first_viscosity(part, row):
        store(visc, part, row, [0.25 * visc_scale * strain_floor ** (-1.0 / 3.0) * t for t in load(ext, part, row, 0)])

    def viscosity(part, row):
        thickness = load(ext, part, row, 0)
        u, u_n, u_s, v, v_n, v_s = load_around(part, row, 1)
        u_e, u_w = shift_east(u, lane), shift_west(u, lane)
        v_e, v_w = shift_east(v, lane), shift_west(v, lane)
        result = []
        for c in range(len(part)):
            ux, vx = u_e[c] - u_w[c], v_e[c] - v_w[c]
            uy, vy = u_s[c] - u_n[c], v_s[c] - v_n[c]
            shear = uy + vx
            strain = 0.25 * (ux * (ux + vy) + vy * vy) + (0.0625 * (shear * shear) + strain_floor)
            result.append((0.25 * visc_scale) * thickness[c] * jnp.exp(jnp.log(strain) * (-1.0 / 3.0)))
        store(visc, part, row, result)

    def inverse(x):
        near = pl.reciprocal(x, approx=True)
        return near * (2.0 - x * near)

    def coefficients(part, row):
        tiles = range(len(part))
        q, q_n, q_s = load(visc, part, row), load(visc, part, row - 1), load(visc, part, row + 1)
        q_w = shift_west(q, lane)
        w = [q[c] + q_w[c] for c in tiles]
        e = shift_east(w, lane)
        s = [q[c] + q_s[c] for c in tiles]
        n = [q[c] + q_n[c] for c in tiles]
        friction, mask = load(fr, part, row), load(ice, part, row)
        scale_u, scale_v = [], []
        for c in tiles:
            across, along = e[c] + w[c], s[c] + n[c]
            scale_u.append(mask[c] * inverse(friction[c] + along + 4.0 * across))
            scale_v.append(mask[c] * inverse(friction[c] + across + 4.0 * along))
        corners = []
        half = [0.5 * q[c] for c in tiles]
        for shifted in (
            shift_west(q_s, lane), shift_west(q_n, lane), shift_east(q_s, lane), shift_east(q_n, lane),
        ):
            corners.append([q[c] + 0.5 * shifted[c] for c in tiles])
            corners.append([half[c] + shifted[c] for c in tiles])
        k = [e, w, s, n, scale_u, scale_v] + corners
        for i, values in enumerate(k):
            store(coef, part, row, values, i)
        return k

    def relax(part, row, k, now, new):
        tiles = range(len(part))
        e, w, s, n, scale_u, scale_v, sw_u, sw_v, nw_u, nw_v, se_u, se_v, ne_u, ne_v = k
        u, u_n, u_s, v, v_n, v_s = load_around(part, row, now)
        to_west_u, to_east_u, to_west_v, to_east_v = [], [], [], []
        for c in tiles:
            u4 = 4.0 * u[c]
            to_west_u.append(w[c] * u4 + (sw_u[c] * v_s[c] - nw_u[c] * v_n[c]))
            to_east_u.append(e[c] * u4 + (ne_u[c] * v_n[c] - se_u[c] * v_s[c]))
            to_west_v.append(w[c] * v[c] + (sw_v[c] * u_s[c] - nw_v[c] * u_n[c]))
            to_east_v.append(e[c] * v[c] + (ne_v[c] * u_n[c] - se_v[c] * u_s[c]))
        to_west_u, to_west_v = shift_east(to_west_u, lane), shift_east(to_west_v, lane)
        to_east_u, to_east_v = shift_west(to_east_u, lane), shift_west(to_east_v, lane)
        right_u, right_v = load(ext, part, row, 1), load(ext, part, row, 2)
        new_u, new_v = [], []
        for c in tiles:
            mid_u = s[c] * u_s[c] + n[c] * u_n[c]
            mid_v = 4.0 * (s[c] * v_s[c] + n[c] * v_n[c])
            new_u.append(scale_u[c] * (right_u[c] + mid_u + (to_west_u[c] + to_east_u[c])))
            new_v.append(scale_v[c] * (right_v[c] + mid_v + (to_west_v[c] + to_east_v[c])))
        store(vel, part, row, new_u, new, 0)
        store(vel, part, row, new_v, new, 1)

    def sweep(framed, now, new):
        over_rows(framed, lambda part, row: relax(part, row, [load(coef, part, row, i) for i in range(14)], now, new))

    def first_start(part, row):
        k = coefficients(part, row)
        for i in range(2):
            right = load(ext, part, row, 1 + i)
            store(vel, part, row, [a * b for a, b in zip(k[4 + i], right)], 0, i)

    over_rows(True, first_viscosity)
    over_rows(True, first_start)
    sweep(True, 0, 1)

    def iteration(i, carry):
        @pl.when(i == PIC - 1)
        def _():
            join_parts(vel, ((1, 0), (1, 1)), True)

        over_rows(True, viscosity)
        over_rows(True, lambda part, row: relax(part, row, coefficients(part, row), 1, 0))
        sweep(True, 0, 1)
        return carry

    lax.fori_loop(1, PIC, iteration, 0)
    join_parts(vel, ((1, 0), (1, 1)), False)
    copies = []
    for i, out in enumerate((vel_u, vel_v)):
        for c in range(2):
            copies.append(
                pltpu.make_async_copy(
                    vel.at[1, i, MAIN[c] + TOP : MAIN[c] + TOP + TILE, :],
                    out.at[:, c * LANES : (c + 1) * LANES],
                    sems.at[2 * i + c],
                )
            )
            copies[-1].start()

    def first_adjoint(part, row):
        for i in range(2):
            u, seen, scale = load(vel, part, row, 1, i), load(ext, part, row, 3 + i), load(coef, part, row, 4 + i)
            misfit = [0.5 * (a - b) for a, b in zip(u, seen)]
            store(ext, part, row, misfit, 1 + i)
            store(vel, part, row, [a * b for a, b in zip(scale, misfit)], 2, i)

    over_rows(True, first_adjoint)

    def two_sweeps(i, carry):
        sweep(True, 2, 0)
        sweep(True, 0, 2)
        return carry

    lax.fori_loop(0, (ADJ - 2) // 2, two_sweeps, 0)
    sweep(False, 2, 0)

    def gradient(part, row):
        u, v, lu, lv = (load(vel, part, row, j, i) for j in (1, 0) for i in range(2))
        friction = load(fr, part, row)
        store(visc, part, row, [-2.0 * friction[c] * (u[c] * lu[c] + v[c] * lv[c]) for c in range(len(part))])

    over_rows(False, gradient)
    join_parts(visc, ((),), False)
    down = [sum(visc[pl.ds(MAIN[c] + TOP + j, CT, stride=4), :] for j in range(4)) for c in range(2)]
    k = lax.broadcasted_iota(jnp.int32, (LANES, LANES), 0)
    l = lanes_of(LANES) % CT
    total = jnp.zeros((CT, LANES), jnp.float32)
    for c in range(2):
        total += jnp.dot(
            down[c],
            (k // 4 + 32 * c == l).astype(jnp.float32),
            precision=lax.Precision.HIGHEST,
            preferred_element_type=jnp.float32,
        )
    small[...] = total
    packed = jnp.where(
        lanes_of(PACK) < CT, small[pl.ds(0, PACK, stride=2), :], small[pl.ds(1, PACK, stride=2), :]
    )
    part = PACK // sums.shape[0]
    for i in range(sums.shape[0]):
        for j in range(sums.shape[1]):
            sums[i, j] = packed[i * part : (i + 1) * part]
    for copy in copies:
        copy.wait()


def pick_kernel(tile_block, gathered, out):
    owned = out.shape[1]
    first = lax.axis_index("gy") * owned
    tile_cols, tile_rows = tile_block.shape
    total = [jnp.zeros(out.shape[2:], jnp.float32) for _ in range(owned)]
    for t in range(tile_cols * tile_rows):
        place = tile_block[t // tile_rows, t % tile_rows] - first
        cells = gathered[t]
        total = [total[b] + jnp.where(place == b, cells, 0.0) for b in range(owned)]
    for b in range(owned):
        for j in range(out.shape[0]):
            out[j, b] = total[b]


def join_kernel(parts, out):
    share = parts.shape[2]
    for i in range(parts.shape[0]):
        for j in range(share):
            at = (i * share + j) * LANES
            out[:, at : at + LANES] = parts[i, :, j, :]


def in_vmem(count):
    return [pl.BlockSpec(memory_space=pltpu.VMEM)] * count


def in_smem(count):
    return [pl.BlockSpec(memory_space=pltpu.SMEM)] * count


def per_device(thickness, driving, observed, control, ice_mask, tile_block):
    f32 = jnp.float32
    rows, cols = lax.axis_size("gy"), lax.axis_size("gx")
    tile_block, ice_mask = tile_block[:, :, 0].T, ice_mask.T
    params = pltpu.CompilerParams(vmem_limit_bytes=VMEM_LIMIT)

    def shape(*sizes):
        return jax.ShapeDtypeStruct(sizes, f32)

    def swap(axis, cells_first, cells_second):
        count = lax.axis_size(axis)
        received = []
        for cells, low in ((cells_second, 1), (cells_first, 0)):
            pairs = [(i, i + 1) for i in range(low, count - 1, 2)]
            received.append(lax.ppermute(cells, axis, pairs + [(j, i) for i, j in pairs]))
        return received[1], received[0]

    fields = thickness, driving, observed
    columns = pl.pallas_call(
        columns_kernel,
        out_shape=[shape(HALF, LANES)] * 2,
        in_specs=[pl.BlockSpec(memory_space=pltpu.HBM)] * 3,
        out_specs=in_vmem(2),
        scratch_shapes=[pltpu.VMEM((5, TILE, TILE), f32), pltpu.SemaphoreType.DMA((5,))],
        compiler_params=pltpu.CompilerParams(vmem_limit_bytes=PACK_VMEM_LIMIT),
        name="columns",
    )(*fields)
    columns_in = swap("gx", *columns)
    patches = pl.pallas_call(
        patches_kernel,
        out_shape=shape(rows, PATCH, LANES),
        in_specs=in_smem(1) + in_vmem(1),
        out_specs=pl.BlockSpec(memory_space=pltpu.VMEM),
        scratch_shapes=[pltpu.VMEM((control.shape[0], PACK, LANES), f32)],
        compiler_params=params,
        name="patches",
    )(tile_block, control)
    patches = lax.all_to_all(patches, "gy", 0, 0, tiled=True)
    strips = pl.pallas_call(
        rows_kernel,
        out_shape=[shape(3, 64, LANES)] * 2,
        in_specs=in_vmem(5),
        out_specs=in_vmem(2),
        compiler_params=params,
        name="rows",
    )(*fields, *columns_in)
    rows_in = swap("gy", *strips)

    vel_u, vel_v, sums = pl.pallas_call(
        model_kernel,
        out_shape=(shape(TILE, TILE), shape(TILE, TILE), shape(cols, rows, PACK // cols, LANES)),
        in_specs=in_smem(1) + in_vmem(8),
        out_specs=[pl.BlockSpec(memory_space=pltpu.HBM)] * 2 + in_vmem(1),
        scratch_shapes=[
            pltpu.VMEM((5, ALL_ROWS, LANES), f32),
            pltpu.VMEM((ALL_ROWS, LANES), f32),
            pltpu.VMEM((ALL_ROWS, LANES), f32),
            pltpu.VMEM((ALL_ROWS, LANES), f32),
            pltpu.VMEM((3, 2, ALL_ROWS, LANES), f32),
            pltpu.VMEM((14, ALL_ROWS, LANES), f32),
            pltpu.VMEM((CT, LANES), f32),
            pltpu.SemaphoreType.DMA((4,)),
        ],
        compiler_params=params,
        name="model",
    )(ice_mask, patches, *fields, *rows_in, *columns_in)

    share = (control.shape[0], PACK // cols, LANES)
    sums = lax.all_to_all(sums.reshape(cols * rows, *share[1:]), ("gx", "gy"), 0, 0, tiled=True)
    parts = pl.pallas_call(
        pick_kernel,
        out_shape=shape(cols, *share),
        in_specs=in_smem(1) + in_vmem(1),
        out_specs=pl.BlockSpec(memory_space=pltpu.VMEM),
        compiler_params=params,
        name="pick",
    )(tile_block, sums)
    gradient = pl.pallas_call(
        join_kernel,
        out_shape=shape(*control.shape),
        in_specs=in_vmem(1),
        out_specs=pl.BlockSpec(memory_space=pltpu.VMEM),
        compiler_params=params,
        name="join",
    )(lax.all_to_all(parts, "gx", 0, 0, tiled=True))
    return vel_u, vel_v, gradient


def solution(mesh):
    return jax.shard_map(
        per_device,
        mesh=mesh,
        in_specs=(P("gy", "gx"), P(None, "gy", "gx"), P(None, "gy", "gx"), P("gy", None), P(), P()),
        out_specs=(P("gy", "gx"), P("gy", "gx"), P("gy", None)),
        check_vma=False,
    )
```

```python
import jax
import jax.numpy as jnp
from jax import lax
from jax.experimental import pallas as pl
from jax.experimental.pallas import tpu as pltpu
from jax.sharding import PartitionSpec as P

TILE = 256
PIC = 4
SW = 2
ADJ = 6
CT = 64
COARSE = 4096

LANES = 128
HALO = 16
OBS = 8
MARGIN = 8
TOP = MARGIN + HALO
ROWS = TILE + 2 * TOP
HALF = TILE // 2
SIDE = 2 * ROWS
BAND = LANES // 2
ALL_ROWS = SIDE + HALF + 2 * TOP
MAIN = (0, ROWS)
SIDES = (SIDE,)
BLOCKS = 4
AHEAD = 2
PACK = COARSE // LANES
VMEM_LIMIT = 40 * 1024 * 1024
PACK_VMEM_LIMIT = 62 * 1024 * 1024

STRIP = ((0, HALO), (HALO, HALO), (2 * HALO, HALO), (3 * HALO, OBS), (3 * HALO + OBS, OBS))

PATCH_ROWS = ((-1, PACK - 2, 2, 0), (0, 0, PACK, 4), (1, 0, 2, CT + 4))
PATCH = CT + 8

visc_scale = 0.1
strain_floor = 0.05


def lanes_of(rows):
    return lax.broadcasted_iota(jnp.int32, (rows, LANES), 1)


def patch_lanes(count, ds):
    lane = lanes_of(count)
    return (lane < CT) if ds == 0 else ((lane >= CT) & (lane < 96) if ds > 0 else lane >= 96)


def is_even(axis):
    return lax.axis_index(axis) % 2 == 0


def columns_kernel(thick, drive, obs, first_pair, second_pair, held, sems):
    copies = []
    for f, field in enumerate((thick, drive.at[0], drive.at[1], obs.at[0], obs.at[1])):
        copies.append(pltpu.make_async_copy(field, held.at[f], sems.at[f]))
        copies[-1].start()
    lane = lanes_of(HALF)
    left = jnp.zeros((HALF, LANES), jnp.float32)
    right = jnp.zeros((HALF, LANES), jnp.float32)
    for f, (first, count) in enumerate(STRIP):
        copies[f].wait()
        for part in range(2):
            rows = slice(part * HALF, (part + 1) * HALF)
            start = part * BAND + first
            inside = (lane >= start) & (lane < start + count)
            left = jnp.where(inside, pltpu.roll(held[f, rows, :LANES], start, 1), left)
            right = jnp.where(inside, pltpu.roll(held[f, rows, LANES:], (start + count) % LANES, 1), right)
    even = is_even("gx")
    first_pair[...] = jnp.where(even, right, left)
    second_pair[...] = jnp.where(even, left, right)


def patches_kernel(tile_block, control, patches, owned_blocks):
    tile_cols, tile_rows = tile_block.shape
    owned = control.shape[0]
    mine = lax.axis_index("gy") * owned
    col_tile = lax.axis_index("gx")
    for j in range(PACK):
        owned_blocks[:, j, :] = control[:, j * LANES : (j + 1) * LANES]
    patches[...] = jnp.zeros_like(patches)

    def spread(row, carry):
        for ds in (-1, 0, 1):
            col = col_tile + ds
            place = tile_block[jnp.clip(col, 0, tile_cols - 1), row] - mine

            @pl.when((col >= 0) & (col < tile_cols) & (place >= 0) & (place < owned))
            def _():
                for dr, first, count, at in PATCH_ROWS:
                    target = row - dr

                    @pl.when((target >= 0) & (target < tile_rows))
                    def _():
                        cells = owned_blocks[place, first : first + count, :]
                        turned = pltpu.roll(cells, CT, 1)
                        inside = patch_lanes(count, ds)
                        for j, new in enumerate((cells, turned) if ds == 0 else (turned, cells)):
                            rows = pl.ds(at + j, count, stride=2)
                            patches[target, rows, :] = jnp.where(inside, new, patches[target, rows, :])

        return carry

    lax.fori_loop(0, tile_rows, spread, 0)


def sides(axis, first_pair, second_pair):
    even = is_even(axis)
    return jnp.where(even, second_pair, first_pair), jnp.where(even, first_pair, second_pair)


def choose_side(lane, high, east, west, low):
    place = lane % BAND
    return jnp.where(
        place < HALO, high, jnp.where(place < 2 * HALO, east, jnp.where(place < 3 * HALO, west, low))
    )


def turn(cells, source, target):
    shift = (target - source) % LANES
    return pltpu.roll(cells, shift, 1) if shift else cells


def rows_kernel(thick, drive, obs, first_col, second_col, first_pair, second_pair):
    west, east = sides("gx", first_col[...], second_col[...])
    even = is_even("gy")
    for field, (first, count) in zip((thick, drive.at[0], drive.at[1], obs.at[0], obs.at[1]), STRIP):
        strips = []
        for rows, packed_rows, source, target in (
            (slice(0, count), slice(0, count), first, BAND),
            (slice(TILE - count, TILE), slice(HALF - count, HALF), BAND + first, 0),
        ):
            low, high = field[rows, :LANES], field[rows, LANES:]
            sides_row = choose_side(
                lanes_of(count),
                turn(high, LANES - HALO, target),
                turn(east[packed_rows], source, target + HALO),
                turn(west[packed_rows], source, target + 3 * HALO - count),
                turn(low, 0, target + 3 * HALO),
            )
            strips.append((low, high, sides_row))
        for c in range(3):
            top, bottom = strips[0][c], strips[1][c]
            first_pair[c, first : first + count, :] = jnp.where(even, bottom, top)
            second_pair[c, first : first + count, :] = jnp.where(even, top, bottom)


def shift_east(tiles, lane):
    rolled = [pltpu.roll(t, LANES - 1, 1) for t in tiles]
    if len(tiles) == 1:
        return rolled
    return [jnp.where(lane == LANES - 1, rolled[1 - c], rolled[c]) for c in range(2)]


def shift_west(tiles, lane):
    rolled = [pltpu.roll(t, 1, 1) for t in tiles]
    if len(tiles) == 1:
        return rolled
    return [jnp.where(lane == 0, rolled[1 - c], rolled[c]) for c in range(2)]


def over_rows(framed, read, work):
    start = MARGIN if framed else TOP
    wide = 2 * HALO if framed else 0
    main, side = (TILE + wide) // BLOCKS, (HALF + wide) // BLOCKS
    step = 24 if framed else 32
    groups = [(MAIN, g, step) for g in range(0, main, step)]
    groups[1:1] = [(SIDES, 0, 16)]
    groups[3:3] = [(SIDES, 16, side - 16)]

    def block(i, carry):
        first = {MAIN: pl.multiple_of(start + i * main, 8), SIDES: pl.multiple_of(start + i * side, 8)}
        rows = [(part, first[part] + g, count) for part, g, count in groups]
        pending = [read(*group) for group in rows[:AHEAD]]
        for k, (part, row, count) in enumerate(rows):
            if k + AHEAD < len(rows):
                pending.append(read(*rows[k + AHEAD]))
            for ref, lead, values in work(part, pending[k], lanes_of(count)):
                for tile, value in zip(part, values):
                    ref[(*lead, pl.ds(row + tile, count), slice(None))] = value
        return carry

    lax.fori_loop(0, BLOCKS, block, 0)


def join_parts(ref, leads, whole):
    edge = HALO // 2

    def join(row, upper, lower, count):
        lane = lanes_of(count)
        for lead in leads:
            def at(tile_row):
                return (*lead, pl.ds(tile_row, count), slice(None))

            mixed = ref[at(SIDE + row)]
            if whole:
                place = lane % BAND
                upper_lane = lane < BAND
                from_high = jnp.where(
                    upper_lane,
                    turn(ref[at(ROWS + row)], LANES - HALO, 0),
                    turn(ref[at(ROWS + row + HALF)], LANES - HALO, BAND),
                )
                from_low = jnp.where(
                    upper_lane,
                    turn(ref[at(row)], edge, BAND - edge),
                    turn(ref[at(row + HALF)], edge, LANES - edge),
                )
                ref[at(SIDE + row)] = jnp.where(
                    place < edge, from_high, jnp.where(place >= BAND - edge, from_low, mixed)
                )
            for wanted, band, main_row in ((upper, 0, row), (lower, BAND, row + HALF)):
                if wanted:
                    low = turn(mixed, band + 3 * HALO, 0)
                    high = turn(mixed, band + edge, LANES - edge)
                    ref[at(main_row)] = jnp.where(lane < edge, low, ref[at(main_row)])
                    ref[at(ROWS + main_row)] = jnp.where(lane >= LANES - edge, high, ref[at(ROWS + main_row)])

    step = 32

    def middle(i, carry):
        join(pl.multiple_of(TOP + i * step, 8), True, True, step)
        return carry

    lax.fori_loop(0, HALF // step, middle, 0)
    if whole:
        join(MARGIN, True, False, HALO)
        join(TOP + HALF, False, True, HALO)


def model_kernel(
    ice_mask, patches, thick, drive, obs, first_row, second_row, first_col, second_col,
    vel_u, vel_v, sums,
    ext, fr, ice, visc, vel_a, vel_b, vel_c, coef, small, sems,
):
    tile_cols, tile_rows = ice_mask.shape
    row_tile = lax.axis_index("gy")
    col_tile = lax.axis_index("gx")

    cells = 0.5 * jnp.exp(sum(patches[j] for j in range(tile_rows)))
    lane = lanes_of(PATCH)
    for c in range(2):
        wide = jnp.take_along_axis(cells, 32 * c + lane // 4, axis=1)
        for j in range(4):
            fr[pl.ds(MAIN[c] + MARGIN + j, PATCH, stride=4), :] = wide
    lane = lanes_of(40)
    place = lane % BAND // 4
    source = jnp.where(place < 8, 60 + place, (116 + place) % LANES)
    wide = jnp.where(
        lane < BAND,
        jnp.take_along_axis(cells[:40], source, axis=1),
        jnp.take_along_axis(cells[PATCH - 40 :], source, axis=1),
    )
    for j in range(4):
        fr[pl.ds(SIDE + MARGIN + j, 40, stride=4), :] = wide

    west, east = sides("gx", first_col[...], second_col[...])
    even = is_even("gy")
    lane = lanes_of(HALF)
    upper = lane < BAND
    for f, (field, (first, count)) in enumerate(zip((thick, drive.at[0], drive.at[1], obs.at[0], obs.at[1]), STRIP)):
        scale = 0.5 if f in (1, 2) else 1.0
        frames = []
        for c in range(3):
            one, two = scale * first_row[c, first : first + count, :], scale * second_row[c, first : first + count, :]
            frames.append((jnp.where(even, two, one), jnp.where(even, one, two)))
        for c in range(2):
            ext[f, MAIN[c] + TOP : MAIN[c] + TOP + TILE, :] = scale * field[:, c * LANES : (c + 1) * LANES]
            ext[f, MAIN[c] + TOP - count : MAIN[c] + TOP, :] = frames[c][0]
            ext[f, MAIN[c] + TOP + TILE : MAIN[c] + TOP + TILE + count, :] = frames[c][1]
        halves = (slice(0, HALF), slice(HALF, TILE))
        high = [turn(field[halves[b], LANES:], LANES - HALO, BAND * b) for b in range(2)]
        low = [turn(field[halves[b], :LANES], 0, BAND * b + 3 * HALO) for b in range(2)]
        here = SIDE + TOP
        ext[f, here : here + HALF, :] = scale * choose_side(
            lane,
            jnp.where(upper, high[0], high[1]),
            turn(east, first, HALO),
            turn(west, first, 3 * HALO - count),
            jnp.where(upper, low[0], low[1]),
        )
        upper_few = lanes_of(count) < BAND
        above = turn(ext[f, here + HALF - count : here + HALF, :], 0, BAND)
        below = turn(ext[f, here : here + count, :], 0, BAND)
        ext[f, here - count : here, :] = jnp.where(upper_few, frames[2][0], above)
        ext[f, here + HALF : here + HALF + count, :] = jnp.where(upper_few, below, frames[2][1])

    side_ice = []
    for dr, first, count in ((-1, MARGIN, HALO), (0, TOP, TILE), (1, TOP + TILE, HALO)):
        masks = []
        for ds in (-1, 0, 1):
            row, col = row_tile + dr, col_tile + ds
            inside = (row >= 0) & (row < tile_rows) & (col >= 0) & (col < tile_cols)
            row = jnp.clip(row, 0, tile_rows - 1)
            col = jnp.clip(col, 0, tile_cols - 1)
            masks.append(jnp.where(inside, ice_mask[col, row], 0).astype(jnp.float32))
        for c in range(2):
            ice[MAIN[c] + first : MAIN[c] + first + count, :] = jnp.full((count, LANES), masks[1])
        side_ice.append(choose_side(lanes_of(HALO), masks[1], masks[2], masks[0], masks[1]))
    upper = lanes_of(HALO) < BAND
    for i in range(HALF // HALO):
        ice[SIDE + TOP + i * HALO : SIDE + TOP + (i + 1) * HALO, :] = side_ice[1]
    ice[SIDE + MARGIN : SIDE + TOP, :] = jnp.where(upper, side_ice[0], side_ice[1])
    ice[SIDE + TOP + HALF : SIDE + TOP + HALF + HALO, :] = jnp.where(upper, side_ice[1], side_ice[2])

    def load(ref, part, row, count, *lead):
        return [ref[(*lead, pl.ds(row + tile, count), slice(None))] for tile in part]

    def load_around(part, row, count, now):
        return [load(now, part, r, count, i) for i in range(2) for r in (row, row - 1, row + 1)]

    def load_right(part, row, count):
        return [load(ext, part, row, count, i) for i in (1, 2)]

    def read_thickness(part, row, count):
        return load(ext, part, row, count, 0)

    def first_viscosity(part, thickness, lane):
        factor = 0.25 * visc_scale * strain_floor ** (-1.0 / 3.0)
        return [(visc, (), [factor * t for t in thickness])]

    def read_viscosity(part, row, count):
        return read_thickness(part, row, count), load_around(part, row, count, vel_b)

    def viscosity(part, read, lane):
        thickness, (u, u_n, u_s, v, v_n, v_s) = read
        u_e, u_w = shift_east(u, lane), shift_west(u, lane)
        v_e, v_w = shift_east(v, lane), shift_west(v, lane)
        result = []
        for c in range(len(part)):
            ux, vx = u_e[c] - u_w[c], v_e[c] - v_w[c]
            uy, vy = u_s[c] - u_n[c], v_s[c] - v_n[c]
            shear = uy + vx
            strain = 0.25 * (ux * (ux + vy) + vy * vy) + (0.0625 * (shear * shear) + strain_floor)
            result.append((0.25 * visc_scale) * thickness[c] * jnp.exp(jnp.log(strain) * (-1.0 / 3.0)))
        return [(visc, (), result)]

    def inverse(x):
        near = pl.reciprocal(x, approx=True)
        return near * (2.0 - x * near)

    def read_coefficients(part, row, count):
        around = [load(visc, part, r, count) for r in (row, row - 1, row + 1)]
        return around + [load(fr, part, row, count), load(ice, part, row, count)]

    def coefficients(part, read, lane):
        tiles = range(len(part))
        q, q_n, q_s, friction, mask = read
        q_w = shift_west(q, lane)
        w = [q[c] + q_w[c] for c in tiles]
        e = shift_east(w, lane)
        s = [q[c] + q_s[c] for c in tiles]
        n = [q[c] + q_n[c] for c in tiles]
        scale_u, scale_v = [], []
        for c in tiles:
            across, along = e[c] + w[c], s[c] + n[c]
            scale_u.append(mask[c] * inverse(friction[c] + along + 4.0 * across))
            scale_v.append(mask[c] * inverse(friction[c] + across + 4.0 * along))
        corners = []
        half = [0.5 * q[c] for c in tiles]
        for shifted in (
            shift_west(q_s, lane), shift_west(q_n, lane), shift_east(q_s, lane), shift_east(q_n, lane),
        ):
            corners.append([q[c] + 0.5 * shifted[c] for c in tiles])
            corners.append([half[c] + shifted[c] for c in tiles])
        return [e, w, s, n, scale_u, scale_v] + corners

    def relax(part, k, around, right, lane):
        tiles = range(len(part))
        e, w, s, n, scale_u, scale_v, sw_u, sw_v, nw_u, nw_v, se_u, se_v, ne_u, ne_v = k
        u, u_n, u_s, v, v_n, v_s = around
        to_west_u, to_east_u, to_west_v, to_east_v = [], [], [], []
        for c in tiles:
            u4 = 4.0 * u[c]
            to_west_u.append(w[c] * u4 + (sw_u[c] * v_s[c] - nw_u[c] * v_n[c]))
            to_east_u.append(e[c] * u4 + (ne_u[c] * v_n[c] - se_u[c] * v_s[c]))
            to_west_v.append(w[c] * v[c] + (sw_v[c] * u_s[c] - nw_v[c] * u_n[c]))
            to_east_v.append(e[c] * v[c] + (ne_v[c] * u_n[c] - se_v[c] * u_s[c]))
        to_west_u, to_west_v = shift_east(to_west_u, lane), shift_east(to_west_v, lane)
        to_east_u, to_east_v = shift_west(to_east_u, lane), shift_west(to_east_v, lane)
        new_u, new_v = [], []
        for c in tiles:
            mid_u = s[c] * u_s[c] + n[c] * u_n[c]
            mid_v = 4.0 * (s[c] * v_s[c] + n[c] * v_n[c])
            new_u.append(scale_u[c] * (right[0][c] + mid_u + (to_west_u[c] + to_east_u[c])))
            new_v.append(scale_v[c] * (right[1][c] + mid_v + (to_west_v[c] + to_east_v[c])))
        return new_u, new_v

    def put(new, values):
        return [(new, (i,), values[i]) for i in range(2)]

    def keep(k):
        return [(coef, (i,), k[i]) for i in range(14)]

    def sweep(framed, now, new):
        def read(part, row, count):
            k = [load(coef, part, row, count, i) for i in range(14)]
            return k, load_around(part, row, count, now), load_right(part, row, count)

        over_rows(framed, read, lambda part, read, lane: put(new, relax(part, *read, lane)))

    def read_first(part, row, count):
        return read_coefficients(part, row, count), load_right(part, row, count)

    def first_start(part, read, lane):
        k = coefficients(part, read[0], lane)
        return keep(k) + put(vel_a, [[a * b for a, b in zip(k[4 + i], read[1][i])] for i in range(2)])

    def read_start(part, row, count):
        return (*read_first(part, row, count), load_around(part, row, count, vel_b))

    def start(part, read, lane):
        k = coefficients(part, read[0], lane)
        return keep(k) + put(vel_a, relax(part, k, read[2], read[1], lane))

    over_rows(True, read_thickness, first_viscosity)
    over_rows(True, read_first, first_start)
    sweep(True, vel_a, vel_b)

    def iteration(i, carry):
        @pl.when(i == PIC - 1)
        def _():
            join_parts(vel_b, ((0,), (1,)), True)

        over_rows(True, read_viscosity, viscosity)
        over_rows(True, read_start, start)
        sweep(True, vel_a, vel_b)
        return carry

    lax.fori_loop(1, PIC, iteration, 0)
    join_parts(vel_b, ((0,), (1,)), False)
    copies = []
    for i, out in enumerate((vel_u, vel_v)):
        for c in range(2):
            copies.append(
                pltpu.make_async_copy(
                    vel_b.at[i, MAIN[c] + TOP : MAIN[c] + TOP + TILE, :],
                    out.at[:, c * LANES : (c + 1) * LANES],
                    sems.at[2 * i + c],
                )
            )
            copies[-1].start()

    def read_misfit(part, row, count):
        return [
            [load(vel_b, part, row, count, i), load(ext, part, row, count, 3 + i), load(coef, part, row, count, 4 + i)]
            for i in range(2)
        ]

    def first_adjoint(part, read, lane):
        misfit = [[0.5 * (a - b) for a, b in zip(u, seen)] for u, seen, _ in read]
        first = [[a * b for a, b in zip(read[i][2], misfit[i])] for i in range(2)]
        return put(vel_c, first) + [(ext, (1 + i,), misfit[i]) for i in range(2)]

    over_rows(True, read_misfit, first_adjoint)

    def two_sweeps(i, carry):
        sweep(True, vel_c, vel_a)
        sweep(True, vel_a, vel_c)
        return carry

    lax.fori_loop(0, (ADJ - 2) // 2, two_sweeps, 0)
    sweep(False, vel_c, vel_a)

    def read_gradient(part, row, count):
        return [load(ref, part, row, count, i) for ref in (vel_b, vel_a) for i in range(2)] + [load(fr, part, row, count)]

    def gradient(part, read, lane):
        u, v, lu, lv, friction = read
        return [(visc, (), [-2.0 * friction[c] * (u[c] * lu[c] + v[c] * lv[c]) for c in range(len(part))])]

    over_rows(False, read_gradient, gradient)
    join_parts(visc, ((),), False)
    down = [sum(visc[pl.ds(MAIN[c] + TOP + j, CT, stride=4), :] for j in range(4)) for c in range(2)]
    k = lax.broadcasted_iota(jnp.int32, (LANES, LANES), 0)
    l = lanes_of(LANES) % CT
    total = jnp.zeros((CT, LANES), jnp.float32)
    for c in range(2):
        total += jnp.dot(
            down[c],
            (k // 4 + 32 * c == l).astype(jnp.float32),
            precision=lax.Precision.HIGHEST,
            preferred_element_type=jnp.float32,
        )
    small[...] = total
    packed = jnp.where(
        lanes_of(PACK) < CT, small[pl.ds(0, PACK, stride=2), :], small[pl.ds(1, PACK, stride=2), :]
    )
    part = PACK // sums.shape[0]
    for i in range(sums.shape[0]):
        for j in range(sums.shape[1]):
            sums[i, j] = packed[i * part : (i + 1) * part]
    for copy in copies:
        copy.wait()


def pick_kernel(tile_block, gathered, out):
    owned = out.shape[1]
    first = lax.axis_index("gy") * owned
    tile_cols, tile_rows = tile_block.shape
    total = [jnp.zeros(out.shape[2:], jnp.float32) for _ in range(owned)]
    for t in range(tile_cols * tile_rows):
        place = tile_block[t // tile_rows, t % tile_rows] - first
        cells = gathered[t]
        total = [total[b] + jnp.where(place == b, cells, 0.0) for b in range(owned)]
    for b in range(owned):
        for j in range(out.shape[0]):
            out[j, b] = total[b]


def join_kernel(parts, out):
    share = parts.shape[2]
    for i in range(parts.shape[0]):
        for j in range(share):
            at = (i * share + j) * LANES
            out[:, at : at + LANES] = parts[i, :, j, :]


def in_vmem(count):
    return [pl.BlockSpec(memory_space=pltpu.VMEM)] * count


def in_smem(count):
    return [pl.BlockSpec(memory_space=pltpu.SMEM)] * count


def per_device(thickness, driving, observed, control, ice_mask, tile_block):
    f32 = jnp.float32
    rows, cols = lax.axis_size("gy"), lax.axis_size("gx")
    tile_block, ice_mask = tile_block[:, :, 0].T, ice_mask.T
    params = pltpu.CompilerParams(vmem_limit_bytes=VMEM_LIMIT)

    def shape(*sizes):
        return jax.ShapeDtypeStruct(sizes, f32)

    def swap(axis, cells_first, cells_second):
        count = lax.axis_size(axis)
        received = []
        for cells, low in ((cells_second, 1), (cells_first, 0)):
            pairs = [(i, i + 1) for i in range(low, count - 1, 2)]
            received.append(lax.ppermute(cells, axis, pairs + [(j, i) for i, j in pairs]))
        return received[1], received[0]

    fields = thickness, driving, observed
    columns = pl.pallas_call(
        columns_kernel,
        out_shape=[shape(HALF, LANES)] * 2,
        in_specs=[pl.BlockSpec(memory_space=pltpu.HBM)] * 3,
        out_specs=in_vmem(2),
        scratch_shapes=[pltpu.VMEM((5, TILE, TILE), f32), pltpu.SemaphoreType.DMA((5,))],
        compiler_params=pltpu.CompilerParams(vmem_limit_bytes=PACK_VMEM_LIMIT),
        name="columns",
    )(*fields)
    columns_in = swap("gx", *columns)
    patches = pl.pallas_call(
        patches_kernel,
        out_shape=shape(rows, PATCH, LANES),
        in_specs=in_smem(1) + in_vmem(1),
        out_specs=pl.BlockSpec(memory_space=pltpu.VMEM),
        scratch_shapes=[pltpu.VMEM((control.shape[0], PACK, LANES), f32)],
        compiler_params=params,
        name="patches",
    )(tile_block, control)
    patches = lax.all_to_all(patches, "gy", 0, 0, tiled=True)
    strips = pl.pallas_call(
        rows_kernel,
        out_shape=[shape(3, 64, LANES)] * 2,
        in_specs=in_vmem(5),
        out_specs=in_vmem(2),
        compiler_params=params,
        name="rows",
    )(*fields, *columns_in)
    rows_in = swap("gy", *strips)

    vel_u, vel_v, sums = pl.pallas_call(
        model_kernel,
        out_shape=(shape(TILE, TILE), shape(TILE, TILE), shape(cols, rows, PACK // cols, LANES)),
        in_specs=in_smem(1) + in_vmem(8),
        out_specs=[pl.BlockSpec(memory_space=pltpu.HBM)] * 2 + in_vmem(1),
        scratch_shapes=[
            pltpu.VMEM((5, ALL_ROWS, LANES), f32),
            pltpu.VMEM((ALL_ROWS, LANES), f32),
            pltpu.VMEM((ALL_ROWS, LANES), f32),
            pltpu.VMEM((ALL_ROWS, LANES), f32),
            pltpu.VMEM((2, ALL_ROWS, LANES), f32),
            pltpu.VMEM((2, ALL_ROWS, LANES), f32),
            pltpu.VMEM((2, ALL_ROWS, LANES), f32),
            pltpu.VMEM((14, ALL_ROWS, LANES), f32),
            pltpu.VMEM((CT, LANES), f32),
            pltpu.SemaphoreType.DMA((4,)),
        ],
        compiler_params=params,
        name="model",
    )(ice_mask, patches, *fields, *rows_in, *columns_in)

    share = (control.shape[0], PACK // cols, LANES)
    sums = lax.all_to_all(sums.reshape(cols * rows, *share[1:]), ("gx", "gy"), 0, 0, tiled=True)
    parts = pl.pallas_call(
        pick_kernel,
        out_shape=shape(cols, *share),
        in_specs=in_smem(1) + in_vmem(1),
        out_specs=pl.BlockSpec(memory_space=pltpu.VMEM),
        compiler_params=params,
        name="pick",
    )(tile_block, sums)
    gradient = pl.pallas_call(
        join_kernel,
        out_shape=shape(*control.shape),
        in_specs=in_vmem(1),
        out_specs=pl.BlockSpec(memory_space=pltpu.VMEM),
        compiler_params=params,
        name="join",
    )(lax.all_to_all(parts, "gx", 0, 0, tiled=True))
    return vel_u, vel_v, gradient


def solution(mesh):
    return jax.shard_map(
        per_device,
        mesh=mesh,
        in_specs=(P("gy", "gx"), P(None, "gy", "gx"), P(None, "gy", "gx"), P("gy", None), P(), P()),
        out_specs=(P("gy", "gx"), P("gy", "gx"), P("gy", None)),
        check_vma=False,
    )
```

```python
import jax
import jax.numpy as jnp
from jax import lax
from jax.experimental import pallas as pl
from jax.experimental.pallas import tpu as pltpu
from jax.sharding import PartitionSpec as P

TILE = 256
PIC = 4
SW = 2
ADJ = 6
CT = 64
COARSE = 4096

LANES = 128
HALO = 16
OBS = 8
MARGIN = 8
TOP = MARGIN + HALO
ROWS = TILE + 2 * TOP
HALF = TILE // 2
SIDE = 2 * ROWS
BAND = LANES // 2
ALL_ROWS = SIDE + HALF + 2 * TOP
MAIN = (0, ROWS)
SIDES = (SIDE,)
BLOCKS = 2
AHEAD = 2
PACK = COARSE // LANES
VMEM_LIMIT = 40 * 1024 * 1024
PACK_VMEM_LIMIT = 62 * 1024 * 1024

STRIP = ((0, HALO), (HALO, HALO), (2 * HALO, HALO), (3 * HALO, OBS), (3 * HALO + OBS, OBS))

CONTROL = ((0, 0, PACK, 0), (-1, PACK - 2, 2, PACK), (1, 0, 2, PACK + 2))
FOLDED = 40
CORNERS = 48
PARCEL = 64
PATCH = CT + 8

visc_scale = 0.1
strain_floor = 0.05


def lanes_of(rows):
    return lax.broadcasted_iota(jnp.int32, (rows, LANES), 1)


def is_even(axis):
    return lax.axis_index(axis) % 2 == 0


def side_lanes(rows, ds, group):
    place = (lanes_of(rows) - 8 * group) % CT
    return place < 4 if ds > 0 else place >= CT - 4


def fill_parcels(tile_block, owned_blocks, parcels):
    tile_cols, tile_rows = tile_block.shape
    owned = owned_blocks.shape[0]
    mine = lax.axis_index("gy") * owned
    col_tile = lax.axis_index("gx")

    def spread(row, carry):
        for ds in (-1, 0, 1):
            col = col_tile + ds
            place = tile_block[jnp.clip(col, 0, tile_cols - 1), row] - mine

            @pl.when((col >= 0) & (col < tile_cols) & (place >= 0) & (place < owned))
            def _():
                for dr, first, count, at in CONTROL:
                    target = row - dr

                    @pl.when((target >= 0) & (target < tile_rows))
                    def _():
                        if ds == 0:
                            parcels[target, at : at + count, :] = owned_blocks[place, first : first + count, :]
                            return
                        start = FOLDED + at % 8
                        rows = min(count, 8)
                        folded = parcels[target, start : start + rows, :]
                        for i in range(count // rows):
                            group = at // 8 + i
                            cells = owned_blocks[place, first + 8 * i : first + 8 * i + rows, :]
                            folded = jnp.where(side_lanes(rows, ds, group), turn(cells, 0, 8 * group), folded)
                        parcels[target, start : start + rows, :] = folded

        return carry

    lax.fori_loop(0, tile_rows, spread, 0)


def pack_kernel(
    tile_block, control, thick, drive, obs, first_col, second_col, first_row, second_row, parcels,
    held, held_control, owned_blocks, sems,
):
    copies = [pltpu.make_async_copy(control, held_control, sems.at[5])]
    for f, field in enumerate((thick, drive.at[0], drive.at[1], obs.at[0], obs.at[1])):
        copies.append(pltpu.make_async_copy(field, held.at[f], sems.at[f]))
    for copy in copies:
        copy.start()
    parcels[...] = jnp.zeros_like(parcels)
    copies[0].wait()
    for j in range(PACK):
        owned_blocks[:, j, :] = held_control[:, j * LANES : (j + 1) * LANES]
    fill_parcels(tile_block, owned_blocks, parcels)

    lane = lanes_of(HALF)
    left = jnp.zeros((HALF, LANES), jnp.float32)
    right = jnp.zeros((HALF, LANES), jnp.float32)
    even_row, even_col = is_even("gy"), is_even("gx")
    for f, (first, count) in enumerate(STRIP):
        copies[1 + f].wait()
        for c in range(2):
            cols = slice(c * LANES, (c + 1) * LANES)
            top, bottom = held[f, 0:count, cols], held[f, TILE - count : TILE, cols]
            first_row[c, first : first + count, :] = jnp.where(even_row, bottom, top)
            second_row[c, first : first + count, :] = jnp.where(even_row, top, bottom)
        for part in range(2):
            rows = slice(part * HALF, (part + 1) * HALF)
            start = part * BAND + first
            inside = (lane >= start) & (lane < start + count)
            left = jnp.where(inside, turn(held[f, rows, :LANES], 0, start), left)
            right = jnp.where(inside, turn(held[f, rows, LANES:], LANES - count, start), right)
    first_col[...] = jnp.where(even_col, right, left)
    second_col[...] = jnp.where(even_col, left, right)


def corners_kernel(parcels_in, first_col, second_col, parcels):
    west, east = sides("gx", first_col[...], second_col[...])
    row_tile = lax.axis_index("gy")
    lane = lanes_of(8)
    parcels[...] = parcels_in[...]
    for bottom, target, inside in (
        (0, row_tile - 1, row_tile > 0),
        (1, row_tile + 1, row_tile < parcels.shape[0] - 1),
    ):
        @pl.when(inside)
        def _():
            for half in range(2):
                packed = jnp.zeros((8, LANES), jnp.float32)
                for q, f in enumerate((0, 1, 2, 3 + half)):
                    first, count = STRIP[f]
                    row = 8 * half if q < 3 else 0
                    row = HALF - count + row if bottom else row
                    source = BAND * bottom + first
                    start = 2 * HALO * q
                    from_east = turn(east[row : row + 8], source, start)
                    from_west = turn(west[row : row + 8], source, start + 2 * HALO - count)
                    packed = jnp.where((lane >= start) & (lane < start + HALO), from_east, packed)
                    packed = jnp.where((lane >= start + HALO) & (lane < start + 2 * HALO), from_west, packed)
                at = CORNERS + 8 * half
                parcels[target, at : at + 8, :] = packed


def sides(axis, first_pair, second_pair):
    even = is_even(axis)
    return jnp.where(even, second_pair, first_pair), jnp.where(even, first_pair, second_pair)


def choose_side(lane, high, east, west, low):
    place = lane % BAND
    return jnp.where(
        place < HALO, high, jnp.where(place < 2 * HALO, east, jnp.where(place < 3 * HALO, west, low))
    )


def turn(cells, source, target):
    shift = (target - source) % LANES
    return pltpu.roll(cells, shift, 1) if shift else cells


def shift_east(tiles, lane):
    rolled = [pltpu.roll(t, LANES - 1, 1) for t in tiles]
    if len(tiles) == 1:
        return rolled
    return [jnp.where(lane == LANES - 1, rolled[1 - c], rolled[c]) for c in range(2)]


def shift_west(tiles, lane):
    rolled = [pltpu.roll(t, 1, 1) for t in tiles]
    if len(tiles) == 1:
        return rolled
    return [jnp.where(lane == 0, rolled[1 - c], rolled[c]) for c in range(2)]


def over_rows(framed, read, work):
    start = MARGIN if framed else TOP
    wide = 2 * HALO if framed else 0
    main, side = (TILE + wide) // BLOCKS, (HALF + wide) // BLOCKS
    step = 24 if framed else 32
    groups = [(g / main, MAIN, g, step) for g in range(0, main, step)]
    groups += [((g + 1) / side, SIDES, g, 16) for g in range(0, side, 16)]
    groups = [group[1:] for group in sorted(groups)]

    def block(i, carry):
        first = {MAIN: pl.multiple_of(start + i * main, 8), SIDES: pl.multiple_of(start + i * side, 8)}
        rows = [(part, first[part] + g, count) for part, g, count in groups]
        pending = [read(*group) for group in rows[:AHEAD]]
        for k, (part, row, count) in enumerate(rows):
            if k + AHEAD < len(rows):
                pending.append(read(*rows[k + AHEAD]))
            for ref, lead, values in work(part, pending[k], lanes_of(count)):
                for tile, value in zip(part, values):
                    ref[(*lead, pl.ds(row + tile, count), slice(None))] = value
        return carry

    lax.fori_loop(0, BLOCKS, block, 0)


def join_parts(ref, leads, whole):
    edge = HALO // 2

    def join(row, upper, lower, count):
        lane = lanes_of(count)
        for lead in leads:
            def at(tile_row):
                return (*lead, pl.ds(tile_row, count), slice(None))

            mixed = ref[at(SIDE + row)]
            if whole:
                place = lane % BAND
                upper_lane = lane < BAND
                from_high = jnp.where(
                    upper_lane,
                    turn(ref[at(ROWS + row)], LANES - HALO, 0),
                    turn(ref[at(ROWS + row + HALF)], LANES - HALO, BAND),
                )
                from_low = jnp.where(
                    upper_lane,
                    turn(ref[at(row)], edge, BAND - edge),
                    turn(ref[at(row + HALF)], edge, LANES - edge),
                )
                ref[at(SIDE + row)] = jnp.where(
                    place < edge, from_high, jnp.where(place >= BAND - edge, from_low, mixed)
                )
            for wanted, band, main_row in ((upper, 0, row), (lower, BAND, row + HALF)):
                if wanted:
                    low = turn(mixed, band + 3 * HALO, 0)
                    high = turn(mixed, band + edge, LANES - edge)
                    ref[at(main_row)] = jnp.where(lane < edge, low, ref[at(main_row)])
                    ref[at(ROWS + main_row)] = jnp.where(lane >= LANES - edge, high, ref[at(ROWS + main_row)])

    step = 32

    def middle(i, carry):
        join(pl.multiple_of(TOP + i * step, 8), True, True, step)
        return carry

    lax.fori_loop(0, HALF // step, middle, 0)
    if whole:
        join(MARGIN, True, False, HALO)
        join(TOP + HALF, False, True, HALO)


def model_kernel(
    ice_mask, parcels, thick, drive, obs, first_row, second_row, first_col, second_col,
    vel_u, vel_v, sums,
    ext, fr, ice, visc, vel_a, vel_b, vel_c, coef, small, patch, sems,
):
    tile_cols, tile_rows = ice_mask.shape
    row_tile = lax.axis_index("gy")
    col_tile = lax.axis_index("gx")

    flat = sum(parcels[j, :CORNERS, :] for j in range(tile_rows))
    folded = flat[FOLDED:]
    for dr, _, count, at in CONTROL:
        cells = flat[at : at + count]
        if dr == 0:
            side = jnp.concatenate([turn(folded, 8 * g, 0) for g in range(PACK // 8)], axis=0)
        else:
            side = turn(folded, PACK, 0)[at % 8 : at % 8 + count]
        inner = lanes_of(count) < CT
        row = 4 + {-1: -4, 0: 0, 1: CT}[dr]
        patch[pl.ds(row, count, stride=2), :] = jnp.where(inner, cells, turn(side, 0, CT))
        patch[pl.ds(row + 1, count, stride=2), :] = jnp.where(inner, turn(cells, 0, CT), side)

    cells = 0.5 * jnp.exp(patch[...])
    lane = lanes_of(PATCH)
    for c in range(2):
        wide = jnp.take_along_axis(cells, 32 * c + lane // 4, axis=1)
        for j in range(4):
            fr[pl.ds(MAIN[c] + MARGIN + j, PATCH, stride=4), :] = wide
    lane = lanes_of(40)
    place = lane % BAND // 4
    source = jnp.where(place < 8, 60 + place, (116 + place) % LANES)
    wide = jnp.where(
        lane < BAND,
        jnp.take_along_axis(cells[:40], source, axis=1),
        jnp.take_along_axis(cells[PATCH - 40 :], source, axis=1),
    )
    for j in range(4):
        fr[pl.ds(SIDE + MARGIN + j, 40, stride=4), :] = wide

    west, east = sides("gx", first_col[...], second_col[...])
    corners = []
    for target, inside in ((row_tile - 1, row_tile > 0), (row_tile + 1, row_tile < tile_rows - 1)):
        cells = parcels[jnp.clip(target, 0, tile_rows - 1), CORNERS:, :]
        corners.append(jnp.where(inside, cells, 0.0))
    even = is_even("gy")
    lane = lanes_of(HALF)
    upper = lane < BAND
    for f, (field, (first, count)) in enumerate(zip((thick, drive.at[0], drive.at[1], obs.at[0], obs.at[1]), STRIP)):
        scale = 0.5 if f in (1, 2) else 1.0
        north, south = [], []
        for c in range(2):
            one, two = scale * first_row[c, first : first + count, :], scale * second_row[c, first : first + count, :]
            north.append(jnp.where(even, two, one))
            south.append(jnp.where(even, one, two))
            ext[f, MAIN[c] + TOP : MAIN[c] + TOP + TILE, :] = scale * field[:, c * LANES : (c + 1) * LANES]
            ext[f, MAIN[c] + TOP - count : MAIN[c] + TOP, :] = north[c]
            ext[f, MAIN[c] + TOP + TILE : MAIN[c] + TOP + TILE + count, :] = south[c]
        halves = (slice(0, HALF), slice(HALF, TILE))
        high = [turn(field[halves[b], LANES:], LANES - HALO, BAND * b) for b in range(2)]
        low = [turn(field[halves[b], :LANES], 0, BAND * b + 3 * HALO) for b in range(2)]
        here = SIDE + TOP
        ext[f, here : here + HALF, :] = scale * choose_side(
            lane,
            jnp.where(upper, high[0], high[1]),
            turn(east, first, HALO),
            turn(west, first, 3 * HALO - count),
            jnp.where(upper, low[0], low[1]),
        )
        few = lanes_of(count)
        ends = []
        for band, (low, high), cells in ((0, north, corners[0]), (BAND, south, corners[1])):
            cells = cells if f < 3 else cells[8 * (f - 3) : 8 * (f - 2)]
            frame = scale * turn(cells, 2 * HALO * min(f, 3), band + HALO)
            ends.append(
                choose_side(few, turn(high, LANES - HALO, band), frame, frame, turn(low, 0, band + 3 * HALO))
            )
        above = turn(ext[f, here + HALF - count : here + HALF, :], 0, BAND)
        below = turn(ext[f, here : here + count, :], 0, BAND)
        ext[f, here - count : here, :] = jnp.where(few < BAND, ends[0], above)
        ext[f, here + HALF : here + HALF + count, :] = jnp.where(few < BAND, below, ends[1])

    side_ice = []
    for dr, first, count in ((-1, MARGIN, HALO), (0, TOP, TILE), (1, TOP + TILE, HALO)):
        masks = []
        for ds in (-1, 0, 1):
            row, col = row_tile + dr, col_tile + ds
            inside = (row >= 0) & (row < tile_rows) & (col >= 0) & (col < tile_cols)
            row = jnp.clip(row, 0, tile_rows - 1)
            col = jnp.clip(col, 0, tile_cols - 1)
            masks.append(jnp.where(inside, ice_mask[col, row], 0).astype(jnp.float32))
        for c in range(2):
            ice[MAIN[c] + first : MAIN[c] + first + count, :] = jnp.full((count, LANES), masks[1])
        side_ice.append(choose_side(lanes_of(HALO), masks[1], masks[2], masks[0], masks[1]))
    upper = lanes_of(HALO) < BAND
    for i in range(HALF // HALO):
        ice[SIDE + TOP + i * HALO : SIDE + TOP + (i + 1) * HALO, :] = side_ice[1]
    ice[SIDE + MARGIN : SIDE + TOP, :] = jnp.where(upper, side_ice[0], side_ice[1])
    ice[SIDE + TOP + HALF : SIDE + TOP + HALF + HALO, :] = jnp.where(upper, side_ice[1], side_ice[2])

    def load(ref, part, row, count, *lead):
        return [ref[(*lead, pl.ds(row + tile, count), slice(None))] for tile in part]

    def load_around(part, row, count, now):
        return [load(now, part, r, count, i) for i in range(2) for r in (row, row - 1, row + 1)]

    def load_right(part, row, count):
        return [load(ext, part, row, count, i) for i in (1, 2)]

    def read_thickness(part, row, count):
        return load(ext, part, row, count, 0)

    def first_viscosity(part, thickness, lane):
        factor = 0.25 * visc_scale * strain_floor ** (-1.0 / 3.0)
        return [(visc, (), [factor * t for t in thickness])]

    def read_viscosity(part, row, count):
        return read_thickness(part, row, count), load_around(part, row, count, vel_b)

    def viscosity(part, read, lane):
        thickness, (u, u_n, u_s, v, v_n, v_s) = read
        u_e, u_w = shift_east(u, lane), shift_west(u, lane)
        v_e, v_w = shift_east(v, lane), shift_west(v, lane)
        result = []
        for c in range(len(part)):
            ux, vx = u_e[c] - u_w[c], v_e[c] - v_w[c]
            uy, vy = u_s[c] - u_n[c], v_s[c] - v_n[c]
            shear = uy + vx
            strain = 0.25 * (ux * (ux + vy) + vy * vy) + (0.0625 * (shear * shear) + strain_floor)
            result.append((0.25 * visc_scale) * thickness[c] * jnp.exp(jnp.log(strain) * (-1.0 / 3.0)))
        return [(visc, (), result)]

    def inverse(x):
        near = pl.reciprocal(x, approx=True)
        return near * (2.0 - x * near)

    def read_coefficients(part, row, count):
        around = [load(visc, part, r, count) for r in (row, row - 1, row + 1)]
        return around + [load(fr, part, row, count), load(ice, part, row, count)]

    def coefficients(part, read, lane):
        tiles = range(len(part))
        q, q_n, q_s, friction, mask = read
        q_w = shift_west(q, lane)
        w = [q[c] + q_w[c] for c in tiles]
        e = shift_east(w, lane)
        s = [q[c] + q_s[c] for c in tiles]
        n = [q[c] + q_n[c] for c in tiles]
        scale_u, scale_v = [], []
        for c in tiles:
            across, along = e[c] + w[c], s[c] + n[c]
            scale_u.append(mask[c] * inverse(friction[c] + along + 4.0 * across))
            scale_v.append(mask[c] * inverse(friction[c] + across + 4.0 * along))
        corners = []
        half = [0.5 * q[c] for c in tiles]
        for shifted in (
            shift_west(q_s, lane), shift_west(q_n, lane), shift_east(q_s, lane), shift_east(q_n, lane),
        ):
            corners.append([q[c] + 0.5 * shifted[c] for c in tiles])
            corners.append([half[c] + shifted[c] for c in tiles])
        return [e, w, s, n, scale_u, scale_v] + corners

    def relax(part, k, around, right, lane):
        tiles = range(len(part))
        e, w, s, n, scale_u, scale_v, sw_u, sw_v, nw_u, nw_v, se_u, se_v, ne_u, ne_v = k
        u, u_n, u_s, v, v_n, v_s = around
        to_west_u, to_east_u, to_west_v, to_east_v = [], [], [], []
        for c in tiles:
            u4 = 4.0 * u[c]
            to_west_u.append(w[c] * u4 + (sw_u[c] * v_s[c] - nw_u[c] * v_n[c]))
            to_east_u.append(e[c] * u4 + (ne_u[c] * v_n[c] - se_u[c] * v_s[c]))
            to_west_v.append(w[c] * v[c] + (sw_v[c] * u_s[c] - nw_v[c] * u_n[c]))
            to_east_v.append(e[c] * v[c] + (ne_v[c] * u_n[c] - se_v[c] * u_s[c]))
        to_west_u, to_west_v = shift_east(to_west_u, lane), shift_east(to_west_v, lane)
        to_east_u, to_east_v = shift_west(to_east_u, lane), shift_west(to_east_v, lane)
        new_u, new_v = [], []
        for c in tiles:
            mid_u = s[c] * u_s[c] + n[c] * u_n[c]
            mid_v = 4.0 * (s[c] * v_s[c] + n[c] * v_n[c])
            new_u.append(scale_u[c] * (right[0][c] + mid_u + (to_west_u[c] + to_east_u[c])))
            new_v.append(scale_v[c] * (right[1][c] + mid_v + (to_west_v[c] + to_east_v[c])))
        return new_u, new_v

    def put(new, values):
        return [(new, (i,), values[i]) for i in range(2)]

    def keep(k):
        return [(coef, (i,), k[i]) for i in range(14)]

    def sweep(framed, now, new):
        def read(part, row, count):
            k = [load(coef, part, row, count, i) for i in range(14)]
            return k, load_around(part, row, count, now), load_right(part, row, count)

        over_rows(framed, read, lambda part, read, lane: put(new, relax(part, *read, lane)))

    def read_first(part, row, count):
        return read_coefficients(part, row, count), load_right(part, row, count)

    def first_start(part, read, lane):
        k = coefficients(part, read[0], lane)
        return keep(k) + put(vel_a, [[a * b for a, b in zip(k[4 + i], read[1][i])] for i in range(2)])

    def read_start(part, row, count):
        return (*read_first(part, row, count), load_around(part, row, count, vel_b))

    def start(part, read, lane):
        k = coefficients(part, read[0], lane)
        return keep(k) + put(vel_a, relax(part, k, read[2], read[1], lane))

    over_rows(True, read_thickness, first_viscosity)
    over_rows(True, read_first, first_start)
    sweep(True, vel_a, vel_b)

    def iteration(i, carry):
        @pl.when(i == PIC - 1)
        def _():
            join_parts(vel_b, ((0,), (1,)), True)

        over_rows(True, read_viscosity, viscosity)
        over_rows(True, read_start, start)
        sweep(True, vel_a, vel_b)
        return carry

    lax.fori_loop(1, PIC, iteration, 0)
    join_parts(vel_b, ((0,), (1,)), False)
    copies = []
    for i, out in enumerate((vel_u, vel_v)):
        for c in range(2):
            copies.append(
                pltpu.make_async_copy(
                    vel_b.at[i, MAIN[c] + TOP : MAIN[c] + TOP + TILE, :],
                    out.at[:, c * LANES : (c + 1) * LANES],
                    sems.at[2 * i + c],
                )
            )
            copies[-1].start()

    def read_misfit(part, row, count):
        return [
            [load(vel_b, part, row, count, i), load(ext, part, row, count, 3 + i), load(coef, part, row, count, 4 + i)]
            for i in range(2)
        ]

    def first_adjoint(part, read, lane):
        misfit = [[0.5 * (a - b) for a, b in zip(u, seen)] for u, seen, _ in read]
        first = [[a * b for a, b in zip(read[i][2], misfit[i])] for i in range(2)]
        return put(vel_c, first) + [(ext, (1 + i,), misfit[i]) for i in range(2)]

    over_rows(True, read_misfit, first_adjoint)

    def two_sweeps(i, carry):
        sweep(True, vel_c, vel_a)
        sweep(True, vel_a, vel_c)
        return carry

    lax.fori_loop(0, (ADJ - 2) // 2, two_sweeps, 0)
    sweep(False, vel_c, vel_a)

    def read_gradient(part, row, count):
        return [load(ref, part, row, count, i) for ref in (vel_b, vel_a) for i in range(2)] + [load(fr, part, row, count)]

    def gradient(part, read, lane):
        u, v, lu, lv, friction = read
        return [(visc, (), [-2.0 * friction[c] * (u[c] * lu[c] + v[c] * lv[c]) for c in range(len(part))])]

    over_rows(False, read_gradient, gradient)
    join_parts(visc, ((),), False)
    down = [sum(visc[pl.ds(MAIN[c] + TOP + j, CT, stride=4), :] for j in range(4)) for c in range(2)]
    k = lax.broadcasted_iota(jnp.int32, (LANES, LANES), 0)
    l = lanes_of(LANES) % CT
    total = jnp.zeros((CT, LANES), jnp.float32)
    for c in range(2):
        total += jnp.dot(
            down[c],
            (k // 4 + 32 * c == l).astype(jnp.float32),
            precision=lax.Precision.HIGHEST,
            preferred_element_type=jnp.float32,
        )
    small[...] = total
    packed = jnp.where(
        lanes_of(PACK) < CT, small[pl.ds(0, PACK, stride=2), :], small[pl.ds(1, PACK, stride=2), :]
    )
    part = PACK // sums.shape[0]
    for i in range(sums.shape[0]):
        for j in range(sums.shape[1]):
            sums[i, j] = packed[i * part : (i + 1) * part]
    for copy in copies:
        copy.wait()


def pick_kernel(tile_block, gathered, out):
    owned = out.shape[1]
    first = lax.axis_index("gy") * owned
    tile_cols, tile_rows = tile_block.shape
    total = [jnp.zeros(out.shape[2:], jnp.float32) for _ in range(owned)]
    for t in range(tile_cols * tile_rows):
        place = tile_block[t // tile_rows, t % tile_rows] - first
        cells = gathered[t]
        total = [total[b] + jnp.where(place == b, cells, 0.0) for b in range(owned)]
    for b in range(owned):
        for j in range(out.shape[0]):
            out[j, b] = total[b]


def join_kernel(parts, out):
    share = parts.shape[2]
    for i in range(parts.shape[0]):
        for j in range(share):
            at = (i * share + j) * LANES
            out[:, at : at + LANES] = parts[i, :, j, :]


def in_vmem(count):
    return [pl.BlockSpec(memory_space=pltpu.VMEM)] * count


def in_smem(count):
    return [pl.BlockSpec(memory_space=pltpu.SMEM)] * count


def per_device(thickness, driving, observed, control, ice_mask, tile_block):
    f32 = jnp.float32
    rows, cols = lax.axis_size("gy"), lax.axis_size("gx")
    tile_block, ice_mask = tile_block[:, :, 0].T, ice_mask.T
    params = pltpu.CompilerParams(vmem_limit_bytes=VMEM_LIMIT)

    def shape(*sizes):
        return jax.ShapeDtypeStruct(sizes, f32)

    def swap(axis, cells_first, cells_second):
        count = lax.axis_size(axis)
        received = []
        for cells, low in ((cells_second, 1), (cells_first, 0)):
            pairs = [(i, i + 1) for i in range(low, count - 1, 2)]
            received.append(lax.ppermute(cells, axis, pairs + [(j, i) for i, j in pairs]))
        return received[1], received[0]

    fields = thickness, driving, observed
    owned = control.shape[0]
    *edges, parcels = pl.pallas_call(
        pack_kernel,
        out_shape=[shape(HALF, LANES)] * 2 + [shape(2, 64, LANES)] * 2 + [shape(rows, PARCEL, LANES)],
        in_specs=in_smem(1) + [pl.BlockSpec(memory_space=pltpu.HBM)] * 4,
        out_specs=in_vmem(5),
        scratch_shapes=[
            pltpu.VMEM((5, TILE, TILE), f32),
            pltpu.VMEM(control.shape, f32),
            pltpu.VMEM((owned, PACK, LANES), f32),
            pltpu.SemaphoreType.DMA((6,)),
        ],
        compiler_params=pltpu.CompilerParams(vmem_limit_bytes=PACK_VMEM_LIMIT),
        name="pack",
    )(tile_block, control, *fields)
    columns_in = swap("gx", *edges[:2])
    rows_in = swap("gy", *edges[2:])
    parcels = pl.pallas_call(
        corners_kernel,
        out_shape=shape(*parcels.shape),
        in_specs=in_vmem(3),
        out_specs=pl.BlockSpec(memory_space=pltpu.VMEM),
        compiler_params=params,
        name="corners",
    )(parcels, *columns_in)
    parcels = lax.all_to_all(parcels, "gy", 0, 0, tiled=True)

    vel_u, vel_v, sums = pl.pallas_call(
        model_kernel,
        out_shape=(shape(TILE, TILE), shape(TILE, TILE), shape(cols, rows, PACK // cols, LANES)),
        in_specs=in_smem(1) + in_vmem(8),
        out_specs=[pl.BlockSpec(memory_space=pltpu.HBM)] * 2 + in_vmem(1),
        scratch_shapes=[
            pltpu.VMEM((5, ALL_ROWS, LANES), f32),
            pltpu.VMEM((ALL_ROWS, LANES), f32),
            pltpu.VMEM((ALL_ROWS, LANES), f32),
            pltpu.VMEM((ALL_ROWS, LANES), f32),
            pltpu.VMEM((2, ALL_ROWS, LANES), f32),
            pltpu.VMEM((2, ALL_ROWS, LANES), f32),
            pltpu.VMEM((2, ALL_ROWS, LANES), f32),
            pltpu.VMEM((14, ALL_ROWS, LANES), f32),
            pltpu.VMEM((CT, LANES), f32),
            pltpu.VMEM((PATCH, LANES), f32),
            pltpu.SemaphoreType.DMA((4,)),
        ],
        compiler_params=params,
        name="model",
    )(ice_mask, parcels, *fields, *rows_in, *columns_in)

    share = (control.shape[0], PACK // cols, LANES)
    sums = lax.all_to_all(sums.reshape(cols * rows, *share[1:]), ("gx", "gy"), 0, 0, tiled=True)
    parts = pl.pallas_call(
        pick_kernel,
        out_shape=shape(cols, *share),
        in_specs=in_smem(1) + in_vmem(1),
        out_specs=pl.BlockSpec(memory_space=pltpu.VMEM),
        compiler_params=params,
        name="pick",
    )(tile_block, sums)
    gradient = pl.pallas_call(
        join_kernel,
        out_shape=shape(*control.shape),
        in_specs=in_vmem(1),
        out_specs=pl.BlockSpec(memory_space=pltpu.VMEM),
        compiler_params=params,
        name="join",
    )(lax.all_to_all(parts, "gx", 0, 0, tiled=True))
    return vel_u, vel_v, gradient


def solution(mesh):
    return jax.shard_map(
        per_device,
        mesh=mesh,
        in_specs=(P("gy", "gx"), P(None, "gy", "gx"), P(None, "gy", "gx"), P("gy", None), P(), P()),
        out_specs=(P("gy", "gx"), P("gy", "gx"), P("gy", None)),
        check_vma=False,
    )
```

```python
import jax
import jax.numpy as jnp
from jax import lax
from jax.experimental import pallas as pl
from jax.experimental.pallas import tpu as pltpu
from jax.sharding import PartitionSpec as P

TILE = 256
PIC = 4
SW = 2
ADJ = 6
CT = 64
COARSE = 4096

LANES = 128
HALO = 16
OBS = 8
MARGIN = 8
TOP = MARGIN + HALO
ROWS = TILE + 2 * TOP
HALF = TILE // 2
SIDE = 2 * ROWS
BAND = LANES // 2
ALL_ROWS = SIDE + HALF + 2 * TOP
MAIN = (0, ROWS)
SIDES = (SIDE,)
BLOCKS = 4
AHEAD = 2
PACK = COARSE // LANES
VMEM_LIMIT = 40 * 1024 * 1024
PACK_VMEM_LIMIT = 62 * 1024 * 1024

STRIP = ((0, HALO), (HALO, HALO), (2 * HALO, HALO), (3 * HALO, OBS), (3 * HALO + OBS, OBS))

CONTROL = ((0, 0, PACK, 0), (-1, PACK - 2, 2, PACK), (1, 0, 2, PACK + 2))
FOLDED = 40
PARCEL = 48
PATCH = CT + 8

visc_scale = 0.1
strain_floor = 0.05


def lanes_of(rows):
    return lax.broadcasted_iota(jnp.int32, (rows, LANES), 1)


def is_even(axis):
    return lax.axis_index(axis) % 2 == 0


def side_lanes(rows, ds, group):
    place = (lanes_of(rows) - 8 * group) % CT
    return place < 4 if ds > 0 else place >= CT - 4


def fill_parcels(tile_block, owned_blocks, parcels):
    tile_cols, tile_rows = tile_block.shape
    owned = owned_blocks.shape[0]
    mine = lax.axis_index("gy") * owned
    col_tile = lax.axis_index("gx")

    def spread(row, carry):
        for ds in (-1, 0, 1):
            col = col_tile + ds
            place = tile_block[jnp.clip(col, 0, tile_cols - 1), row] - mine

            @pl.when((col >= 0) & (col < tile_cols) & (place >= 0) & (place < owned))
            def _():
                for dr, first, count, at in CONTROL:
                    target = row - dr

                    @pl.when((target >= 0) & (target < tile_rows))
                    def _():
                        if ds == 0:
                            parcels[target, at : at + count, :] = owned_blocks[place, first : first + count, :]
                            return
                        start = FOLDED + at % 8
                        rows = min(count, 8)
                        folded = parcels[target, start : start + rows, :]
                        for i in range(count // rows):
                            group = at // 8 + i
                            cells = owned_blocks[place, first + 8 * i : first + 8 * i + rows, :]
                            folded = jnp.where(side_lanes(rows, ds, group), turn(cells, 0, 8 * group), folded)
                        parcels[target, start : start + rows, :] = folded

        return carry

    lax.fori_loop(0, tile_rows, spread, 0)


def pack_kernel(
    tile_block, control, thick, drive, obs, first_col, second_col, parcels,
    held, held_control, owned_blocks, sems,
):
    copies = [pltpu.make_async_copy(control, held_control, sems.at[5])]
    for f, field in enumerate((thick, drive.at[0], drive.at[1], obs.at[0], obs.at[1])):
        copies.append(pltpu.make_async_copy(field, held.at[f], sems.at[f]))
    for copy in copies:
        copy.start()
    parcels[...] = jnp.zeros_like(parcels)
    copies[0].wait()
    for j in range(PACK):
        owned_blocks[:, j, :] = held_control[:, j * LANES : (j + 1) * LANES]
    fill_parcels(tile_block, owned_blocks, parcels)

    lane = lanes_of(HALF)
    left = jnp.zeros((HALF, LANES), jnp.float32)
    right = jnp.zeros((HALF, LANES), jnp.float32)
    for f, (first, count) in enumerate(STRIP):
        copies[1 + f].wait()
        for part in range(2):
            rows = slice(part * HALF, (part + 1) * HALF)
            start = part * BAND + first
            inside = (lane >= start) & (lane < start + count)
            left = jnp.where(inside, turn(held[f, rows, :LANES], 0, start), left)
            right = jnp.where(inside, turn(held[f, rows, LANES:], LANES - count, start), right)
    even = is_even("gx")
    first_col[...] = jnp.where(even, right, left)
    second_col[...] = jnp.where(even, left, right)


def sides(axis, first_pair, second_pair):
    even = is_even(axis)
    return jnp.where(even, second_pair, first_pair), jnp.where(even, first_pair, second_pair)


def choose_side(lane, high, east, west, low):
    place = lane % BAND
    return jnp.where(
        place < HALO, high, jnp.where(place < 2 * HALO, east, jnp.where(place < 3 * HALO, west, low))
    )


def turn(cells, source, target):
    shift = (target - source) % LANES
    return pltpu.roll(cells, shift, 1) if shift else cells


def rows_kernel(thick, drive, obs, first_col, second_col, first_pair, second_pair):
    west, east = sides("gx", first_col[...], second_col[...])
    even = is_even("gy")
    for field, (first, count) in zip((thick, drive.at[0], drive.at[1], obs.at[0], obs.at[1]), STRIP):
        strips = []
        for rows, packed_rows, source, target in (
            (slice(0, count), slice(0, count), first, BAND),
            (slice(TILE - count, TILE), slice(HALF - count, HALF), BAND + first, 0),
        ):
            low, high = field[rows, :LANES], field[rows, LANES:]
            sides_row = choose_side(
                lanes_of(count),
                turn(high, LANES - HALO, target),
                turn(east[packed_rows], source, target + HALO),
                turn(west[packed_rows], source, target + 3 * HALO - count),
                turn(low, 0, target + 3 * HALO),
            )
            strips.append((low, high, sides_row))
        for c in range(3):
            top, bottom = strips[0][c], strips[1][c]
            first_pair[c, first : first + count, :] = jnp.where(even, bottom, top)
            second_pair[c, first : first + count, :] = jnp.where(even, top, bottom)


def shift_east(tiles, lane):
    rolled = [pltpu.roll(t, LANES - 1, 1) for t in tiles]
    if len(tiles) == 1:
        return rolled
    return [jnp.where(lane == LANES - 1, rolled[1 - c], rolled[c]) for c in range(2)]


def shift_west(tiles, lane):
    rolled = [pltpu.roll(t, 1, 1) for t in tiles]
    if len(tiles) == 1:
        return rolled
    return [jnp.where(lane == 0, rolled[1 - c], rolled[c]) for c in range(2)]


def over_rows(framed, read, work):
    start = MARGIN if framed else TOP
    wide = 2 * HALO if framed else 0
    main, side = (TILE + wide) // BLOCKS, (HALF + wide) // BLOCKS
    step = 24 if framed else 32
    groups = [(MAIN, g, step) for g in range(0, main, step)]
    groups[1:1] = [(SIDES, 0, 16)]
    groups[3:3] = [(SIDES, 16, side - 16)]

    def block(i, carry):
        first = {MAIN: pl.multiple_of(start + i * main, 8), SIDES: pl.multiple_of(start + i * side, 8)}
        rows = [(part, first[part] + g, count) for part, g, count in groups]
        pending = [read(*group) for group in rows[:AHEAD]]
        for k, (part, row, count) in enumerate(rows):
            if k + AHEAD < len(rows):
                pending.append(read(*rows[k + AHEAD]))
            for ref, lead, values in work(part, pending[k], lanes_of(count)):
                for tile, value in zip(part, values):
                    ref[(*lead, pl.ds(row + tile, count), slice(None))] = value
        return carry

    lax.fori_loop(0, BLOCKS, block, 0)


def join_parts(ref, leads, whole):
    edge = HALO // 2

    def join(row, upper, lower, count):
        lane = lanes_of(count)
        for lead in leads:
            def at(tile_row):
                return (*lead, pl.ds(tile_row, count), slice(None))

            mixed = ref[at(SIDE + row)]
            if whole:
                place = lane % BAND
                upper_lane = lane < BAND
                from_high = jnp.where(
                    upper_lane,
                    turn(ref[at(ROWS + row)], LANES - HALO, 0),
                    turn(ref[at(ROWS + row + HALF)], LANES - HALO, BAND),
                )
                from_low = jnp.where(
                    upper_lane,
                    turn(ref[at(row)], edge, BAND - edge),
                    turn(ref[at(row + HALF)], edge, LANES - edge),
                )
                ref[at(SIDE + row)] = jnp.where(
                    place < edge, from_high, jnp.where(place >= BAND - edge, from_low, mixed)
                )
            for wanted, band, main_row in ((upper, 0, row), (lower, BAND, row + HALF)):
                if wanted:
                    low = turn(mixed, band + 3 * HALO, 0)
                    high = turn(mixed, band + edge, LANES - edge)
                    ref[at(main_row)] = jnp.where(lane < edge, low, ref[at(main_row)])
                    ref[at(ROWS + main_row)] = jnp.where(lane >= LANES - edge, high, ref[at(ROWS + main_row)])

    step = 32

    def middle(i, carry):
        join(pl.multiple_of(TOP + i * step, 8), True, True, step)
        return carry

    lax.fori_loop(0, HALF // step, middle, 0)
    if whole:
        join(MARGIN, True, False, HALO)
        join(TOP + HALF, False, True, HALO)


def setup_kernel(
    ice_mask, parcels, thick, drive, obs, first_col, second_col,
    fr, ice, middle,
    patch,
):
    tile_cols, tile_rows = ice_mask.shape
    row_tile = lax.axis_index("gy")
    col_tile = lax.axis_index("gx")

    flat = sum(parcels[j] for j in range(tile_rows))
    folded = flat[FOLDED:]
    for dr, _, count, at in CONTROL:
        cells = flat[at : at + count]
        if dr == 0:
            side = jnp.concatenate([turn(folded, 8 * g, 0) for g in range(PACK // 8)], axis=0)
        else:
            side = turn(folded, PACK, 0)[at % 8 : at % 8 + count]
        inner = lanes_of(count) < CT
        row = 4 + {-1: -4, 0: 0, 1: CT}[dr]
        patch[pl.ds(row, count, stride=2), :] = jnp.where(inner, cells, turn(side, 0, CT))
        patch[pl.ds(row + 1, count, stride=2), :] = jnp.where(inner, turn(cells, 0, CT), side)

    cells = 0.5 * jnp.exp(patch[...])
    lane = lanes_of(PATCH)
    for c in range(2):
        wide = jnp.take_along_axis(cells, 32 * c + lane // 4, axis=1)
        for j in range(4):
            fr[pl.ds(MAIN[c] + MARGIN + j, PATCH, stride=4), :] = wide
    lane = lanes_of(40)
    place = lane % BAND // 4
    source = jnp.where(place < 8, 60 + place, (116 + place) % LANES)
    wide = jnp.where(
        lane < BAND,
        jnp.take_along_axis(cells[:40], source, axis=1),
        jnp.take_along_axis(cells[PATCH - 40 :], source, axis=1),
    )
    for j in range(4):
        fr[pl.ds(SIDE + MARGIN + j, 40, stride=4), :] = wide

    west, east = sides("gx", first_col[...], second_col[...])
    lane = lanes_of(HALF)
    upper = lane < BAND
    for f, (field, (first, count)) in enumerate(zip((thick, drive.at[0], drive.at[1], obs.at[0], obs.at[1]), STRIP)):
        halves = (slice(0, HALF), slice(HALF, TILE))
        high = [turn(field[halves[b], LANES:], LANES - HALO, BAND * b) for b in range(2)]
        low = [turn(field[halves[b], :LANES], 0, BAND * b + 3 * HALO) for b in range(2)]
        middle[f] = (0.5 if f in (1, 2) else 1.0) * choose_side(
            lane,
            jnp.where(upper, high[0], high[1]),
            turn(east, first, HALO),
            turn(west, first, 3 * HALO - count),
            jnp.where(upper, low[0], low[1]),
        )

    side_ice = []
    for dr, first, count in ((-1, MARGIN, HALO), (0, TOP, TILE), (1, TOP + TILE, HALO)):
        masks = []
        for ds in (-1, 0, 1):
            row, col = row_tile + dr, col_tile + ds
            inside = (row >= 0) & (row < tile_rows) & (col >= 0) & (col < tile_cols)
            row = jnp.clip(row, 0, tile_rows - 1)
            col = jnp.clip(col, 0, tile_cols - 1)
            masks.append(jnp.where(inside, ice_mask[col, row], 0).astype(jnp.float32))
        for c in range(2):
            ice[MAIN[c] + first : MAIN[c] + first + count, :] = jnp.full((count, LANES), masks[1])
        side_ice.append(choose_side(lanes_of(HALO), masks[1], masks[2], masks[0], masks[1]))
    upper = lanes_of(HALO) < BAND
    for i in range(HALF // HALO):
        ice[SIDE + TOP + i * HALO : SIDE + TOP + (i + 1) * HALO, :] = side_ice[1]
    ice[SIDE + MARGIN : SIDE + TOP, :] = jnp.where(upper, side_ice[0], side_ice[1])
    ice[SIDE + TOP + HALF : SIDE + TOP + HALF + HALO, :] = jnp.where(upper, side_ice[1], side_ice[2])


def model_kernel(
    fr, ice, middle, thick, drive, obs, first_row, second_row,
    vel_u, vel_v, sums,
    ext, visc, vel_a, vel_b, vel_c, coef, small, sems,
):
    even = is_even("gy")
    for f, (field, (first, count)) in enumerate(zip((thick, drive.at[0], drive.at[1], obs.at[0], obs.at[1]), STRIP)):
        scale = 0.5 if f in (1, 2) else 1.0
        frames = []
        for c in range(3):
            one, two = scale * first_row[c, first : first + count, :], scale * second_row[c, first : first + count, :]
            frames.append((jnp.where(even, two, one), jnp.where(even, one, two)))
        for c in range(2):
            ext[f, MAIN[c] + TOP : MAIN[c] + TOP + TILE, :] = scale * field[:, c * LANES : (c + 1) * LANES]
            ext[f, MAIN[c] + TOP - count : MAIN[c] + TOP, :] = frames[c][0]
            ext[f, MAIN[c] + TOP + TILE : MAIN[c] + TOP + TILE + count, :] = frames[c][1]
        here = SIDE + TOP
        ext[f, here : here + HALF, :] = middle[f]
        upper = lanes_of(count) < BAND
        above = turn(middle[f, HALF - count :, :], 0, BAND)
        below = turn(middle[f, :count, :], 0, BAND)
        ext[f, here - count : here, :] = jnp.where(upper, frames[2][0], above)
        ext[f, here + HALF : here + HALF + count, :] = jnp.where(upper, below, frames[2][1])

    def load(ref, part, row, count, *lead):
        return [ref[(*lead, pl.ds(row + tile, count), slice(None))] for tile in part]

    def load_around(part, row, count, now):
        return [load(now, part, r, count, i) for i in range(2) for r in (row, row - 1, row + 1)]

    def load_right(part, row, count):
        return [load(ext, part, row, count, i) for i in (1, 2)]

    def read_thickness(part, row, count):
        return load(ext, part, row, count, 0)

    def first_viscosity(part, thickness, lane):
        factor = 0.25 * visc_scale * strain_floor ** (-1.0 / 3.0)
        return [(visc, (), [factor * t for t in thickness])]

    def read_viscosity(part, row, count):
        return read_thickness(part, row, count), load_around(part, row, count, vel_b)

    def viscosity(part, read, lane):
        thickness, (u, u_n, u_s, v, v_n, v_s) = read
        u_e, u_w = shift_east(u, lane), shift_west(u, lane)
        v_e, v_w = shift_east(v, lane), shift_west(v, lane)
        result = []
        for c in range(len(part)):
            ux, vx = u_e[c] - u_w[c], v_e[c] - v_w[c]
            uy, vy = u_s[c] - u_n[c], v_s[c] - v_n[c]
            shear = uy + vx
            strain = 0.25 * (ux * (ux + vy) + vy * vy) + (0.0625 * (shear * shear) + strain_floor)
            result.append((0.25 * visc_scale) * thickness[c] * jnp.exp(jnp.log(strain) * (-1.0 / 3.0)))
        return [(visc, (), result)]

    def inverse(x):
        near = pl.reciprocal(x, approx=True)
        return near * (2.0 - x * near)

    def read_coefficients(part, row, count):
        around = [load(visc, part, r, count) for r in (row, row - 1, row + 1)]
        return around + [load(fr, part, row, count), load(ice, part, row, count)]

    def coefficients(part, read, lane):
        tiles = range(len(part))
        q, q_n, q_s, friction, mask = read
        q_w = shift_west(q, lane)
        w = [q[c] + q_w[c] for c in tiles]
        e = shift_east(w, lane)
        s = [q[c] + q_s[c] for c in tiles]
        n = [q[c] + q_n[c] for c in tiles]
        scale_u, scale_v = [], []
        for c in tiles:
            across, along = e[c] + w[c], s[c] + n[c]
            scale_u.append(mask[c] * inverse(friction[c] + along + 4.0 * across))
            scale_v.append(mask[c] * inverse(friction[c] + across + 4.0 * along))
        corners = []
        half = [0.5 * q[c] for c in tiles]
        for shifted in (
            shift_west(q_s, lane), shift_west(q_n, lane), shift_east(q_s, lane), shift_east(q_n, lane),
        ):
            corners.append([q[c] + 0.5 * shifted[c] for c in tiles])
            corners.append([half[c] + shifted[c] for c in tiles])
        return [e, w, s, n, scale_u, scale_v] + corners

    def relax(part, k, around, right, lane):
        tiles = range(len(part))
        e, w, s, n, scale_u, scale_v, sw_u, sw_v, nw_u, nw_v, se_u, se_v, ne_u, ne_v = k
        u, u_n, u_s, v, v_n, v_s = around
        to_west_u, to_east_u, to_west_v, to_east_v = [], [], [], []
        for c in tiles:
            u4 = 4.0 * u[c]
            to_west_u.append(w[c] * u4 + (sw_u[c] * v_s[c] - nw_u[c] * v_n[c]))
            to_east_u.append(e[c] * u4 + (ne_u[c] * v_n[c] - se_u[c] * v_s[c]))
            to_west_v.append(w[c] * v[c] + (sw_v[c] * u_s[c] - nw_v[c] * u_n[c]))
            to_east_v.append(e[c] * v[c] + (ne_v[c] * u_n[c] - se_v[c] * u_s[c]))
        to_west_u, to_west_v = shift_east(to_west_u, lane), shift_east(to_west_v, lane)
        to_east_u, to_east_v = shift_west(to_east_u, lane), shift_west(to_east_v, lane)
        new_u, new_v = [], []
        for c in tiles:
            mid_u = s[c] * u_s[c] + n[c] * u_n[c]
            mid_v = 4.0 * (s[c] * v_s[c] + n[c] * v_n[c])
            new_u.append(scale_u[c] * (right[0][c] + mid_u + (to_west_u[c] + to_east_u[c])))
            new_v.append(scale_v[c] * (right[1][c] + mid_v + (to_west_v[c] + to_east_v[c])))
        return new_u, new_v

    def put(new, values):
        return [(new, (i,), values[i]) for i in range(2)]

    def keep(k):
        return [(coef, (i,), k[i]) for i in range(14)]

    def sweep(framed, now, new):
        def read(part, row, count):
            k = [load(coef, part, row, count, i) for i in range(14)]
            return k, load_around(part, row, count, now), load_right(part, row, count)

        over_rows(framed, read, lambda part, read, lane: put(new, relax(part, *read, lane)))

    def read_first(part, row, count):
        return read_coefficients(part, row, count), load_right(part, row, count)

    def first_start(part, read, lane):
        k = coefficients(part, read[0], lane)
        return keep(k) + put(vel_a, [[a * b for a, b in zip(k[4 + i], read[1][i])] for i in range(2)])

    def read_start(part, row, count):
        return (*read_first(part, row, count), load_around(part, row, count, vel_b))

    def start(part, read, lane):
        k = coefficients(part, read[0], lane)
        return keep(k) + put(vel_a, relax(part, k, read[2], read[1], lane))

    over_rows(True, read_thickness, first_viscosity)
    over_rows(True, read_first, first_start)
    sweep(True, vel_a, vel_b)

    def iteration(i, carry):
        @pl.when(i == PIC - 1)
        def _():
            join_parts(vel_b, ((0,), (1,)), True)

        over_rows(True, read_viscosity, viscosity)
        over_rows(True, read_start, start)
        sweep(True, vel_a, vel_b)
        return carry

    lax.fori_loop(1, PIC, iteration, 0)
    join_parts(vel_b, ((0,), (1,)), False)
    copies = []
    for i, out in enumerate((vel_u, vel_v)):
        for c in range(2):
            copies.append(
                pltpu.make_async_copy(
                    vel_b.at[i, MAIN[c] + TOP : MAIN[c] + TOP + TILE, :],
                    out.at[:, c * LANES : (c + 1) * LANES],
                    sems.at[2 * i + c],
                )
            )
            copies[-1].start()

    def read_misfit(part, row, count):
        return [
            [load(vel_b, part, row, count, i), load(ext, part, row, count, 3 + i), load(coef, part, row, count, 4 + i)]
            for i in range(2)
        ]

    def first_adjoint(part, read, lane):
        misfit = [[0.5 * (a - b) for a, b in zip(u, seen)] for u, seen, _ in read]
        first = [[a * b for a, b in zip(read[i][2], misfit[i])] for i in range(2)]
        return put(vel_c, first) + [(ext, (1 + i,), misfit[i]) for i in range(2)]

    over_rows(True, read_misfit, first_adjoint)

    def two_sweeps(i, carry):
        sweep(True, vel_c, vel_a)
        sweep(True, vel_a, vel_c)
        return carry

    lax.fori_loop(0, (ADJ - 2) // 2, two_sweeps, 0)
    sweep(False, vel_c, vel_a)

    def read_gradient(part, row, count):
        return [load(ref, part, row, count, i) for ref in (vel_b, vel_a) for i in range(2)] + [load(fr, part, row, count)]

    def gradient(part, read, lane):
        u, v, lu, lv, friction = read
        return [(visc, (), [-2.0 * friction[c] * (u[c] * lu[c] + v[c] * lv[c]) for c in range(len(part))])]

    over_rows(False, read_gradient, gradient)
    join_parts(visc, ((),), False)
    down = [sum(visc[pl.ds(MAIN[c] + TOP + j, CT, stride=4), :] for j in range(4)) for c in range(2)]
    k = lax.broadcasted_iota(jnp.int32, (LANES, LANES), 0)
    l = lanes_of(LANES) % CT
    total = jnp.zeros((CT, LANES), jnp.float32)
    for c in range(2):
        total += jnp.dot(
            down[c],
            (k // 4 + 32 * c == l).astype(jnp.float32),
            precision=lax.Precision.HIGHEST,
            preferred_element_type=jnp.float32,
        )
    small[...] = total
    packed = jnp.where(
        lanes_of(PACK) < CT, small[pl.ds(0, PACK, stride=2), :], small[pl.ds(1, PACK, stride=2), :]
    )
    part = PACK // sums.shape[0]
    for i in range(sums.shape[0]):
        for j in range(sums.shape[1]):
            sums[i, j] = packed[i * part : (i + 1) * part]
    for copy in copies:
        copy.wait()


def pick_kernel(tile_block, gathered, out):
    owned = out.shape[1]
    first = lax.axis_index("gy") * owned
    tile_cols, tile_rows = tile_block.shape
    total = [jnp.zeros(out.shape[2:], jnp.float32) for _ in range(owned)]
    for t in range(tile_cols * tile_rows):
        place = tile_block[t // tile_rows, t % tile_rows] - first
        cells = gathered[t]
        total = [total[b] + jnp.where(place == b, cells, 0.0) for b in range(owned)]
    for b in range(owned):
        for j in range(out.shape[0]):
            out[j, b] = total[b]


def join_kernel(parts, out):
    share = parts.shape[2]
    for i in range(parts.shape[0]):
        for j in range(share):
            at = (i * share + j) * LANES
            out[:, at : at + LANES] = parts[i, :, j, :]


def in_vmem(count):
    return [pl.BlockSpec(memory_space=pltpu.VMEM)] * count


def in_smem(count):
    return [pl.BlockSpec(memory_space=pltpu.SMEM)] * count


def per_device(thickness, driving, observed, control, ice_mask, tile_block):
    f32 = jnp.float32
    rows, cols = lax.axis_size("gy"), lax.axis_size("gx")
    tile_block, ice_mask = tile_block[:, :, 0].T, ice_mask.T
    params = pltpu.CompilerParams(vmem_limit_bytes=VMEM_LIMIT)

    def shape(*sizes):
        return jax.ShapeDtypeStruct(sizes, f32)

    def swap(axis, cells_first, cells_second):
        count = lax.axis_size(axis)
        received = []
        for cells, low in ((cells_second, 1), (cells_first, 0)):
            pairs = [(i, i + 1) for i in range(low, count - 1, 2)]
            received.append(lax.ppermute(cells, axis, pairs + [(j, i) for i, j in pairs]))
        return received[1], received[0]

    fields = thickness, driving, observed
    owned = control.shape[0]
    *edges, parcels = pl.pallas_call(
        pack_kernel,
        out_shape=[shape(HALF, LANES)] * 2 + [shape(rows, PARCEL, LANES)],
        in_specs=in_smem(1) + [pl.BlockSpec(memory_space=pltpu.HBM)] * 4,
        out_specs=in_vmem(3),
        scratch_shapes=[
            pltpu.VMEM((5, TILE, TILE), f32),
            pltpu.VMEM(control.shape, f32),
            pltpu.VMEM((owned, PACK, LANES), f32),
            pltpu.SemaphoreType.DMA((6,)),
        ],
        compiler_params=pltpu.CompilerParams(vmem_limit_bytes=PACK_VMEM_LIMIT),
        name="pack",
    )(tile_block, control, *fields)
    parcels = lax.all_to_all(parcels, "gy", 0, 0, tiled=True)
    columns_in = swap("gx", *edges)
    strips = pl.pallas_call(
        rows_kernel,
        out_shape=[shape(3, 64, LANES)] * 2,
        in_specs=in_vmem(5),
        out_specs=in_vmem(2),
        compiler_params=params,
        name="rows",
    )(*fields, *columns_in)
    rows_in = swap("gy", *strips)
    prepared = pl.pallas_call(
        setup_kernel,
        out_shape=[shape(ALL_ROWS, LANES)] * 2 + [shape(5, HALF, LANES)],
        in_specs=in_smem(1) + in_vmem(6),
        out_specs=in_vmem(3),
        scratch_shapes=[pltpu.VMEM((PATCH, LANES), f32)],
        compiler_params=params,
        name="setup",
    )(ice_mask, parcels, *fields, *columns_in)

    vel_u, vel_v, sums = pl.pallas_call(
        model_kernel,
        out_shape=(shape(TILE, TILE), shape(TILE, TILE), shape(cols, rows, PACK // cols, LANES)),
        in_specs=in_vmem(8),
        out_specs=[pl.BlockSpec(memory_space=pltpu.HBM)] * 2 + in_vmem(1),
        scratch_shapes=[
            pltpu.VMEM((5, ALL_ROWS, LANES), f32),
            pltpu.VMEM((ALL_ROWS, LANES), f32),
            pltpu.VMEM((2, ALL_ROWS, LANES), f32),
            pltpu.VMEM((2, ALL_ROWS, LANES), f32),
            pltpu.VMEM((2, ALL_ROWS, LANES), f32),
            pltpu.VMEM((14, ALL_ROWS, LANES), f32),
            pltpu.VMEM((CT, LANES), f32),
            pltpu.SemaphoreType.DMA((4,)),
        ],
        compiler_params=params,
        name="model",
    )(*prepared, *fields, *rows_in)

    share = (control.shape[0], PACK // cols, LANES)
    sums = lax.all_to_all(sums.reshape(cols * rows, *share[1:]), ("gx", "gy"), 0, 0, tiled=True)
    parts = pl.pallas_call(
        pick_kernel,
        out_shape=shape(cols, *share),
        in_specs=in_smem(1) + in_vmem(1),
        out_specs=pl.BlockSpec(memory_space=pltpu.VMEM),
        compiler_params=params,
        name="pick",
    )(tile_block, sums)
    gradient = pl.pallas_call(
        join_kernel,
        out_shape=shape(*control.shape),
        in_specs=in_vmem(1),
        out_specs=pl.BlockSpec(memory_space=pltpu.VMEM),
        compiler_params=params,
        name="join",
    )(lax.all_to_all(parts, "gx", 0, 0, tiled=True))
    return vel_u, vel_v, gradient


def solution(mesh):
    return jax.shard_map(
        per_device,
        mesh=mesh,
        in_specs=(P("gy", "gx"), P(None, "gy", "gx"), P(None, "gy", "gx"), P("gy", None), P(), P()),
        out_specs=(P("gy", "gx"), P("gy", "gx"), P("gy", None)),
        check_vma=False,
    )
```

```python
import jax
import jax.numpy as jnp
from jax import lax
from jax.experimental import pallas as pl
from jax.experimental.pallas import tpu as pltpu
from jax.sharding import PartitionSpec as P

TILE = 256
PIC = 4
SW = 2
ADJ = 6
CT = 64
COARSE = 4096

LANES = 128
HALO = 16
OBS = 8
MARGIN = 8
TOP = MARGIN + HALO
ROWS = TILE + 2 * TOP
HALF = TILE // 2
SIDE = 2 * ROWS
BAND = LANES // 2
ALL_ROWS = SIDE + HALF + 2 * TOP
MAIN = (0, ROWS)
SIDES = (SIDE,)
BLOCKS = 4
FACTORS = 10
AHEAD = 2
PACK = COARSE // LANES
VMEM_LIMIT = 40 * 1024 * 1024
PACK_VMEM_LIMIT = 62 * 1024 * 1024

STRIP = ((0, HALO), (HALO, HALO), (2 * HALO, HALO), (3 * HALO, OBS), (3 * HALO + OBS, OBS))

CONTROL = ((0, 0, PACK, 0), (-1, PACK - 2, 2, PACK), (1, 0, 2, PACK + 2))
FOLDED = 40
PARCEL = 48
PATCH = CT + 8

visc_scale = 0.1
strain_floor = 0.05


def lanes_of(rows):
    return lax.broadcasted_iota(jnp.int32, (rows, LANES), 1)


def is_even(axis):
    return lax.axis_index(axis) % 2 == 0


def side_lanes(rows, ds, group):
    place = (lanes_of(rows) - 8 * group) % CT
    return place < 4 if ds > 0 else place >= CT - 4


def fill_parcels(tile_block, owned_blocks, parcels):
    tile_cols, tile_rows = tile_block.shape
    owned = owned_blocks.shape[0]
    mine = lax.axis_index("gy") * owned
    col_tile = lax.axis_index("gx")

    def spread(row, carry):
        for ds in (-1, 0, 1):
            col = col_tile + ds
            place = tile_block[jnp.clip(col, 0, tile_cols - 1), row] - mine

            @pl.when((col >= 0) & (col < tile_cols) & (place >= 0) & (place < owned))
            def _():
                for dr, first, count, at in CONTROL:
                    target = row - dr

                    @pl.when((target >= 0) & (target < tile_rows))
                    def _():
                        if ds == 0:
                            parcels[target, at : at + count, :] = owned_blocks[place, first : first + count, :]
                            return
                        start = FOLDED + at % 8
                        rows = min(count, 8)
                        folded = parcels[target, start : start + rows, :]
                        for i in range(count // rows):
                            group = at // 8 + i
                            cells = owned_blocks[place, first + 8 * i : first + 8 * i + rows, :]
                            folded = jnp.where(side_lanes(rows, ds, group), turn(cells, 0, 8 * group), folded)
                        parcels[target, start : start + rows, :] = folded

        return carry

    lax.fori_loop(0, tile_rows, spread, 0)


def pack_kernel(
    tile_block, control, thick, drive, obs, first_col, second_col, parcels,
    held, held_control, owned_blocks, sems,
):
    copies = [pltpu.make_async_copy(control, held_control, sems.at[5])]
    for f, field in enumerate((thick, drive.at[0], drive.at[1], obs.at[0], obs.at[1])):
        copies.append(pltpu.make_async_copy(field, held.at[f], sems.at[f]))
    for copy in copies:
        copy.start()
    parcels[...] = jnp.zeros_like(parcels)
    copies[0].wait()
    for j in range(PACK):
        owned_blocks[:, j, :] = held_control[:, j * LANES : (j + 1) * LANES]
    fill_parcels(tile_block, owned_blocks, parcels)

    lane = lanes_of(HALF)
    left = jnp.zeros((HALF, LANES), jnp.float32)
    right = jnp.zeros((HALF, LANES), jnp.float32)
    for f, (first, count) in enumerate(STRIP):
        copies[1 + f].wait()
        for part in range(2):
            rows = slice(part * HALF, (part + 1) * HALF)
            start = part * BAND + first
            inside = (lane >= start) & (lane < start + count)
            left = jnp.where(inside, turn(held[f, rows, :LANES], 0, start), left)
            right = jnp.where(inside, turn(held[f, rows, LANES:], LANES - count, start), right)
    even = is_even("gx")
    first_col[...] = jnp.where(even, right, left)
    second_col[...] = jnp.where(even, left, right)


def sides(axis, first_pair, second_pair):
    even = is_even(axis)
    return jnp.where(even, second_pair, first_pair), jnp.where(even, first_pair, second_pair)


def choose_side(lane, high, east, west, low):
    place = lane % BAND
    return jnp.where(
        place < HALO, high, jnp.where(place < 2 * HALO, east, jnp.where(place < 3 * HALO, west, low))
    )


def turn(cells, source, target):
    shift = (target - source) % LANES
    return pltpu.roll(cells, shift, 1) if shift else cells


def rows_kernel(thick, drive, obs, first_col, second_col, first_pair, second_pair):
    west, east = sides("gx", first_col[...], second_col[...])
    even = is_even("gy")
    for field, (first, count) in zip((thick, drive.at[0], drive.at[1], obs.at[0], obs.at[1]), STRIP):
        strips = []
        for rows, packed_rows, source, target in (
            (slice(0, count), slice(0, count), first, BAND),
            (slice(TILE - count, TILE), slice(HALF - count, HALF), BAND + first, 0),
        ):
            low, high = field[rows, :LANES], field[rows, LANES:]
            sides_row = choose_side(
                lanes_of(count),
                turn(high, LANES - HALO, target),
                turn(east[packed_rows], source, target + HALO),
                turn(west[packed_rows], source, target + 3 * HALO - count),
                turn(low, 0, target + 3 * HALO),
            )
            strips.append((low, high, sides_row))
        for c in range(3):
            top, bottom = strips[0][c], strips[1][c]
            first_pair[c, first : first + count, :] = jnp.where(even, bottom, top)
            second_pair[c, first : first + count, :] = jnp.where(even, top, bottom)


def shift_east(tiles, lane):
    rolled = [pltpu.roll(t, LANES - 1, 1) for t in tiles]
    if len(tiles) == 1:
        return rolled
    return [jnp.where(lane == LANES - 1, rolled[1 - c], rolled[c]) for c in range(2)]


def shift_west(tiles, lane):
    rolled = [pltpu.roll(t, 1, 1) for t in tiles]
    if len(tiles) == 1:
        return rolled
    return [jnp.where(lane == 0, rolled[1 - c], rolled[c]) for c in range(2)]


def over_rows(framed, read, work):
    start = MARGIN if framed else TOP
    wide = 2 * HALO if framed else 0
    main, side = (TILE + wide) // BLOCKS, (HALF + wide) // BLOCKS
    step = 24 if framed else 32
    groups = [(MAIN, g, step) for g in range(0, main, step)]
    groups[1:1] = [(SIDES, 0, 16)]
    groups[3:3] = [(SIDES, 16, side - 16)]

    def block(i, carry):
        first = {MAIN: pl.multiple_of(start + i * main, 8), SIDES: pl.multiple_of(start + i * side, 8)}
        rows = [(part, first[part] + g, count) for part, g, count in groups]
        pending = [read(*group) for group in rows[:AHEAD]]
        for k, (part, row, count) in enumerate(rows):
            if k + AHEAD < len(rows):
                pending.append(read(*rows[k + AHEAD]))
            for ref, lead, values in work(part, pending[k], lanes_of(count)):
                for tile, value in zip(part, values):
                    ref[(*lead, pl.ds(row + tile, count), slice(None))] = value
        return carry

    lax.fori_loop(0, BLOCKS, block, 0)


def join_parts(ref, leads, whole):
    edge = HALO // 2

    def join(row, upper, lower, count):
        lane = lanes_of(count)
        for lead in leads:
            def at(tile_row):
                return (*lead, pl.ds(tile_row, count), slice(None))

            mixed = ref[at(SIDE + row)]
            if whole:
                place = lane % BAND
                upper_lane = lane < BAND
                from_high = jnp.where(
                    upper_lane,
                    turn(ref[at(ROWS + row)], LANES - HALO, 0),
                    turn(ref[at(ROWS + row + HALF)], LANES - HALO, BAND),
                )
                from_low = jnp.where(
                    upper_lane,
                    turn(ref[at(row)], edge, BAND - edge),
                    turn(ref[at(row + HALF)], edge, LANES - edge),
                )
                ref[at(SIDE + row)] = jnp.where(
                    place < edge, from_high, jnp.where(place >= BAND - edge, from_low, mixed)
                )
            for wanted, band, main_row in ((upper, 0, row), (lower, BAND, row + HALF)):
                if wanted:
                    low = turn(mixed, band + 3 * HALO, 0)
                    high = turn(mixed, band + edge, LANES - edge)
                    ref[at(main_row)] = jnp.where(lane < edge, low, ref[at(main_row)])
                    ref[at(ROWS + main_row)] = jnp.where(lane >= LANES - edge, high, ref[at(ROWS + main_row)])

    step = 32

    def middle(i, carry):
        join(pl.multiple_of(TOP + i * step, 8), True, True, step)
        return carry

    lax.fori_loop(0, HALF // step, middle, 0)
    if whole:
        join(MARGIN, True, False, HALO)
        join(TOP + HALF, False, True, HALO)


def setup_kernel(
    ice_mask, parcels, thick, drive, obs, first_col, second_col,
    fr, ice, middle,
    patch,
):
    tile_cols, tile_rows = ice_mask.shape
    row_tile = lax.axis_index("gy")
    col_tile = lax.axis_index("gx")

    flat = sum(parcels[j] for j in range(tile_rows))
    folded = flat[FOLDED:]
    for dr, _, count, at in CONTROL:
        cells = flat[at : at + count]
        if dr == 0:
            side = jnp.concatenate([turn(folded, 8 * g, 0) for g in range(PACK // 8)], axis=0)
        else:
            side = turn(folded, PACK, 0)[at % 8 : at % 8 + count]
        inner = lanes_of(count) < CT
        row = 4 + {-1: -4, 0: 0, 1: CT}[dr]
        patch[pl.ds(row, count, stride=2), :] = jnp.where(inner, cells, turn(side, 0, CT))
        patch[pl.ds(row + 1, count, stride=2), :] = jnp.where(inner, turn(cells, 0, CT), side)

    cells = 0.5 * jnp.exp(patch[...])
    lane = lanes_of(PATCH)
    for c in range(2):
        wide = jnp.take_along_axis(cells, 32 * c + lane // 4, axis=1)
        for j in range(4):
            fr[pl.ds(MAIN[c] + MARGIN + j, PATCH, stride=4), :] = wide
    lane = lanes_of(40)
    place = lane % BAND // 4
    source = jnp.where(place < 8, 60 + place, (116 + place) % LANES)
    wide = jnp.where(
        lane < BAND,
        jnp.take_along_axis(cells[:40], source, axis=1),
        jnp.take_along_axis(cells[PATCH - 40 :], source, axis=1),
    )
    for j in range(4):
        fr[pl.ds(SIDE + MARGIN + j, 40, stride=4), :] = wide

    west, east = sides("gx", first_col[...], second_col[...])
    lane = lanes_of(HALF)
    upper = lane < BAND
    for f, (field, (first, count)) in enumerate(zip((thick, drive.at[0], drive.at[1], obs.at[0], obs.at[1]), STRIP)):
        halves = (slice(0, HALF), slice(HALF, TILE))
        high = [turn(field[halves[b], LANES:], LANES - HALO, BAND * b) for b in range(2)]
        low = [turn(field[halves[b], :LANES], 0, BAND * b + 3 * HALO) for b in range(2)]
        middle[f] = (0.5 if f in (1, 2) else 1.0) * choose_side(
            lane,
            jnp.where(upper, high[0], high[1]),
            turn(east, first, HALO),
            turn(west, first, 3 * HALO - count),
            jnp.where(upper, low[0], low[1]),
        )

    side_ice = []
    for dr, first, count in ((-1, MARGIN, HALO), (0, TOP, TILE), (1, TOP + TILE, HALO)):
        masks = []
        for ds in (-1, 0, 1):
            row, col = row_tile + dr, col_tile + ds
            inside = (row >= 0) & (row < tile_rows) & (col >= 0) & (col < tile_cols)
            row = jnp.clip(row, 0, tile_rows - 1)
            col = jnp.clip(col, 0, tile_cols - 1)
            masks.append(jnp.where(inside, ice_mask[col, row], 0).astype(jnp.float32))
        for c in range(2):
            ice[MAIN[c] + first : MAIN[c] + first + count, :] = jnp.full((count, LANES), masks[1])
        side_ice.append(choose_side(lanes_of(HALO), masks[1], masks[2], masks[0], masks[1]))
    upper = lanes_of(HALO) < BAND
    for i in range(HALF // HALO):
        ice[SIDE + TOP + i * HALO : SIDE + TOP + (i + 1) * HALO, :] = side_ice[1]
    ice[SIDE + MARGIN : SIDE + TOP, :] = jnp.where(upper, side_ice[0], side_ice[1])
    ice[SIDE + TOP + HALF : SIDE + TOP + HALF + HALO, :] = jnp.where(upper, side_ice[1], side_ice[2])


def model_kernel(
    fr, ice, middle, thick, drive, obs, first_row, second_row,
    vel_u, vel_v, sums,
    ext, visc, vel_a, vel_b, vel_c, coef, small, sems,
):
    even = is_even("gy")
    for f, (field, (first, count)) in enumerate(zip((thick, drive.at[0], drive.at[1], obs.at[0], obs.at[1]), STRIP)):
        scale = 0.5 if f in (1, 2) else 1.0
        frames = []
        for c in range(3):
            one, two = scale * first_row[c, first : first + count, :], scale * second_row[c, first : first + count, :]
            frames.append((jnp.where(even, two, one), jnp.where(even, one, two)))
        for c in range(2):
            ext[f, MAIN[c] + TOP : MAIN[c] + TOP + TILE, :] = scale * field[:, c * LANES : (c + 1) * LANES]
            ext[f, MAIN[c] + TOP - count : MAIN[c] + TOP, :] = frames[c][0]
            ext[f, MAIN[c] + TOP + TILE : MAIN[c] + TOP + TILE + count, :] = frames[c][1]
        here = SIDE + TOP
        ext[f, here : here + HALF, :] = middle[f]
        upper = lanes_of(count) < BAND
        above = turn(middle[f, HALF - count :, :], 0, BAND)
        below = turn(middle[f, :count, :], 0, BAND)
        ext[f, here - count : here, :] = jnp.where(upper, frames[2][0], above)
        ext[f, here + HALF : here + HALF + count, :] = jnp.where(upper, below, frames[2][1])

    def load(ref, part, row, count, *lead):
        return [ref[(*lead, pl.ds(row + tile, count), slice(None))] for tile in part]

    def load_around(part, row, count, now):
        return [load(now, part, r, count, i) for i in range(2) for r in (row, row - 1, row + 1)]

    def load_right(part, row, count):
        return [load(ext, part, row, count, i) for i in (1, 2)]

    def read_thickness(part, row, count):
        return load(ext, part, row, count, 0)

    def first_viscosity(part, thickness, lane):
        factor = 0.25 * visc_scale * strain_floor ** (-1.0 / 3.0)
        return [(visc, (), [factor * t for t in thickness])]

    def read_viscosity(part, row, count):
        return read_thickness(part, row, count), load_around(part, row, count, vel_b)

    def viscosity(part, read, lane):
        thickness, (u, u_n, u_s, v, v_n, v_s) = read
        u_e, u_w = shift_east(u, lane), shift_west(u, lane)
        v_e, v_w = shift_east(v, lane), shift_west(v, lane)
        result = []
        for c in range(len(part)):
            ux, vx = u_e[c] - u_w[c], v_e[c] - v_w[c]
            uy, vy = u_s[c] - u_n[c], v_s[c] - v_n[c]
            shear = uy + vx
            strain = 0.25 * (ux * (ux + vy) + vy * vy) + (0.0625 * (shear * shear) + strain_floor)
            result.append((0.25 * visc_scale) * thickness[c] * jnp.exp(jnp.log(strain) * (-1.0 / 3.0)))
        return [(visc, (), result)]

    def inverse(x):
        near = pl.reciprocal(x, approx=True)
        return near * (2.0 - x * near)

    def read_coefficients(part, row, count):
        around = [load(visc, part, r, count) for r in (row, row - 1, row + 1)]
        return around + [load(fr, part, row, count), load(ice, part, row, count)]

    def coefficients(part, read, lane):
        tiles = range(len(part))
        q, q_n, q_s, friction, mask = read
        q_w = shift_west(q, lane)
        w = [q[c] + q_w[c] for c in tiles]
        e = shift_east(w, lane)
        s = [q[c] + q_s[c] for c in tiles]
        n = [q[c] + q_n[c] for c in tiles]
        scale_u, scale_v = [], []
        for c in tiles:
            across, along = e[c] + w[c], s[c] + n[c]
            scale_u.append(mask[c] * inverse(friction[c] + along + 4.0 * across))
            scale_v.append(mask[c] * inverse(friction[c] + across + 4.0 * along))
        turned = [
            shift_west(q_s, lane), shift_west(q_n, lane), shift_east(q_s, lane), shift_east(q_n, lane),
        ]
        return [e, w, s, n, scale_u, scale_v] + turned

    def relax(part, q, k, around, right, lane):
        tiles = range(len(part))
        e, w, s, n, scale_u, scale_v, q_sw, q_nw, q_se, q_ne = k
        u, u_n, u_s, v, v_n, v_s = around
        to_west_u, to_east_u, to_west_v, to_east_v = [], [], [], []
        for c in tiles:
            u4 = 4.0 * u[c]
            cross_u, cross_v = q[c] * (v_s[c] - v_n[c]), 0.5 * q[c] * (u_s[c] - u_n[c])
            to_west_u.append((w[c] * u4 + cross_u) + 0.5 * (q_sw[c] * v_s[c] - q_nw[c] * v_n[c]))
            to_east_u.append((e[c] * u4 - cross_u) + 0.5 * (q_ne[c] * v_n[c] - q_se[c] * v_s[c]))
            to_west_v.append((w[c] * v[c] + cross_v) + (q_sw[c] * u_s[c] - q_nw[c] * u_n[c]))
            to_east_v.append((e[c] * v[c] - cross_v) + (q_ne[c] * u_n[c] - q_se[c] * u_s[c]))
        to_west_u, to_west_v = shift_east(to_west_u, lane), shift_east(to_west_v, lane)
        to_east_u, to_east_v = shift_west(to_east_u, lane), shift_west(to_east_v, lane)
        new_u, new_v = [], []
        for c in tiles:
            mid_u = s[c] * u_s[c] + n[c] * u_n[c]
            mid_v = 4.0 * (s[c] * v_s[c] + n[c] * v_n[c])
            new_u.append(scale_u[c] * (right[0][c] + mid_u + (to_west_u[c] + to_east_u[c])))
            new_v.append(scale_v[c] * (right[1][c] + mid_v + (to_west_v[c] + to_east_v[c])))
        return new_u, new_v

    def put(new, values):
        return [(new, (i,), values[i]) for i in range(2)]

    def keep(k):
        return [(coef, (i,), k[i]) for i in range(FACTORS)]

    def sweep(framed, now, new):
        def read(part, row, count):
            k = [load(coef, part, row, count, i) for i in range(FACTORS)]
            return load(visc, part, row, count), k, load_around(part, row, count, now), load_right(part, row, count)

        over_rows(framed, read, lambda part, read, lane: put(new, relax(part, *read, lane)))

    def read_first(part, row, count):
        return read_coefficients(part, row, count), load_right(part, row, count)

    def first_start(part, read, lane):
        k = coefficients(part, read[0], lane)
        return keep(k) + put(vel_a, [[a * b for a, b in zip(k[4 + i], read[1][i])] for i in range(2)])

    def read_start(part, row, count):
        return (*read_first(part, row, count), load_around(part, row, count, vel_b))

    def start(part, read, lane):
        k = coefficients(part, read[0], lane)
        return keep(k) + put(vel_a, relax(part, read[0][0], k, read[2], read[1], lane))

    over_rows(True, read_thickness, first_viscosity)
    over_rows(True, read_first, first_start)
    sweep(True, vel_a, vel_b)

    def iteration(i, carry):
        @pl.when(i == PIC - 1)
        def _():
            join_parts(vel_b, ((0,), (1,)), True)

        over_rows(True, read_viscosity, viscosity)
        over_rows(True, read_start, start)
        sweep(True, vel_a, vel_b)
        return carry

    lax.fori_loop(1, PIC, iteration, 0)
    join_parts(vel_b, ((0,), (1,)), False)
    copies = []
    for i, out in enumerate((vel_u, vel_v)):
        for c in range(2):
            copies.append(
                pltpu.make_async_copy(
                    vel_b.at[i, MAIN[c] + TOP : MAIN[c] + TOP + TILE, :],
                    out.at[:, c * LANES : (c + 1) * LANES],
                    sems.at[2 * i + c],
                )
            )
            copies[-1].start()

    def read_misfit(part, row, count):
        return [
            [load(vel_b, part, row, count, i), load(ext, part, row, count, 3 + i), load(coef, part, row, count, 4 + i)]
            for i in range(2)
        ]

    def first_adjoint(part, read, lane):
        misfit = [[0.5 * (a - b) for a, b in zip(u, seen)] for u, seen, _ in read]
        first = [[a * b for a, b in zip(read[i][2], misfit[i])] for i in range(2)]
        return put(vel_c, first) + [(ext, (1 + i,), misfit[i]) for i in range(2)]

    over_rows(True, read_misfit, first_adjoint)

    def two_sweeps(i, carry):
        sweep(True, vel_c, vel_a)
        sweep(True, vel_a, vel_c)
        return carry

    lax.fori_loop(0, (ADJ - 2) // 2, two_sweeps, 0)
    sweep(False, vel_c, vel_a)

    def read_gradient(part, row, count):
        return [load(ref, part, row, count, i) for ref in (vel_b, vel_a) for i in range(2)] + [load(fr, part, row, count)]

    def gradient(part, read, lane):
        u, v, lu, lv, friction = read
        return [(visc, (), [-2.0 * friction[c] * (u[c] * lu[c] + v[c] * lv[c]) for c in range(len(part))])]

    over_rows(False, read_gradient, gradient)
    join_parts(visc, ((),), False)
    down = [sum(visc[pl.ds(MAIN[c] + TOP + j, CT, stride=4), :] for j in range(4)) for c in range(2)]
    k = lax.broadcasted_iota(jnp.int32, (LANES, LANES), 0)
    l = lanes_of(LANES) % CT
    total = jnp.zeros((CT, LANES), jnp.float32)
    for c in range(2):
        total += jnp.dot(
            down[c],
            (k // 4 + 32 * c == l).astype(jnp.float32),
            precision=lax.Precision.HIGHEST,
            preferred_element_type=jnp.float32,
        )
    small[...] = total
    packed = jnp.where(
        lanes_of(PACK) < CT, small[pl.ds(0, PACK, stride=2), :], small[pl.ds(1, PACK, stride=2), :]
    )
    for j in range(sums.shape[0]):
        sums[j] = packed
    for copy in copies:
        copy.wait()


def pick_kernel(tile_block, gathered, own, other, total):
    owned = own.shape[0]
    row_tile = lax.axis_index("gy")
    core = row_tile % 2
    first = (row_tile - core) * owned
    tile_cols, tile_rows = tile_block.shape
    total[...] = jnp.zeros_like(total)
    for t in range(tile_cols * tile_rows // 2):
        place = tile_block[t // (tile_rows // 2), t % (tile_rows // 2) * 2 + core] - first

        @pl.when((place >= 0) & (place < 2 * owned))
        def _():
            total[place] += gathered[t]

    own[...] = total[pl.ds(core * owned, owned)]
    other[...] = total[pl.ds((1 - core) * owned, owned)]


def join_kernel(own, received, out):
    total = own[...] + received[...]
    for j in range(PACK):
        out[:, j * LANES : (j + 1) * LANES] = total[:, j, :]


def in_vmem(count):
    return [pl.BlockSpec(memory_space=pltpu.VMEM)] * count


def in_smem(count):
    return [pl.BlockSpec(memory_space=pltpu.SMEM)] * count


def per_device(thickness, driving, observed, control, ice_mask, tile_block):
    f32 = jnp.float32
    rows, cols = lax.axis_size("gy"), lax.axis_size("gx")
    tile_block, ice_mask = tile_block[:, :, 0].T, ice_mask.T
    params = pltpu.CompilerParams(vmem_limit_bytes=VMEM_LIMIT)

    def shape(*sizes):
        return jax.ShapeDtypeStruct(sizes, f32)

    def swap(axis, cells_first, cells_second):
        count = lax.axis_size(axis)
        received = []
        for cells, low in ((cells_second, 1), (cells_first, 0)):
            pairs = [(i, i + 1) for i in range(low, count - 1, 2)]
            received.append(lax.ppermute(cells, axis, pairs + [(j, i) for i, j in pairs]))
        return received[1], received[0]

    fields = thickness, driving, observed
    owned = control.shape[0]
    *edges, parcels = pl.pallas_call(
        pack_kernel,
        out_shape=[shape(HALF, LANES)] * 2 + [shape(rows, PARCEL, LANES)],
        in_specs=in_smem(1) + [pl.BlockSpec(memory_space=pltpu.HBM)] * 4,
        out_specs=in_vmem(3),
        scratch_shapes=[
            pltpu.VMEM((5, TILE, TILE), f32),
            pltpu.VMEM(control.shape, f32),
            pltpu.VMEM((owned, PACK, LANES), f32),
            pltpu.SemaphoreType.DMA((6,)),
        ],
        compiler_params=pltpu.CompilerParams(vmem_limit_bytes=PACK_VMEM_LIMIT),
        name="pack",
    )(tile_block, control, *fields)
    parcels = lax.all_to_all(parcels, "gy", 0, 0, tiled=True)
    columns_in = swap("gx", *edges)
    strips = pl.pallas_call(
        rows_kernel,
        out_shape=[shape(3, 64, LANES)] * 2,
        in_specs=in_vmem(5),
        out_specs=in_vmem(2),
        compiler_params=params,
        name="rows",
    )(*fields, *columns_in)
    rows_in = swap("gy", *strips)
    prepared = pl.pallas_call(
        setup_kernel,
        out_shape=[shape(ALL_ROWS, LANES)] * 2 + [shape(5, HALF, LANES)],
        in_specs=in_smem(1) + in_vmem(6),
        out_specs=in_vmem(3),
        scratch_shapes=[pltpu.VMEM((PATCH, LANES), f32)],
        compiler_params=params,
        name="setup",
    )(ice_mask, parcels, *fields, *columns_in)

    vel_u, vel_v, sums = pl.pallas_call(
        model_kernel,
        out_shape=(shape(TILE, TILE), shape(TILE, TILE), shape(cols * rows // 2, PACK, LANES)),
        in_specs=in_vmem(8),
        out_specs=[pl.BlockSpec(memory_space=pltpu.HBM)] * 2 + in_vmem(1),
        scratch_shapes=[
            pltpu.VMEM((5, ALL_ROWS, LANES), f32),
            pltpu.VMEM((ALL_ROWS, LANES), f32),
            pltpu.VMEM((2, ALL_ROWS, LANES), f32),
            pltpu.VMEM((2, ALL_ROWS, LANES), f32),
            pltpu.VMEM((2, ALL_ROWS, LANES), f32),
            pltpu.VMEM((FACTORS, ALL_ROWS, LANES), f32),
            pltpu.VMEM((CT, LANES), f32),
            pltpu.SemaphoreType.DMA((4,)),
        ],
        compiler_params=params,
        name="model",
    )(*prepared, *fields, *rows_in)

    same_core = [[i * rows + j for i in range(cols) for j in range(core, rows, 2)] for core in range(2)]
    sums = lax.all_to_all(sums, ("gx", "gy"), 0, 0, tiled=True, axis_index_groups=same_core)
    own, other = pl.pallas_call(
        pick_kernel,
        out_shape=[shape(owned, PACK, LANES)] * 2,
        in_specs=in_smem(1) + in_vmem(1),
        out_specs=in_vmem(2),
        scratch_shapes=[pltpu.VMEM((2 * owned, PACK, LANES), f32)],
        compiler_params=params,
        name="pick",
    )(tile_block, sums)
    received = lax.ppermute(other, "gy", [(j, j ^ 1) for j in range(rows)])
    gradient = pl.pallas_call(
        join_kernel,
        out_shape=shape(*control.shape),
        in_specs=in_vmem(2),
        out_specs=pl.BlockSpec(memory_space=pltpu.VMEM),
        compiler_params=params,
        name="join",
    )(own, received)
    return vel_u, vel_v, gradient


def solution(mesh):
    return jax.shard_map(
        per_device,
        mesh=mesh,
        in_specs=(P("gy", "gx"), P(None, "gy", "gx"), P(None, "gy", "gx"), P("gy", None), P(), P()),
        out_specs=(P("gy", "gx"), P("gy", "gx"), P("gy", None)),
        check_vma=False,
    )
```

```python
import jax
import jax.numpy as jnp
from jax import lax
from jax.experimental import pallas as pl
from jax.experimental.pallas import tpu as pltpu
from jax.sharding import PartitionSpec as P

TILE = 256
PIC = 4
SW = 2
ADJ = 6
CT = 64
COARSE = 4096

LANES = 128
HALO = 16
OBS = 8
MARGIN = 8
TOP = MARGIN + HALO
ROWS = TILE + 2 * TOP
HALF = TILE // 2
SIDE = 2 * ROWS
BAND = LANES // 2
ALL_ROWS = SIDE + HALF + 2 * TOP
MAIN = (0, ROWS)
SIDES = (SIDE,)
BLOCKS = 4
FACTORS = 14
AHEAD = 2
PACK = COARSE // LANES
VMEM_LIMIT = 40 * 1024 * 1024
PACK_VMEM_LIMIT = 62 * 1024 * 1024

STRIP = ((0, HALO), (HALO, HALO), (2 * HALO, HALO), (3 * HALO, OBS), (3 * HALO + OBS, OBS))

CONTROL = ((0, 0, PACK, 0), (-1, PACK - 2, 2, PACK), (1, 0, 2, PACK + 2))
FOLDED = 40
PARCEL = 48
PATCH = CT + 8

visc_scale = 0.1
strain_floor = 0.05


def lanes_of(rows):
    return lax.broadcasted_iota(jnp.int32, (rows, LANES), 1)


def is_even(axis):
    return lax.axis_index(axis) % 2 == 0


def side_lanes(rows, ds, group):
    place = (lanes_of(rows) - 8 * group) % CT
    return place < 4 if ds > 0 else place >= CT - 4


def fill_parcels(tile_block, owned_blocks, parcels):
    tile_cols, tile_rows = tile_block.shape
    owned = owned_blocks.shape[0]
    mine = lax.axis_index("gy") * owned
    col_tile = lax.axis_index("gx")

    def spread(row, carry):
        for ds in (-1, 0, 1):
            col = col_tile + ds
            place = tile_block[jnp.clip(col, 0, tile_cols - 1), row] - mine

            @pl.when((col >= 0) & (col < tile_cols) & (place >= 0) & (place < owned))
            def _():
                for dr, first, count, at in CONTROL:
                    target = row - dr

                    @pl.when((target >= 0) & (target < tile_rows))
                    def _():
                        if ds == 0:
                            parcels[target, at : at + count, :] = owned_blocks[place, first : first + count, :]
                            return
                        start = FOLDED + at % 8
                        rows = min(count, 8)
                        folded = parcels[target, start : start + rows, :]
                        for i in range(count // rows):
                            group = at // 8 + i
                            cells = owned_blocks[place, first + 8 * i : first + 8 * i + rows, :]
                            folded = jnp.where(side_lanes(rows, ds, group), turn(cells, 0, 8 * group), folded)
                        parcels[target, start : start + rows, :] = folded

        return carry

    lax.fori_loop(0, tile_rows, spread, 0)


def parcels_kernel(tile_block, control, parcels, held, owned_blocks, sem):
    copy = pltpu.make_async_copy(control, held, sem)
    copy.start()
    parcels[...] = jnp.zeros_like(parcels)
    copy.wait()
    for j in range(PACK):
        owned_blocks[:, j, :] = held[:, j * LANES : (j + 1) * LANES]
    fill_parcels(tile_block, owned_blocks, parcels)


def columns_kernel(thick, drive, obs, first_col, second_col):
    lane = lanes_of(HALF)
    left = jnp.zeros((HALF, LANES), jnp.float32)
    right = jnp.zeros((HALF, LANES), jnp.float32)
    for field, (first, count) in zip((thick, drive.at[0], drive.at[1], obs.at[0], obs.at[1]), STRIP):
        for part in range(2):
            rows = slice(part * HALF, (part + 1) * HALF)
            start = part * BAND + first
            inside = (lane >= start) & (lane < start + count)
            left = jnp.where(inside, turn(field[rows, :LANES], 0, start), left)
            right = jnp.where(inside, turn(field[rows, LANES:], LANES - count, start), right)
    even = is_even("gx")
    first_col[...] = jnp.where(even, right, left)
    second_col[...] = jnp.where(even, left, right)


def sides(axis, first_pair, second_pair):
    even = is_even(axis)
    return jnp.where(even, second_pair, first_pair), jnp.where(even, first_pair, second_pair)


def choose_side(lane, high, east, west, low):
    place = lane % BAND
    return jnp.where(
        place < HALO, high, jnp.where(place < 2 * HALO, east, jnp.where(place < 3 * HALO, west, low))
    )


def turn(cells, source, target):
    shift = (target - source) % LANES
    return pltpu.roll(cells, shift, 1) if shift else cells


def rows_kernel(thick, drive, obs, first_col, second_col, first_pair, second_pair):
    west, east = sides("gx", first_col[...], second_col[...])
    even = is_even("gy")
    for field, (first, count) in zip((thick, drive.at[0], drive.at[1], obs.at[0], obs.at[1]), STRIP):
        strips = []
        for rows, packed_rows, source, target in (
            (slice(0, count), slice(0, count), first, BAND),
            (slice(TILE - count, TILE), slice(HALF - count, HALF), BAND + first, 0),
        ):
            low, high = field[rows, :LANES], field[rows, LANES:]
            sides_row = choose_side(
                lanes_of(count),
                turn(high, LANES - HALO, target),
                turn(east[packed_rows], source, target + HALO),
                turn(west[packed_rows], source, target + 3 * HALO - count),
                turn(low, 0, target + 3 * HALO),
            )
            strips.append((low, high, sides_row))
        for c in range(3):
            top, bottom = strips[0][c], strips[1][c]
            first_pair[c, first : first + count, :] = jnp.where(even, bottom, top)
            second_pair[c, first : first + count, :] = jnp.where(even, top, bottom)


def shift_east(tiles, lane):
    rolled = [pltpu.roll(t, LANES - 1, 1) for t in tiles]
    if len(tiles) == 1:
        return rolled
    return [jnp.where(lane == LANES - 1, rolled[1 - c], rolled[c]) for c in range(2)]


def shift_west(tiles, lane):
    rolled = [pltpu.roll(t, 1, 1) for t in tiles]
    if len(tiles) == 1:
        return rolled
    return [jnp.where(lane == 0, rolled[1 - c], rolled[c]) for c in range(2)]


def over_rows(framed, read, work):
    start = MARGIN if framed else TOP
    wide = 2 * HALO if framed else 0
    main, side = (TILE + wide) // BLOCKS, (HALF + wide) // BLOCKS
    step = 24 if framed else 32
    groups = [(MAIN, g, step) for g in range(0, main, step)]
    groups[1:1] = [(SIDES, 0, 16)]
    groups[3:3] = [(SIDES, 16, side - 16)]

    def block(i, carry):
        first = {MAIN: pl.multiple_of(start + i * main, 8), SIDES: pl.multiple_of(start + i * side, 8)}
        rows = [(part, first[part] + g, count) for part, g, count in groups]
        pending = [read(*group) for group in rows[:AHEAD]]
        for k, (part, row, count) in enumerate(rows):
            if k + AHEAD < len(rows):
                pending.append(read(*rows[k + AHEAD]))
            for ref, lead, values in work(part, pending[k], lanes_of(count)):
                for tile, value in zip(part, values):
                    ref[(*lead, pl.ds(row + tile, count), slice(None))] = value
        return carry

    lax.fori_loop(0, BLOCKS, block, 0)


def join_parts(ref, leads, whole):
    edge = HALO // 2

    def join(row, upper, lower, count):
        lane = lanes_of(count)
        for lead in leads:
            def at(tile_row):
                return (*lead, pl.ds(tile_row, count), slice(None))

            mixed = ref[at(SIDE + row)]
            if whole:
                place = lane % BAND
                upper_lane = lane < BAND
                from_high = jnp.where(
                    upper_lane,
                    turn(ref[at(ROWS + row)], LANES - HALO, 0),
                    turn(ref[at(ROWS + row + HALF)], LANES - HALO, BAND),
                )
                from_low = jnp.where(
                    upper_lane,
                    turn(ref[at(row)], edge, BAND - edge),
                    turn(ref[at(row + HALF)], edge, LANES - edge),
                )
                ref[at(SIDE + row)] = jnp.where(
                    place < edge, from_high, jnp.where(place >= BAND - edge, from_low, mixed)
                )
            for wanted, band, main_row in ((upper, 0, row), (lower, BAND, row + HALF)):
                if wanted:
                    low = turn(mixed, band + 3 * HALO, 0)
                    high = turn(mixed, band + edge, LANES - edge)
                    ref[at(main_row)] = jnp.where(lane < edge, low, ref[at(main_row)])
                    ref[at(ROWS + main_row)] = jnp.where(lane >= LANES - edge, high, ref[at(ROWS + main_row)])

    step = 32

    def middle(i, carry):
        join(pl.multiple_of(TOP + i * step, 8), True, True, step)
        return carry

    lax.fori_loop(0, HALF // step, middle, 0)
    if whole:
        join(MARGIN, True, False, HALO)
        join(TOP + HALF, False, True, HALO)


def setup_kernel(
    ice_mask, parcels, thick, drive, obs, first_col, second_col,
    fr, ice, middle,
    patch,
):
    tile_cols, tile_rows = ice_mask.shape
    row_tile = lax.axis_index("gy")
    col_tile = lax.axis_index("gx")

    flat = sum(parcels[j] for j in range(tile_rows))
    folded = flat[FOLDED:]
    for dr, _, count, at in CONTROL:
        cells = flat[at : at + count]
        if dr == 0:
            side = jnp.concatenate([turn(folded, 8 * g, 0) for g in range(PACK // 8)], axis=0)
        else:
            side = turn(folded, PACK, 0)[at % 8 : at % 8 + count]
        inner = lanes_of(count) < CT
        row = 4 + {-1: -4, 0: 0, 1: CT}[dr]
        patch[pl.ds(row, count, stride=2), :] = jnp.where(inner, cells, turn(side, 0, CT))
        patch[pl.ds(row + 1, count, stride=2), :] = jnp.where(inner, turn(cells, 0, CT), side)

    cells = 0.5 * jnp.exp(patch[...])
    lane = lanes_of(PATCH)
    for c in range(2):
        wide = jnp.take_along_axis(cells, 32 * c + lane // 4, axis=1)
        for j in range(4):
            fr[pl.ds(MAIN[c] + MARGIN + j, PATCH, stride=4), :] = wide
    lane = lanes_of(40)
    place = lane % BAND // 4
    source = jnp.where(place < 8, 60 + place, (116 + place) % LANES)
    wide = jnp.where(
        lane < BAND,
        jnp.take_along_axis(cells[:40], source, axis=1),
        jnp.take_along_axis(cells[PATCH - 40 :], source, axis=1),
    )
    for j in range(4):
        fr[pl.ds(SIDE + MARGIN + j, 40, stride=4), :] = wide

    west, east = sides("gx", first_col[...], second_col[...])
    lane = lanes_of(HALF)
    upper = lane < BAND
    for f, (field, (first, count)) in enumerate(zip((thick, drive.at[0], drive.at[1], obs.at[0], obs.at[1]), STRIP)):
        halves = (slice(0, HALF), slice(HALF, TILE))
        high = [turn(field[halves[b], LANES:], LANES - HALO, BAND * b) for b in range(2)]
        low = [turn(field[halves[b], :LANES], 0, BAND * b + 3 * HALO) for b in range(2)]
        middle[f] = (0.5 if f in (1, 2) else 1.0) * choose_side(
            lane,
            jnp.where(upper, high[0], high[1]),
            turn(east, first, HALO),
            turn(west, first, 3 * HALO - count),
            jnp.where(upper, low[0], low[1]),
        )

    side_ice = []
    for dr, first, count in ((-1, MARGIN, HALO), (0, TOP, TILE), (1, TOP + TILE, HALO)):
        masks = []
        for ds in (-1, 0, 1):
            row, col = row_tile + dr, col_tile + ds
            inside = (row >= 0) & (row < tile_rows) & (col >= 0) & (col < tile_cols)
            row = jnp.clip(row, 0, tile_rows - 1)
            col = jnp.clip(col, 0, tile_cols - 1)
            masks.append(jnp.where(inside, ice_mask[col, row], 0).astype(jnp.float32))
        for c in range(2):
            ice[MAIN[c] + first : MAIN[c] + first + count, :] = jnp.full((count, LANES), masks[1])
        side_ice.append(choose_side(lanes_of(HALO), masks[1], masks[2], masks[0], masks[1]))
    upper = lanes_of(HALO) < BAND
    for i in range(HALF // HALO):
        ice[SIDE + TOP + i * HALO : SIDE + TOP + (i + 1) * HALO, :] = side_ice[1]
    ice[SIDE + MARGIN : SIDE + TOP, :] = jnp.where(upper, side_ice[0], side_ice[1])
    ice[SIDE + TOP + HALF : SIDE + TOP + HALF + HALO, :] = jnp.where(upper, side_ice[1], side_ice[2])


def model_kernel(
    fr, ice, middle, thick, drive, obs, first_row, second_row,
    vel_u, vel_v, sums,
    ext, visc, vel_a, vel_b, vel_c, coef, small, sems,
):
    even = is_even("gy")
    for f, (field, (first, count)) in enumerate(zip((thick, drive.at[0], drive.at[1], obs.at[0], obs.at[1]), STRIP)):
        scale = 0.5 if f in (1, 2) else 1.0
        frames = []
        for c in range(3):
            one, two = scale * first_row[c, first : first + count, :], scale * second_row[c, first : first + count, :]
            frames.append((jnp.where(even, two, one), jnp.where(even, one, two)))
        for c in range(2):
            ext[f, MAIN[c] + TOP : MAIN[c] + TOP + TILE, :] = scale * field[:, c * LANES : (c + 1) * LANES]
            ext[f, MAIN[c] + TOP - count : MAIN[c] + TOP, :] = frames[c][0]
            ext[f, MAIN[c] + TOP + TILE : MAIN[c] + TOP + TILE + count, :] = frames[c][1]
        here = SIDE + TOP
        ext[f, here : here + HALF, :] = middle[f]
        upper = lanes_of(count) < BAND
        above = turn(middle[f, HALF - count :, :], 0, BAND)
        below = turn(middle[f, :count, :], 0, BAND)
        ext[f, here - count : here, :] = jnp.where(upper, frames[2][0], above)
        ext[f, here + HALF : here + HALF + count, :] = jnp.where(upper, below, frames[2][1])

    def load(ref, part, row, count, *lead):
        return [ref[(*lead, pl.ds(row + tile, count), slice(None))] for tile in part]

    def load_around(part, row, count, now):
        return [load(now, part, r, count, i) for i in range(2) for r in (row, row - 1, row + 1)]

    def load_right(part, row, count):
        return [load(ext, part, row, count, i) for i in (1, 2)]

    def read_thickness(part, row, count):
        return load(ext, part, row, count, 0)

    def keep_viscosity(q, lane):
        return [(visc, (0,), q), (visc, (1,), shift_west(q, lane)), (visc, (2,), shift_east(q, lane))]

    def first_viscosity(part, thickness, lane):
        factor = 0.25 * visc_scale * strain_floor ** (-1.0 / 3.0)
        return keep_viscosity([factor * t for t in thickness], lane)

    def read_viscosity(part, row, count):
        return read_thickness(part, row, count), load_around(part, row, count, vel_b)

    def viscosity(part, read, lane):
        thickness, (u, u_n, u_s, v, v_n, v_s) = read
        u_e, u_w = shift_east(u, lane), shift_west(u, lane)
        v_e, v_w = shift_east(v, lane), shift_west(v, lane)
        result = []
        for c in range(len(part)):
            ux, vx = u_e[c] - u_w[c], v_e[c] - v_w[c]
            uy, vy = u_s[c] - u_n[c], v_s[c] - v_n[c]
            shear = uy + vx
            strain = 0.25 * (ux * (ux + vy) + vy * vy) + (0.0625 * (shear * shear) + strain_floor)
            result.append((0.25 * visc_scale) * thickness[c] * jnp.exp(jnp.log(strain) * (-1.0 / 3.0)))
        return keep_viscosity(result, lane)

    def inverse(x):
        near = pl.reciprocal(x, approx=True)
        return near * (2.0 - x * near)

    def read_coefficients(part, row, count):
        around = [load(visc, part, r, count, i) for i in range(3) for r in (row, row - 1, row + 1)]
        return around + [load(fr, part, row, count), load(ice, part, row, count)]

    def coefficients(part, read):
        tiles = range(len(part))
        q, q_n, q_s, q_w, q_nw, q_sw, q_e, q_ne, q_se, friction, mask = read
        w = [q[c] + q_w[c] for c in tiles]
        e = [q[c] + q_e[c] for c in tiles]
        s = [q[c] + q_s[c] for c in tiles]
        n = [q[c] + q_n[c] for c in tiles]
        scale_u, scale_v = [], []
        for c in tiles:
            across, along = e[c] + w[c], s[c] + n[c]
            scale_u.append(mask[c] * inverse(friction[c] + along + 4.0 * across))
            scale_v.append(mask[c] * inverse(friction[c] + across + 4.0 * along))
        corners = []
        half = [0.5 * q[c] for c in tiles]
        for shifted in (q_sw, q_nw, q_se, q_ne):
            corners.append([q[c] + 0.5 * shifted[c] for c in tiles])
            corners.append([half[c] + shifted[c] for c in tiles])
        return [e, w, s, n, scale_u, scale_v] + corners

    def relax(part, k, around, right, lane):
        tiles = range(len(part))
        e, w, s, n, scale_u, scale_v, sw_u, sw_v, nw_u, nw_v, se_u, se_v, ne_u, ne_v = k
        u, u_n, u_s, v, v_n, v_s = around
        to_west_u, to_east_u, to_west_v, to_east_v = [], [], [], []
        for c in tiles:
            u4 = 4.0 * u[c]
            to_west_u.append(w[c] * u4 + (sw_u[c] * v_s[c] - nw_u[c] * v_n[c]))
            to_east_u.append(e[c] * u4 + (ne_u[c] * v_n[c] - se_u[c] * v_s[c]))
            to_west_v.append(w[c] * v[c] + (sw_v[c] * u_s[c] - nw_v[c] * u_n[c]))
            to_east_v.append(e[c] * v[c] + (ne_v[c] * u_n[c] - se_v[c] * u_s[c]))
        to_west_u, to_west_v = shift_east(to_west_u, lane), shift_east(to_west_v, lane)
        to_east_u, to_east_v = shift_west(to_east_u, lane), shift_west(to_east_v, lane)
        new_u, new_v = [], []
        for c in tiles:
            mid_u = s[c] * u_s[c] + n[c] * u_n[c]
            mid_v = 4.0 * (s[c] * v_s[c] + n[c] * v_n[c])
            new_u.append(scale_u[c] * (right[0][c] + mid_u + (to_west_u[c] + to_east_u[c])))
            new_v.append(scale_v[c] * (right[1][c] + mid_v + (to_west_v[c] + to_east_v[c])))
        return new_u, new_v

    def put(new, values):
        return [(new, (i,), values[i]) for i in range(2)]

    def keep(k):
        return [(coef, (i,), k[i]) for i in range(FACTORS)]

    def sweep(framed, now, new):
        def read(part, row, count):
            k = [load(coef, part, row, count, i) for i in range(FACTORS)]
            return k, load_around(part, row, count, now), load_right(part, row, count)

        over_rows(framed, read, lambda part, read, lane: put(new, relax(part, *read, lane)))

    def read_first(part, row, count):
        return read_coefficients(part, row, count), load_right(part, row, count)

    def first_start(part, read, lane):
        k = coefficients(part, read[0])
        return keep(k) + put(vel_a, [[a * b for a, b in zip(k[4 + i], read[1][i])] for i in range(2)])

    def read_start(part, row, count):
        return (*read_first(part, row, count), load_around(part, row, count, vel_b))

    def start(part, read, lane):
        k = coefficients(part, read[0])
        return keep(k) + put(vel_a, relax(part, k, read[2], read[1], lane))

    over_rows(True, read_thickness, first_viscosity)
    over_rows(True, read_first, first_start)
    sweep(True, vel_a, vel_b)

    def iteration(i, carry):
        @pl.when(i == PIC - 1)
        def _():
            join_parts(vel_b, ((0,), (1,)), True)

        over_rows(True, read_viscosity, viscosity)
        over_rows(True, read_start, start)
        sweep(True, vel_a, vel_b)
        return carry

    lax.fori_loop(1, PIC, iteration, 0)
    join_parts(vel_b, ((0,), (1,)), False)
    copies = []
    for i, out in enumerate((vel_u, vel_v)):
        for c in range(2):
            copies.append(
                pltpu.make_async_copy(
                    vel_b.at[i, MAIN[c] + TOP : MAIN[c] + TOP + TILE, :],
                    out.at[:, c * LANES : (c + 1) * LANES],
                    sems.at[2 * i + c],
                )
            )
            copies[-1].start()

    def read_misfit(part, row, count):
        return [
            [load(vel_b, part, row, count, i), load(ext, part, row, count, 3 + i), load(coef, part, row, count, 4 + i)]
            for i in range(2)
        ]

    def first_adjoint(part, read, lane):
        misfit = [[0.5 * (a - b) for a, b in zip(u, seen)] for u, seen, _ in read]
        first = [[a * b for a, b in zip(read[i][2], misfit[i])] for i in range(2)]
        return put(vel_c, first) + [(ext, (1 + i,), misfit[i]) for i in range(2)]

    over_rows(True, read_misfit, first_adjoint)

    def two_sweeps(i, carry):
        sweep(True, vel_c, vel_a)
        sweep(True, vel_a, vel_c)
        return carry

    lax.fori_loop(0, (ADJ - 2) // 2, two_sweeps, 0)
    sweep(False, vel_c, vel_a)

    def read_gradient(part, row, count):
        return [load(ref, part, row, count, i) for ref in (vel_b, vel_a) for i in range(2)] + [load(fr, part, row, count)]

    def gradient(part, read, lane):
        u, v, lu, lv, friction = read
        return [(visc, (0,), [-2.0 * friction[c] * (u[c] * lu[c] + v[c] * lv[c]) for c in range(len(part))])]

    over_rows(False, read_gradient, gradient)
    join_parts(visc, ((0,),), False)
    down = [sum(visc[0, pl.ds(MAIN[c] + TOP + j, CT, stride=4), :] for j in range(4)) for c in range(2)]
    k = lax.broadcasted_iota(jnp.int32, (LANES, LANES), 0)
    l = lanes_of(LANES) % CT
    total = jnp.zeros((CT, LANES), jnp.float32)
    for c in range(2):
        total += jnp.dot(
            down[c],
            (k // 4 + 32 * c == l).astype(jnp.float32),
            precision=lax.Precision.HIGHEST,
            preferred_element_type=jnp.float32,
        )
    small[...] = total
    packed = jnp.where(
        lanes_of(PACK) < CT, small[pl.ds(0, PACK, stride=2), :], small[pl.ds(1, PACK, stride=2), :]
    )
    for j in range(sums.shape[0]):
        sums[j] = packed
    for copy in copies:
        copy.wait()


def pick_kernel(tile_block, gathered, own, other, total):
    owned = own.shape[0]
    row_tile = lax.axis_index("gy")
    core = row_tile % 2
    first = (row_tile - core) * owned
    tile_cols, tile_rows = tile_block.shape
    total[...] = jnp.zeros_like(total)
    for t in range(tile_cols * tile_rows // 2):
        place = tile_block[t // (tile_rows // 2), t % (tile_rows // 2) * 2 + core] - first

        @pl.when((place >= 0) & (place < 2 * owned))
        def _():
            total[place] += gathered[t]

    own[...] = total[pl.ds(core * owned, owned)]
    other[...] = total[pl.ds((1 - core) * owned, owned)]


def join_kernel(own, received, out):
    total = own[...] + received[...]
    for j in range(PACK):
        out[:, j * LANES : (j + 1) * LANES] = total[:, j, :]


def in_vmem(count):
    return [pl.BlockSpec(memory_space=pltpu.VMEM)] * count


def in_smem(count):
    return [pl.BlockSpec(memory_space=pltpu.SMEM)] * count


def per_device(thickness, driving, observed, control, ice_mask, tile_block):
    f32 = jnp.float32
    rows, cols = lax.axis_size("gy"), lax.axis_size("gx")
    tile_block, ice_mask = tile_block[:, :, 0].T, ice_mask.T
    params = pltpu.CompilerParams(vmem_limit_bytes=VMEM_LIMIT)

    def shape(*sizes):
        return jax.ShapeDtypeStruct(sizes, f32)

    def swap(axis, cells_first, cells_second):
        count = lax.axis_size(axis)
        received = []
        for cells, low in ((cells_second, 1), (cells_first, 0)):
            pairs = [(i, i + 1) for i in range(low, count - 1, 2)]
            received.append(lax.ppermute(cells, axis, pairs + [(j, i) for i, j in pairs]))
        return received[1], received[0]

    fields = thickness, driving, observed
    owned = control.shape[0]
    parcels = pl.pallas_call(
        parcels_kernel,
        out_shape=shape(rows, PARCEL, LANES),
        in_specs=in_smem(1) + [pl.BlockSpec(memory_space=pltpu.HBM)],
        out_specs=pl.BlockSpec(memory_space=pltpu.VMEM),
        scratch_shapes=[
            pltpu.VMEM(control.shape, f32),
            pltpu.VMEM((owned, PACK, LANES), f32),
            pltpu.SemaphoreType.DMA,
        ],
        compiler_params=pltpu.CompilerParams(vmem_limit_bytes=PACK_VMEM_LIMIT),
        name="parcels",
    )(tile_block, control)
    parcels = lax.all_to_all(parcels, "gy", 0, 0, tiled=True)
    edges = pl.pallas_call(
        columns_kernel,
        out_shape=[shape(HALF, LANES)] * 2,
        in_specs=in_vmem(3),
        out_specs=in_vmem(2),
        compiler_params=params,
        name="columns",
    )(*fields)
    columns_in = swap("gx", *edges)
    strips = pl.pallas_call(
        rows_kernel,
        out_shape=[shape(3, 64, LANES)] * 2,
        in_specs=in_vmem(5),
        out_specs=in_vmem(2),
        compiler_params=params,
        name="rows",
    )(*fields, *columns_in)
    rows_in = swap("gy", *strips)
    prepared = pl.pallas_call(
        setup_kernel,
        out_shape=[shape(ALL_ROWS, LANES)] * 2 + [shape(5, HALF, LANES)],
        in_specs=in_smem(1) + in_vmem(6),
        out_specs=in_vmem(3),
        scratch_shapes=[pltpu.VMEM((PATCH, LANES), f32)],
        compiler_params=params,
        name="setup",
    )(ice_mask, parcels, *fields, *columns_in)

    vel_u, vel_v, sums = pl.pallas_call(
        model_kernel,
        out_shape=(shape(TILE, TILE), shape(TILE, TILE), shape(cols * rows // 2, PACK, LANES)),
        in_specs=in_vmem(8),
        out_specs=[pl.BlockSpec(memory_space=pltpu.HBM)] * 2 + in_vmem(1),
        scratch_shapes=[
            pltpu.VMEM((5, ALL_ROWS, LANES), f32),
            pltpu.VMEM((3, ALL_ROWS, LANES), f32),
            pltpu.VMEM((2, ALL_ROWS, LANES), f32),
            pltpu.VMEM((2, ALL_ROWS, LANES), f32),
            pltpu.VMEM((2, ALL_ROWS, LANES), f32),
            pltpu.VMEM((FACTORS, ALL_ROWS, LANES), f32),
            pltpu.VMEM((CT, LANES), f32),
            pltpu.SemaphoreType.DMA((4,)),
        ],
        compiler_params=params,
        name="model",
    )(*prepared, *fields, *rows_in)

    same_core = [[i * rows + j for i in range(cols) for j in range(core, rows, 2)] for core in range(2)]
    sums = lax.all_to_all(sums, ("gx", "gy"), 0, 0, tiled=True, axis_index_groups=same_core)
    own, other = pl.pallas_call(
        pick_kernel,
        out_shape=[shape(owned, PACK, LANES)] * 2,
        in_specs=in_smem(1) + in_vmem(1),
        out_specs=in_vmem(2),
        scratch_shapes=[pltpu.VMEM((2 * owned, PACK, LANES), f32)],
        compiler_params=params,
        name="pick",
    )(tile_block, sums)
    received = lax.ppermute(other, "gy", [(j, j ^ 1) for j in range(rows)])
    gradient = pl.pallas_call(
        join_kernel,
        out_shape=shape(*control.shape),
        in_specs=in_vmem(2),
        out_specs=pl.BlockSpec(memory_space=pltpu.VMEM),
        compiler_params=params,
        name="join",
    )(own, received)
    return vel_u, vel_v, gradient


def solution(mesh):
    return jax.shard_map(
        per_device,
        mesh=mesh,
        in_specs=(P("gy", "gx"), P(None, "gy", "gx"), P(None, "gy", "gx"), P("gy", None), P(), P()),
        out_specs=(P("gy", "gx"), P("gy", "gx"), P("gy", None)),
        check_vma=False,
    )
```

```python
from types import SimpleNamespace

import jax
import jax.numpy as jnp
from jax import lax
from jax.experimental import pallas as pl
from jax.experimental.pallas import tpu as pltpu
from jax.sharding import PartitionSpec as P

TILE = 256
PIC = 4
SW = 2
ADJ = 6
CT = 64
COARSE = 4096

LANES = 128
HALO = 16
OBS = 8
MARGIN = 8
TOP = MARGIN + HALO
ROWS = TILE + 2 * TOP
HALF = TILE // 2
SIDE = 2 * ROWS
BAND = LANES // 2
ALL_ROWS = SIDE + HALF + 2 * TOP
MAIN = (0, ROWS)
SIDES = (SIDE,)
SPANS = {
    "frame": (MARGIN, 4, 72, MARGIN, 40, 0, 0),
    "inner": (MARGIN + 8, 3, 72, MARGIN + 8, 40, 56, 24),
    "tile": (TOP, 4, 64, TOP, 32, 0, 0),
}
FACTORS = 14
AHEAD = 2
PACK = COARSE // LANES
VMEM_LIMIT = 40 * 1024 * 1024
PACK_VMEM_LIMIT = 62 * 1024 * 1024

STRIP = ((0, HALO), (HALO, HALO), (2 * HALO, HALO), (3 * HALO, OBS), (3 * HALO + OBS, OBS))

CONTROL = ((0, 0, PACK, 0), (-1, PACK - 2, 2, PACK), (1, 0, 2, PACK + 2))
FOLDED = 40
PARCEL = 48
PATCH = CT + 8

visc_scale = 0.1
strain_floor = 0.05


def lanes_of(rows):
    return lax.broadcasted_iota(jnp.int32, (rows, LANES), 1)


def is_even(axis):
    return lax.axis_index(axis) % 2 == 0


def side_lanes(rows, ds, group):
    place = (lanes_of(rows) - 8 * group) % CT
    return place < 4 if ds > 0 else place >= CT - 4


def fill_parcels(tile_block, owned_blocks, parcels):
    tile_cols, tile_rows = tile_block.shape
    owned = owned_blocks.shape[0]
    mine = lax.axis_index("gy") * owned
    col_tile = lax.axis_index("gx")

    def spread(row, carry):
        for ds in (-1, 0, 1):
            col = col_tile + ds
            place = tile_block[jnp.clip(col, 0, tile_cols - 1), row] - mine

            @pl.when((col >= 0) & (col < tile_cols) & (place >= 0) & (place < owned))
            def _():
                for dr, first, count, at in CONTROL:
                    target = row - dr

                    @pl.when((target >= 0) & (target < tile_rows))
                    def _():
                        if ds == 0:
                            parcels[target, at : at + count, :] = owned_blocks[place, first : first + count, :]
                            return
                        start = FOLDED + at % 8
                        rows = min(count, 8)
                        folded = parcels[target, start : start + rows, :]
                        for i in range(count // rows):
                            group = at // 8 + i
                            cells = owned_blocks[place, first + 8 * i : first + 8 * i + rows, :]
                            folded = jnp.where(side_lanes(rows, ds, group), turn(cells, 0, 8 * group), folded)
                        parcels[target, start : start + rows, :] = folded

        return carry

    lax.fori_loop(0, tile_rows, spread, 0)


def pack_kernel(
    tile_block, control, thick, drive, obs, first_col, second_col, parcels,
    held, held_control, owned_blocks, packed_parcels, packed_cols, sems,
):
    copies = [pltpu.make_async_copy(control, held_control, sems.at[5])]
    for f, field in enumerate((thick, drive.at[0], drive.at[1], obs.at[0], obs.at[1])):
        copies.append(pltpu.make_async_copy(field, held.at[f], sems.at[f]))
    for copy in copies:
        copy.start()
    packed_parcels[...] = jnp.zeros_like(packed_parcels)
    copies[0].wait()
    for j in range(PACK):
        owned_blocks[:, j, :] = held_control[:, j * LANES : (j + 1) * LANES]
    fill_parcels(tile_block, owned_blocks, packed_parcels)
    results = [pltpu.make_async_copy(packed_parcels, parcels, sems.at[6])]
    results[0].start()

    lane = lanes_of(HALF)
    left = jnp.zeros((HALF, LANES), jnp.float32)
    right = jnp.zeros((HALF, LANES), jnp.float32)
    for f, (first, count) in enumerate(STRIP):
        copies[1 + f].wait()
        for part in range(2):
            rows = slice(part * HALF, (part + 1) * HALF)
            start = part * BAND + first
            inside = (lane >= start) & (lane < start + count)
            left = jnp.where(inside, turn(held[f, rows, :LANES], 0, start), left)
            right = jnp.where(inside, turn(held[f, rows, LANES:], LANES - count, start), right)
    even = is_even("gx")
    packed_cols[0] = jnp.where(even, right, left)
    packed_cols[1] = jnp.where(even, left, right)
    for i, out in enumerate((first_col, second_col)):
        results.append(pltpu.make_async_copy(packed_cols.at[i], out, sems.at[7 + i]))
        results[-1].start()
    for copy in results:
        copy.wait()


def sides(axis, first_pair, second_pair):
    even = is_even(axis)
    return jnp.where(even, second_pair, first_pair), jnp.where(even, first_pair, second_pair)


def choose_side(lane, high, east, west, low):
    place = lane % BAND
    return jnp.where(
        place < HALO, high, jnp.where(place < 2 * HALO, east, jnp.where(place < 3 * HALO, west, low))
    )


def turn(cells, source, target):
    shift = (target - source) % LANES
    return pltpu.roll(cells, shift, 1) if shift else cells


def rows_kernel(thick, drive, obs, first_col, second_col, first_pair, second_pair):
    west, east = sides("gx", first_col[...], second_col[...])
    even = is_even("gy")
    for field, (first, count) in zip((thick, drive.at[0], drive.at[1], obs.at[0], obs.at[1]), STRIP):
        strips = []
        for rows, packed_rows, source, target in (
            (slice(0, count), slice(0, count), first, BAND),
            (slice(TILE - count, TILE), slice(HALF - count, HALF), BAND + first, 0),
        ):
            low, high = field[rows, :LANES], field[rows, LANES:]
            sides_row = choose_side(
                lanes_of(count),
                turn(high, LANES - HALO, target),
                turn(east[packed_rows], source, target + HALO),
                turn(west[packed_rows], source, target + 3 * HALO - count),
                turn(low, 0, target + 3 * HALO),
            )
            strips.append((low, high, sides_row))
        for c in range(3):
            top, bottom = strips[0][c], strips[1][c]
            first_pair[c, first : first + count, :] = jnp.where(even, bottom, top)
            second_pair[c, first : first + count, :] = jnp.where(even, top, bottom)


def shift_east(tiles, lane):
    rolled = [pltpu.roll(t, LANES - 1, 1) for t in tiles]
    if len(tiles) == 1:
        return rolled
    return [jnp.where(lane == LANES - 1, rolled[1 - c], rolled[c]) for c in range(2)]


def shift_west(tiles, lane):
    rolled = [pltpu.roll(t, 1, 1) for t in tiles]
    if len(tiles) == 1:
        return rolled
    return [jnp.where(lane == 0, rolled[1 - c], rolled[c]) for c in range(2)]


def run_groups(groups, read, work):
    pending = [read(*group) for group in groups[:AHEAD]]
    for k, (part, row, count) in enumerate(groups):
        if k + AHEAD < len(groups):
            pending.append(read(*groups[k + AHEAD]))
        for ref, lead, values in work(part, pending[k], lanes_of(count)):
            for tile, value in zip(part, values):
                ref[(*lead, pl.ds(row + tile, count), slice(None))] = value


def block_groups(row, main, side_row, side):
    step = 32 if main % 32 == 0 else 24
    first = side // 16 * 8 if side > 24 else side
    groups = [(MAIN, row + g, min(step, main - g)) for g in range(0, main, step)]
    groups[1:1] = [(SIDES, side_row, first)]
    if first < side:
        groups[3:3] = [(SIDES, side_row + first, side - first)]
    return groups


def over_rows(span, read, work):
    start, blocks, main, side_start, side, main_rest, side_rest = SPANS[span]

    def block(i, carry):
        row, side_row = pl.multiple_of(start + i * main, 8), pl.multiple_of(side_start + i * side, 8)
        run_groups(block_groups(row, main, side_row, side), read, work)
        return carry

    lax.fori_loop(0, blocks, block, 0)
    if main_rest:
        none = 8 * jnp.minimum(lax.axis_index("gx"), 0)
        row = pl.multiple_of(none + start + blocks * main, 8)
        side_row = pl.multiple_of(none + side_start + blocks * side, 8)
        run_groups(block_groups(row, main_rest, side_row, side_rest), read, work)


def over_ends(count, read, work):
    def block(i, carry):
        row = pl.multiple_of(MARGIN + i * (TILE + 2 * HALO - count), 8)
        side_row = pl.multiple_of(MARGIN + i * (HALF + 2 * HALO - count), 8)
        run_groups([(MAIN, row, count), (SIDES, side_row, count)], read, work)
        return carry

    lax.fori_loop(0, 2, block, 0)


def join_parts(ref, leads, whole):
    edge = HALO // 2

    def join(row, upper, lower, count):
        lane = lanes_of(count)
        for lead in leads:
            def at(tile_row):
                return (*lead, pl.ds(tile_row, count), slice(None))

            mixed = ref[at(SIDE + row)]
            if whole:
                place = lane % BAND
                upper_lane = lane < BAND
                from_high = jnp.where(
                    upper_lane,
                    turn(ref[at(ROWS + row)], LANES - HALO, 0),
                    turn(ref[at(ROWS + row + HALF)], LANES - HALO, BAND),
                )
                from_low = jnp.where(
                    upper_lane,
                    turn(ref[at(row)], edge, BAND - edge),
                    turn(ref[at(row + HALF)], edge, LANES - edge),
                )
                ref[at(SIDE + row)] = jnp.where(
                    place < edge, from_high, jnp.where(place >= BAND - edge, from_low, mixed)
                )
            for wanted, band, main_row in ((upper, 0, row), (lower, BAND, row + HALF)):
                if wanted:
                    low = turn(mixed, band + 3 * HALO, 0)
                    high = turn(mixed, band + edge, LANES - edge)
                    ref[at(main_row)] = jnp.where(lane < edge, low, ref[at(main_row)])
                    ref[at(ROWS + main_row)] = jnp.where(lane >= LANES - edge, high, ref[at(ROWS + main_row)])

    step = 32

    def middle(i, carry):
        join(pl.multiple_of(TOP + i * step, 8), True, True, step)
        return carry

    lax.fori_loop(0, HALF // step, middle, 0)
    if whole:
        join(MARGIN, True, False, HALO)
        join(TOP + HALF, False, True, HALO)


def friction_kernel(ice_mask, parcels, fr, ice, patch):
    tile_cols, tile_rows = ice_mask.shape
    row_tile = lax.axis_index("gy")
    col_tile = lax.axis_index("gx")

    flat = sum(parcels[j] for j in range(tile_rows))
    folded = flat[FOLDED:]
    for dr, _, count, at in CONTROL:
        cells = flat[at : at + count]
        if dr == 0:
            side = jnp.concatenate([turn(folded, 8 * g, 0) for g in range(PACK // 8)], axis=0)
        else:
            side = turn(folded, PACK, 0)[at % 8 : at % 8 + count]
        inner = lanes_of(count) < CT
        row = 4 + {-1: -4, 0: 0, 1: CT}[dr]
        patch[pl.ds(row, count, stride=2), :] = jnp.where(inner, cells, turn(side, 0, CT))
        patch[pl.ds(row + 1, count, stride=2), :] = jnp.where(inner, turn(cells, 0, CT), side)

    cells = 0.5 * jnp.exp(patch[...])
    lane = lanes_of(PATCH)
    for c in range(2):
        wide = jnp.take_along_axis(cells, 32 * c + lane // 4, axis=1)
        for j in range(4):
            fr[pl.ds(MAIN[c] + MARGIN + j, PATCH, stride=4), :] = wide
    lane = lanes_of(40)
    place = lane % BAND // 4
    source = jnp.where(place < 8, 60 + place, (116 + place) % LANES)
    wide = jnp.where(
        lane < BAND,
        jnp.take_along_axis(cells[:40], source, axis=1),
        jnp.take_along_axis(cells[PATCH - 40 :], source, axis=1),
    )
    for j in range(4):
        fr[pl.ds(SIDE + MARGIN + j, 40, stride=4), :] = wide

    side_ice = []
    for dr, first, count in ((-1, MARGIN, HALO), (0, TOP, TILE), (1, TOP + TILE, HALO)):
        masks = []
        for ds in (-1, 0, 1):
            row, col = row_tile + dr, col_tile + ds
            inside = (row >= 0) & (row < tile_rows) & (col >= 0) & (col < tile_cols)
            row = jnp.clip(row, 0, tile_rows - 1)
            col = jnp.clip(col, 0, tile_cols - 1)
            masks.append(jnp.where(inside, ice_mask[col, row], 0).astype(jnp.float32))
        for c in range(2):
            ice[MAIN[c] + first : MAIN[c] + first + count, :] = jnp.full((count, LANES), masks[1])
        side_ice.append(choose_side(lanes_of(HALO), masks[1], masks[2], masks[0], masks[1]))
    upper = lanes_of(HALO) < BAND
    for i in range(HALF // HALO):
        ice[SIDE + TOP + i * HALO : SIDE + TOP + (i + 1) * HALO, :] = side_ice[1]
    ice[SIDE + MARGIN : SIDE + TOP, :] = jnp.where(upper, side_ice[0], side_ice[1])
    ice[SIDE + TOP + HALF : SIDE + TOP + HALF + HALO, :] = jnp.where(upper, side_ice[1], side_ice[2])


def make_stages(ext, fr, ice, visc, vel_a, vel_b, coef):
    def load(ref, part, row, count, *lead):
        return [ref[(*lead, pl.ds(row + tile, count), slice(None))] for tile in part]

    def load_around(part, row, count, now):
        return [load(now, part, r, count, i) for i in range(2) for r in (row, row - 1, row + 1)]

    def load_right(part, row, count):
        return [load(ext, part, row, count, i) for i in (1, 2)]

    def read_thickness(part, row, count):
        return load(ext, part, row, count, 0)

    def keep_viscosity(q, lane):
        return [(visc, (0,), q), (visc, (1,), shift_west(q, lane)), (visc, (2,), shift_east(q, lane))]

    def first_viscosity(part, thickness, lane):
        factor = 0.25 * visc_scale * strain_floor ** (-1.0 / 3.0)
        return keep_viscosity([factor * t for t in thickness], lane)

    def read_viscosity(part, row, count):
        return read_thickness(part, row, count), load_around(part, row, count, vel_b)

    def viscosity(part, read, lane):
        thickness, (u, u_n, u_s, v, v_n, v_s) = read
        u_e, u_w = shift_east(u, lane), shift_west(u, lane)
        v_e, v_w = shift_east(v, lane), shift_west(v, lane)
        result = []
        for c in range(len(part)):
            ux, vx = u_e[c] - u_w[c], v_e[c] - v_w[c]
            uy, vy = u_s[c] - u_n[c], v_s[c] - v_n[c]
            shear = uy + vx
            strain = 0.25 * (ux * (ux + vy) + vy * vy) + (0.0625 * (shear * shear) + strain_floor)
            result.append((0.25 * visc_scale) * thickness[c] * jnp.exp(jnp.log(strain) * (-1.0 / 3.0)))
        return keep_viscosity(result, lane)

    def inverse(x):
        near = pl.reciprocal(x, approx=True)
        return near * (2.0 - x * near)

    def read_coefficients(part, row, count):
        around = [load(visc, part, r, count, i) for i in range(3) for r in (row, row - 1, row + 1)]
        return around + [load(fr, part, row, count), load(ice, part, row, count)]

    def coefficients(part, read):
        tiles = range(len(part))
        q, q_n, q_s, q_w, q_nw, q_sw, q_e, q_ne, q_se, friction, mask = read
        w = [q[c] + q_w[c] for c in tiles]
        e = [q[c] + q_e[c] for c in tiles]
        s = [q[c] + q_s[c] for c in tiles]
        n = [q[c] + q_n[c] for c in tiles]
        scale_u, scale_v = [], []
        for c in tiles:
            across, along = e[c] + w[c], s[c] + n[c]
            scale_u.append(mask[c] * inverse(friction[c] + along + 4.0 * across))
            scale_v.append(mask[c] * inverse(friction[c] + across + 4.0 * along))
        corners = []
        half = [0.5 * q[c] for c in tiles]
        for shifted in (q_sw, q_nw, q_se, q_ne):
            corners.append([q[c] + 0.5 * shifted[c] for c in tiles])
            corners.append([half[c] + shifted[c] for c in tiles])
        return [e, w, s, n, scale_u, scale_v] + corners

    def relax(part, k, around, right, lane):
        tiles = range(len(part))
        e, w, s, n, scale_u, scale_v, sw_u, sw_v, nw_u, nw_v, se_u, se_v, ne_u, ne_v = k
        u, u_n, u_s, v, v_n, v_s = around
        to_west_u, to_east_u, to_west_v, to_east_v = [], [], [], []
        for c in tiles:
            u4 = 4.0 * u[c]
            to_west_u.append(w[c] * u4 + (sw_u[c] * v_s[c] - nw_u[c] * v_n[c]))
            to_east_u.append(e[c] * u4 + (ne_u[c] * v_n[c] - se_u[c] * v_s[c]))
            to_west_v.append(w[c] * v[c] + (sw_v[c] * u_s[c] - nw_v[c] * u_n[c]))
            to_east_v.append(e[c] * v[c] + (ne_v[c] * u_n[c] - se_v[c] * u_s[c]))
        to_west_u, to_west_v = shift_east(to_west_u, lane), shift_east(to_west_v, lane)
        to_east_u, to_east_v = shift_west(to_east_u, lane), shift_west(to_east_v, lane)
        new_u, new_v = [], []
        for c in tiles:
            mid_u = s[c] * u_s[c] + n[c] * u_n[c]
            mid_v = 4.0 * (s[c] * v_s[c] + n[c] * v_n[c])
            new_u.append(scale_u[c] * (right[0][c] + mid_u + (to_west_u[c] + to_east_u[c])))
            new_v.append(scale_v[c] * (right[1][c] + mid_v + (to_west_v[c] + to_east_v[c])))
        return new_u, new_v

    def put(new, values):
        return [(new, (i,), values[i]) for i in range(2)]

    def keep(k):
        return [(coef, (i,), k[i]) for i in range(FACTORS)]

    def read_sweep(now):
        def read(part, row, count):
            k = [load(coef, part, row, count, i) for i in range(FACTORS)]
            return k, load_around(part, row, count, now), load_right(part, row, count)

        return read

    def sweep(new):
        return lambda part, read, lane: put(new, relax(part, *read, lane))

    def read_first(part, row, count):
        return read_coefficients(part, row, count), load_right(part, row, count)

    def first_start(part, read, lane):
        k = coefficients(part, read[0])
        return keep(k) + put(vel_a, [[a * b for a, b in zip(k[4 + i], read[1][i])] for i in range(2)])

    def read_start(part, row, count):
        return (*read_first(part, row, count), load_around(part, row, count, vel_b))

    def start(part, read, lane):
        k = coefficients(part, read[0])
        return keep(k) + put(vel_a, relax(part, k, read[2], read[1], lane))

    return SimpleNamespace(**locals())


def setup_kernel(
    fr, ice, thick, drive, obs, first_col, second_col,
    ext, vel_b,
    visc, vel_a, coef,
):
    west, east = sides("gx", first_col[...], second_col[...])
    lane = lanes_of(HALF)
    upper = lane < BAND
    for f, (field, (first, count)) in enumerate(zip((thick, drive.at[0], drive.at[1], obs.at[0], obs.at[1]), STRIP)):
        scale = 0.5 if f in (1, 2) else 1.0
        for c in range(2):
            ext[f, MAIN[c] + TOP : MAIN[c] + TOP + TILE, :] = scale * field[:, c * LANES : (c + 1) * LANES]
        halves = (slice(0, HALF), slice(HALF, TILE))
        high = [turn(field[halves[b], LANES:], LANES - HALO, BAND * b) for b in range(2)]
        low = [turn(field[halves[b], :LANES], 0, BAND * b + 3 * HALO) for b in range(2)]
        ext[f, SIDE + TOP : SIDE + TOP + HALF, :] = scale * choose_side(
            lane,
            jnp.where(upper, high[0], high[1]),
            turn(east, first, HALO),
            turn(west, first, 3 * HALO - count),
            jnp.where(upper, low[0], low[1]),
        )
    step = make_stages(ext, fr, ice, visc, vel_a, vel_b, coef)
    over_rows("tile", step.read_thickness, step.first_viscosity)
    over_rows("tile", step.read_first, step.first_start)
    over_rows("tile", step.read_sweep(vel_a), step.sweep(vel_b))


def model_kernel(
    fr, ice, ext_in, vel_in, first_row, second_row,
    vel_u, vel_v, sums,
    ext, visc, vel_a, vel_b, vel_c, coef, small, sems,
):
    ext[...] = ext_in[...]
    vel_b[...] = vel_in[...]
    even = is_even("gy")
    here = SIDE + TOP
    for f, (first, count) in enumerate(STRIP):
        scale = 0.5 if f in (1, 2) else 1.0
        frames = []
        for c in range(3):
            one, two = scale * first_row[c, first : first + count, :], scale * second_row[c, first : first + count, :]
            frames.append((jnp.where(even, two, one), jnp.where(even, one, two)))
        for c in range(2):
            ext[f, MAIN[c] + TOP - count : MAIN[c] + TOP, :] = frames[c][0]
            ext[f, MAIN[c] + TOP + TILE : MAIN[c] + TOP + TILE + count, :] = frames[c][1]
        upper = lanes_of(count) < BAND
        above = turn(ext_in[f, here + HALF - count : here + HALF, :], 0, BAND)
        below = turn(ext_in[f, here : here + count, :], 0, BAND)
        ext[f, here - count : here, :] = jnp.where(upper, frames[2][0], above)
        ext[f, here + HALF : here + HALF + count, :] = jnp.where(upper, below, frames[2][1])

    step = make_stages(ext, fr, ice, visc, vel_a, vel_b, coef)
    over_ends(32, step.read_thickness, step.first_viscosity)
    over_ends(32, step.read_first, step.first_start)
    over_ends(24, step.read_sweep(vel_a), step.sweep(vel_b))

    def iterate(span):
        over_rows(span, step.read_viscosity, step.viscosity)
        over_rows(span, step.read_start, step.start)
        over_rows(span, step.read_sweep(vel_a), step.sweep(vel_b))

    def iteration(i, carry):
        iterate("frame")
        return carry

    lax.fori_loop(1, PIC - 1, iteration, 0)
    join_parts(vel_b, ((0,), (1,)), True)
    iterate("inner")
    join_parts(vel_b, ((0,), (1,)), False)
    copies = []
    for i, out in enumerate((vel_u, vel_v)):
        for c in range(2):
            copies.append(
                pltpu.make_async_copy(
                    vel_b.at[i, MAIN[c] + TOP : MAIN[c] + TOP + TILE, :],
                    out.at[:, c * LANES : (c + 1) * LANES],
                    sems.at[2 * i + c],
                )
            )
            copies[-1].start()

    load = step.load

    def read_misfit(part, row, count):
        return [
            [load(vel_b, part, row, count, i), load(ext, part, row, count, 3 + i), load(coef, part, row, count, 4 + i)]
            for i in range(2)
        ]

    def first_adjoint(part, read, lane):
        misfit = [[0.5 * (a - b) for a, b in zip(u, seen)] for u, seen, _ in read]
        first = [[a * b for a, b in zip(read[i][2], misfit[i])] for i in range(2)]
        return step.put(vel_c, first) + [(ext, (1 + i,), misfit[i]) for i in range(2)]

    over_rows("inner", read_misfit, first_adjoint)

    def two_sweeps(i, carry):
        over_rows("inner", step.read_sweep(vel_c), step.sweep(vel_a))
        over_rows("inner", step.read_sweep(vel_a), step.sweep(vel_c))
        return carry

    lax.fori_loop(0, (ADJ - 2) // 2, two_sweeps, 0)
    over_rows("tile", step.read_sweep(vel_c), step.sweep(vel_a))

    def read_gradient(part, row, count):
        return [load(ref, part, row, count, i) for ref in (vel_b, vel_a) for i in range(2)] + [load(fr, part, row, count)]

    def gradient(part, read, lane):
        u, v, lu, lv, friction = read
        return [(visc, (0,), [-2.0 * friction[c] * (u[c] * lu[c] + v[c] * lv[c]) for c in range(len(part))])]

    over_rows("tile", read_gradient, gradient)
    join_parts(visc, ((0,),), False)
    down = [sum(visc[0, pl.ds(MAIN[c] + TOP + j, CT, stride=4), :] for j in range(4)) for c in range(2)]
    k = lax.broadcasted_iota(jnp.int32, (LANES, LANES), 0)
    l = lanes_of(LANES) % CT
    total = jnp.zeros((CT, LANES), jnp.float32)
    for c in range(2):
        total += jnp.dot(
            down[c],
            (k // 4 + 32 * c == l).astype(jnp.float32),
            precision=lax.Precision.HIGHEST,
            preferred_element_type=jnp.float32,
        )
    small[...] = total
    packed = jnp.where(
        lanes_of(PACK) < CT, small[pl.ds(0, PACK, stride=2), :], small[pl.ds(1, PACK, stride=2), :]
    )
    for j in range(sums.shape[0]):
        sums[j] = packed
    for copy in copies:
        copy.wait()


def pick_kernel(tile_block, gathered, own, other, total):
    owned = own.shape[0]
    row_tile = lax.axis_index("gy")
    core = row_tile % 2
    first = (row_tile - core) * owned
    tile_cols, tile_rows = tile_block.shape
    total[...] = jnp.zeros_like(total)
    for t in range(tile_cols * tile_rows // 2):
        place = tile_block[t // (tile_rows // 2), t % (tile_rows // 2) * 2 + core] - first

        @pl.when((place >= 0) & (place < 2 * owned))
        def _():
            total[place] += gathered[t]

    own[...] = total[pl.ds(core * owned, owned)]
    other[...] = total[pl.ds((1 - core) * owned, owned)]


def join_kernel(own, received, out):
    total = own[...] + received[...]
    for j in range(PACK):
        out[:, j * LANES : (j + 1) * LANES] = total[:, j, :]


def in_vmem(count):
    return [pl.BlockSpec(memory_space=pltpu.VMEM)] * count


def in_smem(count):
    return [pl.BlockSpec(memory_space=pltpu.SMEM)] * count


def per_device(thickness, driving, observed, control, ice_mask, tile_block):
    f32 = jnp.float32
    rows, cols = lax.axis_size("gy"), lax.axis_size("gx")
    tile_block, ice_mask = tile_block[:, :, 0].T, ice_mask.T
    params = pltpu.CompilerParams(vmem_limit_bytes=VMEM_LIMIT)

    def shape(*sizes):
        return jax.ShapeDtypeStruct(sizes, f32)

    def swap(axis, cells_first, cells_second):
        count = lax.axis_size(axis)
        received = []
        for cells, low in ((cells_second, 1), (cells_first, 0)):
            pairs = [(i, i + 1) for i in range(low, count - 1, 2)]
            received.append(lax.ppermute(cells, axis, pairs + [(j, i) for i, j in pairs]))
        return received[1], received[0]

    fields = thickness, driving, observed
    owned = control.shape[0]
    *edges, parcels = pl.pallas_call(
        pack_kernel,
        out_shape=[shape(HALF, LANES)] * 2 + [shape(rows, PARCEL, LANES)],
        in_specs=in_smem(1) + [pl.BlockSpec(memory_space=pltpu.HBM)] * 4,
        out_specs=[pl.BlockSpec(memory_space=pltpu.HBM)] * 3,
        scratch_shapes=[
            pltpu.VMEM((5, TILE, TILE), f32),
            pltpu.VMEM(control.shape, f32),
            pltpu.VMEM((owned, PACK, LANES), f32),
            pltpu.VMEM((rows, PARCEL, LANES), f32),
            pltpu.VMEM((2, HALF, LANES), f32),
            pltpu.SemaphoreType.DMA((9,)),
        ],
        compiler_params=pltpu.CompilerParams(vmem_limit_bytes=PACK_VMEM_LIMIT),
        name="pack",
    )(tile_block, control, *fields)
    parcels = lax.all_to_all(parcels, "gy", 0, 0, tiled=True)
    columns_in = swap("gx", *edges)
    strips = pl.pallas_call(
        rows_kernel,
        out_shape=[shape(3, 64, LANES)] * 2,
        in_specs=in_vmem(5),
        out_specs=in_vmem(2),
        compiler_params=params,
        name="rows",
    )(*fields, *columns_in)
    rows_in = swap("gy", *strips)
    friction = pl.pallas_call(
        friction_kernel,
        out_shape=[shape(ALL_ROWS, LANES)] * 2,
        in_specs=in_smem(1) + in_vmem(1),
        out_specs=in_vmem(2),
        scratch_shapes=[pltpu.VMEM((PATCH, LANES), f32)],
        compiler_params=params,
        name="friction",
    )(ice_mask, parcels)
    prepared = pl.pallas_call(
        setup_kernel,
        out_shape=[shape(5, ALL_ROWS, LANES), shape(2, ALL_ROWS, LANES)],
        in_specs=in_vmem(7),
        out_specs=in_vmem(2),
        scratch_shapes=[
            pltpu.VMEM((3, ALL_ROWS, LANES), f32),
            pltpu.VMEM((2, ALL_ROWS, LANES), f32),
            pltpu.VMEM((FACTORS, ALL_ROWS, LANES), f32),
        ],
        compiler_params=params,
        name="setup",
    )(*friction, *fields, *columns_in)

    vel_u, vel_v, sums = pl.pallas_call(
        model_kernel,
        out_shape=(shape(TILE, TILE), shape(TILE, TILE), shape(cols * rows // 2, PACK, LANES)),
        in_specs=in_vmem(6),
        out_specs=[pl.BlockSpec(memory_space=pltpu.HBM)] * 2 + in_vmem(1),
        scratch_shapes=[
            pltpu.VMEM((5, ALL_ROWS, LANES), f32),
            pltpu.VMEM((3, ALL_ROWS, LANES), f32),
            pltpu.VMEM((2, ALL_ROWS, LANES), f32),
            pltpu.VMEM((2, ALL_ROWS, LANES), f32),
            pltpu.VMEM((2, ALL_ROWS, LANES), f32),
            pltpu.VMEM((FACTORS, ALL_ROWS, LANES), f32),
            pltpu.VMEM((CT, LANES), f32),
            pltpu.SemaphoreType.DMA((4,)),
        ],
        compiler_params=params,
        name="model",
    )(*friction, *prepared, *rows_in)

    same_core = [[i * rows + j for i in range(cols) for j in range(core, rows, 2)] for core in range(2)]
    sums = lax.all_to_all(sums, ("gx", "gy"), 0, 0, tiled=True, axis_index_groups=same_core)
    own, other = pl.pallas_call(
        pick_kernel,
        out_shape=[shape(owned, PACK, LANES)] * 2,
        in_specs=in_smem(1) + in_vmem(1),
        out_specs=in_vmem(2),
        scratch_shapes=[pltpu.VMEM((2 * owned, PACK, LANES), f32)],
        compiler_params=params,
        name="pick",
    )(tile_block, sums)
    received = lax.ppermute(other, "gy", [(j, j ^ 1) for j in range(rows)])
    gradient = pl.pallas_call(
        join_kernel,
        out_shape=shape(*control.shape),
        in_specs=in_vmem(2),
        out_specs=pl.BlockSpec(memory_space=pltpu.VMEM),
        compiler_params=params,
        name="join",
    )(own, received)
    return vel_u, vel_v, gradient


def solution(mesh):
    return jax.shard_map(
        per_device,
        mesh=mesh,
        in_specs=(P("gy", "gx"), P(None, "gy", "gx"), P(None, "gy", "gx"), P("gy", None), P(), P()),
        out_specs=(P("gy", "gx"), P("gy", "gx"), P("gy", None)),
        check_vma=False,
    )
```

```python
from types import SimpleNamespace

import jax
import jax.numpy as jnp
from jax import lax
from jax.experimental import pallas as pl
from jax.experimental.pallas import tpu as pltpu
from jax.sharding import PartitionSpec as P

TILE = 256
PIC = 4
SW = 2
ADJ = 6
CT = 64
COARSE = 4096

LANES = 128
HALO = 16
OBS = 8
MARGIN = 8
TOP = MARGIN + HALO
ROWS = TILE + 2 * TOP
HALF = TILE // 2
SIDE = 2 * ROWS
BAND = LANES // 2
ALL_ROWS = SIDE + HALF + 2 * TOP
MAIN = (0, ROWS)
SIDES = (SIDE,)
SPANS = {
    "frame": (MARGIN, 4, 72, MARGIN, 40, 0, 0),
    "inner": (MARGIN + 8, 3, 72, MARGIN + 8, 40, 56, 24),
    "tile": (TOP, 4, 64, TOP, 32, 0, 0),
}
FACTORS = 14
AHEAD = 2
PACK = COARSE // LANES
VMEM_LIMIT = 24 * 1024 * 1024
PACK_VMEM_LIMIT = 62 * 1024 * 1024

STRIP = ((0, HALO), (HALO, HALO), (2 * HALO, HALO), (3 * HALO, OBS), (3 * HALO + OBS, OBS))

CONTROL = ((0, 0, PACK, 0), (-1, PACK - 2, 2, PACK), (1, 0, 2, PACK + 2))
FOLDED = 40
PARCEL = 48
PATCH = CT + 8

visc_scale = 0.1
strain_floor = 0.05


def lanes_of(rows):
    return lax.broadcasted_iota(jnp.int32, (rows, LANES), 1)


def is_even(axis):
    return lax.axis_index(axis) % 2 == 0


def side_lanes(rows, ds, group):
    place = (lanes_of(rows) - 8 * group) % CT
    return place < 4 if ds > 0 else place >= CT - 4


def fill_parcels(tile_block, owned_blocks, parcels):
    tile_cols, tile_rows = tile_block.shape
    owned = owned_blocks.shape[0]
    mine = lax.axis_index("gy") * owned
    col_tile = lax.axis_index("gx")

    def spread(row, carry):
        for ds in (-1, 0, 1):
            col = col_tile + ds
            place = tile_block[jnp.clip(col, 0, tile_cols - 1), row] - mine

            @pl.when((col >= 0) & (col < tile_cols) & (place >= 0) & (place < owned))
            def _():
                for dr, first, count, at in CONTROL:
                    target = row - dr

                    @pl.when((target >= 0) & (target < tile_rows))
                    def _():
                        if ds == 0:
                            parcels[target, at : at + count, :] = owned_blocks[place, first : first + count, :]
                            return
                        start = FOLDED + at % 8
                        rows = min(count, 8)
                        folded = parcels[target, start : start + rows, :]
                        for i in range(count // rows):
                            group = at // 8 + i
                            cells = owned_blocks[place, first + 8 * i : first + 8 * i + rows, :]
                            folded = jnp.where(side_lanes(rows, ds, group), turn(cells, 0, 8 * group), folded)
                        parcels[target, start : start + rows, :] = folded

        return carry

    lax.fori_loop(0, tile_rows, spread, 0)


def pack_kernel(
    tile_block, control, thick, drive, obs, first_col, second_col, parcels,
    held, held_control, owned_blocks, packed_parcels, packed_cols, sems,
):
    copies = [pltpu.make_async_copy(control, held_control, sems.at[5])]
    for f, field in enumerate((thick, drive.at[0], drive.at[1], obs.at[0], obs.at[1])):
        copies.append(pltpu.make_async_copy(field, held.at[f], sems.at[f]))
    for copy in copies:
        copy.start()
    packed_parcels[...] = jnp.zeros_like(packed_parcels)
    copies[0].wait()
    for j in range(PACK):
        owned_blocks[:, j, :] = held_control[:, j * LANES : (j + 1) * LANES]
    fill_parcels(tile_block, owned_blocks, packed_parcels)
    results = [pltpu.make_async_copy(packed_parcels, parcels, sems.at[6])]
    results[0].start()

    lane = lanes_of(HALF)
    left = jnp.zeros((HALF, LANES), jnp.float32)
    right = jnp.zeros((HALF, LANES), jnp.float32)
    for f, (first, count) in enumerate(STRIP):
        copies[1 + f].wait()
        for part in range(2):
            rows = slice(part * HALF, (part + 1) * HALF)
            start = part * BAND + first
            inside = (lane >= start) & (lane < start + count)
            left = jnp.where(inside, turn(held[f, rows, :LANES], 0, start), left)
            right = jnp.where(inside, turn(held[f, rows, LANES:], LANES - count, start), right)
    even = is_even("gx")
    packed_cols[0] = jnp.where(even, right, left)
    packed_cols[1] = jnp.where(even, left, right)
    for i, out in enumerate((first_col, second_col)):
        results.append(pltpu.make_async_copy(packed_cols.at[i], out, sems.at[7 + i]))
        results[-1].start()
    for copy in results:
        copy.wait()


def sides(axis, first_pair, second_pair):
    even = is_even(axis)
    return jnp.where(even, second_pair, first_pair), jnp.where(even, first_pair, second_pair)


def choose_side(lane, high, east, west, low):
    place = lane % BAND
    return jnp.where(
        place < HALO, high, jnp.where(place < 2 * HALO, east, jnp.where(place < 3 * HALO, west, low))
    )


def turn(cells, source, target):
    shift = (target - source) % LANES
    return pltpu.roll(cells, shift, 1) if shift else cells


def gather(cells, source):
    return jnp.take_along_axis(cells, source, axis=1)


def scale_of(f):
    return 0.5 if f in (1, 2) else 1.0


def weave_kernel(thick, drive, obs, woven, own_sides, edges):
    lane, half_lane = lanes_of(TILE), lanes_of(HALF)
    source = 2 * lane % LANES
    for f, (field, (first, count)) in enumerate(zip((thick, drive.at[0], drive.at[1], obs.at[0], obs.at[1]), STRIP)):
        low, high = scale_of(f) * field[:, :LANES], scale_of(f) * field[:, LANES:]
        tiles = [jnp.where(lane < BAND, gather(low, source + i), gather(high, source + i)) for i in range(2)]
        bands = []
        for band in (0, BAND):
            bands.append(
                jnp.where(lane % BAND < BAND // 2, turn(high, LANES - HALO, band), turn(low, 0, band + 3 * HALO))
            )
        own_sides[f] = jnp.where(half_lane < BAND, bands[0][:HALF], bands[1][HALF:])
        for c in range(2):
            woven[f, c] = tiles[c]
        for c, tile in enumerate(tiles + [bands[1]]):
            edges[0, c, first : first + count, :] = tile[:count]
        for c, tile in enumerate(tiles + [bands[0]]):
            edges[1, c, first : first + count, :] = tile[TILE - count :]


def rows_kernel(edges, first_col, second_col, first_pair, second_pair):
    west, east = sides("gx", first_col[...], second_col[...])
    even = is_even("gy")
    for c in range(2):
        top, bottom = edges[0, c], edges[1, c]
        first_pair[c] = jnp.where(even, bottom, top)
        second_pair[c] = jnp.where(even, top, bottom)
    for f, (first, count) in enumerate(STRIP):
        strips = []
        for i, packed, source, target in (
            (0, slice(0, count), first, BAND),
            (1, slice(HALF - count, HALF), BAND + first, 0),
        ):
            own = edges[i, 2, first : first + count, :]
            from_east = scale_of(f) * turn(east[packed], source, target + HALO)
            from_west = scale_of(f) * turn(west[packed], source, target + 3 * HALO - count)
            strips.append(choose_side(lanes_of(count), own, from_east, from_west, own))
        top, bottom = strips
        first_pair[2, first : first + count, :] = jnp.where(even, bottom, top)
        second_pair[2, first : first + count, :] = jnp.where(even, top, bottom)


def shift_east(tiles):
    turned = pltpu.roll(tiles[0], LANES - 1, 1)
    return [turned] if len(tiles) == 1 else [tiles[1], turned]


def shift_west(tiles):
    turned = pltpu.roll(tiles[-1], 1, 1)
    return [turned] if len(tiles) == 1 else [turned, tiles[0]]


def run_groups(groups, read, work):
    pending = [read(*group) for group in groups[:AHEAD]]
    for k, (part, row, count) in enumerate(groups):
        if k + AHEAD < len(groups):
            pending.append(read(*groups[k + AHEAD]))
        for ref, lead, values in work(part, pending[k]):
            for tile, value in zip(part, values):
                ref[(*lead, pl.ds(row + tile, count), slice(None))] = value


def block_groups(row, main, side_row, side):
    step = 32 if main % 32 == 0 else 24
    first = side // 16 * 8 if side > 24 else side
    groups = [(MAIN, row + g, min(step, main - g)) for g in range(0, main, step)]
    groups[1:1] = [(SIDES, side_row, first)]
    if first < side:
        groups[3:3] = [(SIDES, side_row + first, side - first)]
    return groups


def over_rows(span, read, work):
    start, blocks, main, side_start, side, main_rest, side_rest = SPANS[span]

    def block(i, carry):
        row, side_row = pl.multiple_of(start + i * main, 8), pl.multiple_of(side_start + i * side, 8)
        run_groups(block_groups(row, main, side_row, side), read, work)
        return carry

    lax.fori_loop(0, blocks, block, 0)
    if main_rest:
        none = 8 * jnp.minimum(lax.axis_index("gx"), 0)
        row = pl.multiple_of(none + start + blocks * main, 8)
        side_row = pl.multiple_of(none + side_start + blocks * side, 8)
        run_groups(block_groups(row, main_rest, side_row, side_rest), read, work)


def over_ends(count, read, work):
    def block(i, carry):
        row = pl.multiple_of(MARGIN + i * (TILE + 2 * HALO - count), 8)
        side_row = pl.multiple_of(MARGIN + i * (HALF + 2 * HALO - count), 8)
        run_groups([(MAIN, row, count), (SIDES, side_row, count)], read, work)
        return carry

    lax.fori_loop(0, 2, block, 0)


def join_parts(ref, leads, whole):
    edge = HALO // 2

    def join(row, upper, lower, count):
        lane = lanes_of(count)
        place = lane % BAND
        for lead in leads:
            def at(tile_row):
                return (*lead, pl.ds(tile_row, count), slice(None))

            mixed = ref[at(SIDE + row)]
            if whole:
                source = jnp.where(place < edge, LANES - edge + place // 2, place // 2 - 24)
                source = jnp.clip(source, 0, LANES - 1)
                halves = []
                for main_row in (row, row + HALF):
                    even, odd = (gather(ref[at(tile + main_row)], source) for tile in MAIN)
                    halves.append(jnp.where(lane % 2 == 0, even, odd))
                outer = (place < edge) | (place >= BAND - edge)
                ref[at(SIDE + row)] = jnp.where(outer, jnp.where(lane < BAND, halves[0], halves[1]), mixed)
            for wanted, band, main_row in ((upper, 0, row), (lower, BAND, row + HALF)):
                if wanted:
                    few = edge // 2
                    source = band + jnp.where(lane < few, 3 * HALO + 2 * lane, edge + 2 * (lane - LANES + few))
                    source = jnp.clip(source, 0, LANES - 2)
                    outer = (lane < few) | (lane >= LANES - few)
                    for c, tile in enumerate(MAIN):
                        ref[at(tile + main_row)] = jnp.where(outer, gather(mixed, source + c), ref[at(tile + main_row)])

    step = 32

    def middle(i, carry):
        join(pl.multiple_of(TOP + i * step, 8), True, True, step)
        return carry

    lax.fori_loop(0, HALF // step, middle, 0)
    if whole:
        join(MARGIN, True, False, HALO)
        join(TOP + HALF, False, True, HALO)


def friction_kernel(ice_mask, parcels, fr, ice, patch):
    tile_cols, tile_rows = ice_mask.shape
    row_tile = lax.axis_index("gy")
    col_tile = lax.axis_index("gx")

    flat = sum(parcels[j] for j in range(tile_rows))
    folded = flat[FOLDED:]
    for dr, _, count, at in CONTROL:
        cells = flat[at : at + count]
        if dr == 0:
            side = jnp.concatenate([turn(folded, 8 * g, 0) for g in range(PACK // 8)], axis=0)
        else:
            side = turn(folded, PACK, 0)[at % 8 : at % 8 + count]
        inner = lanes_of(count) < CT
        row = 4 + {-1: -4, 0: 0, 1: CT}[dr]
        patch[pl.ds(row, count, stride=2), :] = jnp.where(inner, cells, turn(side, 0, CT))
        patch[pl.ds(row + 1, count, stride=2), :] = jnp.where(inner, turn(cells, 0, CT), side)

    cells = 0.5 * jnp.exp(patch[...])
    lane = lanes_of(PATCH)
    wide = gather(cells, lane // 2)
    for tile in MAIN:
        for j in range(4):
            fr[pl.ds(tile + MARGIN + j, PATCH, stride=4), :] = wide
    lane = lanes_of(40)
    place = lane % BAND // 4
    source = jnp.where(place < 8, 60 + place, (116 + place) % LANES)
    wide = jnp.where(
        lane < BAND,
        gather(cells[:40], source),
        gather(cells[PATCH - 40 :], source),
    )
    for j in range(4):
        fr[pl.ds(SIDE + MARGIN + j, 40, stride=4), :] = wide

    side_ice = []
    for dr, first, count in ((-1, MARGIN, HALO), (0, TOP, TILE), (1, TOP + TILE, HALO)):
        masks = []
        for ds in (-1, 0, 1):
            row, col = row_tile + dr, col_tile + ds
            inside = (row >= 0) & (row < tile_rows) & (col >= 0) & (col < tile_cols)
            row = jnp.clip(row, 0, tile_rows - 1)
            col = jnp.clip(col, 0, tile_cols - 1)
            masks.append(jnp.where(inside, ice_mask[col, row], 0).astype(jnp.float32))
        for c in range(2):
            ice[MAIN[c] + first : MAIN[c] + first + count, :] = jnp.full((count, LANES), masks[1])
        side_ice.append(choose_side(lanes_of(HALO), masks[1], masks[2], masks[0], masks[1]))
    upper = lanes_of(HALO) < BAND
    for i in range(HALF // HALO):
        ice[SIDE + TOP + i * HALO : SIDE + TOP + (i + 1) * HALO, :] = side_ice[1]
    ice[SIDE + MARGIN : SIDE + TOP, :] = jnp.where(upper, side_ice[0], side_ice[1])
    ice[SIDE + TOP + HALF : SIDE + TOP + HALF + HALO, :] = jnp.where(upper, side_ice[1], side_ice[2])


def make_stages(ext, fr, ice, visc, vel_a, vel_b, coef):
    def load(ref, part, row, count, *lead):
        return [ref[(*lead, pl.ds(row + tile, count), slice(None))] for tile in part]

    def load_around(part, row, count, now):
        return [load(now, part, r, count, i) for i in range(2) for r in (row, row - 1, row + 1)]

    def load_right(part, row, count):
        return [load(ext, part, row, count, i) for i in (1, 2)]

    def read_thickness(part, row, count):
        return load(ext, part, row, count, 0)

    def keep_viscosity(q):
        return [(visc, (0,), q), (visc, (1,), shift_west(q)), (visc, (2,), shift_east(q))]

    def first_viscosity(part, thickness):
        factor = 0.25 * visc_scale * strain_floor ** (-1.0 / 3.0)
        return keep_viscosity([factor * t for t in thickness])

    def read_viscosity(part, row, count):
        return read_thickness(part, row, count), load_around(part, row, count, vel_b)

    def viscosity(part, read):
        thickness, (u, u_n, u_s, v, v_n, v_s) = read
        u_e, u_w = shift_east(u), shift_west(u)
        v_e, v_w = shift_east(v), shift_west(v)
        result = []
        for c in range(len(part)):
            ux, vx = u_e[c] - u_w[c], v_e[c] - v_w[c]
            uy, vy = u_s[c] - u_n[c], v_s[c] - v_n[c]
            shear = uy + vx
            strain = 0.25 * (ux * (ux + vy) + vy * vy) + (0.0625 * (shear * shear) + strain_floor)
            result.append((0.25 * visc_scale) * thickness[c] * jnp.exp(jnp.log(strain) * (-1.0 / 3.0)))
        return keep_viscosity(result)

    def inverse(x):
        near = pl.reciprocal(x, approx=True)
        return near * (2.0 - x * near)

    def read_coefficients(part, row, count):
        around = [load(visc, part, r, count, i) for i in range(3) for r in (row, row - 1, row + 1)]
        return around + [load(fr, part, row, count), load(ice, part, row, count)]

    def coefficients(part, read):
        tiles = range(len(part))
        q, q_n, q_s, q_w, q_nw, q_sw, q_e, q_ne, q_se, friction, mask = read
        w = [q[c] + q_w[c] for c in tiles]
        e = [q[c] + q_e[c] for c in tiles]
        s = [q[c] + q_s[c] for c in tiles]
        n = [q[c] + q_n[c] for c in tiles]
        scale_u, scale_v = [], []
        for c in tiles:
            across, along = e[c] + w[c], s[c] + n[c]
            scale_u.append(mask[c] * inverse(friction[c] + along + 4.0 * across))
            scale_v.append(mask[c] * inverse(friction[c] + across + 4.0 * along))
        corners = []
        half = [0.5 * q[c] for c in tiles]
        for shifted in (q_sw, q_nw, q_se, q_ne):
            corners.append([q[c] + 0.5 * shifted[c] for c in tiles])
            corners.append([half[c] + shifted[c] for c in tiles])
        return [e, w, s, n, scale_u, scale_v] + corners

    def relax(part, k, around, right):
        tiles = range(len(part))
        e, w, s, n, scale_u, scale_v, sw_u, sw_v, nw_u, nw_v, se_u, se_v, ne_u, ne_v = k
        u, u_n, u_s, v, v_n, v_s = around
        to_west_u, to_east_u, to_west_v, to_east_v = [], [], [], []
        for c in tiles:
            u4 = 4.0 * u[c]
            to_west_u.append(w[c] * u4 + (sw_u[c] * v_s[c] - nw_u[c] * v_n[c]))
            to_east_u.append(e[c] * u4 + (ne_u[c] * v_n[c] - se_u[c] * v_s[c]))
            to_west_v.append(w[c] * v[c] + (sw_v[c] * u_s[c] - nw_v[c] * u_n[c]))
            to_east_v.append(e[c] * v[c] + (ne_v[c] * u_n[c] - se_v[c] * u_s[c]))
        to_west_u, to_west_v = shift_east(to_west_u), shift_east(to_west_v)
        to_east_u, to_east_v = shift_west(to_east_u), shift_west(to_east_v)
        new_u, new_v = [], []
        for c in tiles:
            mid_u = s[c] * u_s[c] + n[c] * u_n[c]
            mid_v = 4.0 * (s[c] * v_s[c] + n[c] * v_n[c])
            new_u.append(scale_u[c] * (right[0][c] + mid_u + (to_west_u[c] + to_east_u[c])))
            new_v.append(scale_v[c] * (right[1][c] + mid_v + (to_west_v[c] + to_east_v[c])))
        return new_u, new_v

    def put(new, values):
        return [(new, (i,), values[i]) for i in range(2)]

    def keep(k):
        return [(coef, (i,), k[i]) for i in range(FACTORS)]

    def read_sweep(now):
        def read(part, row, count):
            k = [load(coef, part, row, count, i) for i in range(FACTORS)]
            return k, load_around(part, row, count, now), load_right(part, row, count)

        return read

    def sweep(new):
        return lambda part, read: put(new, relax(part, *read))

    def read_first(part, row, count):
        return read_coefficients(part, row, count), load_right(part, row, count)

    def first_start(part, read):
        k = coefficients(part, read[0])
        return keep(k) + put(vel_a, [[a * b for a, b in zip(k[4 + i], read[1][i])] for i in range(2)])

    def read_start(part, row, count):
        return (*read_first(part, row, count), load_around(part, row, count, vel_b))

    def start(part, read):
        k = coefficients(part, read[0])
        return keep(k) + put(vel_a, relax(part, k, read[2], read[1]))

    return SimpleNamespace(**locals())


def setup_kernel(
    fr, ice, woven, own_sides, first_col, second_col,
    ext, vel_b,
    visc, vel_a, coef,
):
    west, east = sides("gx", first_col[...], second_col[...])
    lane = lanes_of(HALF)
    for f, (first, count) in enumerate(STRIP):
        for c in range(2):
            ext[f, MAIN[c] + TOP : MAIN[c] + TOP + TILE, :] = woven[f, c]
        from_east = scale_of(f) * turn(east, first, HALO)
        from_west = scale_of(f) * turn(west, first, 3 * HALO - count)
        own = own_sides[f]
        ext[f, SIDE + TOP : SIDE + TOP + HALF, :] = choose_side(lane, own, from_east, from_west, own)
    step = make_stages(ext, fr, ice, visc, vel_a, vel_b, coef)
    over_rows("tile", step.read_thickness, step.first_viscosity)
    over_rows("tile", step.read_first, step.first_start)
    over_rows("tile", step.read_sweep(vel_a), step.sweep(vel_b))


def model_kernel(
    fr, ice, ext_in, vel_in, first_row, second_row,
    vel_u, vel_v, sums,
    ext, visc, vel_a, vel_b, vel_c, coef, plain, small, sems,
):
    ext[...] = ext_in[...]
    vel_b[...] = vel_in[...]
    even = is_even("gy")
    here = SIDE + TOP
    for f, (first, count) in enumerate(STRIP):
        frames = []
        for c in range(3):
            one, two = first_row[c, first : first + count, :], second_row[c, first : first + count, :]
            frames.append((jnp.where(even, two, one), jnp.where(even, one, two)))
        for c in range(2):
            ext[f, MAIN[c] + TOP - count : MAIN[c] + TOP, :] = frames[c][0]
            ext[f, MAIN[c] + TOP + TILE : MAIN[c] + TOP + TILE + count, :] = frames[c][1]
        upper = lanes_of(count) < BAND
        above = turn(ext_in[f, here + HALF - count : here + HALF, :], 0, BAND)
        below = turn(ext_in[f, here : here + count, :], 0, BAND)
        ext[f, here - count : here, :] = jnp.where(upper, frames[2][0], above)
        ext[f, here + HALF : here + HALF + count, :] = jnp.where(upper, below, frames[2][1])

    step = make_stages(ext, fr, ice, visc, vel_a, vel_b, coef)
    over_ends(32, step.read_thickness, step.first_viscosity)
    over_ends(32, step.read_first, step.first_start)
    over_ends(24, step.read_sweep(vel_a), step.sweep(vel_b))

    def iterate(span):
        over_rows(span, step.read_viscosity, step.viscosity)
        over_rows(span, step.read_start, step.start)
        over_rows(span, step.read_sweep(vel_a), step.sweep(vel_b))

    def iteration(i, carry):
        iterate("frame")
        return carry

    lax.fori_loop(1, PIC - 1, iteration, 0)
    join_parts(vel_b, ((0,), (1,)), True)
    iterate("inner")
    join_parts(vel_b, ((0,), (1,)), False)
    lane = lanes_of(TILE)
    copies = []
    for i, out in enumerate((vel_u, vel_v)):
        even, odd = (vel_b[i, tile + TOP : tile + TOP + TILE, :] for tile in MAIN)
        for c in range(2):
            source = BAND * c + lane // 2
            plain[i, c] = jnp.where(lane % 2 == 0, gather(even, source), gather(odd, source))
            copies.append(
                pltpu.make_async_copy(plain.at[i, c], out.at[:, c * LANES : (c + 1) * LANES], sems.at[2 * i + c])
            )
            copies[-1].start()

    load = step.load

    def read_misfit(part, row, count):
        return [
            [load(vel_b, part, row, count, i), load(ext, part, row, count, 3 + i), load(coef, part, row, count, 4 + i)]
            for i in range(2)
        ]

    def first_adjoint(part, read):
        misfit = [[0.5 * (a - b) for a, b in zip(u, seen)] for u, seen, _ in read]
        first = [[a * b for a, b in zip(read[i][2], misfit[i])] for i in range(2)]
        return step.put(vel_c, first) + [(ext, (1 + i,), misfit[i]) for i in range(2)]

    over_rows("inner", read_misfit, first_adjoint)

    def two_sweeps(i, carry):
        over_rows("inner", step.read_sweep(vel_c), step.sweep(vel_a))
        over_rows("inner", step.read_sweep(vel_a), step.sweep(vel_c))
        return carry

    lax.fori_loop(0, (ADJ - 2) // 2, two_sweeps, 0)
    over_rows("tile", step.read_sweep(vel_c), step.sweep(vel_a))

    def read_gradient(part, row, count):
        return [load(ref, part, row, count, i) for ref in (vel_b, vel_a) for i in range(2)] + [load(fr, part, row, count)]

    def gradient(part, read):
        u, v, lu, lv, friction = read
        return [(visc, (0,), [-2.0 * friction[c] * (u[c] * lu[c] + v[c] * lv[c]) for c in range(len(part))])]

    over_rows("tile", read_gradient, gradient)
    join_parts(visc, ((0,),), False)
    down = sum(visc[0, pl.ds(tile + TOP + j, CT, stride=4), :] for tile in MAIN for j in range(4))
    k = lax.broadcasted_iota(jnp.int32, (LANES, LANES), 0)
    total = jnp.dot(
        down,
        (k // 2 == lanes_of(LANES) % CT).astype(jnp.float32),
        precision=lax.Precision.HIGHEST,
        preferred_element_type=jnp.float32,
    )
    small[...] = total
    packed = jnp.where(
        lanes_of(PACK) < CT, small[pl.ds(0, PACK, stride=2), :], small[pl.ds(1, PACK, stride=2), :]
    )
    for j in range(sums.shape[0]):
        sums[j] = packed
    for copy in copies:
        copy.wait()


def pick_kernel(tile_block, gathered, own, other, total):
    owned = own.shape[0]
    row_tile = lax.axis_index("gy")
    core = row_tile % 2
    first = (row_tile - core) * owned
    tile_cols, tile_rows = tile_block.shape
    total[...] = jnp.zeros_like(total)
    for t in range(tile_cols * tile_rows // 2):
        place = tile_block[t // (tile_rows // 2), t % (tile_rows // 2) * 2 + core] - first

        @pl.when((place >= 0) & (place < 2 * owned))
        def _():
            total[place] += gathered[t]

    own[...] = total[pl.ds(core * owned, owned)]
    other[...] = total[pl.ds((1 - core) * owned, owned)]


def join_kernel(own, received, out):
    total = own[...] + received[...]
    for j in range(PACK):
        out[:, j * LANES : (j + 1) * LANES] = total[:, j, :]


def in_vmem(count):
    return [pl.BlockSpec(memory_space=pltpu.VMEM)] * count


def in_smem(count):
    return [pl.BlockSpec(memory_space=pltpu.SMEM)] * count


def per_device(thickness, driving, observed, control, ice_mask, tile_block):
    f32 = jnp.float32
    rows, cols = lax.axis_size("gy"), lax.axis_size("gx")
    tile_block, ice_mask = tile_block[:, :, 0].T, ice_mask.T
    params = pltpu.CompilerParams(vmem_limit_bytes=VMEM_LIMIT)

    def shape(*sizes):
        return jax.ShapeDtypeStruct(sizes, f32)

    def swap(axis, cells_first, cells_second):
        count = lax.axis_size(axis)
        received = []
        for cells, low in ((cells_second, 1), (cells_first, 0)):
            pairs = [(i, i + 1) for i in range(low, count - 1, 2)]
            received.append(lax.ppermute(cells, axis, pairs + [(j, i) for i, j in pairs]))
        return received[1], received[0]

    fields = thickness, driving, observed
    owned = control.shape[0]
    *edges, parcels = pl.pallas_call(
        pack_kernel,
        out_shape=[shape(HALF, LANES)] * 2 + [shape(rows, PARCEL, LANES)],
        in_specs=in_smem(1) + [pl.BlockSpec(memory_space=pltpu.HBM)] * 4,
        out_specs=[pl.BlockSpec(memory_space=pltpu.HBM)] * 3,
        scratch_shapes=[
            pltpu.VMEM((5, TILE, TILE), f32),
            pltpu.VMEM(control.shape, f32),
            pltpu.VMEM((owned, PACK, LANES), f32),
            pltpu.VMEM((rows, PARCEL, LANES), f32),
            pltpu.VMEM((2, HALF, LANES), f32),
            pltpu.SemaphoreType.DMA((9,)),
        ],
        compiler_params=pltpu.CompilerParams(vmem_limit_bytes=PACK_VMEM_LIMIT),
        name="pack",
    )(tile_block, control, *fields)
    parcels = lax.all_to_all(parcels, "gy", 0, 0, tiled=True)
    columns_in = swap("gx", *edges)
    woven, own_sides, strips = pl.pallas_call(
        weave_kernel,
        out_shape=[shape(5, 2, TILE, LANES), shape(5, HALF, LANES), shape(2, 3, 64, LANES)],
        in_specs=in_vmem(3),
        out_specs=in_vmem(3),
        compiler_params=params,
        name="weave",
    )(*fields)
    strips = pl.pallas_call(
        rows_kernel,
        out_shape=[shape(3, 64, LANES)] * 2,
        in_specs=in_vmem(3),
        out_specs=in_vmem(2),
        compiler_params=params,
        name="rows",
    )(strips, *columns_in)
    rows_in = swap("gy", *strips)
    friction = pl.pallas_call(
        friction_kernel,
        out_shape=[shape(ALL_ROWS, LANES)] * 2,
        in_specs=in_smem(1) + in_vmem(1),
        out_specs=in_vmem(2),
        scratch_shapes=[pltpu.VMEM((PATCH, LANES), f32)],
        compiler_params=params,
        name="friction",
    )(ice_mask, parcels)
    prepared = pl.pallas_call(
        setup_kernel,
        out_shape=[shape(5, ALL_ROWS, LANES), shape(2, ALL_ROWS, LANES)],
        in_specs=in_vmem(6),
        out_specs=in_vmem(2),
        scratch_shapes=[
            pltpu.VMEM((3, ALL_ROWS, LANES), f32),
            pltpu.VMEM((2, ALL_ROWS, LANES), f32),
            pltpu.VMEM((FACTORS, ALL_ROWS, LANES), f32),
        ],
        compiler_params=params,
        name="setup",
    )(*friction, woven, own_sides, *columns_in)

    vel_u, vel_v, sums = pl.pallas_call(
        model_kernel,
        out_shape=(shape(TILE, TILE), shape(TILE, TILE), shape(cols * rows // 2, PACK, LANES)),
        in_specs=in_vmem(6),
        out_specs=[pl.BlockSpec(memory_space=pltpu.HBM)] * 2 + in_vmem(1),
        scratch_shapes=[
            pltpu.VMEM((5, ALL_ROWS, LANES), f32),
            pltpu.VMEM((3, ALL_ROWS, LANES), f32),
            pltpu.VMEM((2, ALL_ROWS, LANES), f32),
            pltpu.VMEM((2, ALL_ROWS, LANES), f32),
            pltpu.VMEM((2, ALL_ROWS, LANES), f32),
            pltpu.VMEM((FACTORS, ALL_ROWS, LANES), f32),
            pltpu.VMEM((2, 2, TILE, LANES), f32),
            pltpu.VMEM((CT, LANES), f32),
            pltpu.SemaphoreType.DMA((4,)),
        ],
        compiler_params=params,
        name="model",
    )(*friction, *prepared, *rows_in)

    same_core = [[i * rows + j for i in range(cols) for j in range(core, rows, 2)] for core in range(2)]
    sums = lax.all_to_all(sums, ("gx", "gy"), 0, 0, tiled=True, axis_index_groups=same_core)
    own, other = pl.pallas_call(
        pick_kernel,
        out_shape=[shape(owned, PACK, LANES)] * 2,
        in_specs=in_smem(1) + in_vmem(1),
        out_specs=in_vmem(2),
        scratch_shapes=[pltpu.VMEM((2 * owned, PACK, LANES), f32)],
        compiler_params=params,
        name="pick",
    )(tile_block, sums)
    received = lax.ppermute(other, "gy", [(j, j ^ 1) for j in range(rows)])
    gradient = pl.pallas_call(
        join_kernel,
        out_shape=shape(*control.shape),
        in_specs=in_vmem(2),
        out_specs=pl.BlockSpec(memory_space=pltpu.VMEM),
        compiler_params=params,
        name="join",
    )(own, received)
    return vel_u, vel_v, gradient


def solution(mesh):
    return jax.shard_map(
        per_device,
        mesh=mesh,
        in_specs=(P("gy", "gx"), P(None, "gy", "gx"), P(None, "gy", "gx"), P("gy", None), P(), P()),
        out_specs=(P("gy", "gx"), P("gy", "gx"), P("gy", None)),
        check_vma=False,
    )
```

```python
from types import SimpleNamespace

import jax
import jax.numpy as jnp
from jax import lax
from jax.experimental import pallas as pl
from jax.experimental.pallas import tpu as pltpu
from jax.sharding import PartitionSpec as P

TILE = 256
PIC = 4
SW = 2
ADJ = 6
CT = 64
COARSE = 4096

LANES = 128
HALO = 16
OBS = 8
MARGIN = 8
TOP = MARGIN + HALO
ROWS = TILE + 2 * TOP
HALF = TILE // 2
SIDE = 2 * ROWS
BAND = LANES // 2
ALL_ROWS = SIDE + HALF + 2 * TOP
MAIN = (0, ROWS)
SIDES = (SIDE,)
SPANS = {
    "frame": (MARGIN, 4, 72, MARGIN, 40, 0, 0),
    "inner": (MARGIN + 8, 3, 72, MARGIN + 8, 40, 56, 24),
    "tile": (TOP, 4, 64, TOP, 32, 0, 0),
}
FACTORS = 14
AHEAD = 5
PACK = COARSE // LANES
VMEM_LIMIT = 24 * 1024 * 1024
PACK_VMEM_LIMIT = 62 * 1024 * 1024

STRIP = ((0, HALO), (HALO, HALO), (2 * HALO, HALO), (3 * HALO, OBS), (3 * HALO + OBS, OBS))

CONTROL = ((0, 0, PACK, 0), (-1, PACK - 2, 2, PACK), (1, 0, 2, PACK + 2))
FOLDED = 40
PARCEL = 48
PATCH = CT + 8

visc_scale = 0.1
strain_floor = 0.05


def lanes_of(rows):
    return lax.broadcasted_iota(jnp.int32, (rows, LANES), 1)


def is_even(axis):
    return lax.axis_index(axis) % 2 == 0


def side_lanes(rows, ds, group):
    place = (lanes_of(rows) - 8 * group) % CT
    return place < 4 if ds > 0 else place >= CT - 4


def fill_parcels(tile_block, owned_blocks, parcels):
    tile_cols, tile_rows = tile_block.shape
    owned = owned_blocks.shape[0]
    mine = lax.axis_index("gy") * owned
    col_tile = lax.axis_index("gx")

    def spread(row, carry):
        for ds in (-1, 0, 1):
            col = col_tile + ds
            place = tile_block[jnp.clip(col, 0, tile_cols - 1), row] - mine

            @pl.when((col >= 0) & (col < tile_cols) & (place >= 0) & (place < owned))
            def _():
                for dr, first, count, at in CONTROL:
                    target = row - dr

                    @pl.when((target >= 0) & (target < tile_rows))
                    def _():
                        if ds == 0:
                            parcels[target, at : at + count, :] = owned_blocks[place, first : first + count, :]
                            return
                        start = FOLDED + at % 8
                        rows = min(count, 8)
                        folded = parcels[target, start : start + rows, :]
                        for i in range(count // rows):
                            group = at // 8 + i
                            cells = owned_blocks[place, first + 8 * i : first + 8 * i + rows, :]
                            folded = jnp.where(side_lanes(rows, ds, group), turn(cells, 0, 8 * group), folded)
                        parcels[target, start : start + rows, :] = folded

        return carry

    lax.fori_loop(0, tile_rows, spread, 0)


def pack_kernel(
    tile_block, control, thick, drive, obs, first_col, second_col, parcels,
    held, held_control, owned_blocks, packed_parcels, packed_cols, sems,
):
    copies = [pltpu.make_async_copy(control, held_control, sems.at[5])]
    for f, field in enumerate((thick, drive.at[0], drive.at[1], obs.at[0], obs.at[1])):
        copies.append(pltpu.make_async_copy(field, held.at[f], sems.at[f]))
    for copy in copies:
        copy.start()
    packed_parcels[...] = jnp.zeros_like(packed_parcels)
    copies[0].wait()
    for j in range(PACK):
        owned_blocks[:, j, :] = held_control[:, j * LANES : (j + 1) * LANES]
    fill_parcels(tile_block, owned_blocks, packed_parcels)
    results = [pltpu.make_async_copy(packed_parcels, parcels, sems.at[6])]
    results[0].start()

    lane = lanes_of(HALF)
    left = jnp.zeros((HALF, LANES), jnp.float32)
    right = jnp.zeros((HALF, LANES), jnp.float32)
    for f, (first, count) in enumerate(STRIP):
        copies[1 + f].wait()
        for part in range(2):
            rows = slice(part * HALF, (part + 1) * HALF)
            start = part * BAND + first
            inside = (lane >= start) & (lane < start + count)
            left = jnp.where(inside, turn(held[f, rows, :LANES], 0, start), left)
            right = jnp.where(inside, turn(held[f, rows, LANES:], LANES - count, start), right)
    even = is_even("gx")
    packed_cols[0] = jnp.where(even, right, left)
    packed_cols[1] = jnp.where(even, left, right)
    for i, out in enumerate((first_col, second_col)):
        results.append(pltpu.make_async_copy(packed_cols.at[i], out, sems.at[7 + i]))
        results[-1].start()
    for copy in results:
        copy.wait()


def pass_kernel(parcels, after, out):
    pass


def sides(axis, first_pair, second_pair):
    even = is_even(axis)
    return jnp.where(even, second_pair, first_pair), jnp.where(even, first_pair, second_pair)


def choose_side(lane, high, east, west, low):
    place = lane % BAND
    return jnp.where(
        place < HALO, high, jnp.where(place < 2 * HALO, east, jnp.where(place < 3 * HALO, west, low))
    )


def turn(cells, source, target):
    shift = (target - source) % LANES
    return pltpu.roll(cells, shift, 1) if shift else cells


def gather(cells, source):
    return jnp.take_along_axis(cells, source, axis=1)


def scale_of(f):
    return 0.5 if f in (1, 2) else 1.0


def weave_kernel(thick, drive, obs, woven, own_sides, edges):
    lane, half_lane = lanes_of(TILE), lanes_of(HALF)
    source = 2 * lane % LANES
    for f, (field, (first, count)) in enumerate(zip((thick, drive.at[0], drive.at[1], obs.at[0], obs.at[1]), STRIP)):
        low, high = scale_of(f) * field[:, :LANES], scale_of(f) * field[:, LANES:]
        tiles = [jnp.where(lane < BAND, gather(low, source + i), gather(high, source + i)) for i in range(2)]
        bands = []
        for band in (0, BAND):
            bands.append(
                jnp.where(lane % BAND < BAND // 2, turn(high, LANES - HALO, band), turn(low, 0, band + 3 * HALO))
            )
        own_sides[f] = jnp.where(half_lane < BAND, bands[0][:HALF], bands[1][HALF:])
        for c in range(2):
            woven[f, c] = tiles[c]
        for c, tile in enumerate(tiles + [bands[1]]):
            edges[0, c, first : first + count, :] = tile[:count]
        for c, tile in enumerate(tiles + [bands[0]]):
            edges[1, c, first : first + count, :] = tile[TILE - count :]


def rows_kernel(edges, first_col, second_col, first_pair, second_pair):
    west, east = sides("gx", first_col[...], second_col[...])
    even = is_even("gy")
    for c in range(2):
        top, bottom = edges[0, c], edges[1, c]
        first_pair[c] = jnp.where(even, bottom, top)
        second_pair[c] = jnp.where(even, top, bottom)
    for f, (first, count) in enumerate(STRIP):
        strips = []
        for i, packed, source, target in (
            (0, slice(0, count), first, BAND),
            (1, slice(HALF - count, HALF), BAND + first, 0),
        ):
            own = edges[i, 2, first : first + count, :]
            from_east = scale_of(f) * turn(east[packed], source, target + HALO)
            from_west = scale_of(f) * turn(west[packed], source, target + 3 * HALO - count)
            strips.append(choose_side(lanes_of(count), own, from_east, from_west, own))
        top, bottom = strips
        first_pair[2, first : first + count, :] = jnp.where(even, bottom, top)
        second_pair[2, first : first + count, :] = jnp.where(even, top, bottom)


def shift_east(tiles):
    turned = pltpu.roll(tiles[0], LANES - 1, 1)
    return [turned] if len(tiles) == 1 else [tiles[1], turned]


def shift_west(tiles):
    turned = pltpu.roll(tiles[-1], 1, 1)
    return [turned] if len(tiles) == 1 else [turned, tiles[0]]


def run_groups(groups, read, work):
    pending = [read(*group) for group in groups[:AHEAD]]
    for k, (part, row, count) in enumerate(groups):
        if k + AHEAD < len(groups):
            pending.append(read(*groups[k + AHEAD]))
        for ref, lead, values in work(part, pending[k]):
            for tile, value in zip(part, values):
                ref[(*lead, pl.ds(row + tile, count), slice(None))] = value


def block_groups(row, main, side_row, side):
    step = 32 if main % 32 == 0 else 24
    first = side // 16 * 8 if side > 24 else side
    groups = [(MAIN, row + g, min(step, main - g)) for g in range(0, main, step)]
    groups[1:1] = [(SIDES, side_row, first)]
    if first < side:
        groups[3:3] = [(SIDES, side_row + first, side - first)]
    return groups


def over_rows(span, read, work):
    start, blocks, main, side_start, side, main_rest, side_rest = SPANS[span]

    def block(i, carry):
        row, side_row = pl.multiple_of(start + i * main, 8), pl.multiple_of(side_start + i * side, 8)
        run_groups(block_groups(row, main, side_row, side), read, work)
        return carry

    lax.fori_loop(0, blocks, block, 0)
    if main_rest:
        none = 8 * jnp.minimum(lax.axis_index("gx"), 0)
        row = pl.multiple_of(none + start + blocks * main, 8)
        side_row = pl.multiple_of(none + side_start + blocks * side, 8)
        run_groups(block_groups(row, main_rest, side_row, side_rest), read, work)


def over_ends(count, read, work):
    def block(i, carry):
        row = pl.multiple_of(MARGIN + i * (TILE + 2 * HALO - count), 8)
        side_row = pl.multiple_of(MARGIN + i * (HALF + 2 * HALO - count), 8)
        run_groups([(MAIN, row, count), (SIDES, side_row, count)], read, work)
        return carry

    lax.fori_loop(0, 2, block, 0)


def join_parts(ref, leads, whole):
    edge = HALO // 2

    def join(row, upper, lower, count):
        lane = lanes_of(count)
        place = lane % BAND
        for lead in leads:
            def at(tile_row):
                return (*lead, pl.ds(tile_row, count), slice(None))

            mixed = ref[at(SIDE + row)]
            if whole:
                source = jnp.where(place < edge, LANES - edge + place // 2, place // 2 - 24)
                source = jnp.clip(source, 0, LANES - 1)
                halves = []
                for main_row in (row, row + HALF):
                    even, odd = (gather(ref[at(tile + main_row)], source) for tile in MAIN)
                    halves.append(jnp.where(lane % 2 == 0, even, odd))
                outer = (place < edge) | (place >= BAND - edge)
                ref[at(SIDE + row)] = jnp.where(outer, jnp.where(lane < BAND, halves[0], halves[1]), mixed)
            for wanted, band, main_row in ((upper, 0, row), (lower, BAND, row + HALF)):
                if wanted:
                    few = edge // 2
                    source = band + jnp.where(lane < few, 3 * HALO + 2 * lane, edge + 2 * (lane - LANES + few))
                    source = jnp.clip(source, 0, LANES - 2)
                    outer = (lane < few) | (lane >= LANES - few)
                    for c, tile in enumerate(MAIN):
                        ref[at(tile + main_row)] = jnp.where(outer, gather(mixed, source + c), ref[at(tile + main_row)])

    step = 32

    def middle(i, carry):
        join(pl.multiple_of(TOP + i * step, 8), True, True, step)
        return carry

    lax.fori_loop(0, HALF // step, middle, 0)
    if whole:
        join(MARGIN, True, False, HALO)
        join(TOP + HALF, False, True, HALO)


def friction_kernel(ice_mask, parcels, fr, ice, patch):
    tile_cols, tile_rows = ice_mask.shape
    row_tile = lax.axis_index("gy")
    col_tile = lax.axis_index("gx")

    flat = sum(parcels[j] for j in range(tile_rows))
    folded = flat[FOLDED:]
    for dr, _, count, at in CONTROL:
        cells = flat[at : at + count]
        if dr == 0:
            side = jnp.concatenate([turn(folded, 8 * g, 0) for g in range(PACK // 8)], axis=0)
        else:
            side = turn(folded, PACK, 0)[at % 8 : at % 8 + count]
        inner = lanes_of(count) < CT
        row = 4 + {-1: -4, 0: 0, 1: CT}[dr]
        patch[pl.ds(row, count, stride=2), :] = jnp.where(inner, cells, turn(side, 0, CT))
        patch[pl.ds(row + 1, count, stride=2), :] = jnp.where(inner, turn(cells, 0, CT), side)

    cells = 0.5 * jnp.exp(patch[...])
    lane = lanes_of(PATCH)
    wide = gather(cells, lane // 2)
    for tile in MAIN:
        for j in range(4):
            fr[pl.ds(tile + MARGIN + j, PATCH, stride=4), :] = wide
    lane = lanes_of(40)
    place = lane % BAND // 4
    source = jnp.where(place < 8, 60 + place, (116 + place) % LANES)
    wide = jnp.where(
        lane < BAND,
        gather(cells[:40], source),
        gather(cells[PATCH - 40 :], source),
    )
    for j in range(4):
        fr[pl.ds(SIDE + MARGIN + j, 40, stride=4), :] = wide

    side_ice = []
    for dr, first, count in ((-1, MARGIN, HALO), (0, TOP, TILE), (1, TOP + TILE, HALO)):
        masks = []
        for ds in (-1, 0, 1):
            row, col = row_tile + dr, col_tile + ds
            inside = (row >= 0) & (row < tile_rows) & (col >= 0) & (col < tile_cols)
            row = jnp.clip(row, 0, tile_rows - 1)
            col = jnp.clip(col, 0, tile_cols - 1)
            masks.append(jnp.where(inside, ice_mask[col, row], 0).astype(jnp.float32))
        for c in range(2):
            ice[MAIN[c] + first : MAIN[c] + first + count, :] = jnp.full((count, LANES), masks[1])
        side_ice.append(choose_side(lanes_of(HALO), masks[1], masks[2], masks[0], masks[1]))
    upper = lanes_of(HALO) < BAND
    for i in range(HALF // HALO):
        ice[SIDE + TOP + i * HALO : SIDE + TOP + (i + 1) * HALO, :] = side_ice[1]
    ice[SIDE + MARGIN : SIDE + TOP, :] = jnp.where(upper, side_ice[0], side_ice[1])
    ice[SIDE + TOP + HALF : SIDE + TOP + HALF + HALO, :] = jnp.where(upper, side_ice[1], side_ice[2])


def make_stages(ext, fr, ice, visc, vel_a, vel_b, coef):
    def load(ref, part, row, count, *lead):
        return [ref[(*lead, pl.ds(row + tile, count), slice(None))] for tile in part]

    def load_around(part, row, count, now):
        return [load(now, part, r, count, i) for i in range(2) for r in (row, row - 1, row + 1)]

    def load_right(part, row, count):
        return [load(ext, part, row, count, i) for i in (1, 2)]

    def read_thickness(part, row, count):
        return load(ext, part, row, count, 0)

    def keep_viscosity(q):
        return [(visc, (0,), q), (visc, (1,), shift_west(q)), (visc, (2,), shift_east(q))]

    def first_viscosity(part, thickness):
        factor = 0.25 * visc_scale * strain_floor ** (-1.0 / 3.0)
        return keep_viscosity([factor * t for t in thickness])

    def read_viscosity(part, row, count):
        return read_thickness(part, row, count), load_around(part, row, count, vel_b)

    def viscosity(part, read):
        thickness, (u, u_n, u_s, v, v_n, v_s) = read
        u_e, u_w = shift_east(u), shift_west(u)
        v_e, v_w = shift_east(v), shift_west(v)
        result = []
        for c in range(len(part)):
            ux, vx = u_e[c] - u_w[c], v_e[c] - v_w[c]
            uy, vy = u_s[c] - u_n[c], v_s[c] - v_n[c]
            shear = uy + vx
            strain = 0.25 * (ux * (ux + vy) + vy * vy) + (0.0625 * (shear * shear) + strain_floor)
            result.append((0.25 * visc_scale) * thickness[c] * jnp.exp(jnp.log(strain) * (-1.0 / 3.0)))
        return keep_viscosity(result)

    def inverse(x):
        near = pl.reciprocal(x, approx=True)
        return near * (2.0 - x * near)

    def read_coefficients(part, row, count):
        around = [load(visc, part, r, count, i) for i in range(3) for r in (row, row - 1, row + 1)]
        return around + [load(fr, part, row, count), load(ice, part, row, count)]

    def coefficients(part, read):
        tiles = range(len(part))
        q, q_n, q_s, q_w, q_nw, q_sw, q_e, q_ne, q_se, friction, mask = read
        w = [q[c] + q_w[c] for c in tiles]
        e = [q[c] + q_e[c] for c in tiles]
        s = [q[c] + q_s[c] for c in tiles]
        n = [q[c] + q_n[c] for c in tiles]
        scale_u, scale_v = [], []
        for c in tiles:
            across, along = e[c] + w[c], s[c] + n[c]
            scale_u.append(mask[c] * inverse(friction[c] + along + 4.0 * across))
            scale_v.append(mask[c] * inverse(friction[c] + across + 4.0 * along))
        corners = []
        half = [0.5 * q[c] for c in tiles]
        for shifted in (q_sw, q_nw, q_se, q_ne):
            corners.append([q[c] + 0.5 * shifted[c] for c in tiles])
            corners.append([half[c] + shifted[c] for c in tiles])
        return [e, w, s, n, scale_u, scale_v] + corners

    def relax(part, k, around, right):
        tiles = range(len(part))
        e, w, s, n, scale_u, scale_v, sw_u, sw_v, nw_u, nw_v, se_u, se_v, ne_u, ne_v = k
        u, u_n, u_s, v, v_n, v_s = around
        to_west_u, to_east_u, to_west_v, to_east_v = [], [], [], []
        for c in tiles:
            u4 = 4.0 * u[c]
            to_west_u.append(w[c] * u4 + (sw_u[c] * v_s[c] - nw_u[c] * v_n[c]))
            to_east_u.append(e[c] * u4 + (ne_u[c] * v_n[c] - se_u[c] * v_s[c]))
            to_west_v.append(w[c] * v[c] + (sw_v[c] * u_s[c] - nw_v[c] * u_n[c]))
            to_east_v.append(e[c] * v[c] + (ne_v[c] * u_n[c] - se_v[c] * u_s[c]))
        to_west_u, to_west_v = shift_east(to_west_u), shift_east(to_west_v)
        to_east_u, to_east_v = shift_west(to_east_u), shift_west(to_east_v)
        new_u, new_v = [], []
        for c in tiles:
            mid_u = s[c] * u_s[c] + n[c] * u_n[c]
            mid_v = 4.0 * (s[c] * v_s[c] + n[c] * v_n[c])
            new_u.append(scale_u[c] * (right[0][c] + mid_u + (to_west_u[c] + to_east_u[c])))
            new_v.append(scale_v[c] * (right[1][c] + mid_v + (to_west_v[c] + to_east_v[c])))
        return new_u, new_v

    def put(new, values):
        return [(new, (i,), values[i]) for i in range(2)]

    def keep(k):
        return [(coef, (i,), k[i]) for i in range(FACTORS)]

    def read_sweep(now):
        def read(part, row, count):
            k = [load(coef, part, row, count, i) for i in range(FACTORS)]
            return k, load_around(part, row, count, now), load_right(part, row, count)

        return read

    def sweep(new):
        return lambda part, read: put(new, relax(part, *read))

    def read_first(part, row, count):
        return read_coefficients(part, row, count), load_right(part, row, count)

    def first_start(part, read):
        k = coefficients(part, read[0])
        return keep(k) + put(vel_a, [[a * b for a, b in zip(k[4 + i], read[1][i])] for i in range(2)])

    def read_start(part, row, count):
        return (*read_first(part, row, count), load_around(part, row, count, vel_b))

    def start(part, read):
        k = coefficients(part, read[0])
        return keep(k) + put(vel_a, relax(part, k, read[2], read[1]))

    return SimpleNamespace(**locals())


def setup_kernel(
    fr, ice, woven, own_sides, first_col, second_col,
    ext, vel_b,
    visc, vel_a, coef,
):
    west, east = sides("gx", first_col[...], second_col[...])
    lane = lanes_of(HALF)
    for f, (first, count) in enumerate(STRIP):
        for c in range(2):
            ext[f, MAIN[c] + TOP : MAIN[c] + TOP + TILE, :] = woven[f, c]
        from_east = scale_of(f) * turn(east, first, HALO)
        from_west = scale_of(f) * turn(west, first, 3 * HALO - count)
        own = own_sides[f]
        ext[f, SIDE + TOP : SIDE + TOP + HALF, :] = choose_side(lane, own, from_east, from_west, own)
    step = make_stages(ext, fr, ice, visc, vel_a, vel_b, coef)
    over_rows("tile", step.read_thickness, step.first_viscosity)
    over_rows("tile", step.read_first, step.first_start)
    over_rows("tile", step.read_sweep(vel_a), step.sweep(vel_b))


def model_kernel(
    fr, ice, ext_in, vel_in, first_row, second_row,
    vel_u, vel_v, sums,
    ext, visc, vel_a, vel_b, vel_c, coef, plain, small, sems,
):
    ext[...] = ext_in[...]
    vel_b[...] = vel_in[...]
    even = is_even("gy")
    here = SIDE + TOP
    for f, (first, count) in enumerate(STRIP):
        frames = []
        for c in range(3):
            one, two = first_row[c, first : first + count, :], second_row[c, first : first + count, :]
            frames.append((jnp.where(even, two, one), jnp.where(even, one, two)))
        for c in range(2):
            ext[f, MAIN[c] + TOP - count : MAIN[c] + TOP, :] = frames[c][0]
            ext[f, MAIN[c] + TOP + TILE : MAIN[c] + TOP + TILE + count, :] = frames[c][1]
        upper = lanes_of(count) < BAND
        above = turn(ext_in[f, here + HALF - count : here + HALF, :], 0, BAND)
        below = turn(ext_in[f, here : here + count, :], 0, BAND)
        ext[f, here - count : here, :] = jnp.where(upper, frames[2][0], above)
        ext[f, here + HALF : here + HALF + count, :] = jnp.where(upper, below, frames[2][1])

    step = make_stages(ext, fr, ice, visc, vel_a, vel_b, coef)
    over_ends(32, step.read_thickness, step.first_viscosity)
    over_ends(32, step.read_first, step.first_start)
    over_ends(24, step.read_sweep(vel_a), step.sweep(vel_b))

    def iterate(span):
        over_rows(span, step.read_viscosity, step.viscosity)
        over_rows(span, step.read_start, step.start)
        over_rows(span, step.read_sweep(vel_a), step.sweep(vel_b))

    def iteration(i, carry):
        iterate("frame")
        return carry

    lax.fori_loop(1, PIC - 1, iteration, 0)
    join_parts(vel_b, ((0,), (1,)), True)
    iterate("inner")
    join_parts(vel_b, ((0,), (1,)), False)
    lane = lanes_of(TILE)
    copies = []
    for i, out in enumerate((vel_u, vel_v)):
        even, odd = (vel_b[i, tile + TOP : tile + TOP + TILE, :] for tile in MAIN)
        for c in range(2):
            source = BAND * c + lane // 2
            plain[i, c] = jnp.where(lane % 2 == 0, gather(even, source), gather(odd, source))
            copies.append(
                pltpu.make_async_copy(plain.at[i, c], out.at[:, c * LANES : (c + 1) * LANES], sems.at[2 * i + c])
            )
            copies[-1].start()

    load = step.load

    def read_misfit(part, row, count):
        return [
            [load(vel_b, part, row, count, i), load(ext, part, row, count, 3 + i), load(coef, part, row, count, 4 + i)]
            for i in range(2)
        ]

    def first_adjoint(part, read):
        misfit = [[0.5 * (a - b) for a, b in zip(u, seen)] for u, seen, _ in read]
        first = [[a * b for a, b in zip(read[i][2], misfit[i])] for i in range(2)]
        return step.put(vel_c, first) + [(ext, (1 + i,), misfit[i]) for i in range(2)]

    over_rows("inner", read_misfit, first_adjoint)

    def two_sweeps(i, carry):
        over_rows("inner", step.read_sweep(vel_c), step.sweep(vel_a))
        over_rows("inner", step.read_sweep(vel_a), step.sweep(vel_c))
        return carry

    lax.fori_loop(0, (ADJ - 2) // 2, two_sweeps, 0)
    over_rows("tile", step.read_sweep(vel_c), step.sweep(vel_a))

    def read_gradient(part, row, count):
        return [load(ref, part, row, count, i) for ref in (vel_b, vel_a) for i in range(2)] + [load(fr, part, row, count)]

    def gradient(part, read):
        u, v, lu, lv, friction = read
        return [(visc, (0,), [-2.0 * friction[c] * (u[c] * lu[c] + v[c] * lv[c]) for c in range(len(part))])]

    over_rows("tile", read_gradient, gradient)
    join_parts(visc, ((0,),), False)
    down = sum(visc[0, pl.ds(tile + TOP + j, CT, stride=4), :] for tile in MAIN for j in range(4))
    k = lax.broadcasted_iota(jnp.int32, (LANES, LANES), 0)
    total = jnp.dot(
        down,
        (k // 2 == lanes_of(LANES) % CT).astype(jnp.float32),
        precision=lax.Precision.HIGHEST,
        preferred_element_type=jnp.float32,
    )
    small[...] = total
    packed = jnp.where(
        lanes_of(PACK) < CT, small[pl.ds(0, PACK, stride=2), :], small[pl.ds(1, PACK, stride=2), :]
    )
    for j in range(sums.shape[0]):
        sums[j] = packed
    for copy in copies:
        copy.wait()


def pick_kernel(tile_block, gathered, own, other, total):
    owned = own.shape[0]
    row_tile = lax.axis_index("gy")
    core = row_tile % 2
    first = (row_tile - core) * owned
    tile_cols, tile_rows = tile_block.shape
    total[...] = jnp.zeros_like(total)
    for t in range(tile_cols * tile_rows // 2):
        place = tile_block[t // (tile_rows // 2), t % (tile_rows // 2) * 2 + core] - first

        @pl.when((place >= 0) & (place < 2 * owned))
        def _():
            total[place] += gathered[t]

    own[...] = total[pl.ds(core * owned, owned)]
    other[...] = total[pl.ds((1 - core) * owned, owned)]


def join_kernel(own, received, out):
    total = own[...] + received[...]
    for j in range(PACK):
        out[:, j * LANES : (j + 1) * LANES] = total[:, j, :]


def in_vmem(count):
    return [pl.BlockSpec(memory_space=pltpu.VMEM)] * count


def in_smem(count):
    return [pl.BlockSpec(memory_space=pltpu.SMEM)] * count


def per_device(thickness, driving, observed, control, ice_mask, tile_block):
    f32 = jnp.float32
    rows, cols = lax.axis_size("gy"), lax.axis_size("gx")
    tile_block, ice_mask = tile_block[:, :, 0].T, ice_mask.T
    params = pltpu.CompilerParams(vmem_limit_bytes=VMEM_LIMIT)

    def shape(*sizes):
        return jax.ShapeDtypeStruct(sizes, f32)

    def swap(axis, cells_first, cells_second):
        count = lax.axis_size(axis)
        received = []
        for cells, low in ((cells_second, 1), (cells_first, 0)):
            pairs = [(i, i + 1) for i in range(low, count - 1, 2)]
            received.append(lax.ppermute(cells, axis, pairs + [(j, i) for i, j in pairs]))
        return received[1], received[0]

    fields = thickness, driving, observed
    owned = control.shape[0]
    *edges, parcels = pl.pallas_call(
        pack_kernel,
        out_shape=[shape(HALF, LANES)] * 2 + [shape(rows, PARCEL, LANES)],
        in_specs=in_smem(1) + [pl.BlockSpec(memory_space=pltpu.HBM)] * 4,
        out_specs=[pl.BlockSpec(memory_space=pltpu.HBM)] * 3,
        scratch_shapes=[
            pltpu.VMEM((5, TILE, TILE), f32),
            pltpu.VMEM(control.shape, f32),
            pltpu.VMEM((owned, PACK, LANES), f32),
            pltpu.VMEM((rows, PARCEL, LANES), f32),
            pltpu.VMEM((2, HALF, LANES), f32),
            pltpu.SemaphoreType.DMA((9,)),
        ],
        compiler_params=pltpu.CompilerParams(vmem_limit_bytes=PACK_VMEM_LIMIT),
        name="pack",
    )(tile_block, control, *fields)
    columns_in = swap("gx", *edges)
    parcels = pl.pallas_call(
        pass_kernel,
        out_shape=shape(*parcels.shape),
        in_specs=[pl.BlockSpec(memory_space=pl.ANY)] * 2,
        out_specs=pl.BlockSpec(memory_space=pl.ANY),
        input_output_aliases={0: 0},
        compiler_params=pltpu.CompilerParams(vmem_limit_bytes=1024 * 1024),
        name="pass",
    )(parcels, columns_in[0])
    parcels = lax.all_to_all(parcels, "gy", 0, 0, tiled=True)
    woven, own_sides, strips = pl.pallas_call(
        weave_kernel,
        out_shape=[shape(5, 2, TILE, LANES), shape(5, HALF, LANES), shape(2, 3, 64, LANES)],
        in_specs=in_vmem(3),
        out_specs=in_vmem(3),
        compiler_params=params,
        name="weave",
    )(*fields)
    strips = pl.pallas_call(
        rows_kernel,
        out_shape=[shape(3, 64, LANES)] * 2,
        in_specs=in_vmem(3),
        out_specs=in_vmem(2),
        compiler_params=params,
        name="rows",
    )(strips, *columns_in)
    rows_in = swap("gy", *strips)
    friction = pl.pallas_call(
        friction_kernel,
        out_shape=[shape(ALL_ROWS, LANES)] * 2,
        in_specs=in_smem(1) + in_vmem(1),
        out_specs=in_vmem(2),
        scratch_shapes=[pltpu.VMEM((PATCH, LANES), f32)],
        compiler_params=params,
        name="friction",
    )(ice_mask, parcels)
    prepared = pl.pallas_call(
        setup_kernel,
        out_shape=[shape(5, ALL_ROWS, LANES), shape(2, ALL_ROWS, LANES)],
        in_specs=in_vmem(6),
        out_specs=in_vmem(2),
        scratch_shapes=[
            pltpu.VMEM((3, ALL_ROWS, LANES), f32),
            pltpu.VMEM((2, ALL_ROWS, LANES), f32),
            pltpu.VMEM((FACTORS, ALL_ROWS, LANES), f32),
        ],
        compiler_params=params,
        name="setup",
    )(*friction, woven, own_sides, *columns_in)

    vel_u, vel_v, sums = pl.pallas_call(
        model_kernel,
        out_shape=(shape(TILE, TILE), shape(TILE, TILE), shape(cols * rows // 2, PACK, LANES)),
        in_specs=in_vmem(6),
        out_specs=[pl.BlockSpec(memory_space=pltpu.HBM)] * 2 + in_vmem(1),
        scratch_shapes=[
            pltpu.VMEM((5, ALL_ROWS, LANES), f32),
            pltpu.VMEM((3, ALL_ROWS, LANES), f32),
            pltpu.VMEM((2, ALL_ROWS, LANES), f32),
            pltpu.VMEM((2, ALL_ROWS, LANES), f32),
            pltpu.VMEM((2, ALL_ROWS, LANES), f32),
            pltpu.VMEM((FACTORS, ALL_ROWS, LANES), f32),
            pltpu.VMEM((2, 2, TILE, LANES), f32),
            pltpu.VMEM((CT, LANES), f32),
            pltpu.SemaphoreType.DMA((4,)),
        ],
        compiler_params=params,
        name="model",
    )(*friction, *prepared, *rows_in)

    same_core = [[i * rows + j for i in range(cols) for j in range(core, rows, 2)] for core in range(2)]
    sums = lax.all_to_all(sums, ("gx", "gy"), 0, 0, tiled=True, axis_index_groups=same_core)
    own, other = pl.pallas_call(
        pick_kernel,
        out_shape=[shape(owned, PACK, LANES)] * 2,
        in_specs=in_smem(1) + in_vmem(1),
        out_specs=in_vmem(2),
        scratch_shapes=[pltpu.VMEM((2 * owned, PACK, LANES), f32)],
        compiler_params=params,
        name="pick",
    )(tile_block, sums)
    received = lax.ppermute(other, "gy", [(j, j ^ 1) for j in range(rows)])
    gradient = pl.pallas_call(
        join_kernel,
        out_shape=shape(*control.shape),
        in_specs=in_vmem(2),
        out_specs=pl.BlockSpec(memory_space=pltpu.VMEM),
        compiler_params=params,
        name="join",
    )(own, received)
    return vel_u, vel_v, gradient


def solution(mesh):
    return jax.shard_map(
        per_device,
        mesh=mesh,
        in_specs=(P("gy", "gx"), P(None, "gy", "gx"), P(None, "gy", "gx"), P("gy", None), P(), P()),
        out_specs=(P("gy", "gx"), P("gy", "gx"), P("gy", None)),
        check_vma=False,
    )
```

```python
from types import SimpleNamespace

import jax
import jax.numpy as jnp
from jax import lax
from jax.experimental import pallas as pl
from jax.experimental.pallas import tpu as pltpu
from jax.sharding import PartitionSpec as P

TILE = 256
PIC = 4
SW = 2
ADJ = 6
CT = 64
COARSE = 4096

LANES = 128
HALO = 16
OBS = 8
MARGIN = 8
TOP = MARGIN + HALO
ROWS = TILE + 2 * TOP
HALF = TILE // 2
SIDE = 2 * ROWS
BAND = LANES // 2
ALL_ROWS = SIDE + HALF + 2 * TOP
MAIN = (0, ROWS)
SIDES = (SIDE,)
SPANS = {
    "frame": (MARGIN, 4, 72, MARGIN, 40, 0, 0),
    "inner": (MARGIN + 8, 3, 72, MARGIN + 8, 40, 56, 24),
    "tile": (TOP, 4, 64, TOP, 32, 0, 0),
}
FACTORS = 14
AHEAD = 5
PACK = COARSE // LANES
VMEM_LIMIT = 24 * 1024 * 1024

STRIP = ((0, HALO), (HALO, HALO), (2 * HALO, HALO), (3 * HALO, OBS), (3 * HALO + OBS, OBS))

PATCH_ROWS = ((-1, PACK - 2, 2, 0), (0, 0, PACK, 4), (1, 0, 2, CT + 4))
PATCH = CT + 8

visc_scale = 0.1
strain_floor = 0.05


def lanes_of(rows):
    return lax.broadcasted_iota(jnp.int32, (rows, LANES), 1)


def is_even(axis):
    return lax.axis_index(axis) % 2 == 0


def columns_kernel(thick, drive, obs, first_col, second_col):
    lane = lanes_of(HALF)
    left = jnp.zeros((HALF, LANES), jnp.float32)
    right = jnp.zeros((HALF, LANES), jnp.float32)
    for field, (first, count) in zip((thick, drive.at[0], drive.at[1], obs.at[0], obs.at[1]), STRIP):
        for part in range(2):
            rows = slice(part * HALF, (part + 1) * HALF)
            start = part * BAND + first
            inside = (lane >= start) & (lane < start + count)
            left = jnp.where(inside, turn(field[rows, :LANES], 0, start), left)
            right = jnp.where(inside, turn(field[rows, LANES:], LANES - count, start), right)
    even = is_even("gx")
    first_col[...] = jnp.where(even, right, left)
    second_col[...] = jnp.where(even, left, right)


def sides(axis, first_pair, second_pair):
    even = is_even(axis)
    return jnp.where(even, second_pair, first_pair), jnp.where(even, first_pair, second_pair)


def choose_side(lane, high, east, west, low):
    place = lane % BAND
    return jnp.where(
        place < HALO, high, jnp.where(place < 2 * HALO, east, jnp.where(place < 3 * HALO, west, low))
    )


def turn(cells, source, target):
    shift = (target - source) % LANES
    return pltpu.roll(cells, shift, 1) if shift else cells


def gather(cells, source):
    return jnp.take_along_axis(cells, source, axis=1)


def scale_of(f):
    return 0.5 if f in (1, 2) else 1.0


def weave_kernel(thick, drive, obs, woven, own_sides, edges):
    lane, half_lane = lanes_of(TILE), lanes_of(HALF)
    source = 2 * lane % LANES
    for f, (field, (first, count)) in enumerate(zip((thick, drive.at[0], drive.at[1], obs.at[0], obs.at[1]), STRIP)):
        low, high = scale_of(f) * field[:, :LANES], scale_of(f) * field[:, LANES:]
        tiles = [jnp.where(lane < BAND, gather(low, source + i), gather(high, source + i)) for i in range(2)]
        bands = []
        for band in (0, BAND):
            bands.append(
                jnp.where(lane % BAND < BAND // 2, turn(high, LANES - HALO, band), turn(low, 0, band + 3 * HALO))
            )
        own_sides[f] = jnp.where(half_lane < BAND, bands[0][:HALF], bands[1][HALF:])
        for c in range(2):
            woven[f, c] = tiles[c]
        for c, tile in enumerate(tiles + [bands[0]]):
            edges[0, c, first : first + count, :] = tile[:count]
            edges[1, c, first : first + count, :] = tile[TILE - count :]


def rows_kernel(edges, first_col, second_col, first_pair, second_pair):
    west, east = sides("gx", first_col[...], second_col[...])
    even = is_even("gy")
    for c in range(2):
        top, bottom = edges[0, c], edges[1, c]
        first_pair[64 * c : 64 * c + 64, :] = jnp.where(even, bottom, top)
        second_pair[64 * c : 64 * c + 64, :] = jnp.where(even, top, bottom)
    strips = []
    for i in range(2):
        fields = []
        for f, (first, count) in enumerate(STRIP):
            packed = slice(HALF - count, HALF) if i else slice(0, count)
            source = BAND * i + first
            target = BAND if f >= 2 else 0
            own = turn(edges[i, 2, first : first + count, :], 0, target)
            from_east = scale_of(f) * turn(east[packed], source, target + HALO)
            from_west = scale_of(f) * turn(west[packed], source, target + 3 * HALO - count)
            fields.append(choose_side(lanes_of(count), own, from_east, from_west, own))
        lane = lanes_of(HALO)
        lower = jnp.concatenate(fields[3:], axis=0)
        strips.append((jnp.where(lane < BAND, fields[0], fields[2]), jnp.where(lane < BAND, fields[1], lower)))
    for k in range(2):
        top, bottom = strips[0][k], strips[1][k]
        rows = slice(128 + HALO * k, 128 + HALO * (k + 1))
        first_pair[rows, :] = jnp.where(even, bottom, top)
        second_pair[rows, :] = jnp.where(even, top, bottom)


def shift_east(tiles):
    turned = pltpu.roll(tiles[0], LANES - 1, 1)
    return [turned] if len(tiles) == 1 else [tiles[1], turned]


def shift_west(tiles):
    turned = pltpu.roll(tiles[-1], 1, 1)
    return [turned] if len(tiles) == 1 else [turned, tiles[0]]


def run_groups(groups, read, work):
    pending = [read(*group) for group in groups[:AHEAD]]
    for k, (part, row, count) in enumerate(groups):
        if k + AHEAD < len(groups):
            pending.append(read(*groups[k + AHEAD]))
        for ref, lead, values in work(part, pending[k]):
            for tile, value in zip(part, values):
                ref[(*lead, pl.ds(row + tile, count), slice(None))] = value


def block_groups(row, main, side_row, side):
    step = 32 if main % 32 == 0 else 24
    first = side // 16 * 8 if side > 24 else side
    groups = [(MAIN, row + g, min(step, main - g)) for g in range(0, main, step)]
    groups[1:1] = [(SIDES, side_row, first)]
    if first < side:
        groups[3:3] = [(SIDES, side_row + first, side - first)]
    return groups


def over_rows(span, read, work):
    start, blocks, main, side_start, side, main_rest, side_rest = SPANS[span]

    def block(i, carry):
        row, side_row = pl.multiple_of(start + i * main, 8), pl.multiple_of(side_start + i * side, 8)
        run_groups(block_groups(row, main, side_row, side), read, work)
        return carry

    lax.fori_loop(0, blocks, block, 0)
    if main_rest:
        none = 8 * jnp.minimum(lax.axis_index("gx"), 0)
        row = pl.multiple_of(none + start + blocks * main, 8)
        side_row = pl.multiple_of(none + side_start + blocks * side, 8)
        run_groups(block_groups(row, main_rest, side_row, side_rest), read, work)


def over_ends(count, read, work):
    def block(i, carry):
        row = pl.multiple_of(MARGIN + i * (TILE + 2 * HALO - count), 8)
        side_row = pl.multiple_of(MARGIN + i * (HALF + 2 * HALO - count), 8)
        run_groups([(MAIN, row, count), (SIDES, side_row, count)], read, work)
        return carry

    lax.fori_loop(0, 2, block, 0)


def join_parts(ref, leads, whole):
    edge = HALO // 2

    def join(row, upper, lower, count):
        lane = lanes_of(count)
        place = lane % BAND
        for lead in leads:
            def at(tile_row):
                return (*lead, pl.ds(tile_row, count), slice(None))

            mixed = ref[at(SIDE + row)]
            if whole:
                source = jnp.where(place < edge, LANES - edge + place // 2, place // 2 - 24)
                source = jnp.clip(source, 0, LANES - 1)
                halves = []
                for main_row in (row, row + HALF):
                    even, odd = (gather(ref[at(tile + main_row)], source) for tile in MAIN)
                    halves.append(jnp.where(lane % 2 == 0, even, odd))
                outer = (place < edge) | (place >= BAND - edge)
                ref[at(SIDE + row)] = jnp.where(outer, jnp.where(lane < BAND, halves[0], halves[1]), mixed)
            for wanted, band, main_row in ((upper, 0, row), (lower, BAND, row + HALF)):
                if wanted:
                    few = edge // 2
                    source = band + jnp.where(lane < few, 3 * HALO + 2 * lane, edge + 2 * (lane - LANES + few))
                    source = jnp.clip(source, 0, LANES - 2)
                    outer = (lane < few) | (lane >= LANES - few)
                    for c, tile in enumerate(MAIN):
                        ref[at(tile + main_row)] = jnp.where(outer, gather(mixed, source + c), ref[at(tile + main_row)])

    step = 32

    def middle(i, carry):
        join(pl.multiple_of(TOP + i * step, 8), True, True, step)
        return carry

    lax.fori_loop(0, HALF // step, middle, 0)
    if whole:
        join(MARGIN, True, False, HALO)
        join(TOP + HALF, False, True, HALO)


def friction_kernel(tile_block, ice_mask, control, fr, ice, blocks, patch):
    tile_cols, tile_rows = ice_mask.shape
    row_tile = lax.axis_index("gy")
    col_tile = lax.axis_index("gx")

    owned = control.shape[1]
    owner_row = lax.broadcasted_iota(jnp.int32, (owned, LANES), 0)
    for dr, first, count, at in PATCH_ROWS:
        for ds in (-1, 0, 1):
            row = jnp.clip(row_tile + dr, 0, tile_rows - 1)
            col = jnp.clip(col_tile + ds, 0, tile_cols - 1)
            block = tile_block[col, row]
            holder = block // owned
            here = owner_row == block - holder * owned
            for j in range(first, first + count):
                held = control[holder, :, j * LANES : (j + 1) * LANES]
                blocks[ds + 1, j : j + 1, :] = jnp.sum(jnp.where(here, held, 0.0), axis=0, keepdims=True)
        west, mid, east = (blocks[k, first : first + count, :] for k in range(3))
        lane = lanes_of(count)
        even = jnp.where(lane < CT, mid, jnp.where(lane < 96, turn(east, 0, CT), turn(west, 0, CT)))
        odd = jnp.where(lane < CT, turn(mid, 0, CT), jnp.where(lane < 96, east, west))
        patch[pl.ds(at, count, stride=2), :] = even
        patch[pl.ds(at + 1, count, stride=2), :] = odd

    cells = 0.5 * jnp.exp(patch[...])
    lane = lanes_of(PATCH)
    wide = gather(cells, lane // 2)
    for tile in MAIN:
        for j in range(4):
            fr[pl.ds(tile + MARGIN + j, PATCH, stride=4), :] = wide
    lane = lanes_of(40)
    place = lane % BAND // 4
    source = jnp.where(place < 8, 60 + place, (116 + place) % LANES)
    wide = jnp.where(
        lane < BAND,
        gather(cells[:40], source),
        gather(cells[PATCH - 40 :], source),
    )
    for j in range(4):
        fr[pl.ds(SIDE + MARGIN + j, 40, stride=4), :] = wide

    side_ice = []
    for dr, first, count in ((-1, MARGIN, HALO), (0, TOP, TILE), (1, TOP + TILE, HALO)):
        masks = []
        for ds in (-1, 0, 1):
            row, col = row_tile + dr, col_tile + ds
            inside = (row >= 0) & (row < tile_rows) & (col >= 0) & (col < tile_cols)
            row = jnp.clip(row, 0, tile_rows - 1)
            col = jnp.clip(col, 0, tile_cols - 1)
            masks.append(jnp.where(inside, ice_mask[col, row], 0).astype(jnp.float32))
        for c in range(2):
            ice[MAIN[c] + first : MAIN[c] + first + count, :] = jnp.full((count, LANES), masks[1])
        side_ice.append(choose_side(lanes_of(HALO), masks[1], masks[2], masks[0], masks[1]))
    upper = lanes_of(HALO) < BAND
    for i in range(HALF // HALO):
        ice[SIDE + TOP + i * HALO : SIDE + TOP + (i + 1) * HALO, :] = side_ice[1]
    ice[SIDE + MARGIN : SIDE + TOP, :] = jnp.where(upper, side_ice[0], side_ice[1])
    ice[SIDE + TOP + HALF : SIDE + TOP + HALF + HALO, :] = jnp.where(upper, side_ice[1], side_ice[2])


def make_stages(ext, fr, ice, visc, vel_a, vel_b, coef):
    def load(ref, part, row, count, *lead):
        return [ref[(*lead, pl.ds(row + tile, count), slice(None))] for tile in part]

    def load_around(part, row, count, now):
        return [load(now, part, r, count, i) for i in range(2) for r in (row, row - 1, row + 1)]

    def load_right(part, row, count):
        return [load(ext, part, row, count, i) for i in (1, 2)]

    def read_thickness(part, row, count):
        return load(ext, part, row, count, 0)

    def keep_viscosity(q):
        return [(visc, (0,), q), (visc, (1,), shift_west(q)), (visc, (2,), shift_east(q))]

    def first_viscosity(part, thickness):
        factor = 0.25 * visc_scale * strain_floor ** (-1.0 / 3.0)
        return keep_viscosity([factor * t for t in thickness])

    def read_viscosity(part, row, count):
        return read_thickness(part, row, count), load_around(part, row, count, vel_b)

    def viscosity(part, read):
        thickness, (u, u_n, u_s, v, v_n, v_s) = read
        u_e, u_w = shift_east(u), shift_west(u)
        v_e, v_w = shift_east(v), shift_west(v)
        result = []
        for c in range(len(part)):
            ux, vx = u_e[c] - u_w[c], v_e[c] - v_w[c]
            uy, vy = u_s[c] - u_n[c], v_s[c] - v_n[c]
            shear = uy + vx
            strain = 0.25 * (ux * (ux + vy) + vy * vy) + (0.0625 * (shear * shear) + strain_floor)
            result.append((0.25 * visc_scale) * thickness[c] * jnp.exp(jnp.log(strain) * (-1.0 / 3.0)))
        return keep_viscosity(result)

    def inverse(x):
        near = pl.reciprocal(x, approx=True)
        return near * (2.0 - x * near)

    def read_coefficients(part, row, count):
        around = [load(visc, part, r, count, i) for i in range(3) for r in (row, row - 1, row + 1)]
        return around + [load(fr, part, row, count), load(ice, part, row, count)]

    def coefficients(part, read):
        tiles = range(len(part))
        q, q_n, q_s, q_w, q_nw, q_sw, q_e, q_ne, q_se, friction, mask = read
        w = [q[c] + q_w[c] for c in tiles]
        e = [q[c] + q_e[c] for c in tiles]
        s = [q[c] + q_s[c] for c in tiles]
        n = [q[c] + q_n[c] for c in tiles]
        scale_u, scale_v = [], []
        for c in tiles:
            across, along = e[c] + w[c], s[c] + n[c]
            scale_u.append(mask[c] * inverse(friction[c] + along + 4.0 * across))
            scale_v.append(mask[c] * inverse(friction[c] + across + 4.0 * along))
        corners = []
        half = [0.5 * q[c] for c in tiles]
        for shifted in (q_sw, q_nw, q_se, q_ne):
            corners.append([q[c] + 0.5 * shifted[c] for c in tiles])
            corners.append([half[c] + shifted[c] for c in tiles])
        return [e, w, s, n, scale_u, scale_v] + corners

    def relax(part, k, around, right):
        tiles = range(len(part))
        e, w, s, n, scale_u, scale_v, sw_u, sw_v, nw_u, nw_v, se_u, se_v, ne_u, ne_v = k
        u, u_n, u_s, v, v_n, v_s = around
        to_west_u, to_east_u, to_west_v, to_east_v = [], [], [], []
        for c in tiles:
            u4 = 4.0 * u[c]
            to_west_u.append(w[c] * u4 + (sw_u[c] * v_s[c] - nw_u[c] * v_n[c]))
            to_east_u.append(e[c] * u4 + (ne_u[c] * v_n[c] - se_u[c] * v_s[c]))
            to_west_v.append(w[c] * v[c] + (sw_v[c] * u_s[c] - nw_v[c] * u_n[c]))
            to_east_v.append(e[c] * v[c] + (ne_v[c] * u_n[c] - se_v[c] * u_s[c]))
        to_west_u, to_west_v = shift_east(to_west_u), shift_east(to_west_v)
        to_east_u, to_east_v = shift_west(to_east_u), shift_west(to_east_v)
        new_u, new_v = [], []
        for c in tiles:
            mid_u = s[c] * u_s[c] + n[c] * u_n[c]
            mid_v = 4.0 * (s[c] * v_s[c] + n[c] * v_n[c])
            new_u.append(scale_u[c] * (right[0][c] + mid_u + (to_west_u[c] + to_east_u[c])))
            new_v.append(scale_v[c] * (right[1][c] + mid_v + (to_west_v[c] + to_east_v[c])))
        return new_u, new_v

    def put(new, values):
        return [(new, (i,), values[i]) for i in range(2)]

    def keep(k):
        return [(coef, (i,), k[i]) for i in range(FACTORS)]

    def read_sweep(now):
        def read(part, row, count):
            k = [load(coef, part, row, count, i) for i in range(FACTORS)]
            return k, load_around(part, row, count, now), load_right(part, row, count)

        return read

    def sweep(new):
        return lambda part, read: put(new, relax(part, *read))

    def read_first(part, row, count):
        return read_coefficients(part, row, count), load_right(part, row, count)

    def first_start(part, read):
        k = coefficients(part, read[0])
        return keep(k) + put(vel_a, [[a * b for a, b in zip(k[4 + i], read[1][i])] for i in range(2)])

    def read_start(part, row, count):
        return (*read_first(part, row, count), load_around(part, row, count, vel_b))

    def start(part, read):
        k = coefficients(part, read[0])
        return keep(k) + put(vel_a, relax(part, k, read[2], read[1]))

    return SimpleNamespace(**locals())


def setup_kernel(
    fr, ice, woven, own_sides, first_col, second_col,
    ext, vel_b,
    visc, vel_a, coef,
):
    west, east = sides("gx", first_col[...], second_col[...])
    lane = lanes_of(HALF)
    for f, (first, count) in enumerate(STRIP):
        for c in range(2):
            ext[f, MAIN[c] + TOP : MAIN[c] + TOP + TILE, :] = woven[f, c]
        from_east = scale_of(f) * turn(east, first, HALO)
        from_west = scale_of(f) * turn(west, first, 3 * HALO - count)
        own = own_sides[f]
        ext[f, SIDE + TOP : SIDE + TOP + HALF, :] = choose_side(lane, own, from_east, from_west, own)
    step = make_stages(ext, fr, ice, visc, vel_a, vel_b, coef)
    over_rows("tile", step.read_thickness, step.first_viscosity)
    over_rows("tile", step.read_first, step.first_start)
    over_rows("tile", step.read_sweep(vel_a), step.sweep(vel_b))


def model_kernel(
    fr, ice, ext_in, vel_in, first_row, second_row,
    vel_u, vel_v, sums,
    ext, visc, vel_a, vel_b, vel_c, coef, plain, small, sems,
):
    ext[...] = ext_in[...]
    vel_b[...] = vel_in[...]
    north, south = sides("gy", first_row[...], second_row[...])
    here = SIDE + TOP
    for f, (first, count) in enumerate(STRIP):
        for c in range(2):
            rows = slice(64 * c + first, 64 * c + first + count)
            ext[f, MAIN[c] + TOP - count : MAIN[c] + TOP, :] = north[rows]
            ext[f, MAIN[c] + TOP + TILE : MAIN[c] + TOP + TILE + count, :] = south[rows]
        rows = slice(128 + first % 32, 128 + first % 32 + count)
        source = BAND if f >= 2 else 0
        upper = lanes_of(count) < BAND
        above = turn(ext_in[f, here + HALF - count : here + HALF, :], 0, BAND)
        below = turn(ext_in[f, here : here + count, :], 0, BAND)
        ext[f, here - count : here, :] = jnp.where(upper, turn(north[rows], source, 0), above)
        ext[f, here + HALF : here + HALF + count, :] = jnp.where(upper, below, turn(south[rows], source, BAND))

    step = make_stages(ext, fr, ice, visc, vel_a, vel_b, coef)
    over_ends(32, step.read_thickness, step.first_viscosity)
    over_ends(32, step.read_first, step.first_start)
    over_ends(24, step.read_sweep(vel_a), step.sweep(vel_b))

    def iterate(span):
        over_rows(span, step.read_viscosity, step.viscosity)
        over_rows(span, step.read_start, step.start)
        over_rows(span, step.read_sweep(vel_a), step.sweep(vel_b))

    def iteration(i, carry):
        iterate("frame")
        return carry

    lax.fori_loop(1, PIC - 1, iteration, 0)
    join_parts(vel_b, ((0,), (1,)), True)
    iterate("inner")
    join_parts(vel_b, ((0,), (1,)), False)
    lane = lanes_of(TILE)
    copies = []
    for i, out in enumerate((vel_u, vel_v)):
        even, odd = (vel_b[i, tile + TOP : tile + TOP + TILE, :] for tile in MAIN)
        for c in range(2):
            source = BAND * c + lane // 2
            plain[i, c] = jnp.where(lane % 2 == 0, gather(even, source), gather(odd, source))
            copies.append(
                pltpu.make_async_copy(plain.at[i, c], out.at[:, c * LANES : (c + 1) * LANES], sems.at[2 * i + c])
            )
            copies[-1].start()

    load = step.load

    def read_misfit(part, row, count):
        return [
            [load(vel_b, part, row, count, i), load(ext, part, row, count, 3 + i), load(coef, part, row, count, 4 + i)]
            for i in range(2)
        ]

    def first_adjoint(part, read):
        misfit = [[0.5 * (a - b) for a, b in zip(u, seen)] for u, seen, _ in read]
        first = [[a * b for a, b in zip(read[i][2], misfit[i])] for i in range(2)]
        return step.put(vel_c, first) + [(ext, (1 + i,), misfit[i]) for i in range(2)]

    over_rows("inner", read_misfit, first_adjoint)

    def two_sweeps(i, carry):
        over_rows("inner", step.read_sweep(vel_c), step.sweep(vel_a))
        over_rows("inner", step.read_sweep(vel_a), step.sweep(vel_c))
        return carry

    lax.fori_loop(0, (ADJ - 2) // 2, two_sweeps, 0)
    over_rows("tile", step.read_sweep(vel_c), step.sweep(vel_a))

    def read_gradient(part, row, count):
        return [load(ref, part, row, count, i) for ref in (vel_b, vel_a) for i in range(2)] + [load(fr, part, row, count)]

    def gradient(part, read):
        u, v, lu, lv, friction = read
        return [(visc, (0,), [-2.0 * friction[c] * (u[c] * lu[c] + v[c] * lv[c]) for c in range(len(part))])]

    over_rows("tile", read_gradient, gradient)
    join_parts(visc, ((0,),), False)
    down = sum(visc[0, pl.ds(tile + TOP + j, CT, stride=4), :] for tile in MAIN for j in range(4))
    k = lax.broadcasted_iota(jnp.int32, (LANES, LANES), 0)
    total = jnp.dot(
        down,
        (k // 2 == lanes_of(LANES) % CT).astype(jnp.float32),
        precision=lax.Precision.HIGHEST,
        preferred_element_type=jnp.float32,
    )
    small[...] = total
    packed = jnp.where(
        lanes_of(PACK) < CT, small[pl.ds(0, PACK, stride=2), :], small[pl.ds(1, PACK, stride=2), :]
    )
    for j in range(sums.shape[0]):
        sums[j] = packed
    for copy in copies:
        copy.wait()


def pick_kernel(tile_block, gathered, own, other, total):
    owned = own.shape[0]
    row_tile = lax.axis_index("gy")
    core = row_tile % 2
    first = (row_tile - core) * owned
    tile_cols, tile_rows = tile_block.shape
    total[...] = jnp.zeros_like(total)
    for t in range(tile_cols * tile_rows // 2):
        place = tile_block[t // (tile_rows // 2), t % (tile_rows // 2) * 2 + core] - first

        @pl.when((place >= 0) & (place < 2 * owned))
        def _():
            total[place] += gathered[t]

    own[...] = total[pl.ds(core * owned, owned)]
    other[...] = total[pl.ds((1 - core) * owned, owned)]


def join_kernel(own, received, out):
    total = own[...] + received[...]
    for j in range(PACK):
        out[:, j * LANES : (j + 1) * LANES] = total[:, j, :]


def in_vmem(count):
    return [pl.BlockSpec(memory_space=pltpu.VMEM)] * count


def in_smem(count):
    return [pl.BlockSpec(memory_space=pltpu.SMEM)] * count


def per_device(thickness, driving, observed, control, ice_mask, tile_block):
    f32 = jnp.float32
    rows, cols = lax.axis_size("gy"), lax.axis_size("gx")
    tile_block, ice_mask = tile_block[:, :, 0].T, ice_mask.T
    params = pltpu.CompilerParams(vmem_limit_bytes=VMEM_LIMIT)

    def shape(*sizes):
        return jax.ShapeDtypeStruct(sizes, f32)

    def swap(axis, cells_first, cells_second):
        count = lax.axis_size(axis)
        received = []
        for cells, low in ((cells_second, 1), (cells_first, 0)):
            pairs = [(i, i + 1) for i in range(low, count - 1, 2)]
            received.append(lax.ppermute(cells, axis, pairs + [(j, i) for i, j in pairs]))
        return received[1], received[0]

    fields = thickness, driving, observed
    owned = control.shape[0]
    gathered = lax.all_to_all(jnp.broadcast_to(control, (rows, *control.shape)), "gy", 0, 0, tiled=True)
    edges = pl.pallas_call(
        columns_kernel,
        out_shape=[shape(HALF, LANES)] * 2,
        in_specs=in_vmem(3),
        out_specs=in_vmem(2),
        compiler_params=params,
        name="columns",
    )(*fields)
    columns_in = swap("gx", *edges)
    woven, own_sides, strips = pl.pallas_call(
        weave_kernel,
        out_shape=[shape(5, 2, TILE, LANES), shape(5, HALF, LANES), shape(2, 3, 64, LANES)],
        in_specs=in_vmem(3),
        out_specs=in_vmem(3),
        compiler_params=params,
        name="weave",
    )(*fields)
    strips = pl.pallas_call(
        rows_kernel,
        out_shape=[shape(160, LANES)] * 2,
        in_specs=in_vmem(3),
        out_specs=in_vmem(2),
        compiler_params=params,
        name="rows",
    )(strips, *columns_in)
    rows_in = swap("gy", *strips)
    friction = pl.pallas_call(
        friction_kernel,
        out_shape=[shape(ALL_ROWS, LANES)] * 2,
        in_specs=in_smem(2) + in_vmem(1),
        out_specs=in_vmem(2),
        scratch_shapes=[pltpu.VMEM((3, PACK, LANES), f32), pltpu.VMEM((PATCH, LANES), f32)],
        compiler_params=params,
        name="friction",
    )(tile_block, ice_mask, gathered)
    prepared = pl.pallas_call(
        setup_kernel,
        out_shape=[shape(5, ALL_ROWS, LANES), shape(2, ALL_ROWS, LANES)],
        in_specs=in_vmem(6),
        out_specs=in_vmem(2),
        scratch_shapes=[
            pltpu.VMEM((3, ALL_ROWS, LANES), f32),
            pltpu.VMEM((2, ALL_ROWS, LANES), f32),
            pltpu.VMEM((FACTORS, ALL_ROWS, LANES), f32),
        ],
        compiler_params=params,
        name="setup",
    )(*friction, woven, own_sides, *columns_in)

    vel_u, vel_v, sums = pl.pallas_call(
        model_kernel,
        out_shape=(shape(TILE, TILE), shape(TILE, TILE), shape(cols * rows // 2, PACK, LANES)),
        in_specs=in_vmem(6),
        out_specs=[pl.BlockSpec(memory_space=pltpu.HBM)] * 2 + in_vmem(1),
        scratch_shapes=[
            pltpu.VMEM((5, ALL_ROWS, LANES), f32),
            pltpu.VMEM((3, ALL_ROWS, LANES), f32),
            pltpu.VMEM((2, ALL_ROWS, LANES), f32),
            pltpu.VMEM((2, ALL_ROWS, LANES), f32),
            pltpu.VMEM((2, ALL_ROWS, LANES), f32),
            pltpu.VMEM((FACTORS, ALL_ROWS, LANES), f32),
            pltpu.VMEM((2, 2, TILE, LANES), f32),
            pltpu.VMEM((CT, LANES), f32),
            pltpu.SemaphoreType.DMA((4,)),
        ],
        compiler_params=params,
        name="model",
    )(*friction, *prepared, *rows_in)

    same_core = [[i * rows + j for i in range(cols) for j in range(core, rows, 2)] for core in range(2)]
    sums = lax.all_to_all(sums, ("gx", "gy"), 0, 0, tiled=True, axis_index_groups=same_core)
    own, other = pl.pallas_call(
        pick_kernel,
        out_shape=[shape(owned, PACK, LANES)] * 2,
        in_specs=in_smem(1) + in_vmem(1),
        out_specs=in_vmem(2),
        scratch_shapes=[pltpu.VMEM((2 * owned, PACK, LANES), f32)],
        compiler_params=params,
        name="pick",
    )(tile_block, sums)
    received = lax.ppermute(other, "gy", [(j, j ^ 1) for j in range(rows)])
    gradient = pl.pallas_call(
        join_kernel,
        out_shape=shape(*control.shape),
        in_specs=in_vmem(2),
        out_specs=pl.BlockSpec(memory_space=pltpu.VMEM),
        compiler_params=params,
        name="join",
    )(own, received)
    return vel_u, vel_v, gradient


def solution(mesh):
    return jax.shard_map(
        per_device,
        mesh=mesh,
        in_specs=(P("gy", "gx"), P(None, "gy", "gx"), P(None, "gy", "gx"), P("gy", None), P(), P()),
        out_specs=(P("gy", "gx"), P("gy", "gx"), P("gy", None)),
        check_vma=False,
    )
```

```python
from types import SimpleNamespace

import jax
import jax.numpy as jnp
from jax import lax
from jax.experimental import pallas as pl
from jax.experimental.pallas import tpu as pltpu
from jax.sharding import PartitionSpec as P

TILE = 256
PIC = 4
SW = 2
ADJ = 6
CT = 64
COARSE = 4096

LANES = 128
HALO = 16
OBS = 8
MARGIN = 8
TOP = MARGIN + HALO
ROWS = TILE + 2 * TOP
HALF = TILE // 2
SIDE = 2 * ROWS
BAND = LANES // 2
ALL_ROWS = SIDE + HALF + 2 * TOP
MAIN = (0, ROWS)
SIDES = (SIDE,)
SPANS = {
    "frame": (MARGIN, 4, 72, MARGIN, 40, 0, 0),
    "inner": (MARGIN + 8, 3, 72, MARGIN + 8, 40, 56, 24),
    "tile": (TOP, 4, 64, TOP, 32, 0, 0),
}
FACTORS = 14
AHEAD = 5
PACK = COARSE // LANES
VMEM_LIMIT = 24 * 1024 * 1024
PACK_VMEM_LIMIT = 62 * 1024 * 1024

STRIP = ((0, HALO), (HALO, HALO), (2 * HALO, HALO), (3 * HALO, OBS), (3 * HALO + OBS, OBS))

PATCH_ROWS = ((-1, PACK - 2, 2, 0), (0, 0, PACK, 4), (1, 0, 2, CT + 4))
PATCH = CT + 8

visc_scale = 0.1
strain_floor = 0.05


def lanes_of(rows):
    return lax.broadcasted_iota(jnp.int32, (rows, LANES), 1)


def is_even(axis):
    return lax.axis_index(axis) % 2 == 0


def pack_kernel(control, thick, drive, obs, first_col, second_col, spread, held, packed, field_sems, sems):
    results = [pltpu.make_async_copy(control, spread.at[j], sems.at[2 + j]) for j in range(spread.shape[0])]
    fields = (thick, drive.at[0], drive.at[1], obs.at[0], obs.at[1])
    copies = [pltpu.make_async_copy(field, held.at[f], field_sems.at[f]) for f, field in enumerate(fields)]
    for copy in copies + results:
        copy.start()
    lane = lanes_of(HALF)
    left = jnp.zeros((HALF, LANES), jnp.float32)
    right = jnp.zeros((HALF, LANES), jnp.float32)
    for f, (first, count) in enumerate(STRIP):
        copies[f].wait()
        for part in range(2):
            rows = slice(part * HALF, (part + 1) * HALF)
            start = part * BAND + first
            inside = (lane >= start) & (lane < start + count)
            left = jnp.where(inside, turn(held[f, rows, :LANES], 0, start), left)
            right = jnp.where(inside, turn(held[f, rows, LANES:], LANES - count, start), right)
    even = is_even("gx")
    packed[0] = jnp.where(even, right, left)
    packed[1] = jnp.where(even, left, right)
    for i, out in enumerate((first_col, second_col)):
        results.append(pltpu.make_async_copy(packed.at[i], out, sems.at[i]))
        results[-1].start()
    for copy in results:
        copy.wait()


def sides(axis, first_pair, second_pair):
    even = is_even(axis)
    return jnp.where(even, second_pair, first_pair), jnp.where(even, first_pair, second_pair)


def choose_side(lane, high, east, west, low):
    place = lane % BAND
    return jnp.where(
        place < HALO, high, jnp.where(place < 2 * HALO, east, jnp.where(place < 3 * HALO, west, low))
    )


def turn(cells, source, target):
    shift = (target - source) % LANES
    return pltpu.roll(cells, shift, 1) if shift else cells


def gather(cells, source):
    return jnp.take_along_axis(cells, source, axis=1)


def scale_of(f):
    return 0.5 if f in (1, 2) else 1.0


def weave_kernel(thick, drive, obs, woven, own_sides, edges):
    lane, half_lane = lanes_of(TILE), lanes_of(HALF)
    source = 2 * lane % LANES
    for f, (field, (first, count)) in enumerate(zip((thick, drive.at[0], drive.at[1], obs.at[0], obs.at[1]), STRIP)):
        low, high = scale_of(f) * field[:, :LANES], scale_of(f) * field[:, LANES:]
        tiles = [jnp.where(lane < BAND, gather(low, source + i), gather(high, source + i)) for i in range(2)]
        bands = []
        for band in (0, BAND):
            bands.append(
                jnp.where(lane % BAND < BAND // 2, turn(high, LANES - HALO, band), turn(low, 0, band + 3 * HALO))
            )
        own_sides[f] = jnp.where(half_lane < BAND, bands[0][:HALF], bands[1][HALF:])
        for c in range(2):
            woven[f, c] = tiles[c]
        for c, tile in enumerate(tiles + [bands[0]]):
            edges[0, c, first : first + count, :] = tile[:count]
            edges[1, c, first : first + count, :] = tile[TILE - count :]


def rows_kernel(edges, first_col, second_col, first_pair, second_pair):
    west, east = sides("gx", first_col[...], second_col[...])
    even = is_even("gy")
    for c in range(2):
        top, bottom = edges[0, c], edges[1, c]
        first_pair[64 * c : 64 * c + 64, :] = jnp.where(even, bottom, top)
        second_pair[64 * c : 64 * c + 64, :] = jnp.where(even, top, bottom)
    strips = []
    for i in range(2):
        fields = []
        for f, (first, count) in enumerate(STRIP):
            packed = slice(HALF - count, HALF) if i else slice(0, count)
            source = BAND * i + first
            target = BAND if f >= 2 else 0
            own = turn(edges[i, 2, first : first + count, :], 0, target)
            from_east = scale_of(f) * turn(east[packed], source, target + HALO)
            from_west = scale_of(f) * turn(west[packed], source, target + 3 * HALO - count)
            fields.append(choose_side(lanes_of(count), own, from_east, from_west, own))
        lane = lanes_of(HALO)
        lower = jnp.concatenate(fields[3:], axis=0)
        strips.append((jnp.where(lane < BAND, fields[0], fields[2]), jnp.where(lane < BAND, fields[1], lower)))
    for k in range(2):
        top, bottom = strips[0][k], strips[1][k]
        rows = slice(128 + HALO * k, 128 + HALO * (k + 1))
        first_pair[rows, :] = jnp.where(even, bottom, top)
        second_pair[rows, :] = jnp.where(even, top, bottom)


def shift_east(tiles):
    turned = pltpu.roll(tiles[0], LANES - 1, 1)
    return [turned] if len(tiles) == 1 else [tiles[1], turned]


def shift_west(tiles):
    turned = pltpu.roll(tiles[-1], 1, 1)
    return [turned] if len(tiles) == 1 else [turned, tiles[0]]


def run_groups(groups, read, work):
    pending = [read(*group) for group in groups[:AHEAD]]
    for k, (part, row, count) in enumerate(groups):
        if k + AHEAD < len(groups):
            pending.append(read(*groups[k + AHEAD]))
        for ref, lead, values in work(part, pending[k]):
            for tile, value in zip(part, values):
                ref[(*lead, pl.ds(row + tile, count), slice(None))] = value


def block_groups(row, main, side_row, side):
    step = 32 if main % 32 == 0 else 24
    first = side // 16 * 8 if side > 24 else side
    groups = [(MAIN, row + g, min(step, main - g)) for g in range(0, main, step)]
    groups[1:1] = [(SIDES, side_row, first)]
    if first < side:
        groups[3:3] = [(SIDES, side_row + first, side - first)]
    return groups


def over_rows(span, read, work):
    start, blocks, main, side_start, side, main_rest, side_rest = SPANS[span]

    def block(i, carry):
        row, side_row = pl.multiple_of(start + i * main, 8), pl.multiple_of(side_start + i * side, 8)
        run_groups(block_groups(row, main, side_row, side), read, work)
        return carry

    lax.fori_loop(0, blocks, block, 0)
    if main_rest:
        none = 8 * jnp.minimum(lax.axis_index("gx"), 0)
        row = pl.multiple_of(none + start + blocks * main, 8)
        side_row = pl.multiple_of(none + side_start + blocks * side, 8)
        run_groups(block_groups(row, main_rest, side_row, side_rest), read, work)


def over_ends(count, read, work):
    def block(i, carry):
        row = pl.multiple_of(MARGIN + i * (TILE + 2 * HALO - count), 8)
        side_row = pl.multiple_of(MARGIN + i * (HALF + 2 * HALO - count), 8)
        run_groups([(MAIN, row, count), (SIDES, side_row, count)], read, work)
        return carry

    lax.fori_loop(0, 2, block, 0)


def join_parts(ref, leads, whole):
    edge = HALO // 2

    def join(row, upper, lower, count):
        lane = lanes_of(count)
        place = lane % BAND
        for lead in leads:
            def at(tile_row):
                return (*lead, pl.ds(tile_row, count), slice(None))

            mixed = ref[at(SIDE + row)]
            if whole:
                source = jnp.where(place < edge, LANES - edge + place // 2, place // 2 - 24)
                source = jnp.clip(source, 0, LANES - 1)
                halves = []
                for main_row in (row, row + HALF):
                    even, odd = (gather(ref[at(tile + main_row)], source) for tile in MAIN)
                    halves.append(jnp.where(lane % 2 == 0, even, odd))
                outer = (place < edge) | (place >= BAND - edge)
                ref[at(SIDE + row)] = jnp.where(outer, jnp.where(lane < BAND, halves[0], halves[1]), mixed)
            for wanted, band, main_row in ((upper, 0, row), (lower, BAND, row + HALF)):
                if wanted:
                    few = edge // 2
                    source = band + jnp.where(lane < few, 3 * HALO + 2 * lane, edge + 2 * (lane - LANES + few))
                    source = jnp.clip(source, 0, LANES - 2)
                    outer = (lane < few) | (lane >= LANES - few)
                    for c, tile in enumerate(MAIN):
                        ref[at(tile + main_row)] = jnp.where(outer, gather(mixed, source + c), ref[at(tile + main_row)])

    step = 32

    def middle(i, carry):
        join(pl.multiple_of(TOP + i * step, 8), True, True, step)
        return carry

    lax.fori_loop(0, HALF // step, middle, 0)
    if whole:
        join(MARGIN, True, False, HALO)
        join(TOP + HALF, False, True, HALO)


def friction_kernel(tile_block, ice_mask, control, fr, ice, blocks, patch):
    tile_cols, tile_rows = ice_mask.shape
    row_tile = lax.axis_index("gy")
    col_tile = lax.axis_index("gx")

    owned = control.shape[1]
    owner_row = lax.broadcasted_iota(jnp.int32, (owned, LANES), 0)
    for dr, first, count, at in PATCH_ROWS:
        for ds in (-1, 0, 1):
            row = jnp.clip(row_tile + dr, 0, tile_rows - 1)
            col = jnp.clip(col_tile + ds, 0, tile_cols - 1)
            block = tile_block[col, row]
            holder = block // owned
            here = owner_row == block - holder * owned
            for j in range(first, first + count):
                held = control[holder, :, j * LANES : (j + 1) * LANES]
                blocks[ds + 1, j : j + 1, :] = jnp.sum(jnp.where(here, held, 0.0), axis=0, keepdims=True)
        west, mid, east = (blocks[k, first : first + count, :] for k in range(3))
        lane = lanes_of(count)
        even = jnp.where(lane < CT, mid, jnp.where(lane < 96, turn(east, 0, CT), turn(west, 0, CT)))
        odd = jnp.where(lane < CT, turn(mid, 0, CT), jnp.where(lane < 96, east, west))
        patch[pl.ds(at, count, stride=2), :] = even
        patch[pl.ds(at + 1, count, stride=2), :] = odd

    cells = 0.5 * jnp.exp(patch[...])
    lane = lanes_of(PATCH)
    wide = gather(cells, lane // 2)
    for tile in MAIN:
        for j in range(4):
            fr[pl.ds(tile + MARGIN + j, PATCH, stride=4), :] = wide
    lane = lanes_of(40)
    place = lane % BAND // 4
    source = jnp.where(place < 8, 60 + place, (116 + place) % LANES)
    wide = jnp.where(
        lane < BAND,
        gather(cells[:40], source),
        gather(cells[PATCH - 40 :], source),
    )
    for j in range(4):
        fr[pl.ds(SIDE + MARGIN + j, 40, stride=4), :] = wide

    side_ice = []
    for dr, first, count in ((-1, MARGIN, HALO), (0, TOP, TILE), (1, TOP + TILE, HALO)):
        masks = []
        for ds in (-1, 0, 1):
            row, col = row_tile + dr, col_tile + ds
            inside = (row >= 0) & (row < tile_rows) & (col >= 0) & (col < tile_cols)
            row = jnp.clip(row, 0, tile_rows - 1)
            col = jnp.clip(col, 0, tile_cols - 1)
            masks.append(jnp.where(inside, ice_mask[col, row], 0).astype(jnp.float32))
        for c in range(2):
            ice[MAIN[c] + first : MAIN[c] + first + count, :] = jnp.full((count, LANES), masks[1])
        side_ice.append(choose_side(lanes_of(HALO), masks[1], masks[2], masks[0], masks[1]))
    upper = lanes_of(HALO) < BAND
    for i in range(HALF // HALO):
        ice[SIDE + TOP + i * HALO : SIDE + TOP + (i + 1) * HALO, :] = side_ice[1]
    ice[SIDE + MARGIN : SIDE + TOP, :] = jnp.where(upper, side_ice[0], side_ice[1])
    ice[SIDE + TOP + HALF : SIDE + TOP + HALF + HALO, :] = jnp.where(upper, side_ice[1], side_ice[2])


def make_stages(ext, fr, ice, visc, vel_a, vel_b, coef):
    def load(ref, part, row, count, *lead):
        return [ref[(*lead, pl.ds(row + tile, count), slice(None))] for tile in part]

    def load_around(part, row, count, now):
        return [load(now, part, r, count, i) for i in range(2) for r in (row, row - 1, row + 1)]

    def load_right(part, row, count):
        return [load(ext, part, row, count, i) for i in (1, 2)]

    def read_thickness(part, row, count):
        return load(ext, part, row, count, 0)

    def keep_viscosity(q):
        return [(visc, (0,), q), (visc, (1,), shift_west(q)), (visc, (2,), shift_east(q))]

    def first_viscosity(part, thickness):
        factor = 0.25 * visc_scale * strain_floor ** (-1.0 / 3.0)
        return keep_viscosity([factor * t for t in thickness])

    def read_viscosity(part, row, count):
        return read_thickness(part, row, count), load_around(part, row, count, vel_b)

    def viscosity(part, read):
        thickness, (u, u_n, u_s, v, v_n, v_s) = read
        u_e, u_w = shift_east(u), shift_west(u)
        v_e, v_w = shift_east(v), shift_west(v)
        result = []
        for c in range(len(part)):
            ux, vx = u_e[c] - u_w[c], v_e[c] - v_w[c]
            uy, vy = u_s[c] - u_n[c], v_s[c] - v_n[c]
            shear = uy + vx
            strain = 0.25 * (ux * (ux + vy) + vy * vy) + (0.0625 * (shear * shear) + strain_floor)
            result.append((0.25 * visc_scale) * thickness[c] * jnp.exp(jnp.log(strain) * (-1.0 / 3.0)))
        return keep_viscosity(result)

    def inverse(x):
        near = pl.reciprocal(x, approx=True)
        return near * (2.0 - x * near)

    def read_coefficients(part, row, count):
        around = [load(visc, part, r, count, i) for i in range(3) for r in (row, row - 1, row + 1)]
        return around + [load(fr, part, row, count), load(ice, part, row, count)]

    def coefficients(part, read):
        tiles = range(len(part))
        q, q_n, q_s, q_w, q_nw, q_sw, q_e, q_ne, q_se, friction, mask = read
        w = [q[c] + q_w[c] for c in tiles]
        e = [q[c] + q_e[c] for c in tiles]
        s = [q[c] + q_s[c] for c in tiles]
        n = [q[c] + q_n[c] for c in tiles]
        scale_u, scale_v = [], []
        for c in tiles:
            across, along = e[c] + w[c], s[c] + n[c]
            scale_u.append(mask[c] * inverse(friction[c] + along + 4.0 * across))
            scale_v.append(mask[c] * inverse(friction[c] + across + 4.0 * along))
        corners = []
        half = [0.5 * q[c] for c in tiles]
        for shifted in (q_sw, q_nw, q_se, q_ne):
            corners.append([q[c] + 0.5 * shifted[c] for c in tiles])
            corners.append([half[c] + shifted[c] for c in tiles])
        return [e, w, s, n, scale_u, scale_v] + corners

    def relax(part, k, around, right):
        tiles = range(len(part))
        e, w, s, n, scale_u, scale_v, sw_u, sw_v, nw_u, nw_v, se_u, se_v, ne_u, ne_v = k
        u, u_n, u_s, v, v_n, v_s = around
        to_west_u, to_east_u, to_west_v, to_east_v = [], [], [], []
        for c in tiles:
            u4 = 4.0 * u[c]
            to_west_u.append(w[c] * u4 + (sw_u[c] * v_s[c] - nw_u[c] * v_n[c]))
            to_east_u.append(e[c] * u4 + (ne_u[c] * v_n[c] - se_u[c] * v_s[c]))
            to_west_v.append(w[c] * v[c] + (sw_v[c] * u_s[c] - nw_v[c] * u_n[c]))
            to_east_v.append(e[c] * v[c] + (ne_v[c] * u_n[c] - se_v[c] * u_s[c]))
        to_west_u, to_west_v = shift_east(to_west_u), shift_east(to_west_v)
        to_east_u, to_east_v = shift_west(to_east_u), shift_west(to_east_v)
        new_u, new_v = [], []
        for c in tiles:
            mid_u = s[c] * u_s[c] + n[c] * u_n[c]
            mid_v = 4.0 * (s[c] * v_s[c] + n[c] * v_n[c])
            new_u.append(scale_u[c] * (right[0][c] + mid_u + (to_west_u[c] + to_east_u[c])))
            new_v.append(scale_v[c] * (right[1][c] + mid_v + (to_west_v[c] + to_east_v[c])))
        return new_u, new_v

    def put(new, values):
        return [(new, (i,), values[i]) for i in range(2)]

    def keep(k):
        return [(coef, (i,), k[i]) for i in range(FACTORS)]

    def read_sweep(now):
        def read(part, row, count):
            k = [load(coef, part, row, count, i) for i in range(FACTORS)]
            return k, load_around(part, row, count, now), load_right(part, row, count)

        return read

    def sweep(new):
        return lambda part, read: put(new, relax(part, *read))

    def read_first(part, row, count):
        return read_coefficients(part, row, count), load_right(part, row, count)

    def first_start(part, read):
        k = coefficients(part, read[0])
        return keep(k) + put(vel_a, [[a * b for a, b in zip(k[4 + i], read[1][i])] for i in range(2)])

    def read_start(part, row, count):
        return (*read_first(part, row, count), load_around(part, row, count, vel_b))

    def start(part, read):
        k = coefficients(part, read[0])
        return keep(k) + put(vel_a, relax(part, k, read[2], read[1]))

    return SimpleNamespace(**locals())


def setup_kernel(
    fr, ice, woven, own_sides, first_col, second_col,
    ext, vel_b,
    visc, vel_a, coef,
):
    west, east = sides("gx", first_col[...], second_col[...])
    lane = lanes_of(HALF)
    for f, (first, count) in enumerate(STRIP):
        for c in range(2):
            ext[f, MAIN[c] + TOP : MAIN[c] + TOP + TILE, :] = woven[f, c]
        from_east = scale_of(f) * turn(east, first, HALO)
        from_west = scale_of(f) * turn(west, first, 3 * HALO - count)
        own = own_sides[f]
        ext[f, SIDE + TOP : SIDE + TOP + HALF, :] = choose_side(lane, own, from_east, from_west, own)
    step = make_stages(ext, fr, ice, visc, vel_a, vel_b, coef)
    over_rows("tile", step.read_thickness, step.first_viscosity)
    over_rows("tile", step.read_first, step.first_start)
    over_rows("tile", step.read_sweep(vel_a), step.sweep(vel_b))


def model_kernel(
    fr, ice, ext_in, vel_in, first_row, second_row,
    vel_u, vel_v, sums,
    ext, visc, vel_a, vel_b, vel_c, coef, plain, small, sems,
):
    ext[...] = ext_in[...]
    vel_b[...] = vel_in[...]
    north, south = sides("gy", first_row[...], second_row[...])
    here = SIDE + TOP
    for f, (first, count) in enumerate(STRIP):
        for c in range(2):
            rows = slice(64 * c + first, 64 * c + first + count)
            ext[f, MAIN[c] + TOP - count : MAIN[c] + TOP, :] = north[rows]
            ext[f, MAIN[c] + TOP + TILE : MAIN[c] + TOP + TILE + count, :] = south[rows]
        rows = slice(128 + first % 32, 128 + first % 32 + count)
        source = BAND if f >= 2 else 0
        upper = lanes_of(count) < BAND
        above = turn(ext_in[f, here + HALF - count : here + HALF, :], 0, BAND)
        below = turn(ext_in[f, here : here + count, :], 0, BAND)
        ext[f, here - count : here, :] = jnp.where(upper, turn(north[rows], source, 0), above)
        ext[f, here + HALF : here + HALF + count, :] = jnp.where(upper, below, turn(south[rows], source, BAND))

    step = make_stages(ext, fr, ice, visc, vel_a, vel_b, coef)
    over_ends(32, step.read_thickness, step.first_viscosity)
    over_ends(32, step.read_first, step.first_start)
    over_ends(24, step.read_sweep(vel_a), step.sweep(vel_b))

    def iterate(span):
        over_rows(span, step.read_viscosity, step.viscosity)
        over_rows(span, step.read_start, step.start)
        over_rows(span, step.read_sweep(vel_a), step.sweep(vel_b))

    def iteration(i, carry):
        iterate("frame")
        return carry

    lax.fori_loop(1, PIC - 1, iteration, 0)
    join_parts(vel_b, ((0,), (1,)), True)
    iterate("inner")
    join_parts(vel_b, ((0,), (1,)), False)
    lane = lanes_of(TILE)
    copies = []
    for i, out in enumerate((vel_u, vel_v)):
        even, odd = (vel_b[i, tile + TOP : tile + TOP + TILE, :] for tile in MAIN)
        for c in range(2):
            source = BAND * c + lane // 2
            plain[i, c] = jnp.where(lane % 2 == 0, gather(even, source), gather(odd, source))
            copies.append(
                pltpu.make_async_copy(plain.at[i, c], out.at[:, c * LANES : (c + 1) * LANES], sems.at[2 * i + c])
            )
            copies[-1].start()

    load = step.load

    def read_misfit(part, row, count):
        return [
            [load(vel_b, part, row, count, i), load(ext, part, row, count, 3 + i), load(coef, part, row, count, 4 + i)]
            for i in range(2)
        ]

    def first_adjoint(part, read):
        misfit = [[0.5 * (a - b) for a, b in zip(u, seen)] for u, seen, _ in read]
        first = [[a * b for a, b in zip(read[i][2], misfit[i])] for i in range(2)]
        return step.put(vel_c, first) + [(ext, (1 + i,), misfit[i]) for i in range(2)]

    over_rows("inner", read_misfit, first_adjoint)

    def two_sweeps(i, carry):
        over_rows("inner", step.read_sweep(vel_c), step.sweep(vel_a))
        over_rows("inner", step.read_sweep(vel_a), step.sweep(vel_c))
        return carry

    lax.fori_loop(0, (ADJ - 2) // 2, two_sweeps, 0)
    over_rows("tile", step.read_sweep(vel_c), step.sweep(vel_a))

    def read_gradient(part, row, count):
        return [load(ref, part, row, count, i) for ref in (vel_b, vel_a) for i in range(2)] + [load(fr, part, row, count)]

    def gradient(part, read):
        u, v, lu, lv, friction = read
        return [(visc, (0,), [-2.0 * friction[c] * (u[c] * lu[c] + v[c] * lv[c]) for c in range(len(part))])]

    over_rows("tile", read_gradient, gradient)
    join_parts(visc, ((0,),), False)
    down = sum(visc[0, pl.ds(tile + TOP + j, CT, stride=4), :] for tile in MAIN for j in range(4))
    k = lax.broadcasted_iota(jnp.int32, (LANES, LANES), 0)
    total = jnp.dot(
        down,
        (k // 2 == lanes_of(LANES) % CT).astype(jnp.float32),
        precision=lax.Precision.HIGHEST,
        preferred_element_type=jnp.float32,
    )
    small[...] = total
    packed = jnp.where(
        lanes_of(PACK) < CT, small[pl.ds(0, PACK, stride=2), :], small[pl.ds(1, PACK, stride=2), :]
    )
    for j in range(sums.shape[0]):
        sums[j] = packed
    for copy in copies:
        copy.wait()


def pick_kernel(tile_block, gathered, own, other, total):
    owned = own.shape[0]
    row_tile = lax.axis_index("gy")
    core = row_tile % 2
    first = (row_tile - core) * owned
    tile_cols, tile_rows = tile_block.shape
    total[...] = jnp.zeros_like(total)
    for t in range(tile_cols * tile_rows // 2):
        place = tile_block[t // (tile_rows // 2), t % (tile_rows // 2) * 2 + core] - first

        @pl.when((place >= 0) & (place < 2 * owned))
        def _():
            total[place] += gathered[t]

    own[...] = total[pl.ds(core * owned, owned)]
    other[...] = total[pl.ds((1 - core) * owned, owned)]


def join_kernel(own, received, out):
    total = own[...] + received[...]
    for j in range(PACK):
        out[:, j * LANES : (j + 1) * LANES] = total[:, j, :]


def in_vmem(count):
    return [pl.BlockSpec(memory_space=pltpu.VMEM)] * count


def in_smem(count):
    return [pl.BlockSpec(memory_space=pltpu.SMEM)] * count


def per_device(thickness, driving, observed, control, ice_mask, tile_block):
    f32 = jnp.float32
    rows, cols = lax.axis_size("gy"), lax.axis_size("gx")
    tile_block, ice_mask = tile_block[:, :, 0].T, ice_mask.T
    params = pltpu.CompilerParams(vmem_limit_bytes=VMEM_LIMIT)

    def shape(*sizes):
        return jax.ShapeDtypeStruct(sizes, f32)

    def swap(axis, cells_first, cells_second):
        count = lax.axis_size(axis)
        received = []
        for cells, low in ((cells_second, 1), (cells_first, 0)):
            pairs = [(i, i + 1) for i in range(low, count - 1, 2)]
            received.append(lax.ppermute(cells, axis, pairs + [(j, i) for i, j in pairs]))
        return received[1], received[0]

    fields = thickness, driving, observed
    owned = control.shape[0]
    *edges, spread = pl.pallas_call(
        pack_kernel,
        out_shape=[shape(HALF, LANES)] * 2 + [shape(rows, *control.shape)],
        in_specs=[pl.BlockSpec(memory_space=pltpu.HBM)] * 4,
        out_specs=[pl.BlockSpec(memory_space=pltpu.HBM)] * 3,
        scratch_shapes=[
            pltpu.VMEM((5, TILE, TILE), f32),
            pltpu.VMEM((2, HALF, LANES), f32),
            pltpu.SemaphoreType.DMA((5,)),
            pltpu.SemaphoreType.DMA((2 + rows,)),
        ],
        compiler_params=pltpu.CompilerParams(vmem_limit_bytes=PACK_VMEM_LIMIT),
        name="pack",
    )(control, *fields)
    gathered = lax.all_to_all(spread, "gy", 0, 0, tiled=True)
    columns_in = swap("gx", *edges)
    woven, own_sides, strips = pl.pallas_call(
        weave_kernel,
        out_shape=[shape(5, 2, TILE, LANES), shape(5, HALF, LANES), shape(2, 3, 64, LANES)],
        in_specs=in_vmem(3),
        out_specs=in_vmem(3),
        compiler_params=params,
        name="weave",
    )(*fields)
    strips = pl.pallas_call(
        rows_kernel,
        out_shape=[shape(160, LANES)] * 2,
        in_specs=in_vmem(3),
        out_specs=in_vmem(2),
        compiler_params=params,
        name="rows",
    )(strips, *columns_in)
    rows_in = swap("gy", *strips)
    friction = pl.pallas_call(
        friction_kernel,
        out_shape=[shape(ALL_ROWS, LANES)] * 2,
        in_specs=in_smem(2) + in_vmem(1),
        out_specs=in_vmem(2),
        scratch_shapes=[pltpu.VMEM((3, PACK, LANES), f32), pltpu.VMEM((PATCH, LANES), f32)],
        compiler_params=params,
        name="friction",
    )(tile_block, ice_mask, gathered)
    prepared = pl.pallas_call(
        setup_kernel,
        out_shape=[shape(5, ALL_ROWS, LANES), shape(2, ALL_ROWS, LANES)],
        in_specs=in_vmem(6),
        out_specs=in_vmem(2),
        scratch_shapes=[
            pltpu.VMEM((3, ALL_ROWS, LANES), f32),
            pltpu.VMEM((2, ALL_ROWS, LANES), f32),
            pltpu.VMEM((FACTORS, ALL_ROWS, LANES), f32),
        ],
        compiler_params=params,
        name="setup",
    )(*friction, woven, own_sides, *columns_in)

    vel_u, vel_v, sums = pl.pallas_call(
        model_kernel,
        out_shape=(shape(TILE, TILE), shape(TILE, TILE), shape(cols * rows // 2, PACK, LANES)),
        in_specs=in_vmem(6),
        out_specs=[pl.BlockSpec(memory_space=pltpu.HBM)] * 2 + in_vmem(1),
        scratch_shapes=[
            pltpu.VMEM((5, ALL_ROWS, LANES), f32),
            pltpu.VMEM((3, ALL_ROWS, LANES), f32),
            pltpu.VMEM((2, ALL_ROWS, LANES), f32),
            pltpu.VMEM((2, ALL_ROWS, LANES), f32),
            pltpu.VMEM((2, ALL_ROWS, LANES), f32),
            pltpu.VMEM((FACTORS, ALL_ROWS, LANES), f32),
            pltpu.VMEM((2, 2, TILE, LANES), f32),
            pltpu.VMEM((CT, LANES), f32),
            pltpu.SemaphoreType.DMA((4,)),
        ],
        compiler_params=params,
        name="model",
    )(*friction, *prepared, *rows_in)

    same_core = [[i * rows + j for i in range(cols) for j in range(core, rows, 2)] for core in range(2)]
    sums = lax.all_to_all(sums, ("gx", "gy"), 0, 0, tiled=True, axis_index_groups=same_core)
    own, other = pl.pallas_call(
        pick_kernel,
        out_shape=[shape(owned, PACK, LANES)] * 2,
        in_specs=in_smem(1) + in_vmem(1),
        out_specs=in_vmem(2),
        scratch_shapes=[pltpu.VMEM((2 * owned, PACK, LANES), f32)],
        compiler_params=params,
        name="pick",
    )(tile_block, sums)
    received = lax.ppermute(other, "gy", [(j, j ^ 1) for j in range(rows)])
    gradient = pl.pallas_call(
        join_kernel,
        out_shape=shape(*control.shape),
        in_specs=in_vmem(2),
        out_specs=pl.BlockSpec(memory_space=pltpu.VMEM),
        compiler_params=params,
        name="join",
    )(own, received)
    return vel_u, vel_v, gradient


def solution(mesh):
    return jax.shard_map(
        per_device,
        mesh=mesh,
        in_specs=(P("gy", "gx"), P(None, "gy", "gx"), P(None, "gy", "gx"), P("gy", None), P(), P()),
        out_specs=(P("gy", "gx"), P("gy", "gx"), P("gy", None)),
        check_vma=False,
    )
```

```python
from types import SimpleNamespace

import jax
import jax.numpy as jnp
from jax import lax
from jax.experimental import pallas as pl
from jax.experimental.pallas import tpu as pltpu
from jax.sharding import PartitionSpec as P

TILE = 256
PIC = 4
SW = 2
ADJ = 6
CT = 64
COARSE = 4096

LANES = 128
HALO = 16
OBS = 8
MARGIN = 8
TOP = MARGIN + HALO
ROWS = TILE + 2 * TOP
HALF = TILE // 2
SIDE = 2 * ROWS
BAND = LANES // 2
ALL_ROWS = SIDE + HALF + 2 * TOP
MAIN = (0, ROWS)
SIDES = (SIDE,)
SPANS = {
    "frame": (MARGIN, 4, 72, MARGIN, 40, 0, 0),
    "inner": (MARGIN + 8, 3, 72, MARGIN + 8, 40, 56, 24),
    "tile": (TOP, 4, 64, TOP, 32, 0, 0),
}
FACTORS = 14
AHEAD = 5
PACK = COARSE // LANES
VMEM_LIMIT = 24 * 1024 * 1024
PACK_VMEM_LIMIT = 62 * 1024 * 1024

STRIP = ((0, HALO), (HALO, HALO), (2 * HALO, HALO), (3 * HALO, OBS), (3 * HALO + OBS, OBS))

CONTROL = ((0, 0, PACK, 0), (-1, PACK - 2, 2, PACK), (1, 0, 2, PACK + 2))
FOLDED = 40
PARCEL = 48
PATCH = CT + 8

visc_scale = 0.1
strain_floor = 0.05


def lanes_of(rows):
    return lax.broadcasted_iota(jnp.int32, (rows, LANES), 1)


def is_even(axis):
    return lax.axis_index(axis) % 2 == 0


def side_lanes(rows, ds, group):
    place = (lanes_of(rows) - 8 * group) % CT
    return place < 4 if ds > 0 else place >= CT - 4


def fill_parcels(tile_block, owned_blocks, parcels):
    tile_cols, tile_rows = tile_block.shape
    owned = owned_blocks.shape[0]
    mine = lax.axis_index("gy") * owned
    col_tile = lax.axis_index("gx")

    def spread(row, carry):
        for ds in (-1, 0, 1):
            col = col_tile + ds
            place = tile_block[jnp.clip(col, 0, tile_cols - 1), row] - mine

            @pl.when((col >= 0) & (col < tile_cols) & (place >= 0) & (place < owned))
            def _():
                for dr, first, count, at in CONTROL:
                    target = row - dr

                    @pl.when((target >= 0) & (target < tile_rows))
                    def _():
                        if ds == 0:
                            parcels[target, at : at + count, :] = owned_blocks[place, first : first + count, :]
                            return
                        start = FOLDED + at % 8
                        rows = min(count, 8)
                        folded = parcels[target, start : start + rows, :]
                        for i in range(count // rows):
                            group = at // 8 + i
                            cells = owned_blocks[place, first + 8 * i : first + 8 * i + rows, :]
                            folded = jnp.where(side_lanes(rows, ds, group), turn(cells, 0, 8 * group), folded)
                        parcels[target, start : start + rows, :] = folded

        return carry

    lax.fori_loop(0, tile_rows, spread, 0)


def pack_kernel(
    table, control, thick, drive, obs, first_col, second_col, parcels,
    tile_block, held, held_control, owned_blocks, packed_parcels, packed_cols, sems,
):
    table_copy = pltpu.make_async_copy(table, tile_block, sems.at[9])
    table_copy.start()
    copies = [pltpu.make_async_copy(control, held_control, sems.at[5])]
    for f, field in enumerate((thick, drive.at[0], drive.at[1], obs.at[0], obs.at[1])):
        copies.append(pltpu.make_async_copy(field, held.at[f], sems.at[f]))
    for copy in copies:
        copy.start()
    packed_parcels[...] = jnp.zeros_like(packed_parcels)
    copies[0].wait()
    for j in range(PACK):
        owned_blocks[:, j, :] = held_control[:, j * LANES : (j + 1) * LANES]
    table_copy.wait()
    fill_parcels(tile_block, owned_blocks, packed_parcels)
    results = [pltpu.make_async_copy(packed_parcels, parcels, sems.at[6])]
    results[0].start()

    lane = lanes_of(HALF)
    left = jnp.zeros((HALF, LANES), jnp.float32)
    right = jnp.zeros((HALF, LANES), jnp.float32)
    for f, (first, count) in enumerate(STRIP):
        copies[1 + f].wait()
        for part in range(2):
            rows = slice(part * HALF, (part + 1) * HALF)
            start = part * BAND + first
            inside = (lane >= start) & (lane < start + count)
            left = jnp.where(inside, turn(held[f, rows, :LANES], 0, start), left)
            right = jnp.where(inside, turn(held[f, rows, LANES:], LANES - count, start), right)
    even = is_even("gx")
    packed_cols[0] = jnp.where(even, right, left)
    packed_cols[1] = jnp.where(even, left, right)
    for i, out in enumerate((first_col, second_col)):
        results.append(pltpu.make_async_copy(packed_cols.at[i], out, sems.at[7 + i]))
        results[-1].start()
    for copy in results:
        copy.wait()


def sides(axis, first_pair, second_pair):
    even = is_even(axis)
    return jnp.where(even, second_pair, first_pair), jnp.where(even, first_pair, second_pair)


def choose_side(lane, high, east, west, low):
    place = lane % BAND
    return jnp.where(
        place < HALO, high, jnp.where(place < 2 * HALO, east, jnp.where(place < 3 * HALO, west, low))
    )


def turn(cells, source, target):
    shift = (target - source) % LANES
    return pltpu.roll(cells, shift, 1) if shift else cells


def gather(cells, source):
    return jnp.take_along_axis(cells, source, axis=1)


def scale_of(f):
    return 0.5 if f in (1, 2) else 1.0


def weave_kernel(thick, drive, obs, woven, own_sides, edges):
    lane, half_lane = lanes_of(TILE), lanes_of(HALF)
    source = 2 * lane % LANES
    for f, (field, (first, count)) in enumerate(zip((thick, drive.at[0], drive.at[1], obs.at[0], obs.at[1]), STRIP)):
        low, high = scale_of(f) * field[:, :LANES], scale_of(f) * field[:, LANES:]
        tiles = [jnp.where(lane < BAND, gather(low, source + i), gather(high, source + i)) for i in range(2)]
        bands = []
        for band in (0, BAND):
            bands.append(
                jnp.where(lane % BAND < BAND // 2, turn(high, LANES - HALO, band), turn(low, 0, band + 3 * HALO))
            )
        own_sides[f] = jnp.where(half_lane < BAND, bands[0][:HALF], bands[1][HALF:])
        for c in range(2):
            woven[f, c] = tiles[c]
        for c, tile in enumerate(tiles + [bands[0]]):
            edges[0, c, first : first + count, :] = tile[:count]
            edges[1, c, first : first + count, :] = tile[TILE - count :]


def rows_kernel(edges, first_col, second_col, first_pair, second_pair):
    west, east = sides("gx", first_col[...], second_col[...])
    even = is_even("gy")
    for c in range(2):
        top, bottom = edges[0, c], edges[1, c]
        first_pair[64 * c : 64 * c + 64, :] = jnp.where(even, bottom, top)
        second_pair[64 * c : 64 * c + 64, :] = jnp.where(even, top, bottom)
    strips = []
    for i in range(2):
        fields = []
        for f, (first, count) in enumerate(STRIP):
            packed = slice(HALF - count, HALF) if i else slice(0, count)
            source = BAND * i + first
            target = BAND if f >= 2 else 0
            own = turn(edges[i, 2, first : first + count, :], 0, target)
            from_east = scale_of(f) * turn(east[packed], source, target + HALO)
            from_west = scale_of(f) * turn(west[packed], source, target + 3 * HALO - count)
            fields.append(choose_side(lanes_of(count), own, from_east, from_west, own))
        lane = lanes_of(HALO)
        lower = jnp.concatenate(fields[3:], axis=0)
        strips.append((jnp.where(lane < BAND, fields[0], fields[2]), jnp.where(lane < BAND, fields[1], lower)))
    for k in range(2):
        top, bottom = strips[0][k], strips[1][k]
        rows = slice(128 + HALO * k, 128 + HALO * (k + 1))
        first_pair[rows, :] = jnp.where(even, bottom, top)
        second_pair[rows, :] = jnp.where(even, top, bottom)


def shift_east(tiles):
    turned = pltpu.roll(tiles[0], LANES - 1, 1)
    return [turned] if len(tiles) == 1 else [tiles[1], turned]


def shift_west(tiles):
    turned = pltpu.roll(tiles[-1], 1, 1)
    return [turned] if len(tiles) == 1 else [turned, tiles[0]]


def run_groups(groups, read, work):
    pending = [read(*group) for group in groups[:AHEAD]]
    for k, (part, row, count) in enumerate(groups):
        if k + AHEAD < len(groups):
            pending.append(read(*groups[k + AHEAD]))
        for ref, lead, values in work(part, pending[k]):
            for tile, value in zip(part, values):
                ref[(*lead, pl.ds(row + tile, count), slice(None))] = value


def block_groups(row, main, side_row, side):
    step = 32 if main % 32 == 0 else 24
    first = side // 16 * 8 if side > 24 else side
    groups = [(MAIN, row + g, min(step, main - g)) for g in range(0, main, step)]
    groups[1:1] = [(SIDES, side_row, first)]
    if first < side:
        groups[3:3] = [(SIDES, side_row + first, side - first)]
    return groups


def over_rows(span, read, work):
    start, blocks, main, side_start, side, main_rest, side_rest = SPANS[span]

    def block(i, carry):
        row, side_row = pl.multiple_of(start + i * main, 8), pl.multiple_of(side_start + i * side, 8)
        run_groups(block_groups(row, main, side_row, side), read, work)
        return carry

    lax.fori_loop(0, blocks, block, 0)
    if main_rest:
        none = 8 * jnp.minimum(lax.axis_index("gx"), 0)
        row = pl.multiple_of(none + start + blocks * main, 8)
        side_row = pl.multiple_of(none + side_start + blocks * side, 8)
        run_groups(block_groups(row, main_rest, side_row, side_rest), read, work)


def over_ends(count, read, work):
    def block(i, carry):
        row = pl.multiple_of(MARGIN + i * (TILE + 2 * HALO - count), 8)
        side_row = pl.multiple_of(MARGIN + i * (HALF + 2 * HALO - count), 8)
        run_groups([(MAIN, row, count), (SIDES, side_row, count)], read, work)
        return carry

    lax.fori_loop(0, 2, block, 0)


def join_parts(ref, leads, whole):
    edge = HALO // 2

    def join(row, upper, lower, count):
        lane = lanes_of(count)
        place = lane % BAND
        for lead in leads:
            def at(tile_row):
                return (*lead, pl.ds(tile_row, count), slice(None))

            mixed = ref[at(SIDE + row)]
            if whole:
                source = jnp.where(place < edge, LANES - edge + place // 2, place // 2 - 24)
                source = jnp.clip(source, 0, LANES - 1)
                halves = []
                for main_row in (row, row + HALF):
                    even, odd = (gather(ref[at(tile + main_row)], source) for tile in MAIN)
                    halves.append(jnp.where(lane % 2 == 0, even, odd))
                outer = (place < edge) | (place >= BAND - edge)
                ref[at(SIDE + row)] = jnp.where(outer, jnp.where(lane < BAND, halves[0], halves[1]), mixed)
            for wanted, band, main_row in ((upper, 0, row), (lower, BAND, row + HALF)):
                if wanted:
                    few = edge // 2
                    source = band + jnp.where(lane < few, 3 * HALO + 2 * lane, edge + 2 * (lane - LANES + few))
                    source = jnp.clip(source, 0, LANES - 2)
                    outer = (lane < few) | (lane >= LANES - few)
                    for c, tile in enumerate(MAIN):
                        ref[at(tile + main_row)] = jnp.where(outer, gather(mixed, source + c), ref[at(tile + main_row)])

    step = 32

    def middle(i, carry):
        join(pl.multiple_of(TOP + i * step, 8), True, True, step)
        return carry

    lax.fori_loop(0, HALF // step, middle, 0)
    if whole:
        join(MARGIN, True, False, HALO)
        join(TOP + HALF, False, True, HALO)


def friction_kernel(tile_block, ice_mask, parcels, fr, ice, owners, patch):
    tile_cols, tile_rows = ice_mask.shape
    row_tile = lax.axis_index("gy")
    col_tile = lax.axis_index("gx")
    core = row_tile % 2
    place = lax.broadcasted_iota(jnp.int32, owners.shape[1:], 0)
    for t in range(owners.shape[0]):
        block = tile_block[t // (tile_rows // 2), t % (tile_rows // 2) * 2 + core]
        owners[t] = (place == block - (row_tile - core) * (owners.shape[1] // 2)).astype(jnp.int32)

    flat = sum(parcels[j] for j in range(tile_rows))
    folded = flat[FOLDED:]
    for dr, _, count, at in CONTROL:
        cells = flat[at : at + count]
        if dr == 0:
            side = jnp.concatenate([turn(folded, 8 * g, 0) for g in range(PACK // 8)], axis=0)
        else:
            side = turn(folded, PACK, 0)[at % 8 : at % 8 + count]
        inner = lanes_of(count) < CT
        row = 4 + {-1: -4, 0: 0, 1: CT}[dr]
        patch[pl.ds(row, count, stride=2), :] = jnp.where(inner, cells, turn(side, 0, CT))
        patch[pl.ds(row + 1, count, stride=2), :] = jnp.where(inner, turn(cells, 0, CT), side)

    cells = 0.5 * jnp.exp(patch[...])
    lane = lanes_of(PATCH)
    wide = gather(cells, lane // 2)
    for tile in MAIN:
        for j in range(4):
            fr[pl.ds(tile + MARGIN + j, PATCH, stride=4), :] = wide
    lane = lanes_of(40)
    place = lane % BAND // 4
    source = jnp.where(place < 8, 60 + place, (116 + place) % LANES)
    wide = jnp.where(
        lane < BAND,
        gather(cells[:40], source),
        gather(cells[PATCH - 40 :], source),
    )
    for j in range(4):
        fr[pl.ds(SIDE + MARGIN + j, 40, stride=4), :] = wide

    side_ice = []
    for dr, first, count in ((-1, MARGIN, HALO), (0, TOP, TILE), (1, TOP + TILE, HALO)):
        masks = []
        for ds in (-1, 0, 1):
            row, col = row_tile + dr, col_tile + ds
            inside = (row >= 0) & (row < tile_rows) & (col >= 0) & (col < tile_cols)
            row = jnp.clip(row, 0, tile_rows - 1)
            col = jnp.clip(col, 0, tile_cols - 1)
            masks.append(jnp.where(inside, ice_mask[col, row], 0).astype(jnp.float32))
        for c in range(2):
            ice[MAIN[c] + first : MAIN[c] + first + count, :] = jnp.full((count, LANES), masks[1])
        side_ice.append(choose_side(lanes_of(HALO), masks[1], masks[2], masks[0], masks[1]))
    upper = lanes_of(HALO) < BAND
    for i in range(HALF // HALO):
        ice[SIDE + TOP + i * HALO : SIDE + TOP + (i + 1) * HALO, :] = side_ice[1]
    ice[SIDE + MARGIN : SIDE + TOP, :] = jnp.where(upper, side_ice[0], side_ice[1])
    ice[SIDE + TOP + HALF : SIDE + TOP + HALF + HALO, :] = jnp.where(upper, side_ice[1], side_ice[2])


def make_stages(ext, fr, ice, visc, vel_a, vel_b, coef):
    def load(ref, part, row, count, *lead):
        return [ref[(*lead, pl.ds(row + tile, count), slice(None))] for tile in part]

    def load_around(part, row, count, now):
        return [load(now, part, r, count, i) for i in range(2) for r in (row, row - 1, row + 1)]

    def load_right(part, row, count):
        return [load(ext, part, row, count, i) for i in (1, 2)]

    def read_thickness(part, row, count):
        return load(ext, part, row, count, 0)

    def keep_viscosity(q):
        return [(visc, (0,), q), (visc, (1,), shift_west(q)), (visc, (2,), shift_east(q))]

    def first_viscosity(part, thickness):
        factor = 0.25 * visc_scale * strain_floor ** (-1.0 / 3.0)
        return keep_viscosity([factor * t for t in thickness])

    def read_viscosity(part, row, count):
        return read_thickness(part, row, count), load_around(part, row, count, vel_b)

    def viscosity(part, read):
        thickness, (u, u_n, u_s, v, v_n, v_s) = read
        u_e, u_w = shift_east(u), shift_west(u)
        v_e, v_w = shift_east(v), shift_west(v)
        result = []
        for c in range(len(part)):
            ux, vx = u_e[c] - u_w[c], v_e[c] - v_w[c]
            uy, vy = u_s[c] - u_n[c], v_s[c] - v_n[c]
            shear = uy + vx
            strain = 0.25 * (ux * (ux + vy) + vy * vy) + (0.0625 * (shear * shear) + strain_floor)
            result.append((0.25 * visc_scale) * thickness[c] * jnp.exp(jnp.log(strain) * (-1.0 / 3.0)))
        return keep_viscosity(result)

    def inverse(x):
        near = pl.reciprocal(x, approx=True)
        return near * (2.0 - x * near)

    def read_coefficients(part, row, count):
        around = [load(visc, part, r, count, i) for i in range(3) for r in (row, row - 1, row + 1)]
        return around + [load(fr, part, row, count), load(ice, part, row, count)]

    def coefficients(part, read):
        tiles = range(len(part))
        q, q_n, q_s, q_w, q_nw, q_sw, q_e, q_ne, q_se, friction, mask = read
        w = [q[c] + q_w[c] for c in tiles]
        e = [q[c] + q_e[c] for c in tiles]
        s = [q[c] + q_s[c] for c in tiles]
        n = [q[c] + q_n[c] for c in tiles]
        scale_u, scale_v = [], []
        for c in tiles:
            across, along = e[c] + w[c], s[c] + n[c]
            scale_u.append(mask[c] * inverse(friction[c] + along + 4.0 * across))
            scale_v.append(mask[c] * inverse(friction[c] + across + 4.0 * along))
        corners = []
        half = [0.5 * q[c] for c in tiles]
        for shifted in (q_sw, q_nw, q_se, q_ne):
            corners.append([q[c] + 0.5 * shifted[c] for c in tiles])
            corners.append([half[c] + shifted[c] for c in tiles])
        return [e, w, s, n, scale_u, scale_v] + corners

    def relax(part, k, around, right):
        tiles = range(len(part))
        e, w, s, n, scale_u, scale_v, sw_u, sw_v, nw_u, nw_v, se_u, se_v, ne_u, ne_v = k
        u, u_n, u_s, v, v_n, v_s = around
        to_west_u, to_east_u, to_west_v, to_east_v = [], [], [], []
        for c in tiles:
            u4 = 4.0 * u[c]
            to_west_u.append(w[c] * u4 + (sw_u[c] * v_s[c] - nw_u[c] * v_n[c]))
            to_east_u.append(e[c] * u4 + (ne_u[c] * v_n[c] - se_u[c] * v_s[c]))
            to_west_v.append(w[c] * v[c] + (sw_v[c] * u_s[c] - nw_v[c] * u_n[c]))
            to_east_v.append(e[c] * v[c] + (ne_v[c] * u_n[c] - se_v[c] * u_s[c]))
        to_west_u, to_west_v = shift_east(to_west_u), shift_east(to_west_v)
        to_east_u, to_east_v = shift_west(to_east_u), shift_west(to_east_v)
        new_u, new_v = [], []
        for c in tiles:
            mid_u = s[c] * u_s[c] + n[c] * u_n[c]
            mid_v = 4.0 * (s[c] * v_s[c] + n[c] * v_n[c])
            new_u.append(scale_u[c] * (right[0][c] + mid_u + (to_west_u[c] + to_east_u[c])))
            new_v.append(scale_v[c] * (right[1][c] + mid_v + (to_west_v[c] + to_east_v[c])))
        return new_u, new_v

    def put(new, values):
        return [(new, (i,), values[i]) for i in range(2)]

    def keep(k):
        return [(coef, (i,), k[i]) for i in range(FACTORS)]

    def read_sweep(now):
        def read(part, row, count):
            k = [load(coef, part, row, count, i) for i in range(FACTORS)]
            return k, load_around(part, row, count, now), load_right(part, row, count)

        return read

    def sweep(new):
        return lambda part, read: put(new, relax(part, *read))

    def read_first(part, row, count):
        return read_coefficients(part, row, count), load_right(part, row, count)

    def first_start(part, read):
        k = coefficients(part, read[0])
        return keep(k) + put(vel_a, [[a * b for a, b in zip(k[4 + i], read[1][i])] for i in range(2)])

    def read_start(part, row, count):
        return (*read_first(part, row, count), load_around(part, row, count, vel_b))

    def start(part, read):
        k = coefficients(part, read[0])
        return keep(k) + put(vel_a, relax(part, k, read[2], read[1]))

    return SimpleNamespace(**locals())


def setup_kernel(
    fr, ice, woven, own_sides, first_col, second_col,
    ext, vel_b,
    visc, vel_a, coef,
):
    west, east = sides("gx", first_col[...], second_col[...])
    lane = lanes_of(HALF)
    for f, (first, count) in enumerate(STRIP):
        for c in range(2):
            ext[f, MAIN[c] + TOP : MAIN[c] + TOP + TILE, :] = woven[f, c]
        from_east = scale_of(f) * turn(east, first, HALO)
        from_west = scale_of(f) * turn(west, first, 3 * HALO - count)
        own = own_sides[f]
        ext[f, SIDE + TOP : SIDE + TOP + HALF, :] = choose_side(lane, own, from_east, from_west, own)
    step = make_stages(ext, fr, ice, visc, vel_a, vel_b, coef)
    over_rows("tile", step.read_thickness, step.first_viscosity)
    over_rows("tile", step.read_first, step.first_start)
    over_rows("tile", step.read_sweep(vel_a), step.sweep(vel_b))


def model_kernel(
    fr, ice, ext_in, vel_in, first_row, second_row,
    vel_u, vel_v, sums,
    ext, visc, vel_a, vel_b, vel_c, coef, plain, small, sems,
):
    ext[...] = ext_in[...]
    vel_b[...] = vel_in[...]
    north, south = sides("gy", first_row[...], second_row[...])
    here = SIDE + TOP
    for f, (first, count) in enumerate(STRIP):
        for c in range(2):
            rows = slice(64 * c + first, 64 * c + first + count)
            ext[f, MAIN[c] + TOP - count : MAIN[c] + TOP, :] = north[rows]
            ext[f, MAIN[c] + TOP + TILE : MAIN[c] + TOP + TILE + count, :] = south[rows]
        rows = slice(128 + first % 32, 128 + first % 32 + count)
        source = BAND if f >= 2 else 0
        upper = lanes_of(count) < BAND
        above = turn(ext_in[f, here + HALF - count : here + HALF, :], 0, BAND)
        below = turn(ext_in[f, here : here + count, :], 0, BAND)
        ext[f, here - count : here, :] = jnp.where(upper, turn(north[rows], source, 0), above)
        ext[f, here + HALF : here + HALF + count, :] = jnp.where(upper, below, turn(south[rows], source, BAND))

    step = make_stages(ext, fr, ice, visc, vel_a, vel_b, coef)
    over_ends(32, step.read_thickness, step.first_viscosity)
    over_ends(32, step.read_first, step.first_start)
    over_ends(24, step.read_sweep(vel_a), step.sweep(vel_b))

    def iterate(span):
        over_rows(span, step.read_viscosity, step.viscosity)
        over_rows(span, step.read_start, step.start)
        over_rows(span, step.read_sweep(vel_a), step.sweep(vel_b))

    def iteration(i, carry):
        iterate("frame")
        return carry

    lax.fori_loop(1, PIC - 1, iteration, 0)
    join_parts(vel_b, ((0,), (1,)), True)
    iterate("inner")
    join_parts(vel_b, ((0,), (1,)), False)
    lane = lanes_of(TILE)
    copies = []
    for i, out in enumerate((vel_u, vel_v)):
        even, odd = (vel_b[i, tile + TOP : tile + TOP + TILE, :] for tile in MAIN)
        for c in range(2):
            source = BAND * c + lane // 2
            plain[i, c] = jnp.where(lane % 2 == 0, gather(even, source), gather(odd, source))
            copies.append(
                pltpu.make_async_copy(plain.at[i, c], out.at[:, c * LANES : (c + 1) * LANES], sems.at[2 * i + c])
            )
            copies[-1].start()

    load = step.load

    def read_misfit(part, row, count):
        return [
            [load(vel_b, part, row, count, i), load(ext, part, row, count, 3 + i), load(coef, part, row, count, 4 + i)]
            for i in range(2)
        ]

    def first_adjoint(part, read):
        misfit = [[0.5 * (a - b) for a, b in zip(u, seen)] for u, seen, _ in read]
        first = [[a * b for a, b in zip(read[i][2], misfit[i])] for i in range(2)]
        return step.put(vel_c, first) + [(ext, (1 + i,), misfit[i]) for i in range(2)]

    over_rows("inner", read_misfit, first_adjoint)

    def two_sweeps(i, carry):
        over_rows("inner", step.read_sweep(vel_c), step.sweep(vel_a))
        over_rows("inner", step.read_sweep(vel_a), step.sweep(vel_c))
        return carry

    lax.fori_loop(0, (ADJ - 2) // 2, two_sweeps, 0)
    over_rows("tile", step.read_sweep(vel_c), step.sweep(vel_a))

    def read_gradient(part, row, count):
        return [load(ref, part, row, count, i) for ref in (vel_b, vel_a) for i in range(2)] + [load(fr, part, row, count)]

    def gradient(part, read):
        u, v, lu, lv, friction = read
        return [(visc, (0,), [-2.0 * friction[c] * (u[c] * lu[c] + v[c] * lv[c]) for c in range(len(part))])]

    over_rows("tile", read_gradient, gradient)
    join_parts(visc, ((0,),), False)
    down = sum(visc[0, pl.ds(tile + TOP + j, CT, stride=4), :] for tile in MAIN for j in range(4))
    k = lax.broadcasted_iota(jnp.int32, (LANES, LANES), 0)
    total = jnp.dot(
        down,
        (k // 2 == lanes_of(LANES) % CT).astype(jnp.float32),
        precision=lax.Precision.HIGHEST,
        preferred_element_type=jnp.float32,
    )
    small[...] = total
    packed = jnp.where(
        lanes_of(PACK) < CT, small[pl.ds(0, PACK, stride=2), :], small[pl.ds(1, PACK, stride=2), :]
    )
    for j in range(sums.shape[0]):
        sums[j] = packed
    for copy in copies:
        copy.wait()


def pick_kernel(owners, gathered, own, other):
    owned = own.shape[0]
    first = lax.axis_index("gy") % 2 == 0
    total = []
    for block in range(2 * owned):
        parts = [jnp.where(owners[t, block : block + 1, :] > 0, gathered[t], 0.0) for t in range(owners.shape[0])]
        while len(parts) > 1:
            parts = [sum(parts[i : i + 2]) for i in range(0, len(parts), 2)]
        total.append(parts[0])
    for block in range(owned):
        low, high = total[block], total[block + owned]
        for out, cells in ((own, jnp.where(first, low, high)), (other, jnp.where(first, high, low))):
            for j in range(PACK):
                out[block : block + 1, j * LANES : (j + 1) * LANES] = cells[j : j + 1]


def in_vmem(count):
    return [pl.BlockSpec(memory_space=pltpu.VMEM)] * count


def in_smem(count):
    return [pl.BlockSpec(memory_space=pltpu.SMEM)] * count


def per_device(thickness, driving, observed, control, ice_mask, tile_block):
    f32 = jnp.float32
    rows, cols = lax.axis_size("gy"), lax.axis_size("gx")
    tile_block, ice_mask = tile_block[:, :, 0].T, ice_mask.T
    params = pltpu.CompilerParams(vmem_limit_bytes=VMEM_LIMIT)

    def shape(*sizes):
        return jax.ShapeDtypeStruct(sizes, f32)

    def swap(axis, cells_first, cells_second):
        count = lax.axis_size(axis)
        received = []
        for cells, low in ((cells_second, 1), (cells_first, 0)):
            pairs = [(i, i + 1) for i in range(low, count - 1, 2)]
            received.append(lax.ppermute(cells, axis, pairs + [(j, i) for i, j in pairs]))
        return received[1], received[0]

    fields = thickness, driving, observed
    owned = control.shape[0]
    *edges, parcels = pl.pallas_call(
        pack_kernel,
        out_shape=[shape(HALF, LANES)] * 2 + [shape(rows, PARCEL, LANES)],
        in_specs=[pl.BlockSpec(memory_space=pltpu.HBM)] * 5,
        out_specs=[pl.BlockSpec(memory_space=pltpu.HBM)] * 3,
        scratch_shapes=[
            pltpu.SMEM(tile_block.shape, jnp.int32),
            pltpu.VMEM((5, TILE, TILE), f32),
            pltpu.VMEM(control.shape, f32),
            pltpu.VMEM((owned, PACK, LANES), f32),
            pltpu.VMEM((rows, PARCEL, LANES), f32),
            pltpu.VMEM((2, HALF, LANES), f32),
            pltpu.SemaphoreType.DMA((10,)),
        ],
        compiler_params=pltpu.CompilerParams(vmem_limit_bytes=PACK_VMEM_LIMIT),
        name="pack",
    )(tile_block, control, *fields)
    parcels = lax.all_to_all(parcels, "gy", 0, 0, tiled=True)
    columns_in = swap("gx", *edges)
    woven, own_sides, strips = pl.pallas_call(
        weave_kernel,
        out_shape=[shape(5, 2, TILE, LANES), shape(5, HALF, LANES), shape(2, 3, 64, LANES)],
        in_specs=in_vmem(3),
        out_specs=in_vmem(3),
        compiler_params=params,
        name="weave",
    )(*fields)
    strips = pl.pallas_call(
        rows_kernel,
        out_shape=[shape(160, LANES)] * 2,
        in_specs=in_vmem(3),
        out_specs=in_vmem(2),
        compiler_params=params,
        name="rows",
    )(strips, *columns_in)
    rows_in = swap("gy", *strips)
    *friction, owners = pl.pallas_call(
        friction_kernel,
        out_shape=[shape(ALL_ROWS, LANES)] * 2
        + [jax.ShapeDtypeStruct((cols * rows // 2, 2 * owned, LANES), jnp.int32)],
        in_specs=in_smem(2) + in_vmem(1),
        out_specs=in_vmem(3),
        scratch_shapes=[pltpu.VMEM((PATCH, LANES), f32)],
        compiler_params=params,
        name="friction",
    )(tile_block, ice_mask, parcels)
    prepared = pl.pallas_call(
        setup_kernel,
        out_shape=[shape(5, ALL_ROWS, LANES), shape(2, ALL_ROWS, LANES)],
        in_specs=in_vmem(6),
        out_specs=in_vmem(2),
        scratch_shapes=[
            pltpu.VMEM((3, ALL_ROWS, LANES), f32),
            pltpu.VMEM((2, ALL_ROWS, LANES), f32),
            pltpu.VMEM((FACTORS, ALL_ROWS, LANES), f32),
        ],
        compiler_params=params,
        name="setup",
    )(*friction, woven, own_sides, *columns_in)

    vel_u, vel_v, sums = pl.pallas_call(
        model_kernel,
        out_shape=(shape(TILE, TILE), shape(TILE, TILE), shape(cols * rows // 2, PACK, LANES)),
        in_specs=in_vmem(6),
        out_specs=[pl.BlockSpec(memory_space=pltpu.HBM)] * 2 + in_vmem(1),
        scratch_shapes=[
            pltpu.VMEM((5, ALL_ROWS, LANES), f32),
            pltpu.VMEM((3, ALL_ROWS, LANES), f32),
            pltpu.VMEM((2, ALL_ROWS, LANES), f32),
            pltpu.VMEM((2, ALL_ROWS, LANES), f32),
            pltpu.VMEM((2, ALL_ROWS, LANES), f32),
            pltpu.VMEM((FACTORS, ALL_ROWS, LANES), f32),
            pltpu.VMEM((2, 2, TILE, LANES), f32),
            pltpu.VMEM((CT, LANES), f32),
            pltpu.SemaphoreType.DMA((4,)),
        ],
        compiler_params=params,
        name="model",
    )(*friction, *prepared, *rows_in)

    same_core = [[i * rows + j for i in range(cols) for j in range(core, rows, 2)] for core in range(2)]
    sums = lax.all_to_all(sums, ("gx", "gy"), 0, 0, tiled=True, axis_index_groups=same_core)
    own, other = pl.pallas_call(
        pick_kernel,
        out_shape=[shape(*control.shape)] * 2,
        in_specs=in_vmem(2),
        out_specs=in_vmem(2),
        compiler_params=params,
        name="pick",
    )(owners, sums)
    gradient = own + lax.ppermute(other, "gy", [(j, j ^ 1) for j in range(rows)])
    return vel_u, vel_v, gradient


def solution(mesh):
    return jax.shard_map(
        per_device,
        mesh=mesh,
        in_specs=(P("gy", "gx"), P(None, "gy", "gx"), P(None, "gy", "gx"), P("gy", None), P(), P()),
        out_specs=(P("gy", "gx"), P("gy", "gx"), P("gy", None)),
        check_vma=False,
    )
```

```python
from types import SimpleNamespace

import jax
import jax.numpy as jnp
from jax import lax
from jax.experimental import pallas as pl
from jax.experimental.pallas import tpu as pltpu
from jax.sharding import PartitionSpec as P

TILE = 256
PIC = 4
SW = 2
ADJ = 6
CT = 64
COARSE = 4096

LANES = 128
HALO = 16
OBS = 8
MARGIN = 8
TOP = MARGIN + HALO
ROWS = TILE + 2 * TOP
HALF = TILE // 2
SIDE = 2 * ROWS
BAND = LANES // 2
ALL_ROWS = SIDE + HALF + 2 * TOP
MAIN = (0, ROWS)
SIDES = (SIDE,)
SPANS = {
    "frame": (MARGIN, 4, 72, MARGIN, 40, 0, 0),
    "inner": (MARGIN + 8, 3, 72, MARGIN + 8, 40, 56, 24),
    "tile": (TOP, 4, 64, TOP, 32, 0, 0),
}
FACTORS = 14
AHEAD = 5
PACK = COARSE // LANES
VMEM_LIMIT = 24 * 1024 * 1024
PACK_VMEM_LIMIT = 62 * 1024 * 1024

STRIP = ((0, HALO), (HALO, HALO), (2 * HALO, HALO), (3 * HALO, OBS), (3 * HALO + OBS, OBS))

CONTROL = ((0, 0, PACK, 0), (-1, PACK - 2, 2, PACK), (1, 0, 2, PACK + 2))
FOLDED = 40
PARCEL = 48
PATCH = CT + 8

visc_scale = 0.1
strain_floor = 0.05


def lanes_of(rows):
    return lax.broadcasted_iota(jnp.int32, (rows, LANES), 1)


def is_even(axis):
    return lax.axis_index(axis) % 2 == 0


def side_lanes(rows, ds, group):
    place = (lanes_of(rows) - 8 * group) % CT
    return place < 4 if ds > 0 else place >= CT - 4


def fill_parcels(tile_block, owned_blocks, parcels):
    tile_cols, tile_rows = tile_block.shape
    owned = owned_blocks.shape[0]
    mine = lax.axis_index("gy") * owned
    col_tile = lax.axis_index("gx")

    def spread(row, carry):
        for ds in (-1, 0, 1):
            col = col_tile + ds
            place = tile_block[jnp.clip(col, 0, tile_cols - 1), row] - mine

            @pl.when((col >= 0) & (col < tile_cols) & (place >= 0) & (place < owned))
            def _():
                for dr, first, count, at in CONTROL:
                    target = row - dr

                    @pl.when((target >= 0) & (target < tile_rows))
                    def _():
                        if ds == 0:
                            parcels[target, at : at + count, :] = owned_blocks[place, first : first + count, :]
                            return
                        start = FOLDED + at % 8
                        rows = min(count, 8)
                        folded = parcels[target, start : start + rows, :]
                        for i in range(count // rows):
                            group = at // 8 + i
                            cells = owned_blocks[place, first + 8 * i : first + 8 * i + rows, :]
                            folded = jnp.where(side_lanes(rows, ds, group), turn(cells, 0, 8 * group), folded)
                        parcels[target, start : start + rows, :] = folded

        return carry

    lax.fori_loop(0, tile_rows, spread, 0)


def pack_kernel(
    table, control, thick, drive, obs, first_col, second_col, parcels,
    tile_block, held, held_control, owned_blocks, packed_parcels, packed_cols, sems,
):
    table_copy = pltpu.make_async_copy(table, tile_block, sems.at[9])
    table_copy.start()
    copies = [pltpu.make_async_copy(control, held_control, sems.at[5])]
    for f, field in enumerate((thick, drive.at[0], drive.at[1], obs.at[0], obs.at[1])):
        copies.append(pltpu.make_async_copy(field, held.at[f], sems.at[f]))
    for copy in copies:
        copy.start()
    packed_parcels[...] = jnp.zeros_like(packed_parcels)
    copies[0].wait()
    for j in range(PACK):
        owned_blocks[:, j, :] = held_control[:, j * LANES : (j + 1) * LANES]
    table_copy.wait()
    fill_parcels(tile_block, owned_blocks, packed_parcels)
    results = [pltpu.make_async_copy(packed_parcels, parcels, sems.at[6])]
    results[0].start()

    lane = lanes_of(HALF)
    left = jnp.zeros((HALF, LANES), jnp.float32)
    right = jnp.zeros((HALF, LANES), jnp.float32)
    for f, (first, count) in enumerate(STRIP):
        copies[1 + f].wait()
        for part in range(2):
            rows = slice(part * HALF, (part + 1) * HALF)
            start = part * BAND + first
            inside = (lane >= start) & (lane < start + count)
            left = jnp.where(inside, turn(held[f, rows, :LANES], 0, start), left)
            right = jnp.where(inside, turn(held[f, rows, LANES:], LANES - count, start), right)
    even = is_even("gx")
    packed_cols[0] = jnp.where(even, right, left)
    packed_cols[1] = jnp.where(even, left, right)
    for i, out in enumerate((first_col, second_col)):
        results.append(pltpu.make_async_copy(packed_cols.at[i], out, sems.at[7 + i]))
        results[-1].start()
    for copy in results:
        copy.wait()


def sides(axis, first_pair, second_pair):
    even = is_even(axis)
    return jnp.where(even, second_pair, first_pair), jnp.where(even, first_pair, second_pair)


def choose_side(lane, high, east, west, low):
    place = lane % BAND
    return jnp.where(
        place < HALO, high, jnp.where(place < 2 * HALO, east, jnp.where(place < 3 * HALO, west, low))
    )


def turn(cells, source, target):
    shift = (target - source) % LANES
    return pltpu.roll(cells, shift, 1) if shift else cells


def gather(cells, source):
    return jnp.take_along_axis(cells, source, axis=1)


def scale_of(f):
    return (0.25 * visc_scale * 4.0 ** (1.0 / 3.0), 0.5, 0.5, 1.0, 1.0)[f]


def weave_kernel(thick, drive, obs, woven, own_sides, edges):
    lane, half_lane = lanes_of(TILE), lanes_of(HALF)
    source = 2 * lane % LANES
    for f, (field, (first, count)) in enumerate(zip((thick, drive.at[0], drive.at[1], obs.at[0], obs.at[1]), STRIP)):
        low, high = scale_of(f) * field[:, :LANES], scale_of(f) * field[:, LANES:]
        tiles = [jnp.where(lane < BAND, gather(low, source + i), gather(high, source + i)) for i in range(2)]
        bands = []
        for band in (0, BAND):
            bands.append(
                jnp.where(lane % BAND < BAND // 2, turn(high, LANES - HALO, band), turn(low, 0, band + 3 * HALO))
            )
        own_sides[f] = jnp.where(half_lane < BAND, bands[0][:HALF], bands[1][HALF:])
        for c in range(2):
            woven[f, c] = tiles[c]
        for c, tile in enumerate(tiles + [bands[0]]):
            edges[0, c, first : first + count, :] = tile[:count]
            edges[1, c, first : first + count, :] = tile[TILE - count :]


def rows_kernel(edges, first_col, second_col, first_pair, second_pair):
    west, east = sides("gx", first_col[...], second_col[...])
    even = is_even("gy")
    for c in range(2):
        top, bottom = edges[0, c], edges[1, c]
        first_pair[64 * c : 64 * c + 64, :] = jnp.where(even, bottom, top)
        second_pair[64 * c : 64 * c + 64, :] = jnp.where(even, top, bottom)
    strips = []
    for i in range(2):
        fields = []
        for f, (first, count) in enumerate(STRIP):
            packed = slice(HALF - count, HALF) if i else slice(0, count)
            source = BAND * i + first
            target = BAND if f >= 2 else 0
            own = turn(edges[i, 2, first : first + count, :], 0, target)
            from_east = scale_of(f) * turn(east[packed], source, target + HALO)
            from_west = scale_of(f) * turn(west[packed], source, target + 3 * HALO - count)
            fields.append(choose_side(lanes_of(count), own, from_east, from_west, own))
        lane = lanes_of(HALO)
        lower = jnp.concatenate(fields[3:], axis=0)
        strips.append((jnp.where(lane < BAND, fields[0], fields[2]), jnp.where(lane < BAND, fields[1], lower)))
    for k in range(2):
        top, bottom = strips[0][k], strips[1][k]
        rows = slice(128 + HALO * k, 128 + HALO * (k + 1))
        first_pair[rows, :] = jnp.where(even, bottom, top)
        second_pair[rows, :] = jnp.where(even, top, bottom)


def shift_east(tiles):
    turned = pltpu.roll(tiles[0], LANES - 1, 1)
    return [turned] if len(tiles) == 1 else [tiles[1], turned]


def shift_west(tiles):
    turned = pltpu.roll(tiles[-1], 1, 1)
    return [turned] if len(tiles) == 1 else [turned, tiles[0]]


def run_groups(groups, read, work):
    pending = [read(*group) for group in groups[:AHEAD]]
    for k, (part, row, count) in enumerate(groups):
        if k + AHEAD < len(groups):
            pending.append(read(*groups[k + AHEAD]))
        for ref, lead, values in work(part, pending[k]):
            for tile, value in zip(part, values):
                ref[(*lead, pl.ds(row + tile, count), slice(None))] = value


def block_groups(row, main, side_row, side):
    step = 32 if main % 32 == 0 else 24
    first = side // 16 * 8 if side > 24 else side
    groups = [(MAIN, row + g, min(step, main - g)) for g in range(0, main, step)]
    groups[1:1] = [(SIDES, side_row, first)]
    if first < side:
        groups[3:3] = [(SIDES, side_row + first, side - first)]
    return groups


def over_rows(span, read, work):
    start, blocks, main, side_start, side, main_rest, side_rest = SPANS[span]

    def block(i, carry):
        row, side_row = pl.multiple_of(start + i * main, 8), pl.multiple_of(side_start + i * side, 8)
        run_groups(block_groups(row, main, side_row, side), read, work)
        return carry

    lax.fori_loop(0, blocks, block, 0)
    if main_rest:
        none = 8 * jnp.minimum(lax.axis_index("gx"), 0)
        row = pl.multiple_of(none + start + blocks * main, 8)
        side_row = pl.multiple_of(none + side_start + blocks * side, 8)
        run_groups(block_groups(row, main_rest, side_row, side_rest), read, work)


def over_ends(count, read, work):
    def block(i, carry):
        row = pl.multiple_of(MARGIN + i * (TILE + 2 * HALO - count), 8)
        side_row = pl.multiple_of(MARGIN + i * (HALF + 2 * HALO - count), 8)
        run_groups([(MAIN, row, count), (SIDES, side_row, count)], read, work)
        return carry

    lax.fori_loop(0, 2, block, 0)


def join_parts(ref, leads, whole):
    edge = HALO // 2

    def join(row, upper, lower, count):
        lane = lanes_of(count)
        place = lane % BAND
        for lead in leads:
            def at(tile_row):
                return (*lead, pl.ds(tile_row, count), slice(None))

            mixed = ref[at(SIDE + row)]
            if whole:
                source = jnp.where(place < edge, LANES - edge + place // 2, place // 2 - 24)
                source = jnp.clip(source, 0, LANES - 1)
                halves = []
                for main_row in (row, row + HALF):
                    even, odd = (gather(ref[at(tile + main_row)], source) for tile in MAIN)
                    halves.append(jnp.where(lane % 2 == 0, even, odd))
                outer = (place < edge) | (place >= BAND - edge)
                ref[at(SIDE + row)] = jnp.where(outer, jnp.where(lane < BAND, halves[0], halves[1]), mixed)
            for wanted, band, main_row in ((upper, 0, row), (lower, BAND, row + HALF)):
                if wanted:
                    few = edge // 2
                    source = band + jnp.where(lane < few, 3 * HALO + 2 * lane, edge + 2 * (lane - LANES + few))
                    source = jnp.clip(source, 0, LANES - 2)
                    outer = (lane < few) | (lane >= LANES - few)
                    for c, tile in enumerate(MAIN):
                        ref[at(tile + main_row)] = jnp.where(outer, gather(mixed, source + c), ref[at(tile + main_row)])

    step = 32

    def middle(i, carry):
        join(pl.multiple_of(TOP + i * step, 8), True, True, step)
        return carry

    lax.fori_loop(0, HALF // step, middle, 0)
    if whole:
        join(MARGIN, True, False, HALO)
        join(TOP + HALF, False, True, HALO)


def friction_kernel(tile_block, ice_mask, parcels, fr, ice, owners, patch):
    tile_cols, tile_rows = ice_mask.shape
    row_tile = lax.axis_index("gy")
    col_tile = lax.axis_index("gx")
    core = row_tile % 2
    place = lax.broadcasted_iota(jnp.int32, owners.shape[1:], 0)
    for t in range(owners.shape[0]):
        block = tile_block[t // (tile_rows // 2), t % (tile_rows // 2) * 2 + core]
        owners[t] = (place == block - (row_tile - core) * (owners.shape[1] // 2)).astype(jnp.int32)

    flat = sum(parcels[j] for j in range(tile_rows))
    folded = flat[FOLDED:]
    for dr, _, count, at in CONTROL:
        cells = flat[at : at + count]
        if dr == 0:
            side = jnp.concatenate([turn(folded, 8 * g, 0) for g in range(PACK // 8)], axis=0)
        else:
            side = turn(folded, PACK, 0)[at % 8 : at % 8 + count]
        inner = lanes_of(count) < CT
        row = 4 + {-1: -4, 0: 0, 1: CT}[dr]
        patch[pl.ds(row, count, stride=2), :] = jnp.where(inner, cells, turn(side, 0, CT))
        patch[pl.ds(row + 1, count, stride=2), :] = jnp.where(inner, turn(cells, 0, CT), side)

    cells = 0.5 * jnp.exp(patch[...])
    lane = lanes_of(PATCH)
    wide = gather(cells, lane // 2)
    for tile in MAIN:
        for j in range(4):
            fr[pl.ds(tile + MARGIN + j, PATCH, stride=4), :] = wide
    lane = lanes_of(40)
    place = lane % BAND // 4
    source = jnp.where(place < 8, 60 + place, (116 + place) % LANES)
    wide = jnp.where(
        lane < BAND,
        gather(cells[:40], source),
        gather(cells[PATCH - 40 :], source),
    )
    for j in range(4):
        fr[pl.ds(SIDE + MARGIN + j, 40, stride=4), :] = wide

    side_ice = []
    for dr, first, count in ((-1, MARGIN, HALO), (0, TOP, TILE), (1, TOP + TILE, HALO)):
        masks = []
        for ds in (-1, 0, 1):
            row, col = row_tile + dr, col_tile + ds
            inside = (row >= 0) & (row < tile_rows) & (col >= 0) & (col < tile_cols)
            row = jnp.clip(row, 0, tile_rows - 1)
            col = jnp.clip(col, 0, tile_cols - 1)
            masks.append(jnp.where(inside, ice_mask[col, row], 0).astype(jnp.float32))
        for c in range(2):
            ice[MAIN[c] + first : MAIN[c] + first + count, :] = jnp.full((count, LANES), masks[1])
        side_ice.append(choose_side(lanes_of(HALO), masks[1], masks[2], masks[0], masks[1]))
    upper = lanes_of(HALO) < BAND
    for i in range(HALF // HALO):
        ice[SIDE + TOP + i * HALO : SIDE + TOP + (i + 1) * HALO, :] = side_ice[1]
    ice[SIDE + MARGIN : SIDE + TOP, :] = jnp.where(upper, side_ice[0], side_ice[1])
    ice[SIDE + TOP + HALF : SIDE + TOP + HALF + HALO, :] = jnp.where(upper, side_ice[1], side_ice[2])


def make_stages(ext, fr, ice, visc, vel_a, vel_b, coef):
    def load(ref, part, row, count, *lead):
        return [ref[(*lead, pl.ds(row + tile, count), slice(None))] for tile in part]

    def load_around(part, row, count, now):
        return [load(now, part, r, count, i) for i in range(2) for r in (row, row - 1, row + 1)]

    def load_right(part, row, count):
        return [load(ext, part, row, count, i) for i in (1, 2)]

    def read_thickness(part, row, count):
        return load(ext, part, row, count, 0)

    def keep_viscosity(q):
        return [(visc, (0,), q), (visc, (1,), shift_west(q)), (visc, (2,), shift_east(q))]

    def first_viscosity(part, thickness):
        factor = (4.0 * strain_floor) ** (-1.0 / 3.0)
        return keep_viscosity([factor * t for t in thickness])

    def read_viscosity(part, row, count):
        return read_thickness(part, row, count), load_around(part, row, count, vel_b)

    def viscosity(part, read):
        thickness, (u, u_n, u_s, v, v_n, v_s) = read
        u_e, u_w = shift_east(u), shift_west(u)
        v_e, v_w = shift_east(v), shift_west(v)
        result = []
        for c in range(len(part)):
            ux, vx = u_e[c] - u_w[c], v_e[c] - v_w[c]
            uy, vy = u_s[c] - u_n[c], v_s[c] - v_n[c]
            shear = uy + vx
            strain = (ux * (ux + vy) + vy * vy) + (0.25 * (shear * shear) + 4.0 * strain_floor)
            result.append(thickness[c] * jnp.exp(jnp.log(strain) * (-1.0 / 3.0)))
        return keep_viscosity(result)

    def inverse(x):
        near = pl.reciprocal(x, approx=True)
        return near * (2.0 - x * near)

    def read_coefficients(part, row, count):
        around = [load(visc, part, r, count, i) for i in range(3) for r in (row, row - 1, row + 1)]
        return around + [load(fr, part, row, count), load(ice, part, row, count)]

    def coefficients(part, read):
        tiles = range(len(part))
        q, q_n, q_s, q_w, q_nw, q_sw, q_e, q_ne, q_se, friction, mask = read
        w = [q[c] + q_w[c] for c in tiles]
        e = [q[c] + q_e[c] for c in tiles]
        s = [q[c] + q_s[c] for c in tiles]
        n = [q[c] + q_n[c] for c in tiles]
        scale_u, scale_v = [], []
        for c in tiles:
            across, along = e[c] + w[c], s[c] + n[c]
            scale_u.append(mask[c] * inverse(friction[c] + along + 4.0 * across))
            scale_v.append(mask[c] * inverse(friction[c] + across + 4.0 * along))
        corners = []
        half = [0.5 * q[c] for c in tiles]
        for shifted in (q_sw, q_nw, q_se, q_ne):
            corners.append([q[c] + 0.5 * shifted[c] for c in tiles])
            corners.append([half[c] + shifted[c] for c in tiles])
        return [e, w, s, n, scale_u, scale_v] + corners

    def relax(part, k, around, right):
        tiles = range(len(part))
        e, w, s, n, scale_u, scale_v, sw_u, sw_v, nw_u, nw_v, se_u, se_v, ne_u, ne_v = k
        u, u_n, u_s, v, v_n, v_s = around
        to_west_u, to_east_u, to_west_v, to_east_v = [], [], [], []
        for c in tiles:
            u4 = 4.0 * u[c]
            to_west_u.append(w[c] * u4 + (sw_u[c] * v_s[c] - nw_u[c] * v_n[c]))
            to_east_u.append(e[c] * u4 + (ne_u[c] * v_n[c] - se_u[c] * v_s[c]))
            to_west_v.append(w[c] * v[c] + (sw_v[c] * u_s[c] - nw_v[c] * u_n[c]))
            to_east_v.append(e[c] * v[c] + (ne_v[c] * u_n[c] - se_v[c] * u_s[c]))
        to_west_u, to_west_v = shift_east(to_west_u), shift_east(to_west_v)
        to_east_u, to_east_v = shift_west(to_east_u), shift_west(to_east_v)
        new_u, new_v = [], []
        for c in tiles:
            mid_u = s[c] * u_s[c] + n[c] * u_n[c]
            mid_v = 4.0 * (s[c] * v_s[c] + n[c] * v_n[c])
            new_u.append(scale_u[c] * (right[0][c] + mid_u + (to_west_u[c] + to_east_u[c])))
            new_v.append(scale_v[c] * (right[1][c] + mid_v + (to_west_v[c] + to_east_v[c])))
        return new_u, new_v

    def put(new, values):
        return [(new, (i,), values[i]) for i in range(2)]

    def keep(k):
        return [(coef, (i,), k[i]) for i in range(FACTORS)]

    def read_sweep(now):
        def read(part, row, count):
            k = [load(coef, part, row, count, i) for i in range(FACTORS)]
            return k, load_around(part, row, count, now), load_right(part, row, count)

        return read

    def sweep(new):
        return lambda part, read: put(new, relax(part, *read))

    def read_first(part, row, count):
        return read_coefficients(part, row, count), load_right(part, row, count)

    def first_start(part, read):
        k = coefficients(part, read[0])
        return keep(k) + put(vel_a, [[a * b for a, b in zip(k[4 + i], read[1][i])] for i in range(2)])

    def read_start(part, row, count):
        return (*read_first(part, row, count), load_around(part, row, count, vel_b))

    def start(part, read):
        k = coefficients(part, read[0])
        return keep(k) + put(vel_a, relax(part, k, read[2], read[1]))

    return SimpleNamespace(**locals())


def setup_kernel(
    fr, ice, woven, own_sides, first_col, second_col,
    ext, vel_b,
    visc, vel_a, coef,
):
    west, east = sides("gx", first_col[...], second_col[...])
    lane = lanes_of(HALF)
    for f, (first, count) in enumerate(STRIP):
        for c in range(2):
            ext[f, MAIN[c] + TOP : MAIN[c] + TOP + TILE, :] = woven[f, c]
        from_east = scale_of(f) * turn(east, first, HALO)
        from_west = scale_of(f) * turn(west, first, 3 * HALO - count)
        own = own_sides[f]
        ext[f, SIDE + TOP : SIDE + TOP + HALF, :] = choose_side(lane, own, from_east, from_west, own)
    step = make_stages(ext, fr, ice, visc, vel_a, vel_b, coef)
    over_rows("tile", step.read_thickness, step.first_viscosity)
    over_rows("tile", step.read_first, step.first_start)
    over_rows("tile", step.read_sweep(vel_a), step.sweep(vel_b))


def model_kernel(
    fr, ice, ext_in, vel_in, first_row, second_row,
    vel_b, sums,
    ext, visc, vel_a, vel_c, coef, small,
):
    ext[...] = ext_in[...]
    vel_b[...] = vel_in[...]
    north, south = sides("gy", first_row[...], second_row[...])
    here = SIDE + TOP
    for f, (first, count) in enumerate(STRIP):
        for c in range(2):
            rows = slice(64 * c + first, 64 * c + first + count)
            ext[f, MAIN[c] + TOP - count : MAIN[c] + TOP, :] = north[rows]
            ext[f, MAIN[c] + TOP + TILE : MAIN[c] + TOP + TILE + count, :] = south[rows]
        rows = slice(128 + first % 32, 128 + first % 32 + count)
        source = BAND if f >= 2 else 0
        upper = lanes_of(count) < BAND
        above = turn(ext_in[f, here + HALF - count : here + HALF, :], 0, BAND)
        below = turn(ext_in[f, here : here + count, :], 0, BAND)
        ext[f, here - count : here, :] = jnp.where(upper, turn(north[rows], source, 0), above)
        ext[f, here + HALF : here + HALF + count, :] = jnp.where(upper, below, turn(south[rows], source, BAND))

    step = make_stages(ext, fr, ice, visc, vel_a, vel_b, coef)
    over_ends(32, step.read_thickness, step.first_viscosity)
    over_ends(32, step.read_first, step.first_start)
    over_ends(24, step.read_sweep(vel_a), step.sweep(vel_b))

    def iteration(i, carry):
        over_rows("frame", step.read_viscosity, step.viscosity)
        over_rows("frame", step.read_start, step.start)
        over_rows("frame", step.read_sweep(vel_a), step.sweep(vel_b))
        return carry

    lax.fori_loop(1, PIC - 1, iteration, 0)
    join_parts(vel_b, ((0,), (1,)), True)
    over_rows("inner", step.read_viscosity, step.viscosity)
    over_rows("inner", step.read_start, step.start)

    load = step.load

    def read_last(part, row, count):
        return (*step.read_sweep(vel_a)(part, row, count), [load(ext, part, row, count, 3 + i) for i in range(2)])

    def last_sweep(part, read):
        k, around, right, seen = read
        new = step.relax(part, k, around, right)
        misfit = [[0.5 * (a - b) for a, b in zip(new[i], seen[i])] for i in range(2)]
        first = [[a * b for a, b in zip(k[4 + i], misfit[i])] for i in range(2)]
        return step.put(vel_b, new) + step.put(vel_c, first) + [(ext, (1 + i,), misfit[i]) for i in range(2)]

    over_rows("inner", read_last, last_sweep)

    def two_sweeps(i, carry):
        over_rows("inner", step.read_sweep(vel_c), step.sweep(vel_a))
        over_rows("inner", step.read_sweep(vel_a), step.sweep(vel_c))
        return carry

    lax.fori_loop(0, (ADJ - 2) // 2, two_sweeps, 0)

    def read_gradient(part, row, count):
        others = [load(vel_b, part, row, count, i) for i in range(2)] + [load(fr, part, row, count)]
        return (*step.read_sweep(vel_c)(part, row, count), others)

    def gradient(part, read):
        k, around, right, (u, v, friction) = read
        lu, lv = step.relax(part, k, around, right)
        return [(visc, (0,), [-2.0 * friction[c] * (u[c] * lu[c] + v[c] * lv[c]) for c in range(len(part))])]

    over_rows("tile", read_gradient, gradient)
    join_parts(visc, ((0,),), False)
    down = sum(visc[0, pl.ds(tile + TOP + j, CT, stride=4), :] for tile in MAIN for j in range(4))
    k = lax.broadcasted_iota(jnp.int32, (LANES, LANES), 0)
    total = jnp.dot(
        down,
        (k // 2 == lanes_of(LANES) % CT).astype(jnp.float32),
        precision=lax.Precision.HIGHEST,
        preferred_element_type=jnp.float32,
    )
    small[...] = total
    packed = jnp.where(
        lanes_of(PACK) < CT, small[pl.ds(0, PACK, stride=2), :], small[pl.ds(1, PACK, stride=2), :]
    )
    for j in range(sums.shape[0]):
        sums[j] = packed


def unweave_kernel(vel, vel_u, vel_v):
    lane, half_lane = lanes_of(TILE), lanes_of(HALF)
    edge = HALO // 2
    for i, out in enumerate((vel_u, vel_v)):
        even, odd = (vel[i, tile + TOP : tile + TOP + TILE, :] for tile in MAIN)
        mixed = vel[i, SIDE + TOP : SIDE + TOP + HALF, :]
        for c in range(2):
            source = BAND * c + lane // 2
            cells = jnp.where(lane % 2 == 0, gather(even, source), gather(odd, source))
            for band in range(2):
                rows = slice(HALF * band, HALF * (band + 1))
                if c == 0:
                    outer, side = half_lane < edge, turn(mixed, BAND * band + 3 * HALO, 0)
                else:
                    outer, side = half_lane >= LANES - edge, turn(mixed, BAND * band + edge, LANES - edge)
                out[rows, c * LANES : (c + 1) * LANES] = jnp.where(outer, side, cells[rows])


def pick_kernel(owners, gathered, own, other):
    owned = own.shape[0]
    first = lax.axis_index("gy") % 2 == 0
    total = []
    for block in range(2 * owned):
        parts = [jnp.where(owners[t, block : block + 1, :] > 0, gathered[t], 0.0) for t in range(owners.shape[0])]
        while len(parts) > 1:
            parts = [sum(parts[i : i + 2]) for i in range(0, len(parts), 2)]
        total.append(parts[0])
    for block in range(owned):
        low, high = total[block], total[block + owned]
        for out, cells in ((own, jnp.where(first, low, high)), (other, jnp.where(first, high, low))):
            for j in range(PACK):
                out[block : block + 1, j * LANES : (j + 1) * LANES] = cells[j : j + 1]


def in_vmem(count):
    return [pl.BlockSpec(memory_space=pltpu.VMEM)] * count


def in_smem(count):
    return [pl.BlockSpec(memory_space=pltpu.SMEM)] * count


def per_device(thickness, driving, observed, control, ice_mask, tile_block):
    f32 = jnp.float32
    rows, cols = lax.axis_size("gy"), lax.axis_size("gx")
    tile_block, ice_mask = tile_block[:, :, 0].T, ice_mask.T
    params = pltpu.CompilerParams(vmem_limit_bytes=VMEM_LIMIT)

    def shape(*sizes):
        return jax.ShapeDtypeStruct(sizes, f32)

    def swap(axis, cells_first, cells_second):
        count = lax.axis_size(axis)
        received = []
        for cells, low in ((cells_second, 1), (cells_first, 0)):
            pairs = [(i, i + 1) for i in range(low, count - 1, 2)]
            received.append(lax.ppermute(cells, axis, pairs + [(j, i) for i, j in pairs]))
        return received[1], received[0]

    fields = thickness, driving, observed
    owned = control.shape[0]
    *edges, parcels = pl.pallas_call(
        pack_kernel,
        out_shape=[shape(HALF, LANES)] * 2 + [shape(rows, PARCEL, LANES)],
        in_specs=[pl.BlockSpec(memory_space=pltpu.HBM)] * 5,
        out_specs=[pl.BlockSpec(memory_space=pltpu.HBM)] * 3,
        scratch_shapes=[
            pltpu.SMEM(tile_block.shape, jnp.int32),
            pltpu.VMEM((5, TILE, TILE), f32),
            pltpu.VMEM(control.shape, f32),
            pltpu.VMEM((owned, PACK, LANES), f32),
            pltpu.VMEM((rows, PARCEL, LANES), f32),
            pltpu.VMEM((2, HALF, LANES), f32),
            pltpu.SemaphoreType.DMA((10,)),
        ],
        compiler_params=pltpu.CompilerParams(vmem_limit_bytes=PACK_VMEM_LIMIT),
        name="pack",
    )(tile_block, control, *fields)
    parcels = lax.all_to_all(parcels, "gy", 0, 0, tiled=True)
    columns_in = swap("gx", *edges)
    woven, own_sides, strips = pl.pallas_call(
        weave_kernel,
        out_shape=[shape(5, 2, TILE, LANES), shape(5, HALF, LANES), shape(2, 3, 64, LANES)],
        in_specs=in_vmem(3),
        out_specs=in_vmem(3),
        compiler_params=params,
        name="weave",
    )(*fields)
    strips = pl.pallas_call(
        rows_kernel,
        out_shape=[shape(160, LANES)] * 2,
        in_specs=in_vmem(3),
        out_specs=in_vmem(2),
        compiler_params=params,
        name="rows",
    )(strips, *columns_in)
    rows_in = swap("gy", *strips)
    *friction, owners = pl.pallas_call(
        friction_kernel,
        out_shape=[shape(ALL_ROWS, LANES)] * 2
        + [jax.ShapeDtypeStruct((cols * rows // 2, 2 * owned, LANES), jnp.int32)],
        in_specs=in_smem(2) + in_vmem(1),
        out_specs=in_vmem(3),
        scratch_shapes=[pltpu.VMEM((PATCH, LANES), f32)],
        compiler_params=params,
        name="friction",
    )(tile_block, ice_mask, parcels)
    prepared = pl.pallas_call(
        setup_kernel,
        out_shape=[shape(5, ALL_ROWS, LANES), shape(2, ALL_ROWS, LANES)],
        in_specs=in_vmem(6),
        out_specs=in_vmem(2),
        scratch_shapes=[
            pltpu.VMEM((3, ALL_ROWS, LANES), f32),
            pltpu.VMEM((2, ALL_ROWS, LANES), f32),
            pltpu.VMEM((FACTORS, ALL_ROWS, LANES), f32),
        ],
        compiler_params=params,
        name="setup",
    )(*friction, woven, own_sides, *columns_in)

    vel, sums = pl.pallas_call(
        model_kernel,
        out_shape=(shape(2, ALL_ROWS, LANES), shape(cols * rows // 2, PACK, LANES)),
        in_specs=in_vmem(6),
        out_specs=in_vmem(2),
        scratch_shapes=[
            pltpu.VMEM((5, ALL_ROWS, LANES), f32),
            pltpu.VMEM((3, ALL_ROWS, LANES), f32),
            pltpu.VMEM((2, ALL_ROWS, LANES), f32),
            pltpu.VMEM((2, ALL_ROWS, LANES), f32),
            pltpu.VMEM((FACTORS, ALL_ROWS, LANES), f32),
            pltpu.VMEM((CT, LANES), f32),
        ],
        compiler_params=params,
        name="model",
    )(*friction, *prepared, *rows_in)
    vel_u, vel_v = pl.pallas_call(
        unweave_kernel,
        out_shape=[shape(TILE, TILE)] * 2,
        in_specs=in_vmem(1),
        out_specs=in_vmem(2),
        compiler_params=params,
        name="unweave",
    )(vel)

    same_core = [[i * rows + j for i in range(cols) for j in range(core, rows, 2)] for core in range(2)]
    sums = lax.all_to_all(sums, ("gx", "gy"), 0, 0, tiled=True, axis_index_groups=same_core)
    own, other = pl.pallas_call(
        pick_kernel,
        out_shape=[shape(*control.shape)] * 2,
        in_specs=in_vmem(2),
        out_specs=in_vmem(2),
        compiler_params=params,
        name="pick",
    )(owners, sums)
    gradient = own + lax.ppermute(other, "gy", [(j, j ^ 1) for j in range(rows)])
    return vel_u, vel_v, gradient


def solution(mesh):
    return jax.shard_map(
        per_device,
        mesh=mesh,
        in_specs=(P("gy", "gx"), P(None, "gy", "gx"), P(None, "gy", "gx"), P("gy", None), P(), P()),
        out_specs=(P("gy", "gx"), P("gy", "gx"), P("gy", None)),
        check_vma=False,
    )
```

```python
from types import SimpleNamespace

import jax
import jax.numpy as jnp
from jax import lax
from jax.experimental import pallas as pl
from jax.experimental.pallas import tpu as pltpu
from jax.sharding import PartitionSpec as P

TILE = 256
PIC = 4
SW = 2
ADJ = 6
CT = 64
COARSE = 4096

LANES = 128
HALO = 16
OBS = 8
MARGIN = 8
TOP = MARGIN + HALO
ROWS = TILE + 2 * TOP
HALF = TILE // 2
SIDE = 2 * ROWS
BAND = LANES // 2
ALL_ROWS = SIDE + HALF + 2 * TOP
MAIN = (0, ROWS)
SIDES = (SIDE,)
SPANS = {
    "frame": (MARGIN, 2, 144, MARGIN, 80, 0, 0),
    "inner": (MARGIN + 8, 2, 136, MARGIN + 8, 72, 0, 0),
    "tile": (TOP, 2, 128, TOP, 64, 0, 0),
}
FACTORS = 14
AHEAD = 5
PACK = COARSE // LANES
VMEM_LIMIT = 24 * 1024 * 1024
PACK_VMEM_LIMIT = 62 * 1024 * 1024

STRIP = ((0, HALO), (HALO, HALO), (2 * HALO, HALO), (3 * HALO, OBS), (3 * HALO + OBS, OBS))

CONTROL = ((0, 0, PACK, 0), (-1, PACK - 2, 2, PACK), (1, 0, 2, PACK + 2))
FOLDED = 40
PARCEL = 48
PATCH = CT + 8

visc_scale = 0.1
strain_floor = 0.05


def lanes_of(rows):
    return lax.broadcasted_iota(jnp.int32, (rows, LANES), 1)


def is_even(axis):
    return lax.axis_index(axis) % 2 == 0


def side_lanes(rows, ds, group):
    place = (lanes_of(rows) - 8 * group) % CT
    return place < 4 if ds > 0 else place >= CT - 4


def fill_parcels(tile_block, owned_blocks, parcels):
    tile_cols, tile_rows = tile_block.shape
    owned = owned_blocks.shape[0]
    mine = lax.axis_index("gy") * owned
    col_tile = lax.axis_index("gx")

    def spread(row, carry):
        for ds in (-1, 0, 1):
            col = col_tile + ds
            place = tile_block[jnp.clip(col, 0, tile_cols - 1), row] - mine

            @pl.when((col >= 0) & (col < tile_cols) & (place >= 0) & (place < owned))
            def _():
                for dr, first, count, at in CONTROL:
                    target = row - dr

                    @pl.when((target >= 0) & (target < tile_rows))
                    def _():
                        if ds == 0:
                            parcels[target, at : at + count, :] = owned_blocks[place, first : first + count, :]
                            return
                        start = FOLDED + at % 8
                        rows = min(count, 8)
                        folded = parcels[target, start : start + rows, :]
                        for i in range(count // rows):
                            group = at // 8 + i
                            cells = owned_blocks[place, first + 8 * i : first + 8 * i + rows, :]
                            folded = jnp.where(side_lanes(rows, ds, group), turn(cells, 0, 8 * group), folded)
                        parcels[target, start : start + rows, :] = folded

        return carry

    lax.fori_loop(0, tile_rows, spread, 0)


def pack_kernel(
    table, control, thick, drive, obs, first_col, second_col, parcels,
    tile_block, held, held_control, owned_blocks, packed_parcels, packed_cols, sems,
):
    table_copy = pltpu.make_async_copy(table, tile_block, sems.at[9])
    table_copy.start()
    copies = [pltpu.make_async_copy(control, held_control, sems.at[5])]
    for f, field in enumerate((thick, drive.at[0], drive.at[1], obs.at[0], obs.at[1])):
        copies.append(pltpu.make_async_copy(field, held.at[f], sems.at[f]))
    for copy in copies:
        copy.start()
    packed_parcels[...] = jnp.zeros_like(packed_parcels)
    copies[0].wait()
    for j in range(PACK):
        owned_blocks[:, j, :] = held_control[:, j * LANES : (j + 1) * LANES]
    table_copy.wait()
    fill_parcels(tile_block, owned_blocks, packed_parcels)
    results = [pltpu.make_async_copy(packed_parcels, parcels, sems.at[6])]
    results[0].start()

    lane = lanes_of(HALF)
    left = jnp.zeros((HALF, LANES), jnp.float32)
    right = jnp.zeros((HALF, LANES), jnp.float32)
    for f, (first, count) in enumerate(STRIP):
        copies[1 + f].wait()
        for part in range(2):
            rows = slice(part * HALF, (part + 1) * HALF)
            start = part * BAND + first
            inside = (lane >= start) & (lane < start + count)
            left = jnp.where(inside, turn(held[f, rows, :LANES], 0, start), left)
            right = jnp.where(inside, turn(held[f, rows, LANES:], LANES - count, start), right)
    even = is_even("gx")
    packed_cols[0] = jnp.where(even, right, left)
    packed_cols[1] = jnp.where(even, left, right)
    for i, out in enumerate((first_col, second_col)):
        results.append(pltpu.make_async_copy(packed_cols.at[i], out, sems.at[7 + i]))
        results[-1].start()
    for copy in results:
        copy.wait()


def sides(axis, first_pair, second_pair):
    even = is_even(axis)
    return jnp.where(even, second_pair, first_pair), jnp.where(even, first_pair, second_pair)


def choose_side(lane, high, east, west, low):
    place = lane % BAND
    return jnp.where(
        place < HALO, high, jnp.where(place < 2 * HALO, east, jnp.where(place < 3 * HALO, west, low))
    )


def turn(cells, source, target):
    shift = (target - source) % LANES
    return pltpu.roll(cells, shift, 1) if shift else cells


def gather(cells, source):
    return jnp.take_along_axis(cells, source, axis=1)


def scale_of(f):
    return (0.25 * visc_scale * 4.0 ** (1.0 / 3.0), 0.5, 0.5, 1.0, 1.0)[f]


def weave_kernel(thick, drive, obs, woven, own_sides, edges):
    lane, half_lane = lanes_of(TILE), lanes_of(HALF)
    source = 2 * lane % LANES
    for f, (field, (first, count)) in enumerate(zip((thick, drive.at[0], drive.at[1], obs.at[0], obs.at[1]), STRIP)):
        low, high = scale_of(f) * field[:, :LANES], scale_of(f) * field[:, LANES:]
        tiles = [jnp.where(lane < BAND, gather(low, source + i), gather(high, source + i)) for i in range(2)]
        bands = []
        for band in (0, BAND):
            bands.append(
                jnp.where(lane % BAND < BAND // 2, turn(high, LANES - HALO, band), turn(low, 0, band + 3 * HALO))
            )
        own_sides[f] = jnp.where(half_lane < BAND, bands[0][:HALF], bands[1][HALF:])
        for c in range(2):
            woven[f, c] = tiles[c]
        for c, tile in enumerate(tiles + [bands[0]]):
            edges[0, c, first : first + count, :] = tile[:count]
            edges[1, c, first : first + count, :] = tile[TILE - count :]


def rows_kernel(edges, first_col, second_col, first_pair, second_pair):
    west, east = sides("gx", first_col[...], second_col[...])
    even = is_even("gy")
    for c in range(2):
        top, bottom = edges[0, c], edges[1, c]
        first_pair[64 * c : 64 * c + 64, :] = jnp.where(even, bottom, top)
        second_pair[64 * c : 64 * c + 64, :] = jnp.where(even, top, bottom)
    strips = []
    for i in range(2):
        fields = []
        for f, (first, count) in enumerate(STRIP):
            packed = slice(HALF - count, HALF) if i else slice(0, count)
            source = BAND * i + first
            target = BAND if f >= 2 else 0
            own = turn(edges[i, 2, first : first + count, :], 0, target)
            from_east = scale_of(f) * turn(east[packed], source, target + HALO)
            from_west = scale_of(f) * turn(west[packed], source, target + 3 * HALO - count)
            fields.append(choose_side(lanes_of(count), own, from_east, from_west, own))
        lane = lanes_of(HALO)
        lower = jnp.concatenate(fields[3:], axis=0)
        strips.append((jnp.where(lane < BAND, fields[0], fields[2]), jnp.where(lane < BAND, fields[1], lower)))
    for k in range(2):
        top, bottom = strips[0][k], strips[1][k]
        rows = slice(128 + HALO * k, 128 + HALO * (k + 1))
        first_pair[rows, :] = jnp.where(even, bottom, top)
        second_pair[rows, :] = jnp.where(even, top, bottom)


def shift_east(tiles):
    turned = pltpu.roll(tiles[0], LANES - 1, 1)
    return [turned] if len(tiles) == 1 else [tiles[1], turned]


def shift_west(tiles):
    turned = pltpu.roll(tiles[-1], 1, 1)
    return [turned] if len(tiles) == 1 else [turned, tiles[0]]


def run_groups(groups, read, work):
    pending = [read(*group) for group in groups[:AHEAD]]
    for k, (part, row, count) in enumerate(groups):
        if k + AHEAD < len(groups):
            pending.append(read(*groups[k + AHEAD]))
        for ref, lead, values in work(part, pending[k]):
            for tile, value in zip(part, values):
                ref[(*lead, pl.ds(row + tile, count), slice(None))] = value


def block_groups(row, main, side_row, side):
    step = 32 if main % 32 == 0 else 24
    first = side // 16 * 8 if side > 24 else side
    groups = [(MAIN, row + g, min(step, main - g)) for g in range(0, main, step)]
    groups[1:1] = [(SIDES, side_row, first)]
    if first < side:
        groups[3:3] = [(SIDES, side_row + first, side - first)]
    return groups


def over_rows(span, read, work):
    start, blocks, main, side_start, side, main_rest, side_rest = SPANS[span]

    def block(i, carry):
        row, side_row = pl.multiple_of(start + i * main, 8), pl.multiple_of(side_start + i * side, 8)
        run_groups(block_groups(row, main, side_row, side), read, work)
        return carry

    lax.fori_loop(0, blocks, block, 0)
    if main_rest:
        none = 8 * jnp.minimum(lax.axis_index("gx"), 0)
        row = pl.multiple_of(none + start + blocks * main, 8)
        side_row = pl.multiple_of(none + side_start + blocks * side, 8)
        run_groups(block_groups(row, main_rest, side_row, side_rest), read, work)


def over_ends(count, read, work):
    def block(i, carry):
        row = pl.multiple_of(MARGIN + i * (TILE + 2 * HALO - count), 8)
        side_row = pl.multiple_of(MARGIN + i * (HALF + 2 * HALO - count), 8)
        run_groups([(MAIN, row, count), (SIDES, side_row, count)], read, work)
        return carry

    lax.fori_loop(0, 2, block, 0)


def join_parts(ref, leads, whole):
    edge = HALO // 2

    def join(row, upper, lower, count):
        lane = lanes_of(count)
        place = lane % BAND
        for lead in leads:
            def at(tile_row):
                return (*lead, pl.ds(tile_row, count), slice(None))

            mixed = ref[at(SIDE + row)]
            if whole:
                source = jnp.where(place < edge, LANES - edge + place // 2, place // 2 - 24)
                source = jnp.clip(source, 0, LANES - 1)
                halves = []
                for main_row in (row, row + HALF):
                    even, odd = (gather(ref[at(tile + main_row)], source) for tile in MAIN)
                    halves.append(jnp.where(lane % 2 == 0, even, odd))
                outer = (place < edge) | (place >= BAND - edge)
                ref[at(SIDE + row)] = jnp.where(outer, jnp.where(lane < BAND, halves[0], halves[1]), mixed)
            for wanted, band, main_row in ((upper, 0, row), (lower, BAND, row + HALF)):
                if wanted:
                    few = edge // 2
                    source = band + jnp.where(lane < few, 3 * HALO + 2 * lane, edge + 2 * (lane - LANES + few))
                    source = jnp.clip(source, 0, LANES - 2)
                    outer = (lane < few) | (lane >= LANES - few)
                    for c, tile in enumerate(MAIN):
                        ref[at(tile + main_row)] = jnp.where(outer, gather(mixed, source + c), ref[at(tile + main_row)])

    step = 32

    def middle(i, carry):
        join(pl.multiple_of(TOP + i * step, 8), True, True, step)
        return carry

    lax.fori_loop(0, HALF // step, middle, 0)
    if whole:
        join(MARGIN, True, False, HALO)
        join(TOP + HALF, False, True, HALO)


def friction_kernel(tile_block, ice_mask, parcels, fr, ice, owners, patch):
    tile_cols, tile_rows = ice_mask.shape
    row_tile = lax.axis_index("gy")
    col_tile = lax.axis_index("gx")
    core = row_tile % 2
    place = lax.broadcasted_iota(jnp.int32, owners.shape[1:], 0)
    for t in range(owners.shape[0]):
        block = tile_block[t // (tile_rows // 2), t % (tile_rows // 2) * 2 + core]
        owners[t] = (place == block - (row_tile - core) * (owners.shape[1] // 2)).astype(jnp.int32)

    flat = sum(parcels[j] for j in range(tile_rows))
    folded = flat[FOLDED:]
    for dr, _, count, at in CONTROL:
        cells = flat[at : at + count]
        if dr == 0:
            side = jnp.concatenate([turn(folded, 8 * g, 0) for g in range(PACK // 8)], axis=0)
        else:
            side = turn(folded, PACK, 0)[at % 8 : at % 8 + count]
        inner = lanes_of(count) < CT
        row = 4 + {-1: -4, 0: 0, 1: CT}[dr]
        patch[pl.ds(row, count, stride=2), :] = jnp.where(inner, cells, turn(side, 0, CT))
        patch[pl.ds(row + 1, count, stride=2), :] = jnp.where(inner, turn(cells, 0, CT), side)

    cells = 0.5 * jnp.exp(patch[...])
    lane = lanes_of(PATCH)
    wide = gather(cells, lane // 2)
    for tile in MAIN:
        for j in range(4):
            fr[pl.ds(tile + MARGIN + j, PATCH, stride=4), :] = wide
    lane = lanes_of(40)
    place = lane % BAND // 4
    source = jnp.where(place < 8, 60 + place, (116 + place) % LANES)
    wide = jnp.where(
        lane < BAND,
        gather(cells[:40], source),
        gather(cells[PATCH - 40 :], source),
    )
    for j in range(4):
        fr[pl.ds(SIDE + MARGIN + j, 40, stride=4), :] = wide

    side_ice = []
    for dr, first, count in ((-1, MARGIN, HALO), (0, TOP, TILE), (1, TOP + TILE, HALO)):
        masks = []
        for ds in (-1, 0, 1):
            row, col = row_tile + dr, col_tile + ds
            inside = (row >= 0) & (row < tile_rows) & (col >= 0) & (col < tile_cols)
            row = jnp.clip(row, 0, tile_rows - 1)
            col = jnp.clip(col, 0, tile_cols - 1)
            masks.append(jnp.where(inside, ice_mask[col, row], 0).astype(jnp.float32))
        for c in range(2):
            ice[MAIN[c] + first : MAIN[c] + first + count, :] = jnp.full((count, LANES), masks[1])
        side_ice.append(choose_side(lanes_of(HALO), masks[1], masks[2], masks[0], masks[1]))
    upper = lanes_of(HALO) < BAND
    for i in range(HALF // HALO):
        ice[SIDE + TOP + i * HALO : SIDE + TOP + (i + 1) * HALO, :] = side_ice[1]
    ice[SIDE + MARGIN : SIDE + TOP, :] = jnp.where(upper, side_ice[0], side_ice[1])
    ice[SIDE + TOP + HALF : SIDE + TOP + HALF + HALO, :] = jnp.where(upper, side_ice[1], side_ice[2])


def make_stages(ext, fr, ice, visc, vel_a, vel_b, coef):
    def load(ref, part, row, count, *lead):
        return [ref[(*lead, pl.ds(row + tile, count), slice(None))] for tile in part]

    def load_around(part, row, count, now):
        return [load(now, part, r, count, i) for i in range(2) for r in (row, row - 1, row + 1)]

    def load_right(part, row, count):
        return [load(ext, part, row, count, i) for i in (1, 2)]

    def read_thickness(part, row, count):
        return load(ext, part, row, count, 0)

    def keep_viscosity(q):
        return [(visc, (0,), q), (visc, (1,), shift_west(q)), (visc, (2,), shift_east(q))]

    def first_viscosity(part, thickness):
        factor = (4.0 * strain_floor) ** (-1.0 / 3.0)
        return keep_viscosity([factor * t for t in thickness])

    def read_viscosity(part, row, count):
        return read_thickness(part, row, count), load_around(part, row, count, vel_b)

    def viscosity(part, read):
        thickness, (u, u_n, u_s, v, v_n, v_s) = read
        u_e, u_w = shift_east(u), shift_west(u)
        v_e, v_w = shift_east(v), shift_west(v)
        result = []
        for c in range(len(part)):
            ux, vx = u_e[c] - u_w[c], v_e[c] - v_w[c]
            uy, vy = u_s[c] - u_n[c], v_s[c] - v_n[c]
            shear = uy + vx
            strain = (ux * (ux + vy) + vy * vy) + (0.25 * (shear * shear) + 4.0 * strain_floor)
            result.append(thickness[c] * jnp.exp(jnp.log(strain) * (-1.0 / 3.0)))
        return keep_viscosity(result)

    def inverse(x):
        near = pl.reciprocal(x, approx=True)
        return near * (2.0 - x * near)

    def read_coefficients(part, row, count):
        around = [load(visc, part, r, count, i) for i in range(3) for r in (row, row - 1, row + 1)]
        return around + [load(fr, part, row, count), load(ice, part, row, count)]

    def coefficients(part, read):
        tiles = range(len(part))
        q, q_n, q_s, q_w, q_nw, q_sw, q_e, q_ne, q_se, friction, mask = read
        w = [q[c] + q_w[c] for c in tiles]
        e = [q[c] + q_e[c] for c in tiles]
        s = [q[c] + q_s[c] for c in tiles]
        n = [q[c] + q_n[c] for c in tiles]
        scale_u, scale_v = [], []
        for c in tiles:
            across, along = e[c] + w[c], s[c] + n[c]
            scale_u.append(mask[c] * inverse(friction[c] + along + 4.0 * across))
            scale_v.append(mask[c] * inverse(friction[c] + across + 4.0 * along))
        corners = []
        half = [0.5 * q[c] for c in tiles]
        for shifted in (q_sw, q_nw, q_se, q_ne):
            corners.append([q[c] + 0.5 * shifted[c] for c in tiles])
            corners.append([half[c] + shifted[c] for c in tiles])
        return [e, w, s, n, scale_u, scale_v] + corners

    def relax(part, k, around, right):
        tiles = range(len(part))
        e, w, s, n, scale_u, scale_v, sw_u, sw_v, nw_u, nw_v, se_u, se_v, ne_u, ne_v = k
        u, u_n, u_s, v, v_n, v_s = around
        to_west_u, to_east_u, to_west_v, to_east_v = [], [], [], []
        for c in tiles:
            u4 = 4.0 * u[c]
            to_west_u.append(w[c] * u4 + (sw_u[c] * v_s[c] - nw_u[c] * v_n[c]))
            to_east_u.append(e[c] * u4 + (ne_u[c] * v_n[c] - se_u[c] * v_s[c]))
            to_west_v.append(w[c] * v[c] + (sw_v[c] * u_s[c] - nw_v[c] * u_n[c]))
            to_east_v.append(e[c] * v[c] + (ne_v[c] * u_n[c] - se_v[c] * u_s[c]))
        to_west_u, to_west_v = shift_east(to_west_u), shift_east(to_west_v)
        to_east_u, to_east_v = shift_west(to_east_u), shift_west(to_east_v)
        new_u, new_v = [], []
        for c in tiles:
            mid_u = s[c] * u_s[c] + n[c] * u_n[c]
            mid_v = 4.0 * (s[c] * v_s[c] + n[c] * v_n[c])
            new_u.append(scale_u[c] * (right[0][c] + mid_u + (to_west_u[c] + to_east_u[c])))
            new_v.append(scale_v[c] * (right[1][c] + mid_v + (to_west_v[c] + to_east_v[c])))
        return new_u, new_v

    def put(new, values):
        return [(new, (i,), values[i]) for i in range(2)]

    def keep(k):
        return [(coef, (i,), k[i]) for i in range(FACTORS)]

    def read_sweep(now):
        def read(part, row, count):
            k = [load(coef, part, row, count, i) for i in range(FACTORS)]
            return k, load_around(part, row, count, now), load_right(part, row, count)

        return read

    def sweep(new):
        return lambda part, read: put(new, relax(part, *read))

    def read_first(part, row, count):
        return read_coefficients(part, row, count), load_right(part, row, count)

    def first_start(part, read):
        k = coefficients(part, read[0])
        return keep(k) + put(vel_a, [[a * b for a, b in zip(k[4 + i], read[1][i])] for i in range(2)])

    def read_start(part, row, count):
        return (*read_first(part, row, count), load_around(part, row, count, vel_b))

    def start(part, read):
        k = coefficients(part, read[0])
        return keep(k) + put(vel_a, relax(part, k, read[2], read[1]))

    return SimpleNamespace(**locals())


def setup_kernel(
    fr, ice, woven, own_sides, first_col, second_col,
    ext, vel_b,
    visc, vel_a, coef,
):
    west, east = sides("gx", first_col[...], second_col[...])
    lane = lanes_of(HALF)
    for f, (first, count) in enumerate(STRIP):
        for c in range(2):
            ext[f, MAIN[c] + TOP : MAIN[c] + TOP + TILE, :] = woven[f, c]
        from_east = scale_of(f) * turn(east, first, HALO)
        from_west = scale_of(f) * turn(west, first, 3 * HALO - count)
        own = own_sides[f]
        ext[f, SIDE + TOP : SIDE + TOP + HALF, :] = choose_side(lane, own, from_east, from_west, own)
    step = make_stages(ext, fr, ice, visc, vel_a, vel_b, coef)
    over_rows("tile", step.read_thickness, step.first_viscosity)
    over_rows("tile", step.read_first, step.first_start)
    over_rows("tile", step.read_sweep(vel_a), step.sweep(vel_b))


def model_kernel(
    fr, ice, ext_in, vel_in, first_row, second_row,
    vel_b, sums,
    ext, visc, vel_a, vel_c, coef, small,
):
    ext[...] = ext_in[...]
    vel_b[...] = vel_in[...]
    north, south = sides("gy", first_row[...], second_row[...])
    here = SIDE + TOP
    for f, (first, count) in enumerate(STRIP):
        for c in range(2):
            rows = slice(64 * c + first, 64 * c + first + count)
            ext[f, MAIN[c] + TOP - count : MAIN[c] + TOP, :] = north[rows]
            ext[f, MAIN[c] + TOP + TILE : MAIN[c] + TOP + TILE + count, :] = south[rows]
        rows = slice(128 + first % 32, 128 + first % 32 + count)
        source = BAND if f >= 2 else 0
        upper = lanes_of(count) < BAND
        above = turn(ext_in[f, here + HALF - count : here + HALF, :], 0, BAND)
        below = turn(ext_in[f, here : here + count, :], 0, BAND)
        ext[f, here - count : here, :] = jnp.where(upper, turn(north[rows], source, 0), above)
        ext[f, here + HALF : here + HALF + count, :] = jnp.where(upper, below, turn(south[rows], source, BAND))

    step = make_stages(ext, fr, ice, visc, vel_a, vel_b, coef)
    over_ends(32, step.read_thickness, step.first_viscosity)
    over_ends(32, step.read_first, step.first_start)
    over_ends(24, step.read_sweep(vel_a), step.sweep(vel_b))

    def iteration(i, carry):
        over_rows("frame", step.read_viscosity, step.viscosity)
        over_rows("frame", step.read_start, step.start)
        over_rows("frame", step.read_sweep(vel_a), step.sweep(vel_b))
        return carry

    lax.fori_loop(1, PIC - 1, iteration, 0)
    join_parts(vel_b, ((0,), (1,)), True)
    over_rows("inner", step.read_viscosity, step.viscosity)
    over_rows("inner", step.read_start, step.start)

    load = step.load

    def read_last(part, row, count):
        return (*step.read_sweep(vel_a)(part, row, count), [load(ext, part, row, count, 3 + i) for i in range(2)])

    def last_sweep(part, read):
        k, around, right, seen = read
        new = step.relax(part, k, around, right)
        misfit = [[0.5 * (a - b) for a, b in zip(new[i], seen[i])] for i in range(2)]
        first = [[a * b for a, b in zip(k[4 + i], misfit[i])] for i in range(2)]
        return step.put(vel_b, new) + step.put(vel_c, first) + [(ext, (1 + i,), misfit[i]) for i in range(2)]

    over_rows("inner", read_last, last_sweep)

    def two_sweeps(i, carry):
        over_rows("inner", step.read_sweep(vel_c), step.sweep(vel_a))
        over_rows("inner", step.read_sweep(vel_a), step.sweep(vel_c))
        return carry

    lax.fori_loop(0, (ADJ - 2) // 2, two_sweeps, 0)

    def read_gradient(part, row, count):
        others = [load(vel_b, part, row, count, i) for i in range(2)] + [load(fr, part, row, count)]
        return (*step.read_sweep(vel_c)(part, row, count), others)

    def gradient(part, read):
        k, around, right, (u, v, friction) = read
        lu, lv = step.relax(part, k, around, right)
        return [(visc, (0,), [-2.0 * friction[c] * (u[c] * lu[c] + v[c] * lv[c]) for c in range(len(part))])]

    over_rows("tile", read_gradient, gradient)
    join_parts(visc, ((0,),), False)
    down = sum(visc[0, pl.ds(tile + TOP + j, CT, stride=4), :] for tile in MAIN for j in range(4))
    k = lax.broadcasted_iota(jnp.int32, (LANES, LANES), 0)
    total = jnp.dot(
        down,
        (k // 2 == lanes_of(LANES) % CT).astype(jnp.float32),
        precision=lax.Precision.HIGHEST,
        preferred_element_type=jnp.float32,
    )
    small[...] = total
    packed = jnp.where(
        lanes_of(PACK) < CT, small[pl.ds(0, PACK, stride=2), :], small[pl.ds(1, PACK, stride=2), :]
    )
    for j in range(sums.shape[0]):
        sums[j] = packed


def unweave_kernel(vel, vel_u, vel_v, plain, sems):
    lane = lanes_of(HALF)
    edge = HALO // 2
    copies = []
    for i, out in enumerate((vel_u, vel_v)):
        mixed = vel[i, SIDE + TOP : SIDE + TOP + HALF, :]
        for band in range(2):
            rows = slice(HALF * band, HALF * (band + 1))
            even, odd = (vel[i, tile + TOP + HALF * band : tile + TOP + HALF * (band + 1), :] for tile in MAIN)
            for c in range(2):
                source = BAND * c + lane // 2
                cells = jnp.where(lane % 2 == 0, gather(even, source), gather(odd, source))
                if c == 0:
                    outer, side = lane < edge, turn(mixed, BAND * band + 3 * HALO, 0)
                else:
                    outer, side = lane >= LANES - edge, turn(mixed, BAND * band + edge, LANES - edge)
                plain[i, rows, c * LANES : (c + 1) * LANES] = jnp.where(outer, side, cells)
            copies.append(pltpu.make_async_copy(plain.at[i, rows], out.at[rows], sems.at[2 * i + band]))
            copies[-1].start()
    for copy in copies:
        copy.wait()


def pick_kernel(owners, gathered, own, other):
    owned = own.shape[0]
    first = lax.axis_index("gy") % 2 == 0
    total = []
    for block in range(2 * owned):
        parts = [jnp.where(owners[t, block : block + 1, :] > 0, gathered[t], 0.0) for t in range(owners.shape[0])]
        while len(parts) > 1:
            parts = [sum(parts[i : i + 2]) for i in range(0, len(parts), 2)]
        total.append(parts[0])
    for block in range(owned):
        low, high = total[block], total[block + owned]
        for out, cells in ((own, jnp.where(first, low, high)), (other, jnp.where(first, high, low))):
            for j in range(PACK):
                out[block : block + 1, j * LANES : (j + 1) * LANES] = cells[j : j + 1]


def in_vmem(count):
    return [pl.BlockSpec(memory_space=pltpu.VMEM)] * count


def in_smem(count):
    return [pl.BlockSpec(memory_space=pltpu.SMEM)] * count


def per_device(thickness, driving, observed, control, ice_mask, tile_block):
    f32 = jnp.float32
    rows, cols = lax.axis_size("gy"), lax.axis_size("gx")
    tile_block, ice_mask = tile_block[:, :, 0].T, ice_mask.T
    params = pltpu.CompilerParams(vmem_limit_bytes=VMEM_LIMIT)

    def shape(*sizes):
        return jax.ShapeDtypeStruct(sizes, f32)

    def swap(axis, cells_first, cells_second):
        count = lax.axis_size(axis)
        received = []
        for cells, low in ((cells_second, 1), (cells_first, 0)):
            pairs = [(i, i + 1) for i in range(low, count - 1, 2)]
            received.append(lax.ppermute(cells, axis, pairs + [(j, i) for i, j in pairs]))
        return received[1], received[0]

    fields = thickness, driving, observed
    owned = control.shape[0]
    *edges, parcels = pl.pallas_call(
        pack_kernel,
        out_shape=[shape(HALF, LANES)] * 2 + [shape(rows, PARCEL, LANES)],
        in_specs=[pl.BlockSpec(memory_space=pltpu.HBM)] * 5,
        out_specs=[pl.BlockSpec(memory_space=pltpu.HBM)] * 3,
        scratch_shapes=[
            pltpu.SMEM(tile_block.shape, jnp.int32),
            pltpu.VMEM((5, TILE, TILE), f32),
            pltpu.VMEM(control.shape, f32),
            pltpu.VMEM((owned, PACK, LANES), f32),
            pltpu.VMEM((rows, PARCEL, LANES), f32),
            pltpu.VMEM((2, HALF, LANES), f32),
            pltpu.SemaphoreType.DMA((10,)),
        ],
        compiler_params=pltpu.CompilerParams(vmem_limit_bytes=PACK_VMEM_LIMIT),
        name="pack",
    )(tile_block, control, *fields)
    parcels = lax.all_to_all(parcels, "gy", 0, 0, tiled=True)
    columns_in = swap("gx", *edges)
    woven, own_sides, strips = pl.pallas_call(
        weave_kernel,
        out_shape=[shape(5, 2, TILE, LANES), shape(5, HALF, LANES), shape(2, 3, 64, LANES)],
        in_specs=in_vmem(3),
        out_specs=in_vmem(3),
        compiler_params=params,
        name="weave",
    )(*fields)
    strips = pl.pallas_call(
        rows_kernel,
        out_shape=[shape(160, LANES)] * 2,
        in_specs=in_vmem(3),
        out_specs=in_vmem(2),
        compiler_params=params,
        name="rows",
    )(strips, *columns_in)
    rows_in = swap("gy", *strips)
    *friction, owners = pl.pallas_call(
        friction_kernel,
        out_shape=[shape(ALL_ROWS, LANES)] * 2
        + [jax.ShapeDtypeStruct((cols * rows // 2, 2 * owned, LANES), jnp.int32)],
        in_specs=in_smem(2) + in_vmem(1),
        out_specs=in_vmem(3),
        scratch_shapes=[pltpu.VMEM((PATCH, LANES), f32)],
        compiler_params=params,
        name="friction",
    )(tile_block, ice_mask, parcels)
    prepared = pl.pallas_call(
        setup_kernel,
        out_shape=[shape(5, ALL_ROWS, LANES), shape(2, ALL_ROWS, LANES)],
        in_specs=in_vmem(6),
        out_specs=in_vmem(2),
        scratch_shapes=[
            pltpu.VMEM((3, ALL_ROWS, LANES), f32),
            pltpu.VMEM((2, ALL_ROWS, LANES), f32),
            pltpu.VMEM((FACTORS, ALL_ROWS, LANES), f32),
        ],
        compiler_params=params,
        name="setup",
    )(*friction, woven, own_sides, *columns_in)

    vel, sums = pl.pallas_call(
        model_kernel,
        out_shape=(shape(2, ALL_ROWS, LANES), shape(cols * rows // 2, PACK, LANES)),
        in_specs=in_vmem(6),
        out_specs=in_vmem(2),
        scratch_shapes=[
            pltpu.VMEM((5, ALL_ROWS, LANES), f32),
            pltpu.VMEM((3, ALL_ROWS, LANES), f32),
            pltpu.VMEM((2, ALL_ROWS, LANES), f32),
            pltpu.VMEM((2, ALL_ROWS, LANES), f32),
            pltpu.VMEM((FACTORS, ALL_ROWS, LANES), f32),
            pltpu.VMEM((CT, LANES), f32),
        ],
        compiler_params=params,
        name="model",
    )(*friction, *prepared, *rows_in)
    vel_u, vel_v = pl.pallas_call(
        unweave_kernel,
        out_shape=[shape(TILE, TILE)] * 2,
        in_specs=in_vmem(1),
        out_specs=[pl.BlockSpec(memory_space=pltpu.HBM)] * 2,
        scratch_shapes=[pltpu.VMEM((2, TILE, TILE), f32), pltpu.SemaphoreType.DMA((4,))],
        compiler_params=params,
        name="unweave",
    )(vel)

    same_core = [[i * rows + j for i in range(cols) for j in range(core, rows, 2)] for core in range(2)]
    sums = lax.all_to_all(sums, ("gx", "gy"), 0, 0, tiled=True, axis_index_groups=same_core)
    own, other = pl.pallas_call(
        pick_kernel,
        out_shape=[shape(*control.shape)] * 2,
        in_specs=in_vmem(2),
        out_specs=in_vmem(2),
        compiler_params=params,
        name="pick",
    )(owners, sums)
    gradient = own + lax.ppermute(other, "gy", [(j, j ^ 1) for j in range(rows)])
    return vel_u, vel_v, gradient


def solution(mesh):
    return jax.shard_map(
        per_device,
        mesh=mesh,
        in_specs=(P("gy", "gx"), P(None, "gy", "gx"), P(None, "gy", "gx"), P("gy", None), P(), P()),
        out_specs=(P("gy", "gx"), P("gy", "gx"), P("gy", None)),
        check_vma=False,
    )
```

```python
from types import SimpleNamespace

import jax
import jax.numpy as jnp
from jax import lax
from jax.experimental import pallas as pl
from jax.experimental.pallas import tpu as pltpu
from jax.sharding import PartitionSpec as P

TILE = 256
PIC = 4
SW = 2
ADJ = 6
CT = 64
COARSE = 4096

LANES = 128
HALO = 16
OBS = 8
MARGIN = 8
TOP = MARGIN + HALO
ROWS = TILE + 2 * TOP
HALF = TILE // 2
SIDE = 2 * ROWS
BAND = LANES // 2
ALL_ROWS = SIDE + HALF + 2 * TOP
MAIN = (0, ROWS)
SIDES = (SIDE,)
SPANS = {
    "frame": (MARGIN, 288, 160),
    "inner": (MARGIN + 8, 272, 144),
    "tile": (TOP, 256, 128),
}
FACTORS = 14
AHEAD = 8
PACK = COARSE // LANES
VMEM_LIMIT = 24 * 1024 * 1024
PACK_VMEM_LIMIT = 62 * 1024 * 1024

STRIP = ((0, HALO), (HALO, HALO), (2 * HALO, HALO), (3 * HALO, OBS), (3 * HALO + OBS, OBS))

CONTROL = ((0, 0, PACK, 0), (-1, PACK - 2, 2, PACK), (1, 0, 2, PACK + 2))
FOLDED = 40
PARCEL = 48
PATCH = CT + 8

visc_scale = 0.1
strain_floor = 0.05


def lanes_of(rows):
    return lax.broadcasted_iota(jnp.int32, (rows, LANES), 1)


def is_even(axis):
    return lax.axis_index(axis) % 2 == 0


def side_lanes(rows, ds, group):
    place = (lanes_of(rows) - 8 * group) % CT
    return place < 4 if ds > 0 else place >= CT - 4


def fill_parcels(tile_block, owned_blocks, parcels):
    tile_cols, tile_rows = tile_block.shape
    owned = owned_blocks.shape[0]
    mine = lax.axis_index("gy") * owned
    col_tile = lax.axis_index("gx")

    def spread(row, carry):
        for ds in (-1, 0, 1):
            col = col_tile + ds
            place = tile_block[jnp.clip(col, 0, tile_cols - 1), row] - mine

            @pl.when((col >= 0) & (col < tile_cols) & (place >= 0) & (place < owned))
            def _():
                for dr, first, count, at in CONTROL:
                    target = row - dr

                    @pl.when((target >= 0) & (target < tile_rows))
                    def _():
                        if ds == 0:
                            parcels[target, at : at + count, :] = owned_blocks[place, first : first + count, :]
                            return
                        start = FOLDED + at % 8
                        rows = min(count, 8)
                        folded = parcels[target, start : start + rows, :]
                        for i in range(count // rows):
                            group = at // 8 + i
                            cells = owned_blocks[place, first + 8 * i : first + 8 * i + rows, :]
                            folded = jnp.where(side_lanes(rows, ds, group), turn(cells, 0, 8 * group), folded)
                        parcels[target, start : start + rows, :] = folded

        return carry

    lax.fori_loop(0, tile_rows, spread, 0)


def pack_kernel(
    table, control, thick, drive, obs, first_col, second_col, parcels,
    tile_block, held, held_control, owned_blocks, packed_parcels, packed_cols, sems,
):
    table_copy = pltpu.make_async_copy(table, tile_block, sems.at[9])
    table_copy.start()
    copies = [pltpu.make_async_copy(control, held_control, sems.at[5])]
    for f, field in enumerate((thick, drive.at[0], drive.at[1], obs.at[0], obs.at[1])):
        copies.append(pltpu.make_async_copy(field, held.at[f], sems.at[f]))
    for copy in copies:
        copy.start()
    packed_parcels[...] = jnp.zeros_like(packed_parcels)
    copies[0].wait()
    for j in range(PACK):
        owned_blocks[:, j, :] = held_control[:, j * LANES : (j + 1) * LANES]
    table_copy.wait()
    fill_parcels(tile_block, owned_blocks, packed_parcels)
    results = [pltpu.make_async_copy(packed_parcels, parcels, sems.at[6])]
    results[0].start()

    lane = lanes_of(HALF)
    left = jnp.zeros((HALF, LANES), jnp.float32)
    right = jnp.zeros((HALF, LANES), jnp.float32)
    for f, (first, count) in enumerate(STRIP):
        copies[1 + f].wait()
        for part in range(2):
            rows = slice(part * HALF, (part + 1) * HALF)
            start = part * BAND + first
            inside = (lane >= start) & (lane < start + count)
            left = jnp.where(inside, turn(held[f, rows, :LANES], 0, start), left)
            right = jnp.where(inside, turn(held[f, rows, LANES:], LANES - count, start), right)
    even = is_even("gx")
    packed_cols[0] = jnp.where(even, right, left)
    packed_cols[1] = jnp.where(even, left, right)
    for i, out in enumerate((first_col, second_col)):
        results.append(pltpu.make_async_copy(packed_cols.at[i], out, sems.at[7 + i]))
        results[-1].start()
    for copy in results:
        copy.wait()


def sides(axis, first_pair, second_pair):
    even = is_even(axis)
    return jnp.where(even, second_pair, first_pair), jnp.where(even, first_pair, second_pair)


def choose_side(lane, high, east, west, low):
    place = lane % BAND
    return jnp.where(
        place < HALO, high, jnp.where(place < 2 * HALO, east, jnp.where(place < 3 * HALO, west, low))
    )


def turn(cells, source, target):
    shift = (target - source) % LANES
    return pltpu.roll(cells, shift, 1) if shift else cells


def gather(cells, source):
    return jnp.take_along_axis(cells, source, axis=1)


def scale_of(f):
    return (0.25 * visc_scale * 4.0 ** (1.0 / 3.0), 0.5, 0.5, 1.0, 1.0)[f]


def weave_kernel(thick, drive, obs, woven, own_sides, edges):
    lane, half_lane = lanes_of(TILE), lanes_of(HALF)
    source = 2 * lane % LANES
    for f, (field, (first, count)) in enumerate(zip((thick, drive.at[0], drive.at[1], obs.at[0], obs.at[1]), STRIP)):
        low, high = scale_of(f) * field[:, :LANES], scale_of(f) * field[:, LANES:]
        tiles = [jnp.where(lane < BAND, gather(low, source + i), gather(high, source + i)) for i in range(2)]
        bands = []
        for band in (0, BAND):
            bands.append(
                jnp.where(lane % BAND < BAND // 2, turn(high, LANES - HALO, band), turn(low, 0, band + 3 * HALO))
            )
        own_sides[f] = jnp.where(half_lane < BAND, bands[0][:HALF], bands[1][HALF:])
        for c in range(2):
            woven[f, c] = tiles[c]
        for c, tile in enumerate(tiles + [bands[0]]):
            edges[0, c, first : first + count, :] = tile[:count]
            edges[1, c, first : first + count, :] = tile[TILE - count :]


def rows_kernel(edges, first_col, second_col, first_pair, second_pair):
    west, east = sides("gx", first_col[...], second_col[...])
    even = is_even("gy")
    for c in range(2):
        top, bottom = edges[0, c], edges[1, c]
        first_pair[64 * c : 64 * c + 64, :] = jnp.where(even, bottom, top)
        second_pair[64 * c : 64 * c + 64, :] = jnp.where(even, top, bottom)
    strips = []
    for i in range(2):
        fields = []
        for f, (first, count) in enumerate(STRIP):
            packed = slice(HALF - count, HALF) if i else slice(0, count)
            source = BAND * i + first
            target = BAND if f >= 2 else 0
            own = turn(edges[i, 2, first : first + count, :], 0, target)
            from_east = scale_of(f) * turn(east[packed], source, target + HALO)
            from_west = scale_of(f) * turn(west[packed], source, target + 3 * HALO - count)
            fields.append(choose_side(lanes_of(count), own, from_east, from_west, own))
        lane = lanes_of(HALO)
        lower = jnp.concatenate(fields[3:], axis=0)
        strips.append((jnp.where(lane < BAND, fields[0], fields[2]), jnp.where(lane < BAND, fields[1], lower)))
    for k in range(2):
        top, bottom = strips[0][k], strips[1][k]
        rows = slice(128 + HALO * k, 128 + HALO * (k + 1))
        first_pair[rows, :] = jnp.where(even, bottom, top)
        second_pair[rows, :] = jnp.where(even, top, bottom)


def shift_east(tiles):
    turned = pltpu.roll(tiles[0], LANES - 1, 1)
    return [turned] if len(tiles) == 1 else [tiles[1], turned]


def shift_west(tiles):
    turned = pltpu.roll(tiles[-1], 1, 1)
    return [turned] if len(tiles) == 1 else [turned, tiles[0]]


def run_groups(groups, read, work):
    pending = [read(*group) for group in groups[:AHEAD]]
    for k, (part, row, count) in enumerate(groups):
        if k + AHEAD < len(groups):
            pending.append(read(*groups[k + AHEAD]))
        for ref, lead, values in work(part, pending[k]):
            for tile, value in zip(part, values):
                ref[(*lead, pl.ds(row + tile, count), slice(None))] = value


def over_rows(span, read, work):
    start, main, side = SPANS[span]
    row = pl.multiple_of(start + 8 * jnp.minimum(lax.axis_index("gx"), 0), 8)
    step = 32 if main % 32 == 0 else 16
    groups = [(MAIN, row + g, step) for g in range(0, main, step)]
    side_step = 32 if side % 32 == 0 else 48
    pieces = [(SIDES, row + g, side_step) for g in range(0, side, side_step)]
    for k, piece in enumerate(pieces):
        groups.insert((2 * k + 1) * len(groups) // (2 * len(pieces)), piece)
    run_groups(groups, read, work)


def over_ends(count, read, work):
    def block(i, carry):
        row = pl.multiple_of(MARGIN + i * (TILE + 2 * HALO - count), 8)
        side_row = pl.multiple_of(MARGIN + i * (HALF + 2 * HALO - count), 8)
        run_groups([(MAIN, row, count), (SIDES, side_row, count)], read, work)
        return carry

    lax.fori_loop(0, 2, block, 0)


def join_parts(ref, leads, whole):
    edge = HALO // 2

    def join(row, upper, lower, count):
        lane = lanes_of(count)
        place = lane % BAND
        for lead in leads:
            def at(tile_row):
                return (*lead, pl.ds(tile_row, count), slice(None))

            mixed = ref[at(SIDE + row)]
            if whole:
                source = jnp.where(place < edge, LANES - edge + place // 2, place // 2 - 24)
                source = jnp.clip(source, 0, LANES - 1)
                halves = []
                for main_row in (row, row + HALF):
                    even, odd = (gather(ref[at(tile + main_row)], source) for tile in MAIN)
                    halves.append(jnp.where(lane % 2 == 0, even, odd))
                outer = (place < edge) | (place >= BAND - edge)
                ref[at(SIDE + row)] = jnp.where(outer, jnp.where(lane < BAND, halves[0], halves[1]), mixed)
            for wanted, band, main_row in ((upper, 0, row), (lower, BAND, row + HALF)):
                if wanted:
                    few = edge // 2
                    source = band + jnp.where(lane < few, 3 * HALO + 2 * lane, edge + 2 * (lane - LANES + few))
                    source = jnp.clip(source, 0, LANES - 2)
                    outer = (lane < few) | (lane >= LANES - few)
                    for c, tile in enumerate(MAIN):
                        ref[at(tile + main_row)] = jnp.where(outer, gather(mixed, source + c), ref[at(tile + main_row)])

    step = 32

    def middle(i, carry):
        join(pl.multiple_of(TOP + i * step, 8), True, True, step)
        return carry

    lax.fori_loop(0, HALF // step, middle, 0)
    if whole:
        join(MARGIN, True, False, HALO)
        join(TOP + HALF, False, True, HALO)


def friction_kernel(tile_block, ice_mask, parcels, fr, ice, owners, patch):
    tile_cols, tile_rows = ice_mask.shape
    row_tile = lax.axis_index("gy")
    col_tile = lax.axis_index("gx")
    core = row_tile % 2
    place = lax.broadcasted_iota(jnp.int32, owners.shape[1:], 0)
    for t in range(owners.shape[0]):
        block = tile_block[t // (tile_rows // 2), t % (tile_rows // 2) * 2 + core]
        owners[t] = (place == block - (row_tile - core) * (owners.shape[1] // 2)).astype(jnp.int32)

    flat = sum(parcels[j] for j in range(tile_rows))
    folded = flat[FOLDED:]
    for dr, _, count, at in CONTROL:
        cells = flat[at : at + count]
        if dr == 0:
            side = jnp.concatenate([turn(folded, 8 * g, 0) for g in range(PACK // 8)], axis=0)
        else:
            side = turn(folded, PACK, 0)[at % 8 : at % 8 + count]
        inner = lanes_of(count) < CT
        row = 4 + {-1: -4, 0: 0, 1: CT}[dr]
        patch[pl.ds(row, count, stride=2), :] = jnp.where(inner, cells, turn(side, 0, CT))
        patch[pl.ds(row + 1, count, stride=2), :] = jnp.where(inner, turn(cells, 0, CT), side)

    cells = 0.5 * jnp.exp(patch[...])
    lane = lanes_of(PATCH)
    wide = gather(cells, lane // 2)
    for tile in MAIN:
        for j in range(4):
            fr[pl.ds(tile + MARGIN + j, PATCH, stride=4), :] = wide
    lane = lanes_of(40)
    place = lane % BAND // 4
    source = jnp.where(place < 8, 60 + place, (116 + place) % LANES)
    wide = jnp.where(
        lane < BAND,
        gather(cells[:40], source),
        gather(cells[PATCH - 40 :], source),
    )
    for j in range(4):
        fr[pl.ds(SIDE + MARGIN + j, 40, stride=4), :] = wide

    side_ice = []
    for dr, first, count in ((-1, MARGIN, HALO), (0, TOP, TILE), (1, TOP + TILE, HALO)):
        masks = []
        for ds in (-1, 0, 1):
            row, col = row_tile + dr, col_tile + ds
            inside = (row >= 0) & (row < tile_rows) & (col >= 0) & (col < tile_cols)
            row = jnp.clip(row, 0, tile_rows - 1)
            col = jnp.clip(col, 0, tile_cols - 1)
            masks.append(jnp.where(inside, ice_mask[col, row], 0).astype(jnp.float32))
        for c in range(2):
            ice[MAIN[c] + first : MAIN[c] + first + count, :] = jnp.full((count, LANES), masks[1])
        side_ice.append(choose_side(lanes_of(HALO), masks[1], masks[2], masks[0], masks[1]))
    upper = lanes_of(HALO) < BAND
    for i in range(HALF // HALO):
        ice[SIDE + TOP + i * HALO : SIDE + TOP + (i + 1) * HALO, :] = side_ice[1]
    ice[SIDE + MARGIN : SIDE + TOP, :] = jnp.where(upper, side_ice[0], side_ice[1])
    ice[SIDE + TOP + HALF : SIDE + TOP + HALF + HALO, :] = jnp.where(upper, side_ice[1], side_ice[2])


def make_stages(ext, fr, ice, visc, vel_a, vel_b, coef):
    def load(ref, part, row, count, *lead):
        return [ref[(*lead, pl.ds(row + tile, count), slice(None))] for tile in part]

    def load_around(part, row, count, now):
        return [load(now, part, r, count, i) for i in range(2) for r in (row, row - 1, row + 1)]

    def load_right(part, row, count):
        return [load(ext, part, row, count, i) for i in (1, 2)]

    def read_thickness(part, row, count):
        return load(ext, part, row, count, 0)

    def keep_viscosity(q):
        return [(visc, (0,), q), (visc, (1,), shift_west(q)), (visc, (2,), shift_east(q))]

    def first_viscosity(part, thickness):
        factor = (4.0 * strain_floor) ** (-1.0 / 3.0)
        return keep_viscosity([factor * t for t in thickness])

    def read_viscosity(part, row, count):
        return read_thickness(part, row, count), load_around(part, row, count, vel_b)

    def viscosity(part, read):
        thickness, (u, u_n, u_s, v, v_n, v_s) = read
        u_e, u_w = shift_east(u), shift_west(u)
        v_e, v_w = shift_east(v), shift_west(v)
        result = []
        for c in range(len(part)):
            ux, vx = u_e[c] - u_w[c], v_e[c] - v_w[c]
            uy, vy = u_s[c] - u_n[c], v_s[c] - v_n[c]
            shear = uy + vx
            strain = (ux * (ux + vy) + vy * vy) + (0.25 * (shear * shear) + 4.0 * strain_floor)
            result.append(thickness[c] * jnp.exp(jnp.log(strain) * (-1.0 / 3.0)))
        return keep_viscosity(result)

    def inverse(x):
        near = pl.reciprocal(x, approx=True)
        return near * (2.0 - x * near)

    def read_coefficients(part, row, count):
        around = [load(visc, part, r, count, i) for i in range(3) for r in (row, row - 1, row + 1)]
        return around + [load(fr, part, row, count), load(ice, part, row, count)]

    def coefficients(part, read):
        tiles = range(len(part))
        q, q_n, q_s, q_w, q_nw, q_sw, q_e, q_ne, q_se, friction, mask = read
        w = [q[c] + q_w[c] for c in tiles]
        e = [q[c] + q_e[c] for c in tiles]
        s = [q[c] + q_s[c] for c in tiles]
        n = [q[c] + q_n[c] for c in tiles]
        scale_u, scale_v = [], []
        for c in tiles:
            across, along = e[c] + w[c], s[c] + n[c]
            scale_u.append(mask[c] * inverse(friction[c] + along + 4.0 * across))
            scale_v.append(mask[c] * inverse(friction[c] + across + 4.0 * along))
        corners = []
        half = [0.5 * q[c] for c in tiles]
        for shifted in (q_sw, q_nw, q_se, q_ne):
            corners.append([q[c] + 0.5 * shifted[c] for c in tiles])
            corners.append([half[c] + shifted[c] for c in tiles])
        return [e, w, s, n, scale_u, scale_v] + corners

    def relax(part, k, around, right):
        tiles = range(len(part))
        e, w, s, n, scale_u, scale_v, sw_u, sw_v, nw_u, nw_v, se_u, se_v, ne_u, ne_v = k
        u, u_n, u_s, v, v_n, v_s = around
        to_west_u, to_east_u, to_west_v, to_east_v = [], [], [], []
        for c in tiles:
            u4 = 4.0 * u[c]
            to_west_u.append(w[c] * u4 + (sw_u[c] * v_s[c] - nw_u[c] * v_n[c]))
            to_east_u.append(e[c] * u4 + (ne_u[c] * v_n[c] - se_u[c] * v_s[c]))
            to_west_v.append(w[c] * v[c] + (sw_v[c] * u_s[c] - nw_v[c] * u_n[c]))
            to_east_v.append(e[c] * v[c] + (ne_v[c] * u_n[c] - se_v[c] * u_s[c]))
        to_west_u, to_west_v = shift_east(to_west_u), shift_east(to_west_v)
        to_east_u, to_east_v = shift_west(to_east_u), shift_west(to_east_v)
        new_u, new_v = [], []
        for c in tiles:
            mid_u = s[c] * u_s[c] + n[c] * u_n[c]
            mid_v = 4.0 * (s[c] * v_s[c] + n[c] * v_n[c])
            new_u.append(scale_u[c] * (right[0][c] + mid_u + (to_west_u[c] + to_east_u[c])))
            new_v.append(scale_v[c] * (right[1][c] + mid_v + (to_west_v[c] + to_east_v[c])))
        return new_u, new_v

    def put(new, values):
        return [(new, (i,), values[i]) for i in range(2)]

    def keep(k):
        return [(coef, (i,), k[i]) for i in range(FACTORS)]

    def read_sweep(now):
        def read(part, row, count):
            k = [load(coef, part, row, count, i) for i in range(FACTORS)]
            return k, load_around(part, row, count, now), load_right(part, row, count)

        return read

    def sweep(new):
        return lambda part, read: put(new, relax(part, *read))

    def read_first(part, row, count):
        return read_coefficients(part, row, count), load_right(part, row, count)

    def first_start(part, read):
        k = coefficients(part, read[0])
        return keep(k) + put(vel_a, [[a * b for a, b in zip(k[4 + i], read[1][i])] for i in range(2)])

    def read_start(part, row, count):
        return (*read_first(part, row, count), load_around(part, row, count, vel_b))

    def start(part, read):
        k = coefficients(part, read[0])
        return keep(k) + put(vel_a, relax(part, k, read[2], read[1]))

    return SimpleNamespace(**locals())


def setup_kernel(
    fr, ice, woven, own_sides, first_col, second_col,
    ext, vel_b,
    visc, vel_a, coef,
):
    west, east = sides("gx", first_col[...], second_col[...])
    lane = lanes_of(HALF)
    for f, (first, count) in enumerate(STRIP):
        for c in range(2):
            ext[f, MAIN[c] + TOP : MAIN[c] + TOP + TILE, :] = woven[f, c]
        from_east = scale_of(f) * turn(east, first, HALO)
        from_west = scale_of(f) * turn(west, first, 3 * HALO - count)
        own = own_sides[f]
        ext[f, SIDE + TOP : SIDE + TOP + HALF, :] = choose_side(lane, own, from_east, from_west, own)
    step = make_stages(ext, fr, ice, visc, vel_a, vel_b, coef)
    over_rows("tile", step.read_thickness, step.first_viscosity)
    over_rows("tile", step.read_first, step.first_start)
    over_rows("tile", step.read_sweep(vel_a), step.sweep(vel_b))


def model_kernel(
    fr, ice, ext_in, vel_in, first_row, second_row,
    vel_b, sums,
    ext, visc, vel_a, vel_c, coef, small,
):
    ext[...] = ext_in[...]
    vel_b[...] = vel_in[...]
    north, south = sides("gy", first_row[...], second_row[...])
    here = SIDE + TOP
    for f, (first, count) in enumerate(STRIP):
        for c in range(2):
            rows = slice(64 * c + first, 64 * c + first + count)
            ext[f, MAIN[c] + TOP - count : MAIN[c] + TOP, :] = north[rows]
            ext[f, MAIN[c] + TOP + TILE : MAIN[c] + TOP + TILE + count, :] = south[rows]
        rows = slice(128 + first % 32, 128 + first % 32 + count)
        source = BAND if f >= 2 else 0
        upper = lanes_of(count) < BAND
        above = turn(ext_in[f, here + HALF - count : here + HALF, :], 0, BAND)
        below = turn(ext_in[f, here : here + count, :], 0, BAND)
        ext[f, here - count : here, :] = jnp.where(upper, turn(north[rows], source, 0), above)
        ext[f, here + HALF : here + HALF + count, :] = jnp.where(upper, below, turn(south[rows], source, BAND))

    step = make_stages(ext, fr, ice, visc, vel_a, vel_b, coef)
    over_ends(32, step.read_thickness, step.first_viscosity)
    over_ends(32, step.read_first, step.first_start)
    over_ends(24, step.read_sweep(vel_a), step.sweep(vel_b))

    def iteration(i, carry):
        over_rows("frame", step.read_viscosity, step.viscosity)
        over_rows("frame", step.read_start, step.start)
        over_rows("frame", step.read_sweep(vel_a), step.sweep(vel_b))
        return carry

    lax.fori_loop(1, PIC - 1, iteration, 0)
    join_parts(vel_b, ((0,), (1,)), True)
    over_rows("inner", step.read_viscosity, step.viscosity)
    over_rows("inner", step.read_start, step.start)

    load = step.load

    def read_last(part, row, count):
        return (*step.read_sweep(vel_a)(part, row, count), [load(ext, part, row, count, 3 + i) for i in range(2)])

    def last_sweep(part, read):
        k, around, right, seen = read
        new = step.relax(part, k, around, right)
        misfit = [[0.5 * (a - b) for a, b in zip(new[i], seen[i])] for i in range(2)]
        first = [[a * b for a, b in zip(k[4 + i], misfit[i])] for i in range(2)]
        return step.put(vel_b, new) + step.put(vel_c, first) + [(ext, (1 + i,), misfit[i]) for i in range(2)]

    over_rows("inner", read_last, last_sweep)

    def two_sweeps(i, carry):
        over_rows("inner", step.read_sweep(vel_c), step.sweep(vel_a))
        over_rows("inner", step.read_sweep(vel_a), step.sweep(vel_c))
        return carry

    lax.fori_loop(0, (ADJ - 2) // 2, two_sweeps, 0)

    def read_gradient(part, row, count):
        others = [load(vel_b, part, row, count, i) for i in range(2)] + [load(fr, part, row, count)]
        return (*step.read_sweep(vel_c)(part, row, count), others)

    def gradient(part, read):
        k, around, right, (u, v, friction) = read
        lu, lv = step.relax(part, k, around, right)
        return [(visc, (0,), [-2.0 * friction[c] * (u[c] * lu[c] + v[c] * lv[c]) for c in range(len(part))])]

    over_rows("tile", read_gradient, gradient)
    join_parts(visc, ((0,),), False)
    down = sum(visc[0, pl.ds(tile + TOP + j, CT, stride=4), :] for tile in MAIN for j in range(4))
    k = lax.broadcasted_iota(jnp.int32, (LANES, LANES), 0)
    total = jnp.dot(
        down,
        (k // 2 == lanes_of(LANES) % CT).astype(jnp.float32),
        precision=lax.Precision.HIGHEST,
        preferred_element_type=jnp.float32,
    )
    small[...] = total
    packed = jnp.where(
        lanes_of(PACK) < CT, small[pl.ds(0, PACK, stride=2), :], small[pl.ds(1, PACK, stride=2), :]
    )
    for j in range(sums.shape[0]):
        sums[j] = packed


def unweave_kernel(vel, vel_u, vel_v, token, plain, sems):
    lane = lanes_of(HALF)
    edge = HALO // 2
    copies = []
    for i, out in enumerate((vel_u, vel_v)):
        mixed = vel[i, SIDE + TOP : SIDE + TOP + HALF, :]
        for band in range(2):
            rows = slice(HALF * band, HALF * (band + 1))
            even, odd = (vel[i, tile + TOP + HALF * band : tile + TOP + HALF * (band + 1), :] for tile in MAIN)
            for c in range(2):
                source = BAND * c + lane // 2
                cells = jnp.where(lane % 2 == 0, gather(even, source), gather(odd, source))
                if c == 0:
                    outer, side = lane < edge, turn(mixed, BAND * band + 3 * HALO, 0)
                else:
                    outer, side = lane >= LANES - edge, turn(mixed, BAND * band + edge, LANES - edge)
                plain[i, rows, c * LANES : (c + 1) * LANES] = jnp.where(outer, side, cells)
            copies.append(pltpu.make_async_copy(plain.at[i, rows], out.at[rows], sems.at[2 * i + band]))
            copies[-1].start()
    token[...] = jnp.zeros_like(token)
    for copy in copies:
        copy.wait()


def pick_kernel(owners, gathered, token, own, other):
    owned = own.shape[0]
    first = lax.axis_index("gy") % 2 == 0
    total = []
    for block in range(2 * owned):
        parts = [jnp.where(owners[t, block : block + 1, :] > 0, gathered[t], 0.0) for t in range(owners.shape[0])]
        while len(parts) > 1:
            parts = [sum(parts[i : i + 2]) for i in range(0, len(parts), 2)]
        total.append(parts[0])
    for block in range(owned):
        low, high = total[block], total[block + owned]
        for out, cells in ((own, jnp.where(first, low, high)), (other, jnp.where(first, high, low))):
            for j in range(PACK):
                out[block : block + 1, j * LANES : (j + 1) * LANES] = cells[j : j + 1]


def in_vmem(count):
    return [pl.BlockSpec(memory_space=pltpu.VMEM)] * count


def in_smem(count):
    return [pl.BlockSpec(memory_space=pltpu.SMEM)] * count


def per_device(thickness, driving, observed, control, ice_mask, tile_block):
    f32 = jnp.float32
    rows, cols = lax.axis_size("gy"), lax.axis_size("gx")
    tile_block, ice_mask = tile_block[:, :, 0].T, ice_mask.T
    params = pltpu.CompilerParams(vmem_limit_bytes=VMEM_LIMIT)

    def shape(*sizes):
        return jax.ShapeDtypeStruct(sizes, f32)

    def swap(axis, cells_first, cells_second):
        count = lax.axis_size(axis)
        received = []
        for cells, low in ((cells_second, 1), (cells_first, 0)):
            pairs = [(i, i + 1) for i in range(low, count - 1, 2)]
            received.append(lax.ppermute(cells, axis, pairs + [(j, i) for i, j in pairs]))
        return received[1], received[0]

    fields = thickness, driving, observed
    owned = control.shape[0]
    *edges, parcels = pl.pallas_call(
        pack_kernel,
        out_shape=[shape(HALF, LANES)] * 2 + [shape(rows, PARCEL, LANES)],
        in_specs=[pl.BlockSpec(memory_space=pltpu.HBM)] * 5,
        out_specs=[pl.BlockSpec(memory_space=pltpu.HBM)] * 3,
        scratch_shapes=[
            pltpu.SMEM(tile_block.shape, jnp.int32),
            pltpu.VMEM((5, TILE, TILE), f32),
            pltpu.VMEM(control.shape, f32),
            pltpu.VMEM((owned, PACK, LANES), f32),
            pltpu.VMEM((rows, PARCEL, LANES), f32),
            pltpu.VMEM((2, HALF, LANES), f32),
            pltpu.SemaphoreType.DMA((10,)),
        ],
        compiler_params=pltpu.CompilerParams(vmem_limit_bytes=PACK_VMEM_LIMIT),
        name="pack",
    )(tile_block, control, *fields)
    parcels = lax.all_to_all(parcels, "gy", 0, 0, tiled=True)
    columns_in = swap("gx", *edges)
    woven, own_sides, strips = pl.pallas_call(
        weave_kernel,
        out_shape=[shape(5, 2, TILE, LANES), shape(5, HALF, LANES), shape(2, 3, 64, LANES)],
        in_specs=in_vmem(3),
        out_specs=in_vmem(3),
        compiler_params=params,
        name="weave",
    )(*fields)
    strips = pl.pallas_call(
        rows_kernel,
        out_shape=[shape(160, LANES)] * 2,
        in_specs=in_vmem(3),
        out_specs=in_vmem(2),
        compiler_params=params,
        name="rows",
    )(strips, *columns_in)
    rows_in = swap("gy", *strips)
    *friction, owners = pl.pallas_call(
        friction_kernel,
        out_shape=[shape(ALL_ROWS, LANES)] * 2
        + [jax.ShapeDtypeStruct((cols * rows // 2, 2 * owned, LANES), jnp.int32)],
        in_specs=in_smem(2) + in_vmem(1),
        out_specs=in_vmem(3),
        scratch_shapes=[pltpu.VMEM((PATCH, LANES), f32)],
        compiler_params=params,
        name="friction",
    )(tile_block, ice_mask, parcels)
    prepared = pl.pallas_call(
        setup_kernel,
        out_shape=[shape(5, ALL_ROWS, LANES), shape(2, ALL_ROWS, LANES)],
        in_specs=in_vmem(6),
        out_specs=in_vmem(2),
        scratch_shapes=[
            pltpu.VMEM((3, ALL_ROWS, LANES), f32),
            pltpu.VMEM((2, ALL_ROWS, LANES), f32),
            pltpu.VMEM((FACTORS, ALL_ROWS, LANES), f32),
        ],
        compiler_params=params,
        name="setup",
    )(*friction, woven, own_sides, *columns_in)

    vel, sums = pl.pallas_call(
        model_kernel,
        out_shape=(shape(2, ALL_ROWS, LANES), shape(cols * rows // 2, PACK, LANES)),
        in_specs=in_vmem(6),
        out_specs=in_vmem(2),
        scratch_shapes=[
            pltpu.VMEM((5, ALL_ROWS, LANES), f32),
            pltpu.VMEM((3, ALL_ROWS, LANES), f32),
            pltpu.VMEM((2, ALL_ROWS, LANES), f32),
            pltpu.VMEM((2, ALL_ROWS, LANES), f32),
            pltpu.VMEM((FACTORS, ALL_ROWS, LANES), f32),
            pltpu.VMEM((CT, LANES), f32),
        ],
        compiler_params=params,
        name="model",
    )(*friction, *prepared, *rows_in)
    vel_u, vel_v, token = pl.pallas_call(
        unweave_kernel,
        out_shape=[shape(TILE, TILE)] * 2 + [shape(8, LANES)],
        in_specs=in_vmem(1),
        out_specs=[pl.BlockSpec(memory_space=pltpu.HBM)] * 2 + in_vmem(1),
        scratch_shapes=[pltpu.VMEM((2, TILE, TILE), f32), pltpu.SemaphoreType.DMA((4,))],
        compiler_params=params,
        name="unweave",
    )(vel)

    same_core = [[i * rows + j for i in range(cols) for j in range(core, rows, 2)] for core in range(2)]
    sums = lax.all_to_all(sums, ("gx", "gy"), 0, 0, tiled=True, axis_index_groups=same_core)
    own, other = pl.pallas_call(
        pick_kernel,
        out_shape=[shape(*control.shape)] * 2,
        in_specs=in_vmem(3),
        out_specs=in_vmem(2),
        compiler_params=params,
        name="pick",
    )(owners, sums, token)
    gradient = own + lax.ppermute(other, "gy", [(j, j ^ 1) for j in range(rows)])
    return vel_u, vel_v, gradient


def solution(mesh):
    return jax.shard_map(
        per_device,
        mesh=mesh,
        in_specs=(P("gy", "gx"), P(None, "gy", "gx"), P(None, "gy", "gx"), P("gy", None), P(), P()),
        out_specs=(P("gy", "gx"), P("gy", "gx"), P("gy", None)),
        check_vma=False,
    )
```

```python
from types import SimpleNamespace

import jax
import jax.numpy as jnp
from jax import lax
from jax.experimental import pallas as pl
from jax.experimental.pallas import tpu as pltpu
from jax.sharding import PartitionSpec as P

TILE = 256
PIC = 4
SW = 2
ADJ = 6
CT = 64
COARSE = 4096

LANES = 128
HALO = 16
OBS = 8
MARGIN = 8
TOP = MARGIN + HALO
ROWS = TILE + 2 * TOP
HALF = TILE // 2
SIDE = 2 * ROWS
BAND = LANES // 2
ALL_ROWS = SIDE + HALF + 2 * TOP
MAIN = (0, ROWS)
SIDES = (SIDE,)
SPANS = {
    "frame": (MARGIN, 2, 144, MARGIN, 80, 0, 0),
    "inner": (MARGIN + 8, 2, 136, MARGIN + 8, 72, 0, 0),
    "tile": (TOP, 2, 128, TOP, 64, 0, 0),
}
FACTORS = 14
AHEAD = 8
PACK = COARSE // LANES
VMEM_LIMIT = 24 * 1024 * 1024
PACK_VMEM_LIMIT = 62 * 1024 * 1024

STRIP = ((0, HALO), (HALO, HALO), (2 * HALO, HALO), (3 * HALO, OBS), (3 * HALO + OBS, OBS))

CONTROL = ((0, 0, PACK, 0), (-1, PACK - 2, 2, PACK), (1, 0, 2, PACK + 2))
FOLDED = 40
PARCEL = 48
PATCH = CT + 8

visc_scale = 0.1
strain_floor = 0.05


def lanes_of(rows):
    return lax.broadcasted_iota(jnp.int32, (rows, LANES), 1)


def is_even(axis):
    return lax.axis_index(axis) % 2 == 0


def side_lanes(rows, ds, group):
    place = (lanes_of(rows) - 8 * group) % CT
    return place < 4 if ds > 0 else place >= CT - 4


def fill_parcels(tile_block, owned_blocks, parcels):
    tile_cols, tile_rows = tile_block.shape
    owned = owned_blocks.shape[0]
    mine = lax.axis_index("gy") * owned
    col_tile = lax.axis_index("gx")

    def spread(row, carry):
        for ds in (-1, 0, 1):
            col = col_tile + ds
            place = tile_block[jnp.clip(col, 0, tile_cols - 1), row] - mine

            @pl.when((col >= 0) & (col < tile_cols) & (place >= 0) & (place < owned))
            def _():
                for dr, first, count, at in CONTROL:
                    target = row - dr

                    @pl.when((target >= 0) & (target < tile_rows))
                    def _():
                        if ds == 0:
                            parcels[target, at : at + count, :] = owned_blocks[place, first : first + count, :]
                            return
                        start = FOLDED + at % 8
                        rows = min(count, 8)
                        folded = parcels[target, start : start + rows, :]
                        for i in range(count // rows):
                            group = at // 8 + i
                            cells = owned_blocks[place, first + 8 * i : first + 8 * i + rows, :]
                            folded = jnp.where(side_lanes(rows, ds, group), turn(cells, 0, 8 * group), folded)
                        parcels[target, start : start + rows, :] = folded

        return carry

    lax.fori_loop(0, tile_rows, spread, 0)


def pack_kernel(
    table, control, thick, drive, obs, first_col, second_col, parcels,
    tile_block, held, held_control, owned_blocks, packed_parcels, packed_cols, sems,
):
    table_copy = pltpu.make_async_copy(table, tile_block, sems.at[9])
    table_copy.start()
    copies = [pltpu.make_async_copy(control, held_control, sems.at[5])]
    for f, field in enumerate((thick, drive.at[0], drive.at[1], obs.at[0], obs.at[1])):
        copies.append(pltpu.make_async_copy(field, held.at[f], sems.at[f]))
    for copy in copies:
        copy.start()
    packed_parcels[...] = jnp.zeros_like(packed_parcels)
    copies[0].wait()
    for j in range(PACK):
        owned_blocks[:, j, :] = held_control[:, j * LANES : (j + 1) * LANES]
    table_copy.wait()
    fill_parcels(tile_block, owned_blocks, packed_parcels)
    results = [pltpu.make_async_copy(packed_parcels, parcels, sems.at[6])]
    results[0].start()

    lane = lanes_of(HALF)
    left = jnp.zeros((HALF, LANES), jnp.float32)
    right = jnp.zeros((HALF, LANES), jnp.float32)
    for f, (first, count) in enumerate(STRIP):
        copies[1 + f].wait()
        for part in range(2):
            rows = slice(part * HALF, (part + 1) * HALF)
            start = part * BAND + first
            inside = (lane >= start) & (lane < start + count)
            left = jnp.where(inside, turn(held[f, rows, :LANES], 0, start), left)
            right = jnp.where(inside, turn(held[f, rows, LANES:], LANES - count, start), right)
    even = is_even("gx")
    packed_cols[0] = jnp.where(even, right, left)
    packed_cols[1] = jnp.where(even, left, right)
    for i, out in enumerate((first_col, second_col)):
        results.append(pltpu.make_async_copy(packed_cols.at[i], out, sems.at[7 + i]))
        results[-1].start()
    for copy in results:
        copy.wait()


def sides(axis, first_pair, second_pair):
    even = is_even(axis)
    return jnp.where(even, second_pair, first_pair), jnp.where(even, first_pair, second_pair)


def choose_side(lane, high, east, west, low):
    place = lane % BAND
    return jnp.where(
        place < HALO, high, jnp.where(place < 2 * HALO, east, jnp.where(place < 3 * HALO, west, low))
    )


def turn(cells, source, target):
    shift = (target - source) % LANES
    return pltpu.roll(cells, shift, 1) if shift else cells


def gather(cells, source):
    return jnp.take_along_axis(cells, source, axis=1)


def scale_of(f):
    return (0.25 * visc_scale * 4.0 ** (1.0 / 3.0), 0.5, 0.5, 1.0, 1.0)[f]


def weave_kernel(thick, drive, obs, woven, own_sides, edges):
    lane, half_lane = lanes_of(TILE), lanes_of(HALF)
    source = 2 * lane % LANES
    for f, (field, (first, count)) in enumerate(zip((thick, drive.at[0], drive.at[1], obs.at[0], obs.at[1]), STRIP)):
        low, high = scale_of(f) * field[:, :LANES], scale_of(f) * field[:, LANES:]
        tiles = [jnp.where(lane < BAND, gather(low, source + i), gather(high, source + i)) for i in range(2)]
        bands = []
        for band in (0, BAND):
            bands.append(
                jnp.where(lane % BAND < BAND // 2, turn(high, LANES - HALO, band), turn(low, 0, band + 3 * HALO))
            )
        own_sides[f] = jnp.where(half_lane < BAND, bands[0][:HALF], bands[1][HALF:])
        for c in range(2):
            woven[f, c] = tiles[c]
        for c, tile in enumerate(tiles + [bands[0]]):
            edges[0, c, first : first + count, :] = tile[:count]
            edges[1, c, first : first + count, :] = tile[TILE - count :]


def rows_kernel(edges, first_col, second_col, first_pair, second_pair):
    west, east = sides("gx", first_col[...], second_col[...])
    even = is_even("gy")
    for c in range(2):
        top, bottom = edges[0, c], edges[1, c]
        first_pair[64 * c : 64 * c + 64, :] = jnp.where(even, bottom, top)
        second_pair[64 * c : 64 * c + 64, :] = jnp.where(even, top, bottom)
    strips = []
    for i in range(2):
        fields = []
        for f, (first, count) in enumerate(STRIP):
            packed = slice(HALF - count, HALF) if i else slice(0, count)
            source = BAND * i + first
            target = BAND if f >= 2 else 0
            own = turn(edges[i, 2, first : first + count, :], 0, target)
            from_east = scale_of(f) * turn(east[packed], source, target + HALO)
            from_west = scale_of(f) * turn(west[packed], source, target + 3 * HALO - count)
            fields.append(choose_side(lanes_of(count), own, from_east, from_west, own))
        lane = lanes_of(HALO)
        lower = jnp.concatenate(fields[3:], axis=0)
        strips.append((jnp.where(lane < BAND, fields[0], fields[2]), jnp.where(lane < BAND, fields[1], lower)))
    for k in range(2):
        top, bottom = strips[0][k], strips[1][k]
        rows = slice(128 + HALO * k, 128 + HALO * (k + 1))
        first_pair[rows, :] = jnp.where(even, bottom, top)
        second_pair[rows, :] = jnp.where(even, top, bottom)


def shift_east(tiles):
    turned = pltpu.roll(tiles[0], LANES - 1, 1)
    return [turned] if len(tiles) == 1 else [tiles[1], turned]


def shift_west(tiles):
    turned = pltpu.roll(tiles[-1], 1, 1)
    return [turned] if len(tiles) == 1 else [turned, tiles[0]]


def run_groups(groups, read, work):
    pending = [read(*group) for group in groups[:AHEAD]]
    for k, (part, row, count) in enumerate(groups):
        if k + AHEAD < len(groups):
            pending.append(read(*groups[k + AHEAD]))
        for ref, lead, values in work(part, pending[k]):
            for tile, value in zip(part, values):
                ref[(*lead, pl.ds(row + tile, count), slice(None))] = value


def block_groups(row, main, side_row, side):
    step = 32 if main % 32 == 0 else 24
    first = side // 16 * 8 if side > 24 else side
    groups = [(MAIN, row + g, min(step, main - g)) for g in range(0, main, step)]
    groups[1:1] = [(SIDES, side_row, first)]
    if first < side:
        groups[3:3] = [(SIDES, side_row + first, side - first)]
    return groups


def over_rows(span, read, work):
    start, blocks, main, side_start, side, main_rest, side_rest = SPANS[span]

    def block(i, carry):
        row, side_row = pl.multiple_of(start + i * main, 8), pl.multiple_of(side_start + i * side, 8)
        run_groups(block_groups(row, main, side_row, side), read, work)
        return carry

    lax.fori_loop(0, blocks, block, 0)
    if main_rest:
        none = 8 * jnp.minimum(lax.axis_index("gx"), 0)
        row = pl.multiple_of(none + start + blocks * main, 8)
        side_row = pl.multiple_of(none + side_start + blocks * side, 8)
        run_groups(block_groups(row, main_rest, side_row, side_rest), read, work)


def over_ends(count, read, work):
    def block(i, carry):
        row = pl.multiple_of(MARGIN + i * (TILE + 2 * HALO - count), 8)
        side_row = pl.multiple_of(MARGIN + i * (HALF + 2 * HALO - count), 8)
        run_groups([(MAIN, row, count), (SIDES, side_row, count)], read, work)
        return carry

    lax.fori_loop(0, 2, block, 0)


def join_parts(ref, leads, whole):
    edge = HALO // 2

    def join(row, upper, lower, count):
        lane = lanes_of(count)
        place = lane % BAND
        for lead in leads:
            def at(tile_row):
                return (*lead, pl.ds(tile_row, count), slice(None))

            mixed = ref[at(SIDE + row)]
            if whole:
                source = jnp.where(place < edge, LANES - edge + place // 2, place // 2 - 24)
                source = jnp.clip(source, 0, LANES - 1)
                halves = []
                for main_row in (row, row + HALF):
                    even, odd = (gather(ref[at(tile + main_row)], source) for tile in MAIN)
                    halves.append(jnp.where(lane % 2 == 0, even, odd))
                outer = (place < edge) | (place >= BAND - edge)
                ref[at(SIDE + row)] = jnp.where(outer, jnp.where(lane < BAND, halves[0], halves[1]), mixed)
            for wanted, band, main_row in ((upper, 0, row), (lower, BAND, row + HALF)):
                if wanted:
                    few = edge // 2
                    source = band + jnp.where(lane < few, 3 * HALO + 2 * lane, edge + 2 * (lane - LANES + few))
                    source = jnp.clip(source, 0, LANES - 2)
                    outer = (lane < few) | (lane >= LANES - few)
                    for c, tile in enumerate(MAIN):
                        ref[at(tile + main_row)] = jnp.where(outer, gather(mixed, source + c), ref[at(tile + main_row)])

    step = 32

    def middle(i, carry):
        join(pl.multiple_of(TOP + i * step, 8), True, True, step)
        return carry

    lax.fori_loop(0, HALF // step, middle, 0)
    if whole:
        join(MARGIN, True, False, HALO)
        join(TOP + HALF, False, True, HALO)


def friction_kernel(tile_block, ice_mask, parcels, fr, ice, owners, patch):
    tile_cols, tile_rows = ice_mask.shape
    row_tile = lax.axis_index("gy")
    col_tile = lax.axis_index("gx")
    core = row_tile % 2
    place = lax.broadcasted_iota(jnp.int32, owners.shape[1:], 0)
    for t in range(owners.shape[0]):
        block = tile_block[t // (tile_rows // 2), t % (tile_rows // 2) * 2 + core]
        owners[t] = (place == block - (row_tile - core) * (owners.shape[1] // 2)).astype(jnp.int32)

    flat = sum(parcels[j] for j in range(tile_rows))
    folded = flat[FOLDED:]
    for dr, _, count, at in CONTROL:
        cells = flat[at : at + count]
        if dr == 0:
            side = jnp.concatenate([turn(folded, 8 * g, 0) for g in range(PACK // 8)], axis=0)
        else:
            side = turn(folded, PACK, 0)[at % 8 : at % 8 + count]
        inner = lanes_of(count) < CT
        row = 4 + {-1: -4, 0: 0, 1: CT}[dr]
        patch[pl.ds(row, count, stride=2), :] = jnp.where(inner, cells, turn(side, 0, CT))
        patch[pl.ds(row + 1, count, stride=2), :] = jnp.where(inner, turn(cells, 0, CT), side)

    cells = 0.5 * jnp.exp(patch[...])
    lane = lanes_of(PATCH)
    wide = gather(cells, lane // 2)
    for tile in MAIN:
        for j in range(4):
            fr[pl.ds(tile + MARGIN + j, PATCH, stride=4), :] = wide
    lane = lanes_of(40)
    place = lane % BAND // 4
    source = jnp.where(place < 8, 60 + place, (116 + place) % LANES)
    wide = jnp.where(
        lane < BAND,
        gather(cells[:40], source),
        gather(cells[PATCH - 40 :], source),
    )
    for j in range(4):
        fr[pl.ds(SIDE + MARGIN + j, 40, stride=4), :] = wide

    side_ice = []
    for dr, first, count in ((-1, MARGIN, HALO), (0, TOP, TILE), (1, TOP + TILE, HALO)):
        masks = []
        for ds in (-1, 0, 1):
            row, col = row_tile + dr, col_tile + ds
            inside = (row >= 0) & (row < tile_rows) & (col >= 0) & (col < tile_cols)
            row = jnp.clip(row, 0, tile_rows - 1)
            col = jnp.clip(col, 0, tile_cols - 1)
            masks.append(jnp.where(inside, ice_mask[col, row], 0).astype(jnp.float32))
        for c in range(2):
            ice[MAIN[c] + first : MAIN[c] + first + count, :] = jnp.full((count, LANES), masks[1])
        side_ice.append(choose_side(lanes_of(HALO), masks[1], masks[2], masks[0], masks[1]))
    upper = lanes_of(HALO) < BAND
    for i in range(HALF // HALO):
        ice[SIDE + TOP + i * HALO : SIDE + TOP + (i + 1) * HALO, :] = side_ice[1]
    ice[SIDE + MARGIN : SIDE + TOP, :] = jnp.where(upper, side_ice[0], side_ice[1])
    ice[SIDE + TOP + HALF : SIDE + TOP + HALF + HALO, :] = jnp.where(upper, side_ice[1], side_ice[2])


def make_stages(ext, fr, ice, visc, vel_a, vel_b, coef):
    def load(ref, part, row, count, *lead):
        return [ref[(*lead, pl.ds(row + tile, count), slice(None))] for tile in part]

    def load_around(part, row, count, now):
        return [load(now, part, r, count, i) for i in range(2) for r in (row, row - 1, row + 1)]

    def load_right(part, row, count):
        return [load(ext, part, row, count, i) for i in (1, 2)]

    def read_thickness(part, row, count):
        return load(ext, part, row, count, 0)

    def keep_viscosity(q):
        return [(visc, (0,), q), (visc, (1,), shift_west(q)), (visc, (2,), shift_east(q))]

    def first_viscosity(part, thickness):
        factor = (4.0 * strain_floor) ** (-1.0 / 3.0)
        return keep_viscosity([factor * t for t in thickness])

    def read_viscosity(part, row, count):
        return read_thickness(part, row, count), load_around(part, row, count, vel_b)

    def viscosity(part, read):
        thickness, (u, u_n, u_s, v, v_n, v_s) = read
        u_e, u_w = shift_east(u), shift_west(u)
        v_e, v_w = shift_east(v), shift_west(v)
        result = []
        for c in range(len(part)):
            ux, vx = u_e[c] - u_w[c], v_e[c] - v_w[c]
            uy, vy = u_s[c] - u_n[c], v_s[c] - v_n[c]
            shear = uy + vx
            strain = (ux * (ux + vy) + vy * vy) + (0.25 * (shear * shear) + 4.0 * strain_floor)
            result.append(thickness[c] * jnp.exp(jnp.log(strain) * (-1.0 / 3.0)))
        return keep_viscosity(result)

    def inverse(x):
        near = pl.reciprocal(x, approx=True)
        return near * (2.0 - x * near)

    def read_coefficients(part, row, count):
        around = [load(visc, part, r, count, i) for i in range(3) for r in (row, row - 1, row + 1)]
        return around + [load(fr, part, row, count), load(ice, part, row, count)]

    def coefficients(part, read):
        tiles = range(len(part))
        q, q_n, q_s, q_w, q_nw, q_sw, q_e, q_ne, q_se, friction, mask = read
        w = [q[c] + q_w[c] for c in tiles]
        e = [q[c] + q_e[c] for c in tiles]
        s = [q[c] + q_s[c] for c in tiles]
        n = [q[c] + q_n[c] for c in tiles]
        scale_u, scale_v = [], []
        for c in tiles:
            across, along = e[c] + w[c], s[c] + n[c]
            scale_u.append(mask[c] * inverse(friction[c] + along + 4.0 * across))
            scale_v.append(mask[c] * inverse(friction[c] + across + 4.0 * along))
        corners = []
        half = [0.5 * q[c] for c in tiles]
        for shifted in (q_sw, q_nw, q_se, q_ne):
            corners.append([q[c] + 0.5 * shifted[c] for c in tiles])
            corners.append([half[c] + shifted[c] for c in tiles])
        return [e, w, s, n, scale_u, scale_v] + corners

    def relax(part, k, around, right):
        tiles = range(len(part))
        e, w, s, n, scale_u, scale_v, sw_u, sw_v, nw_u, nw_v, se_u, se_v, ne_u, ne_v = k
        u, u_n, u_s, v, v_n, v_s = around
        to_west_u, to_east_u, to_west_v, to_east_v = [], [], [], []
        for c in tiles:
            u4 = 4.0 * u[c]
            to_west_u.append(w[c] * u4 + (sw_u[c] * v_s[c] - nw_u[c] * v_n[c]))
            to_east_u.append(e[c] * u4 + (ne_u[c] * v_n[c] - se_u[c] * v_s[c]))
            to_west_v.append(w[c] * v[c] + (sw_v[c] * u_s[c] - nw_v[c] * u_n[c]))
            to_east_v.append(e[c] * v[c] + (ne_v[c] * u_n[c] - se_v[c] * u_s[c]))
        to_west_u, to_west_v = shift_east(to_west_u), shift_east(to_west_v)
        to_east_u, to_east_v = shift_west(to_east_u), shift_west(to_east_v)
        new_u, new_v = [], []
        for c in tiles:
            mid_u = s[c] * u_s[c] + n[c] * u_n[c]
            mid_v = 4.0 * (s[c] * v_s[c] + n[c] * v_n[c])
            new_u.append(scale_u[c] * (right[0][c] + mid_u + (to_west_u[c] + to_east_u[c])))
            new_v.append(scale_v[c] * (right[1][c] + mid_v + (to_west_v[c] + to_east_v[c])))
        return new_u, new_v

    def put(new, values):
        return [(new, (i,), values[i]) for i in range(2)]

    def keep(k):
        return [(coef, (i,), k[i]) for i in range(FACTORS)]

    def read_sweep(now):
        def read(part, row, count):
            k = [load(coef, part, row, count, i) for i in range(FACTORS)]
            return k, load_around(part, row, count, now), load_right(part, row, count)

        return read

    def sweep(new):
        return lambda part, read: put(new, relax(part, *read))

    def read_first(part, row, count):
        return read_coefficients(part, row, count), load_right(part, row, count)

    def first_start(part, read):
        k = coefficients(part, read[0])
        return keep(k) + put(vel_a, [[a * b for a, b in zip(k[4 + i], read[1][i])] for i in range(2)])

    def read_start(part, row, count):
        return (*read_first(part, row, count), load_around(part, row, count, vel_b))

    def start(part, read):
        k = coefficients(part, read[0])
        return keep(k) + put(vel_a, relax(part, k, read[2], read[1]))

    return SimpleNamespace(**locals())


def setup_kernel(
    fr, ice, woven, own_sides, first_col, second_col,
    ext, vel_b,
    visc, vel_a, coef,
):
    west, east = sides("gx", first_col[...], second_col[...])
    lane = lanes_of(HALF)
    for f, (first, count) in enumerate(STRIP):
        for c in range(2):
            ext[f, MAIN[c] + TOP : MAIN[c] + TOP + TILE, :] = woven[f, c]
        from_east = scale_of(f) * turn(east, first, HALO)
        from_west = scale_of(f) * turn(west, first, 3 * HALO - count)
        own = own_sides[f]
        ext[f, SIDE + TOP : SIDE + TOP + HALF, :] = choose_side(lane, own, from_east, from_west, own)
    step = make_stages(ext, fr, ice, visc, vel_a, vel_b, coef)
    over_rows("tile", step.read_thickness, step.first_viscosity)
    over_rows("tile", step.read_first, step.first_start)
    over_rows("tile", step.read_sweep(vel_a), step.sweep(vel_b))


def model_kernel(
    fr, ice, ext_in, vel_in, first_row, second_row,
    vel_b, sums,
    ext, visc, vel_a, vel_c, coef, small,
):
    ext[...] = ext_in[...]
    vel_b[...] = vel_in[...]
    north, south = sides("gy", first_row[...], second_row[...])
    here = SIDE + TOP
    for f, (first, count) in enumerate(STRIP):
        for c in range(2):
            rows = slice(64 * c + first, 64 * c + first + count)
            ext[f, MAIN[c] + TOP - count : MAIN[c] + TOP, :] = north[rows]
            ext[f, MAIN[c] + TOP + TILE : MAIN[c] + TOP + TILE + count, :] = south[rows]
        rows = slice(128 + first % 32, 128 + first % 32 + count)
        source = BAND if f >= 2 else 0
        upper = lanes_of(count) < BAND
        above = turn(ext_in[f, here + HALF - count : here + HALF, :], 0, BAND)
        below = turn(ext_in[f, here : here + count, :], 0, BAND)
        ext[f, here - count : here, :] = jnp.where(upper, turn(north[rows], source, 0), above)
        ext[f, here + HALF : here + HALF + count, :] = jnp.where(upper, below, turn(south[rows], source, BAND))

    step = make_stages(ext, fr, ice, visc, vel_a, vel_b, coef)
    over_ends(32, step.read_thickness, step.first_viscosity)
    over_ends(32, step.read_first, step.first_start)
    over_ends(24, step.read_sweep(vel_a), step.sweep(vel_b))

    def iteration(i, carry):
        over_rows("frame", step.read_viscosity, step.viscosity)
        over_rows("frame", step.read_start, step.start)
        over_rows("frame", step.read_sweep(vel_a), step.sweep(vel_b))
        return carry

    lax.fori_loop(1, PIC - 1, iteration, 0)
    join_parts(vel_b, ((0,), (1,)), True)
    over_rows("inner", step.read_viscosity, step.viscosity)
    over_rows("inner", step.read_start, step.start)

    load = step.load

    def read_last(part, row, count):
        return (*step.read_sweep(vel_a)(part, row, count), [load(ext, part, row, count, 3 + i) for i in range(2)])

    def last_sweep(part, read):
        k, around, right, seen = read
        new = step.relax(part, k, around, right)
        misfit = [[0.5 * (a - b) for a, b in zip(new[i], seen[i])] for i in range(2)]
        first = [[a * b for a, b in zip(k[4 + i], misfit[i])] for i in range(2)]
        return step.put(vel_b, new) + step.put(vel_c, first) + [(ext, (1 + i,), misfit[i]) for i in range(2)]

    over_rows("inner", read_last, last_sweep)

    def two_sweeps(i, carry):
        over_rows("inner", step.read_sweep(vel_c), step.sweep(vel_a))
        over_rows("inner", step.read_sweep(vel_a), step.sweep(vel_c))
        return carry

    lax.fori_loop(0, (ADJ - 2) // 2, two_sweeps, 0)

    def read_gradient(part, row, count):
        others = [load(vel_b, part, row, count, i) for i in range(2)] + [load(fr, part, row, count)]
        return (*step.read_sweep(vel_c)(part, row, count), others)

    def gradient(part, read):
        k, around, right, (u, v, friction) = read
        lu, lv = step.relax(part, k, around, right)
        return [(visc, (0,), [-2.0 * friction[c] * (u[c] * lu[c] + v[c] * lv[c]) for c in range(len(part))])]

    over_rows("tile", read_gradient, gradient)
    join_parts(visc, ((0,),), False)
    down = sum(visc[0, pl.ds(tile + TOP + j, CT, stride=4), :] for tile in MAIN for j in range(4))
    k = lax.broadcasted_iota(jnp.int32, (LANES, LANES), 0)
    total = jnp.dot(
        down,
        (k // 2 == lanes_of(LANES) % CT).astype(jnp.float32),
        precision=lax.Precision.HIGHEST,
        preferred_element_type=jnp.float32,
    )
    small[...] = total
    packed = jnp.where(
        lanes_of(PACK) < CT, small[pl.ds(0, PACK, stride=2), :], small[pl.ds(1, PACK, stride=2), :]
    )
    for j in range(sums.shape[0]):
        sums[j] = packed


def unweave_kernel(vel, vel_u, vel_v, plain, sems):
    lane = lanes_of(HALF)
    edge = HALO // 2
    copies = []
    for i, out in enumerate((vel_u, vel_v)):
        mixed = vel[i, SIDE + TOP : SIDE + TOP + HALF, :]
        for band in range(2):
            rows = slice(HALF * band, HALF * (band + 1))
            even, odd = (vel[i, tile + TOP + HALF * band : tile + TOP + HALF * (band + 1), :] for tile in MAIN)
            for c in range(2):
                source = BAND * c + lane // 2
                cells = jnp.where(lane % 2 == 0, gather(even, source), gather(odd, source))
                if c == 0:
                    outer, side = lane < edge, turn(mixed, BAND * band + 3 * HALO, 0)
                else:
                    outer, side = lane >= LANES - edge, turn(mixed, BAND * band + edge, LANES - edge)
                plain[i, rows, c * LANES : (c + 1) * LANES] = jnp.where(outer, side, cells)
            copies.append(pltpu.make_async_copy(plain.at[i, rows], out.at[rows], sems.at[2 * i + band]))
            copies[-1].start()
    for copy in copies:
        copy.wait()


def pick_kernel(owners, gathered, own, other):
    owned = own.shape[0]
    first = lax.axis_index("gy") % 2 == 0
    total = []
    for block in range(2 * owned):
        parts = [jnp.where(owners[t, block : block + 1, :] > 0, gathered[t], 0.0) for t in range(owners.shape[0])]
        while len(parts) > 1:
            parts = [sum(parts[i : i + 2]) for i in range(0, len(parts), 2)]
        total.append(parts[0])
    for block in range(owned):
        low, high = total[block], total[block + owned]
        for out, cells in ((own, jnp.where(first, low, high)), (other, jnp.where(first, high, low))):
            for j in range(PACK):
                out[block : block + 1, j * LANES : (j + 1) * LANES] = cells[j : j + 1]


def in_vmem(count):
    return [pl.BlockSpec(memory_space=pltpu.VMEM)] * count


def in_smem(count):
    return [pl.BlockSpec(memory_space=pltpu.SMEM)] * count


def per_device(thickness, driving, observed, control, ice_mask, tile_block):
    f32 = jnp.float32
    rows, cols = lax.axis_size("gy"), lax.axis_size("gx")
    tile_block, ice_mask = tile_block[:, :, 0].T, ice_mask.T
    params = pltpu.CompilerParams(vmem_limit_bytes=VMEM_LIMIT)

    def shape(*sizes):
        return jax.ShapeDtypeStruct(sizes, f32)

    def swap(axis, cells_first, cells_second):
        count = lax.axis_size(axis)
        received = []
        for cells, low in ((cells_second, 1), (cells_first, 0)):
            pairs = [(i, i + 1) for i in range(low, count - 1, 2)]
            received.append(lax.ppermute(cells, axis, pairs + [(j, i) for i, j in pairs]))
        return received[1], received[0]

    fields = thickness, driving, observed
    owned = control.shape[0]
    *edges, parcels = pl.pallas_call(
        pack_kernel,
        out_shape=[shape(HALF, LANES)] * 2 + [shape(rows, PARCEL, LANES)],
        in_specs=[pl.BlockSpec(memory_space=pltpu.HBM)] * 5,
        out_specs=[pl.BlockSpec(memory_space=pltpu.HBM)] * 3,
        scratch_shapes=[
            pltpu.SMEM(tile_block.shape, jnp.int32),
            pltpu.VMEM((5, TILE, TILE), f32),
            pltpu.VMEM(control.shape, f32),
            pltpu.VMEM((owned, PACK, LANES), f32),
            pltpu.VMEM((rows, PARCEL, LANES), f32),
            pltpu.VMEM((2, HALF, LANES), f32),
            pltpu.SemaphoreType.DMA((10,)),
        ],
        compiler_params=pltpu.CompilerParams(vmem_limit_bytes=PACK_VMEM_LIMIT),
        name="pack",
    )(tile_block, control, *fields)
    parcels = lax.all_to_all(parcels, "gy", 0, 0, tiled=True)
    columns_in = swap("gx", *edges)
    woven, own_sides, strips = pl.pallas_call(
        weave_kernel,
        out_shape=[shape(5, 2, TILE, LANES), shape(5, HALF, LANES), shape(2, 3, 64, LANES)],
        in_specs=in_vmem(3),
        out_specs=in_vmem(3),
        compiler_params=params,
        name="weave",
    )(*fields)
    strips = pl.pallas_call(
        rows_kernel,
        out_shape=[shape(160, LANES)] * 2,
        in_specs=in_vmem(3),
        out_specs=in_vmem(2),
        compiler_params=params,
        name="rows",
    )(strips, *columns_in)
    rows_in = swap("gy", *strips)
    *friction, owners = pl.pallas_call(
        friction_kernel,
        out_shape=[shape(ALL_ROWS, LANES)] * 2
        + [jax.ShapeDtypeStruct((cols * rows // 2, 2 * owned, LANES), jnp.int32)],
        in_specs=in_smem(2) + in_vmem(1),
        out_specs=in_vmem(3),
        scratch_shapes=[pltpu.VMEM((PATCH, LANES), f32)],
        compiler_params=params,
        name="friction",
    )(tile_block, ice_mask, parcels)
    prepared = pl.pallas_call(
        setup_kernel,
        out_shape=[shape(5, ALL_ROWS, LANES), shape(2, ALL_ROWS, LANES)],
        in_specs=in_vmem(6),
        out_specs=in_vmem(2),
        scratch_shapes=[
            pltpu.VMEM((3, ALL_ROWS, LANES), f32),
            pltpu.VMEM((2, ALL_ROWS, LANES), f32),
            pltpu.VMEM((FACTORS, ALL_ROWS, LANES), f32),
        ],
        compiler_params=params,
        name="setup",
    )(*friction, woven, own_sides, *columns_in)

    vel, sums = pl.pallas_call(
        model_kernel,
        out_shape=(shape(2, ALL_ROWS, LANES), shape(cols * rows // 2, PACK, LANES)),
        in_specs=in_vmem(6),
        out_specs=in_vmem(2),
        scratch_shapes=[
            pltpu.VMEM((5, ALL_ROWS, LANES), f32),
            pltpu.VMEM((3, ALL_ROWS, LANES), f32),
            pltpu.VMEM((2, ALL_ROWS, LANES), f32),
            pltpu.VMEM((2, ALL_ROWS, LANES), f32),
            pltpu.VMEM((FACTORS, ALL_ROWS, LANES), f32),
            pltpu.VMEM((CT, LANES), f32),
        ],
        compiler_params=params,
        name="model",
    )(*friction, *prepared, *rows_in)
    vel_u, vel_v = pl.pallas_call(
        unweave_kernel,
        out_shape=[shape(TILE, TILE)] * 2,
        in_specs=in_vmem(1),
        out_specs=[pl.BlockSpec(memory_space=pltpu.HBM)] * 2,
        scratch_shapes=[pltpu.VMEM((2, TILE, TILE), f32), pltpu.SemaphoreType.DMA((4,))],
        compiler_params=params,
        name="unweave",
    )(vel)

    same_core = [[i * rows + j for i in range(cols) for j in range(core, rows, 2)] for core in range(2)]
    sums = lax.all_to_all(sums, ("gx", "gy"), 0, 0, tiled=True, axis_index_groups=same_core)
    own, other = pl.pallas_call(
        pick_kernel,
        out_shape=[shape(*control.shape)] * 2,
        in_specs=in_vmem(2),
        out_specs=in_vmem(2),
        compiler_params=params,
        name="pick",
    )(owners, sums)
    gradient = own + lax.ppermute(other, "gy", [(j, j ^ 1) for j in range(rows)])
    return vel_u, vel_v, gradient


def solution(mesh):
    return jax.shard_map(
        per_device,
        mesh=mesh,
        in_specs=(P("gy", "gx"), P(None, "gy", "gx"), P(None, "gy", "gx"), P("gy", None), P(), P()),
        out_specs=(P("gy", "gx"), P("gy", "gx"), P("gy", None)),
        check_vma=False,
    )
```

```python
from types import SimpleNamespace

import jax
import jax.numpy as jnp
from jax import lax
from jax.experimental import pallas as pl
from jax.experimental.pallas import tpu as pltpu
from jax.sharding import PartitionSpec as P

TILE = 256
PIC = 4
SW = 2
ADJ = 6
CT = 64
COARSE = 4096

LANES = 128
HALO = 16
OBS = 8
MARGIN = 8
TOP = MARGIN + HALO
ROWS = TILE + 2 * TOP
HALF = TILE // 2
SIDE = 2 * ROWS
BAND = LANES // 2
ALL_ROWS = SIDE + HALF + 2 * TOP
MAIN = (0, ROWS)
SIDES = (SIDE,)
SPANS = {
    "frame": (MARGIN, 2, 144, MARGIN, 80, 0, 0),
    "inner": (MARGIN + 8, 2, 136, MARGIN + 8, 72, 0, 0),
    "tile": (TOP, 2, 128, TOP, 64, 0, 0),
}
FACTORS = 14
AHEAD = 8
PACK = COARSE // LANES
VMEM_LIMIT = 24 * 1024 * 1024
PACK_VMEM_LIMIT = 62 * 1024 * 1024

STRIP = ((0, HALO), (HALO, HALO), (2 * HALO, HALO), (3 * HALO, OBS), (3 * HALO + OBS, OBS))

CONTROL = ((0, 0, PACK, 0), (-1, PACK - 2, 2, PACK), (1, 0, 2, PACK + 2))
FOLDED = 40
PARCEL = 48
PATCH = CT + 8

visc_scale = 0.1
strain_floor = 0.05


def lanes_of(rows):
    return lax.broadcasted_iota(jnp.int32, (rows, LANES), 1)


def is_even(axis):
    return lax.axis_index(axis) % 2 == 0


def side_lanes(rows, ds, group):
    place = (lanes_of(rows) - 8 * group) % CT
    return place < 4 if ds > 0 else place >= CT - 4


def fill_parcels(tile_block, owned_blocks, parcels):
    tile_cols, tile_rows = tile_block.shape
    owned = owned_blocks.shape[0]
    mine = lax.axis_index("gy") * owned
    col_tile = lax.axis_index("gx")

    def spread(row, carry):
        for ds in (-1, 0, 1):
            col = col_tile + ds
            place = tile_block[jnp.clip(col, 0, tile_cols - 1), row] - mine

            @pl.when((col >= 0) & (col < tile_cols) & (place >= 0) & (place < owned))
            def _():
                for dr, first, count, at in CONTROL:
                    target = row - dr

                    @pl.when((target >= 0) & (target < tile_rows))
                    def _():
                        if ds == 0:
                            parcels[target, at : at + count, :] = owned_blocks[place, first : first + count, :]
                            return
                        start = FOLDED + at % 8
                        rows = min(count, 8)
                        folded = parcels[target, start : start + rows, :]
                        for i in range(count // rows):
                            group = at // 8 + i
                            cells = owned_blocks[place, first + 8 * i : first + 8 * i + rows, :]
                            folded = jnp.where(side_lanes(rows, ds, group), turn(cells, 0, 8 * group), folded)
                        parcels[target, start : start + rows, :] = folded

        return carry

    lax.fori_loop(0, tile_rows, spread, 0)


def pack_kernel(
    table, control, thick, drive, obs, first_col, second_col, parcels,
    tile_block, held, held_control, owned_blocks, packed_parcels, packed_cols, sems,
):
    table_copy = pltpu.make_async_copy(table, tile_block, sems.at[9])
    table_copy.start()
    copies = [pltpu.make_async_copy(control, held_control, sems.at[5])]
    for f, field in enumerate((thick, drive.at[0], drive.at[1], obs.at[0], obs.at[1])):
        copies.append(pltpu.make_async_copy(field, held.at[f], sems.at[f]))
    for copy in copies:
        copy.start()
    packed_parcels[...] = jnp.zeros_like(packed_parcels)
    copies[0].wait()
    for j in range(PACK):
        owned_blocks[:, j, :] = held_control[:, j * LANES : (j + 1) * LANES]
    table_copy.wait()
    fill_parcels(tile_block, owned_blocks, packed_parcels)
    results = [pltpu.make_async_copy(packed_parcels, parcels, sems.at[6])]
    results[0].start()

    lane = lanes_of(HALF)
    left = jnp.zeros((HALF, LANES), jnp.float32)
    right = jnp.zeros((HALF, LANES), jnp.float32)
    for f, (first, count) in enumerate(STRIP):
        copies[1 + f].wait()
        for part in range(2):
            rows = slice(part * HALF, (part + 1) * HALF)
            start = part * BAND + first
            inside = (lane >= start) & (lane < start + count)
            left = jnp.where(inside, turn(held[f, rows, :LANES], 0, start), left)
            right = jnp.where(inside, turn(held[f, rows, LANES:], LANES - count, start), right)
    even = is_even("gx")
    packed_cols[0] = jnp.where(even, right, left)
    packed_cols[1] = jnp.where(even, left, right)
    for i, out in enumerate((first_col, second_col)):
        results.append(pltpu.make_async_copy(packed_cols.at[i], out, sems.at[7 + i]))
        results[-1].start()
    for copy in results:
        copy.wait()


def sides(axis, first_pair, second_pair):
    even = is_even(axis)
    return jnp.where(even, second_pair, first_pair), jnp.where(even, first_pair, second_pair)


def choose_side(lane, high, east, west, low):
    place = lane % BAND
    return jnp.where(
        place < HALO, high, jnp.where(place < 2 * HALO, east, jnp.where(place < 3 * HALO, west, low))
    )


def turn(cells, source, target):
    shift = (target - source) % LANES
    return pltpu.roll(cells, shift, 1) if shift else cells


def gather(cells, source):
    return jnp.take_along_axis(cells, source, axis=1)


def scale_of(f):
    return (0.25 * visc_scale * 4.0 ** (1.0 / 3.0), 0.5, 0.5, 1.0, 1.0)[f]


def weave_kernel(thick, drive, obs, woven, own_sides, edges):
    lane, half_lane = lanes_of(TILE), lanes_of(HALF)
    source = 2 * lane % LANES
    for f, (field, (first, count)) in enumerate(zip((thick, drive.at[0], drive.at[1], obs.at[0], obs.at[1]), STRIP)):
        low, high = scale_of(f) * field[:, :LANES], scale_of(f) * field[:, LANES:]
        tiles = [jnp.where(lane < BAND, gather(low, source + i), gather(high, source + i)) for i in range(2)]
        bands = []
        for band in (0, BAND):
            bands.append(
                jnp.where(lane % BAND < BAND // 2, turn(high, LANES - HALO, band), turn(low, 0, band + 3 * HALO))
            )
        own_sides[f] = jnp.where(half_lane < BAND, bands[0][:HALF], bands[1][HALF:])
        for c in range(2):
            woven[f, c] = tiles[c]
        for c, tile in enumerate(tiles + [bands[0]]):
            edges[0, c, first : first + count, :] = tile[:count]
            edges[1, c, first : first + count, :] = tile[TILE - count :]


def rows_kernel(edges, first_col, second_col, first_pair, second_pair):
    west, east = sides("gx", first_col[...], second_col[...])
    even = is_even("gy")
    for c in range(2):
        top, bottom = edges[0, c], edges[1, c]
        first_pair[64 * c : 64 * c + 64, :] = jnp.where(even, bottom, top)
        second_pair[64 * c : 64 * c + 64, :] = jnp.where(even, top, bottom)
    strips = []
    for i in range(2):
        fields = []
        for f, (first, count) in enumerate(STRIP):
            packed = slice(HALF - count, HALF) if i else slice(0, count)
            source = BAND * i + first
            target = BAND if f >= 2 else 0
            own = turn(edges[i, 2, first : first + count, :], 0, target)
            from_east = scale_of(f) * turn(east[packed], source, target + HALO)
            from_west = scale_of(f) * turn(west[packed], source, target + 3 * HALO - count)
            fields.append(choose_side(lanes_of(count), own, from_east, from_west, own))
        lane = lanes_of(HALO)
        lower = jnp.concatenate(fields[3:], axis=0)
        strips.append((jnp.where(lane < BAND, fields[0], fields[2]), jnp.where(lane < BAND, fields[1], lower)))
    for k in range(2):
        top, bottom = strips[0][k], strips[1][k]
        rows = slice(128 + HALO * k, 128 + HALO * (k + 1))
        first_pair[rows, :] = jnp.where(even, bottom, top)
        second_pair[rows, :] = jnp.where(even, top, bottom)


def shift_east(tiles):
    turned = pltpu.roll(tiles[0], LANES - 1, 1)
    return [turned] if len(tiles) == 1 else [tiles[1], turned]


def shift_west(tiles):
    turned = pltpu.roll(tiles[-1], 1, 1)
    return [turned] if len(tiles) == 1 else [turned, tiles[0]]


def run_groups(groups, read, work):
    pending = [read(*group) for group in groups[:AHEAD]]
    for k, (part, row, count) in enumerate(groups):
        if k + AHEAD < len(groups):
            pending.append(read(*groups[k + AHEAD]))
        for ref, lead, values in work(part, pending[k]):
            for tile, value in zip(part, values):
                ref[(*lead, pl.ds(row + tile, count), slice(None))] = value


def block_groups(row, main, side_row, side):
    step = 32 if main % 32 == 0 else 24
    first = side // 16 * 8 if side > 24 else side
    groups = [(MAIN, row + g, min(step, main - g)) for g in range(0, main, step)]
    groups[1:1] = [(SIDES, side_row, first)]
    if first < side:
        groups[3:3] = [(SIDES, side_row + first, side - first)]
    return groups


def over_rows(span, read, work):
    start, blocks, main, side_start, side, main_rest, side_rest = SPANS[span]

    def block(i, carry):
        row, side_row = pl.multiple_of(start + i * main, 8), pl.multiple_of(side_start + i * side, 8)
        run_groups(block_groups(row, main, side_row, side), read, work)
        return carry

    lax.fori_loop(0, blocks, block, 0)
    if main_rest:
        none = 8 * jnp.minimum(lax.axis_index("gx"), 0)
        row = pl.multiple_of(none + start + blocks * main, 8)
        side_row = pl.multiple_of(none + side_start + blocks * side, 8)
        run_groups(block_groups(row, main_rest, side_row, side_rest), read, work)


def over_ends(count, read, work):
    row = pl.multiple_of(MARGIN + 8 * jnp.minimum(lax.axis_index("gx"), 0), 8)
    far, side_far = TILE + 2 * HALO - count, HALF + 2 * HALO - count
    run_groups(
        [(MAIN, row, count), (SIDES, row, count), (MAIN, row + far, count), (SIDES, row + side_far, count)], read, work
    )


def join_parts(ref, leads, whole):
    edge = HALO // 2
    few = edge // 2
    frame = HALO if whole else 0
    first, count = TOP - frame, HALF + 2 * frame
    kept = HALF + frame
    lane = lanes_of(kept)
    outer = (lane < few) | (lane >= LANES - few)
    near = jnp.where(lane < few, 3 * HALO + 2 * lane, edge + 2 * (lane - LANES + few))
    near = jnp.clip(near, 0, LANES - 2 - BAND)
    side_lane = lanes_of(count)
    place = side_lane % BAND
    inner = jnp.clip(jnp.where(place < edge, LANES - edge + place // 2, place // 2 - 24), 0, LANES - 1)
    for lead in leads:
        def at(row, rows):
            return (*lead, slice(row, row + rows), slice(None))

        mixed = ref[at(SIDE + first, count)]
        halves = [[ref[at(tile + first + HALF * h, count)] for tile in MAIN] for h in range(2)]
        if whole:
            parts = [jnp.where(side_lane % 2 == 0, gather(even, inner), gather(odd, inner)) for even, odd in halves]
            wanted = (place < edge) | (place >= BAND - edge)
            ref[at(SIDE + first, count)] = jnp.where(wanted, jnp.where(side_lane < BAND, *parts), mixed)
        for h, skip in ((0, 0), (1, frame)):
            cells = mixed[skip : skip + kept]
            for c, tile in enumerate(MAIN):
                new = jnp.where(outer, gather(cells, near + (BAND * h + c)), halves[h][c][skip : skip + kept])
                ref[at(tile + first + HALF * h + skip, kept)] = new


def friction_kernel(tile_block, ice_mask, parcels, fr, ice, owners, patch):
    tile_cols, tile_rows = ice_mask.shape
    row_tile = lax.axis_index("gy")
    col_tile = lax.axis_index("gx")
    core = row_tile % 2
    place = lax.broadcasted_iota(jnp.int32, owners.shape[1:], 0)
    for t in range(owners.shape[0]):
        block = tile_block[t // (tile_rows // 2), t % (tile_rows // 2) * 2 + core]
        owners[t] = (place == block - (row_tile - core) * (owners.shape[1] // 2)).astype(jnp.int32)

    flat = sum(parcels[j] for j in range(tile_rows))
    folded = flat[FOLDED:]
    for dr, _, count, at in CONTROL:
        cells = flat[at : at + count]
        if dr == 0:
            side = jnp.concatenate([turn(folded, 8 * g, 0) for g in range(PACK // 8)], axis=0)
        else:
            side = turn(folded, PACK, 0)[at % 8 : at % 8 + count]
        inner = lanes_of(count) < CT
        row = 4 + {-1: -4, 0: 0, 1: CT}[dr]
        patch[pl.ds(row, count, stride=2), :] = jnp.where(inner, cells, turn(side, 0, CT))
        patch[pl.ds(row + 1, count, stride=2), :] = jnp.where(inner, turn(cells, 0, CT), side)

    cells = 0.5 * jnp.exp(patch[...])
    lane = lanes_of(PATCH)
    wide = gather(cells, lane // 2)
    for tile in MAIN:
        for j in range(4):
            fr[pl.ds(tile + MARGIN + j, PATCH, stride=4), :] = wide
    lane = lanes_of(40)
    place = lane % BAND // 4
    source = jnp.where(place < 8, 60 + place, (116 + place) % LANES)
    wide = jnp.where(
        lane < BAND,
        gather(cells[:40], source),
        gather(cells[PATCH - 40 :], source),
    )
    for j in range(4):
        fr[pl.ds(SIDE + MARGIN + j, 40, stride=4), :] = wide

    side_ice = []
    for dr, first, count in ((-1, MARGIN, HALO), (0, TOP, TILE), (1, TOP + TILE, HALO)):
        masks = []
        for ds in (-1, 0, 1):
            row, col = row_tile + dr, col_tile + ds
            inside = (row >= 0) & (row < tile_rows) & (col >= 0) & (col < tile_cols)
            row = jnp.clip(row, 0, tile_rows - 1)
            col = jnp.clip(col, 0, tile_cols - 1)
            masks.append(jnp.where(inside, ice_mask[col, row], 0).astype(jnp.float32))
        for c in range(2):
            ice[MAIN[c] + first : MAIN[c] + first + count, :] = jnp.full((count, LANES), masks[1])
        side_ice.append(choose_side(lanes_of(HALO), masks[1], masks[2], masks[0], masks[1]))
    upper = lanes_of(HALO) < BAND
    for i in range(HALF // HALO):
        ice[SIDE + TOP + i * HALO : SIDE + TOP + (i + 1) * HALO, :] = side_ice[1]
    ice[SIDE + MARGIN : SIDE + TOP, :] = jnp.where(upper, side_ice[0], side_ice[1])
    ice[SIDE + TOP + HALF : SIDE + TOP + HALF + HALO, :] = jnp.where(upper, side_ice[1], side_ice[2])


def make_stages(ext, fr, ice, visc, vel_a, vel_b, coef):
    def load(ref, part, row, count, *lead):
        return [ref[(*lead, pl.ds(row + tile, count), slice(None))] for tile in part]

    def load_around(part, row, count, now):
        return [load(now, part, r, count, i) for i in range(2) for r in (row, row - 1, row + 1)]

    def load_right(part, row, count):
        return [load(ext, part, row, count, i) for i in (1, 2)]

    def read_thickness(part, row, count):
        return load(ext, part, row, count, 0)

    def keep_viscosity(q):
        return [(visc, (0,), q), (visc, (1,), shift_west(q)), (visc, (2,), shift_east(q))]

    def first_viscosity(part, thickness):
        factor = (4.0 * strain_floor) ** (-1.0 / 3.0)
        return keep_viscosity([factor * t for t in thickness])

    def read_viscosity(part, row, count):
        return read_thickness(part, row, count), load_around(part, row, count, vel_b)

    def viscosity(part, read):
        thickness, (u, u_n, u_s, v, v_n, v_s) = read
        u_e, u_w = shift_east(u), shift_west(u)
        v_e, v_w = shift_east(v), shift_west(v)
        result = []
        for c in range(len(part)):
            ux, vx = u_e[c] - u_w[c], v_e[c] - v_w[c]
            uy, vy = u_s[c] - u_n[c], v_s[c] - v_n[c]
            shear = uy + vx
            strain = (ux * (ux + vy) + vy * vy) + (0.25 * (shear * shear) + 4.0 * strain_floor)
            result.append(thickness[c] * jnp.exp(jnp.log(strain) * (-1.0 / 3.0)))
        return keep_viscosity(result)

    def inverse(x):
        near = pl.reciprocal(x, approx=True)
        return near * (2.0 - x * near)

    def read_coefficients(part, row, count):
        around = [load(visc, part, r, count, i) for i in range(3) for r in (row, row - 1, row + 1)]
        return around + [load(fr, part, row, count), load(ice, part, row, count)]

    def coefficients(part, read):
        tiles = range(len(part))
        q, q_n, q_s, q_w, q_nw, q_sw, q_e, q_ne, q_se, friction, mask = read
        w = [q[c] + q_w[c] for c in tiles]
        e = [q[c] + q_e[c] for c in tiles]
        s = [q[c] + q_s[c] for c in tiles]
        n = [q[c] + q_n[c] for c in tiles]
        scale_u, scale_v = [], []
        for c in tiles:
            across, along = e[c] + w[c], s[c] + n[c]
            scale_u.append(mask[c] * inverse(friction[c] + along + 4.0 * across))
            scale_v.append(mask[c] * inverse(friction[c] + across + 4.0 * along))
        corners = []
        half = [0.5 * q[c] for c in tiles]
        for shifted in (q_sw, q_nw, q_se, q_ne):
            corners.append([q[c] + 0.5 * shifted[c] for c in tiles])
            corners.append([half[c] + shifted[c] for c in tiles])
        return [e, w, s, n, scale_u, scale_v] + corners

    def relax(part, k, around, right):
        tiles = range(len(part))
        e, w, s, n, scale_u, scale_v, sw_u, sw_v, nw_u, nw_v, se_u, se_v, ne_u, ne_v = k
        u, u_n, u_s, v, v_n, v_s = around
        to_west_u, to_east_u, to_west_v, to_east_v = [], [], [], []
        for c in tiles:
            u4 = 4.0 * u[c]
            to_west_u.append(w[c] * u4 + (sw_u[c] * v_s[c] - nw_u[c] * v_n[c]))
            to_east_u.append(e[c] * u4 + (ne_u[c] * v_n[c] - se_u[c] * v_s[c]))
            to_west_v.append(w[c] * v[c] + (sw_v[c] * u_s[c] - nw_v[c] * u_n[c]))
            to_east_v.append(e[c] * v[c] + (ne_v[c] * u_n[c] - se_v[c] * u_s[c]))
        to_west_u, to_west_v = shift_east(to_west_u), shift_east(to_west_v)
        to_east_u, to_east_v = shift_west(to_east_u), shift_west(to_east_v)
        new_u, new_v = [], []
        for c in tiles:
            mid_u = s[c] * u_s[c] + n[c] * u_n[c]
            mid_v = 4.0 * (s[c] * v_s[c] + n[c] * v_n[c])
            new_u.append(scale_u[c] * (right[0][c] + mid_u + (to_west_u[c] + to_east_u[c])))
            new_v.append(scale_v[c] * (right[1][c] + mid_v + (to_west_v[c] + to_east_v[c])))
        return new_u, new_v

    def put(new, values):
        return [(new, (i,), values[i]) for i in range(2)]

    def keep(k):
        return [(coef, (i,), k[i]) for i in range(FACTORS)]

    def read_sweep(now):
        def read(part, row, count):
            k = [load(coef, part, row, count, i) for i in range(FACTORS)]
            return k, load_around(part, row, count, now), load_right(part, row, count)

        return read

    def sweep(new):
        return lambda part, read: put(new, relax(part, *read))

    def read_first(part, row, count):
        return read_coefficients(part, row, count), load_right(part, row, count)

    def first_start(part, read):
        k = coefficients(part, read[0])
        return keep(k) + put(vel_a, [[a * b for a, b in zip(k[4 + i], read[1][i])] for i in range(2)])

    def read_start(part, row, count):
        return (*read_first(part, row, count), load_around(part, row, count, vel_b))

    def start(part, read):
        k = coefficients(part, read[0])
        return keep(k) + put(vel_a, relax(part, k, read[2], read[1]))

    return SimpleNamespace(**locals())


def setup_kernel(
    fr, ice, woven, own_sides, first_col, second_col,
    ext, vel_b,
    visc, vel_a, coef,
):
    west, east = sides("gx", first_col[...], second_col[...])
    lane = lanes_of(HALF)
    for f, (first, count) in enumerate(STRIP):
        for c in range(2):
            ext[f, MAIN[c] + TOP : MAIN[c] + TOP + TILE, :] = woven[f, c]
        from_east = scale_of(f) * turn(east, first, HALO)
        from_west = scale_of(f) * turn(west, first, 3 * HALO - count)
        own = own_sides[f]
        ext[f, SIDE + TOP : SIDE + TOP + HALF, :] = choose_side(lane, own, from_east, from_west, own)
    step = make_stages(ext, fr, ice, visc, vel_a, vel_b, coef)
    over_rows("tile", step.read_thickness, step.first_viscosity)
    over_rows("tile", step.read_first, step.first_start)
    over_rows("tile", step.read_sweep(vel_a), step.sweep(vel_b))


def model_kernel(
    fr, ice, ext_in, vel_in, first_row, second_row,
    vel_b, sums,
    ext, visc, vel_a, vel_c, coef, small,
):
    ext[...] = ext_in[...]
    vel_b[...] = vel_in[...]
    north, south = sides("gy", first_row[...], second_row[...])
    here = SIDE + TOP
    for f, (first, count) in enumerate(STRIP):
        for c in range(2):
            rows = slice(64 * c + first, 64 * c + first + count)
            ext[f, MAIN[c] + TOP - count : MAIN[c] + TOP, :] = north[rows]
            ext[f, MAIN[c] + TOP + TILE : MAIN[c] + TOP + TILE + count, :] = south[rows]
        rows = slice(128 + first % 32, 128 + first % 32 + count)
        source = BAND if f >= 2 else 0
        upper = lanes_of(count) < BAND
        above = turn(ext_in[f, here + HALF - count : here + HALF, :], 0, BAND)
        below = turn(ext_in[f, here : here + count, :], 0, BAND)
        ext[f, here - count : here, :] = jnp.where(upper, turn(north[rows], source, 0), above)
        ext[f, here + HALF : here + HALF + count, :] = jnp.where(upper, below, turn(south[rows], source, BAND))

    step = make_stages(ext, fr, ice, visc, vel_a, vel_b, coef)
    over_ends(32, step.read_thickness, step.first_viscosity)
    over_ends(32, step.read_first, step.first_start)
    over_ends(24, step.read_sweep(vel_a), step.sweep(vel_b))

    def iteration(i, carry):
        over_rows("frame", step.read_viscosity, step.viscosity)
        over_rows("frame", step.read_start, step.start)
        over_rows("frame", step.read_sweep(vel_a), step.sweep(vel_b))
        return carry

    lax.fori_loop(1, PIC - 1, iteration, 0)
    join_parts(vel_b, ((0,), (1,)), True)
    over_rows("inner", step.read_viscosity, step.viscosity)
    over_rows("inner", step.read_start, step.start)

    load = step.load

    def read_last(part, row, count):
        return (*step.read_sweep(vel_a)(part, row, count), [load(ext, part, row, count, 3 + i) for i in range(2)])

    def last_sweep(part, read):
        k, around, right, seen = read
        new = step.relax(part, k, around, right)
        misfit = [[0.5 * (a - b) for a, b in zip(new[i], seen[i])] for i in range(2)]
        first = [[a * b for a, b in zip(k[4 + i], misfit[i])] for i in range(2)]
        return step.put(vel_b, new) + step.put(vel_c, first) + [(ext, (1 + i,), misfit[i]) for i in range(2)]

    over_rows("inner", read_last, last_sweep)

    def two_sweeps(i, carry):
        over_rows("inner", step.read_sweep(vel_c), step.sweep(vel_a))
        over_rows("inner", step.read_sweep(vel_a), step.sweep(vel_c))
        return carry

    lax.fori_loop(0, (ADJ - 2) // 2, two_sweeps, 0)

    def read_gradient(part, row, count):
        others = [load(vel_b, part, row, count, i) for i in range(2)] + [load(fr, part, row, count)]
        return (*step.read_sweep(vel_c)(part, row, count), others)

    def gradient(part, read):
        k, around, right, (u, v, friction) = read
        lu, lv = step.relax(part, k, around, right)
        return [(visc, (0,), [-2.0 * friction[c] * (u[c] * lu[c] + v[c] * lv[c]) for c in range(len(part))])]

    over_rows("tile", read_gradient, gradient)
    join_parts(visc, ((0,),), False)
    down = sum(visc[0, pl.ds(tile + TOP + j, CT, stride=4), :] for tile in MAIN for j in range(4))
    k = lax.broadcasted_iota(jnp.int32, (LANES, LANES), 0)
    total = jnp.dot(
        down,
        (k // 2 == lanes_of(LANES) % CT).astype(jnp.float32),
        precision=lax.Precision.HIGHEST,
        preferred_element_type=jnp.float32,
    )
    small[...] = total
    packed = jnp.where(
        lanes_of(PACK) < CT, small[pl.ds(0, PACK, stride=2), :], small[pl.ds(1, PACK, stride=2), :]
    )
    for j in range(sums.shape[0]):
        sums[j] = packed


def unweave_kernel(vel, vel_u, vel_v, plain, sems):
    lane = lanes_of(HALF)
    edge = HALO // 2
    copies = []
    for i, out in enumerate((vel_u, vel_v)):
        mixed = vel[i, SIDE + TOP : SIDE + TOP + HALF, :]
        for band in range(2):
            rows = slice(HALF * band, HALF * (band + 1))
            even, odd = (vel[i, tile + TOP + HALF * band : tile + TOP + HALF * (band + 1), :] for tile in MAIN)
            for c in range(2):
                source = BAND * c + lane // 2
                cells = jnp.where(lane % 2 == 0, gather(even, source), gather(odd, source))
                if c == 0:
                    outer, side = lane < edge, turn(mixed, BAND * band + 3 * HALO, 0)
                else:
                    outer, side = lane >= LANES - edge, turn(mixed, BAND * band + edge, LANES - edge)
                plain[i, rows, c * LANES : (c + 1) * LANES] = jnp.where(outer, side, cells)
            copies.append(pltpu.make_async_copy(plain.at[i, rows], out.at[rows], sems.at[2 * i + band]))
            copies[-1].start()
    for copy in copies:
        copy.wait()


def pick_kernel(owners, gathered, own, other):
    owned = own.shape[0]
    first = lax.axis_index("gy") % 2 == 0
    total = []
    for block in range(2 * owned):
        parts = [jnp.where(owners[t, block : block + 1, :] > 0, gathered[t], 0.0) for t in range(owners.shape[0])]
        while len(parts) > 1:
            parts = [sum(parts[i : i + 2]) for i in range(0, len(parts), 2)]
        total.append(parts[0])
    for block in range(owned):
        low, high = total[block], total[block + owned]
        for out, cells in ((own, jnp.where(first, low, high)), (other, jnp.where(first, high, low))):
            for j in range(PACK):
                out[block : block + 1, j * LANES : (j + 1) * LANES] = cells[j : j + 1]


def in_vmem(count):
    return [pl.BlockSpec(memory_space=pltpu.VMEM)] * count


def in_smem(count):
    return [pl.BlockSpec(memory_space=pltpu.SMEM)] * count


def per_device(thickness, driving, observed, control, ice_mask, tile_block):
    f32 = jnp.float32
    rows, cols = lax.axis_size("gy"), lax.axis_size("gx")
    tile_block, ice_mask = tile_block[:, :, 0].T, ice_mask.T
    params = pltpu.CompilerParams(vmem_limit_bytes=VMEM_LIMIT)

    def shape(*sizes):
        return jax.ShapeDtypeStruct(sizes, f32)

    def swap(axis, cells_first, cells_second):
        count = lax.axis_size(axis)
        received = []
        for cells, low in ((cells_second, 1), (cells_first, 0)):
            pairs = [(i, i + 1) for i in range(low, count - 1, 2)]
            received.append(lax.ppermute(cells, axis, pairs + [(j, i) for i, j in pairs]))
        return received[1], received[0]

    fields = thickness, driving, observed
    owned = control.shape[0]
    *edges, parcels = pl.pallas_call(
        pack_kernel,
        out_shape=[shape(HALF, LANES)] * 2 + [shape(rows, PARCEL, LANES)],
        in_specs=[pl.BlockSpec(memory_space=pltpu.HBM)] * 5,
        out_specs=[pl.BlockSpec(memory_space=pltpu.HBM)] * 3,
        scratch_shapes=[
            pltpu.SMEM(tile_block.shape, jnp.int32),
            pltpu.VMEM((5, TILE, TILE), f32),
            pltpu.VMEM(control.shape, f32),
            pltpu.VMEM((owned, PACK, LANES), f32),
            pltpu.VMEM((rows, PARCEL, LANES), f32),
            pltpu.VMEM((2, HALF, LANES), f32),
            pltpu.SemaphoreType.DMA((10,)),
        ],
        compiler_params=pltpu.CompilerParams(vmem_limit_bytes=PACK_VMEM_LIMIT),
        name="pack",
    )(tile_block, control, *fields)
    parcels = lax.all_to_all(parcels, "gy", 0, 0, tiled=True)
    columns_in = swap("gx", *edges)
    woven, own_sides, strips = pl.pallas_call(
        weave_kernel,
        out_shape=[shape(5, 2, TILE, LANES), shape(5, HALF, LANES), shape(2, 3, 64, LANES)],
        in_specs=in_vmem(3),
        out_specs=in_vmem(3),
        compiler_params=params,
        name="weave",
    )(*fields)
    strips = pl.pallas_call(
        rows_kernel,
        out_shape=[shape(160, LANES)] * 2,
        in_specs=in_vmem(3),
        out_specs=in_vmem(2),
        compiler_params=params,
        name="rows",
    )(strips, *columns_in)
    rows_in = swap("gy", *strips)
    *friction, owners = pl.pallas_call(
        friction_kernel,
        out_shape=[shape(ALL_ROWS, LANES)] * 2
        + [jax.ShapeDtypeStruct((cols * rows // 2, 2 * owned, LANES), jnp.int32)],
        in_specs=in_smem(2) + in_vmem(1),
        out_specs=in_vmem(3),
        scratch_shapes=[pltpu.VMEM((PATCH, LANES), f32)],
        compiler_params=params,
        name="friction",
    )(tile_block, ice_mask, parcels)
    prepared = pl.pallas_call(
        setup_kernel,
        out_shape=[shape(5, ALL_ROWS, LANES), shape(2, ALL_ROWS, LANES)],
        in_specs=in_vmem(6),
        out_specs=in_vmem(2),
        scratch_shapes=[
            pltpu.VMEM((3, ALL_ROWS, LANES), f32),
            pltpu.VMEM((2, ALL_ROWS, LANES), f32),
            pltpu.VMEM((FACTORS, ALL_ROWS, LANES), f32),
        ],
        compiler_params=params,
        name="setup",
    )(*friction, woven, own_sides, *columns_in)

    vel, sums = pl.pallas_call(
        model_kernel,
        out_shape=(shape(2, ALL_ROWS, LANES), shape(cols * rows // 2, PACK, LANES)),
        in_specs=in_vmem(6),
        out_specs=in_vmem(2),
        scratch_shapes=[
            pltpu.VMEM((5, ALL_ROWS, LANES), f32),
            pltpu.VMEM((3, ALL_ROWS, LANES), f32),
            pltpu.VMEM((2, ALL_ROWS, LANES), f32),
            pltpu.VMEM((2, ALL_ROWS, LANES), f32),
            pltpu.VMEM((FACTORS, ALL_ROWS, LANES), f32),
            pltpu.VMEM((CT, LANES), f32),
        ],
        compiler_params=params,
        name="model",
    )(*friction, *prepared, *rows_in)
    vel_u, vel_v = pl.pallas_call(
        unweave_kernel,
        out_shape=[shape(TILE, TILE)] * 2,
        in_specs=in_vmem(1),
        out_specs=[pl.BlockSpec(memory_space=pltpu.HBM)] * 2,
        scratch_shapes=[pltpu.VMEM((2, TILE, TILE), f32), pltpu.SemaphoreType.DMA((4,))],
        compiler_params=params,
        name="unweave",
    )(vel)

    same_core = [[i * rows + j for i in range(cols) for j in range(core, rows, 2)] for core in range(2)]
    sums = lax.all_to_all(sums, ("gx", "gy"), 0, 0, tiled=True, axis_index_groups=same_core)
    own, other = pl.pallas_call(
        pick_kernel,
        out_shape=[shape(*control.shape)] * 2,
        in_specs=in_vmem(2),
        out_specs=in_vmem(2),
        compiler_params=params,
        name="pick",
    )(owners, sums)
    gradient = own + lax.ppermute(other, "gy", [(j, j ^ 1) for j in range(rows)])
    return vel_u, vel_v, gradient


def solution(mesh):
    return jax.shard_map(
        per_device,
        mesh=mesh,
        in_specs=(P("gy", "gx"), P(None, "gy", "gx"), P(None, "gy", "gx"), P("gy", None), P(), P()),
        out_specs=(P("gy", "gx"), P("gy", "gx"), P("gy", None)),
        check_vma=False,
    )
```

```python
from types import SimpleNamespace

import jax
import jax.numpy as jnp
from jax import lax
from jax.experimental import pallas as pl
from jax.experimental.pallas import tpu as pltpu
from jax.sharding import PartitionSpec as P

TILE = 256
PIC = 4
SW = 2
ADJ = 6
CT = 64
COARSE = 4096

LANES = 128
HALO = 16
OBS = 8
MARGIN = 8
TOP = MARGIN + HALO
ROWS = TILE + 2 * TOP
HALF = TILE // 2
SIDE = 2 * ROWS
BAND = LANES // 2
ALL_ROWS = SIDE + HALF + 2 * TOP
MAIN = (0, ROWS)
SIDES = (SIDE,)
SPANS = {
    "frame": (MARGIN, 2, 144, MARGIN, 80, 0, 0),
    "inner": (MARGIN + 8, 2, 136, MARGIN + 8, 72, 0, 0),
    "tile": (TOP, 2, 128, TOP, 64, 0, 0),
}
FACTORS = 14
AHEAD = 8
PACK = COARSE // LANES
VMEM_LIMIT = 24 * 1024 * 1024
PACK_VMEM_LIMIT = 62 * 1024 * 1024

STRIP = ((0, HALO), (HALO, HALO), (2 * HALO, HALO), (3 * HALO, OBS), (3 * HALO + OBS, OBS))

CONTROL = ((0, 0, PACK, 0), (-1, PACK - 2, 2, PACK), (1, 0, 2, PACK + 2))
FOLDED = 40
PARCEL = 48
PATCH = CT + 8

visc_scale = 0.1
strain_floor = 0.05


def lanes_of(rows):
    return lax.broadcasted_iota(jnp.int32, (rows, LANES), 1)


def is_even(axis):
    return lax.axis_index(axis) % 2 == 0


def side_lanes(rows, ds, group):
    place = (lanes_of(rows) - 8 * group) % CT
    return place < 4 if ds > 0 else place >= CT - 4


def fill_parcels(tile_block, owned_blocks, parcels):
    tile_cols, tile_rows = tile_block.shape
    owned = owned_blocks.shape[0]
    mine = lax.axis_index("gy") * owned
    col_tile = lax.axis_index("gx")

    def spread(row, carry):
        for ds in (-1, 0, 1):
            col = col_tile + ds
            place = tile_block[jnp.clip(col, 0, tile_cols - 1), row] - mine

            @pl.when((col >= 0) & (col < tile_cols) & (place >= 0) & (place < owned))
            def _():
                for dr, first, count, at in CONTROL:
                    target = row - dr

                    @pl.when((target >= 0) & (target < tile_rows))
                    def _():
                        if ds == 0:
                            parcels[target, at : at + count, :] = owned_blocks[place, first : first + count, :]
                            return
                        start = FOLDED + at % 8
                        rows = min(count, 8)
                        folded = parcels[target, start : start + rows, :]
                        for i in range(count // rows):
                            group = at // 8 + i
                            cells = owned_blocks[place, first + 8 * i : first + 8 * i + rows, :]
                            folded = jnp.where(side_lanes(rows, ds, group), turn(cells, 0, 8 * group), folded)
                        parcels[target, start : start + rows, :] = folded

        return carry

    lax.fori_loop(0, tile_rows, spread, 0)


def pack_kernel(
    table, control, thick, drive, obs, first_col, second_col, parcels,
    tile_block, held, held_control, owned_blocks, packed_parcels, packed_cols, sems,
):
    table_copy = pltpu.make_async_copy(table, tile_block, sems.at[9])
    table_copy.start()
    copies = [pltpu.make_async_copy(control, held_control, sems.at[5])]
    for f, field in enumerate((thick, drive.at[0], drive.at[1], obs.at[0], obs.at[1])):
        copies.append(pltpu.make_async_copy(field, held.at[f], sems.at[f]))
    for copy in copies:
        copy.start()
    packed_parcels[...] = jnp.zeros_like(packed_parcels)
    copies[0].wait()
    shard = [held_control[:, j * LANES : (j + 1) * LANES] for j in range(PACK)]
    for j in range(PACK):
        owned_blocks[:, j, :] = shard[j]
    table_copy.wait()
    fill_parcels(tile_block, owned_blocks, packed_parcels)
    results = [pltpu.make_async_copy(packed_parcels, parcels, sems.at[6])]
    results[0].start()

    lane = lanes_of(HALF)
    left = jnp.zeros((HALF, LANES), jnp.float32)
    right = jnp.zeros((HALF, LANES), jnp.float32)
    for f, (first, count) in enumerate(STRIP):
        copies[1 + f].wait()
        for part in range(2):
            rows = slice(part * HALF, (part + 1) * HALF)
            start = part * BAND + first
            inside = (lane >= start) & (lane < start + count)
            left = jnp.where(inside, turn(held[f, rows, :LANES], 0, start), left)
            right = jnp.where(inside, turn(held[f, rows, LANES:], LANES - count, start), right)
    even = is_even("gx")
    packed_cols[0] = jnp.where(even, right, left)
    packed_cols[1] = jnp.where(even, left, right)
    for i, out in enumerate((first_col, second_col)):
        results.append(pltpu.make_async_copy(packed_cols.at[i], out, sems.at[7 + i]))
        results[-1].start()
    for copy in results:
        copy.wait()


def sides(axis, first_pair, second_pair):
    even = is_even(axis)
    return jnp.where(even, second_pair, first_pair), jnp.where(even, first_pair, second_pair)


def choose_side(lane, high, east, west, low):
    place = lane % BAND
    return jnp.where(
        place < HALO, high, jnp.where(place < 2 * HALO, east, jnp.where(place < 3 * HALO, west, low))
    )


def turn(cells, source, target):
    shift = (target - source) % LANES
    return pltpu.roll(cells, shift, 1) if shift else cells


def gather(cells, source):
    return jnp.take_along_axis(cells, source, axis=1)


def scale_of(f):
    return (0.25 * visc_scale * 4.0 ** (1.0 / 3.0), 0.5, 0.5, 1.0, 1.0)[f]


def weave_kernel(thick, drive, obs, woven, own_sides, edges):
    lane, half_lane = lanes_of(TILE), lanes_of(HALF)
    source = 2 * lane % LANES
    for f, (field, (first, count)) in enumerate(zip((thick, drive.at[0], drive.at[1], obs.at[0], obs.at[1]), STRIP)):
        low, high = scale_of(f) * field[:, :LANES], scale_of(f) * field[:, LANES:]
        tiles = [jnp.where(lane < BAND, gather(low, source + i), gather(high, source + i)) for i in range(2)]
        bands = []
        for band in (0, BAND):
            bands.append(
                jnp.where(lane % BAND < BAND // 2, turn(high, LANES - HALO, band), turn(low, 0, band + 3 * HALO))
            )
        own_sides[f] = jnp.where(half_lane < BAND, bands[0][:HALF], bands[1][HALF:])
        for c in range(2):
            woven[f, c] = tiles[c]
        for c, tile in enumerate(tiles + [bands[0]]):
            edges[0, c, first : first + count, :] = tile[:count]
            edges[1, c, first : first + count, :] = tile[TILE - count :]


def rows_kernel(edges, first_col, second_col, first_pair, second_pair):
    west, east = sides("gx", first_col[...], second_col[...])
    even = is_even("gy")
    for c in range(2):
        top, bottom = edges[0, c], edges[1, c]
        first_pair[64 * c : 64 * c + 64, :] = jnp.where(even, bottom, top)
        second_pair[64 * c : 64 * c + 64, :] = jnp.where(even, top, bottom)
    strips = []
    for i in range(2):
        fields = []
        for f, (first, count) in enumerate(STRIP):
            packed = slice(HALF - count, HALF) if i else slice(0, count)
            source = BAND * i + first
            target = BAND if f >= 2 else 0
            own = turn(edges[i, 2, first : first + count, :], 0, target)
            from_east = scale_of(f) * turn(east[packed], source, target + HALO)
            from_west = scale_of(f) * turn(west[packed], source, target + 3 * HALO - count)
            fields.append(choose_side(lanes_of(count), own, from_east, from_west, own))
        lane = lanes_of(HALO)
        lower = jnp.concatenate(fields[3:], axis=0)
        strips.append((jnp.where(lane < BAND, fields[0], fields[2]), jnp.where(lane < BAND, fields[1], lower)))
    for k in range(2):
        top, bottom = strips[0][k], strips[1][k]
        rows = slice(128 + HALO * k, 128 + HALO * (k + 1))
        first_pair[rows, :] = jnp.where(even, bottom, top)
        second_pair[rows, :] = jnp.where(even, top, bottom)


def shift_east(tiles):
    turned = pltpu.roll(tiles[0], LANES - 1, 1)
    return [turned] if len(tiles) == 1 else [tiles[1], turned]


def shift_west(tiles):
    turned = pltpu.roll(tiles[-1], 1, 1)
    return [turned] if len(tiles) == 1 else [turned, tiles[0]]


def run_groups(groups, read, work):
    pending = [read(*group) for group in groups[:AHEAD]]
    for k, (part, row, count) in enumerate(groups):
        if k + AHEAD < len(groups):
            pending.append(read(*groups[k + AHEAD]))
        for ref, lead, values in work(part, pending[k]):
            for tile, value in zip(part, values):
                ref[(*lead, pl.ds(row + tile, count), slice(None))] = value


def block_groups(row, main, side_row, side):
    step = 32 if main % 32 == 0 else 24
    first = side // 16 * 8 if side > 24 else side
    groups = [(MAIN, row + g, min(step, main - g)) for g in range(0, main, step)]
    groups[1:1] = [(SIDES, side_row, first)]
    if first < side:
        groups[3:3] = [(SIDES, side_row + first, side - first)]
    return groups


def over_rows(span, read, work):
    start, blocks, main, side_start, side, main_rest, side_rest = SPANS[span]

    def block(i, carry):
        row, side_row = pl.multiple_of(start + i * main, 8), pl.multiple_of(side_start + i * side, 8)
        run_groups(block_groups(row, main, side_row, side), read, work)
        return carry

    lax.fori_loop(0, blocks, block, 0)
    if main_rest:
        none = 8 * jnp.minimum(lax.axis_index("gx"), 0)
        row = pl.multiple_of(none + start + blocks * main, 8)
        side_row = pl.multiple_of(none + side_start + blocks * side, 8)
        run_groups(block_groups(row, main_rest, side_row, side_rest), read, work)


def over_ends(count, read, work):
    row = pl.multiple_of(MARGIN + 8 * jnp.minimum(lax.axis_index("gx"), 0), 8)
    far, side_far = TILE + 2 * HALO - count, HALF + 2 * HALO - count
    run_groups(
        [(MAIN, row, count), (SIDES, row, count), (MAIN, row + far, count), (SIDES, row + side_far, count)], read, work
    )


def join_parts(ref, leads, whole):
    edge = HALO // 2
    few = edge // 2
    frame = HALO if whole else 0
    first, count = TOP - frame, HALF + 2 * frame
    kept = HALF + frame
    lane = lanes_of(kept)
    outer = (lane < few) | (lane >= LANES - few)
    near = jnp.where(lane < few, 3 * HALO + 2 * lane, edge + 2 * (lane - LANES + few))
    near = jnp.clip(near, 0, LANES - 2 - BAND)
    side_lane = lanes_of(count)
    place = side_lane % BAND
    inner = jnp.clip(jnp.where(place < edge, LANES - edge + place // 2, place // 2 - 24), 0, LANES - 1)
    for lead in leads:
        def at(row, rows):
            return (*lead, slice(row, row + rows), slice(None))

        mixed = ref[at(SIDE + first, count)]
        halves = [[ref[at(tile + first + HALF * h, count)] for tile in MAIN] for h in range(2)]
        if whole:
            parts = [jnp.where(side_lane % 2 == 0, gather(even, inner), gather(odd, inner)) for even, odd in halves]
            wanted = (place < edge) | (place >= BAND - edge)
            ref[at(SIDE + first, count)] = jnp.where(wanted, jnp.where(side_lane < BAND, *parts), mixed)
        for h, skip in ((0, 0), (1, frame)):
            cells = mixed[skip : skip + kept]
            for c, tile in enumerate(MAIN):
                new = jnp.where(outer, gather(cells, near + (BAND * h + c)), halves[h][c][skip : skip + kept])
                ref[at(tile + first + HALF * h + skip, kept)] = new


def friction_kernel(tile_block, ice_mask, parcels, fr, ice, owners, patch):
    tile_cols, tile_rows = ice_mask.shape
    row_tile = lax.axis_index("gy")
    col_tile = lax.axis_index("gx")
    core = row_tile % 2
    place = lax.broadcasted_iota(jnp.int32, owners.shape[1:], 0)
    for t in range(owners.shape[0]):
        block = tile_block[t // (tile_rows // 2), t % (tile_rows // 2) * 2 + core]
        owners[t] = (place == block - (row_tile - core) * (owners.shape[1] // 2)).astype(jnp.int32)

    flat = sum(parcels[j] for j in range(tile_rows))
    folded = flat[FOLDED:]
    for dr, _, count, at in CONTROL:
        cells = flat[at : at + count]
        if dr == 0:
            side = jnp.concatenate([turn(folded, 8 * g, 0) for g in range(PACK // 8)], axis=0)
        else:
            side = turn(folded, PACK, 0)[at % 8 : at % 8 + count]
        inner = lanes_of(count) < CT
        row = 4 + {-1: -4, 0: 0, 1: CT}[dr]
        patch[pl.ds(row, count, stride=2), :] = jnp.where(inner, cells, turn(side, 0, CT))
        patch[pl.ds(row + 1, count, stride=2), :] = jnp.where(inner, turn(cells, 0, CT), side)

    cells = 0.5 * jnp.exp(patch[...])
    lane = lanes_of(PATCH)
    wide = gather(cells, lane // 2)
    for tile in MAIN:
        for j in range(4):
            fr[pl.ds(tile + MARGIN + j, PATCH, stride=4), :] = wide
    lane = lanes_of(40)
    place = lane % BAND // 4
    source = jnp.where(place < 8, 60 + place, (116 + place) % LANES)
    wide = jnp.where(
        lane < BAND,
        gather(cells[:40], source),
        gather(cells[PATCH - 40 :], source),
    )
    for j in range(4):
        fr[pl.ds(SIDE + MARGIN + j, 40, stride=4), :] = wide

    side_ice = []
    for dr, first, count in ((-1, MARGIN, HALO), (0, TOP, TILE), (1, TOP + TILE, HALO)):
        masks = []
        for ds in (-1, 0, 1):
            row, col = row_tile + dr, col_tile + ds
            inside = (row >= 0) & (row < tile_rows) & (col >= 0) & (col < tile_cols)
            row = jnp.clip(row, 0, tile_rows - 1)
            col = jnp.clip(col, 0, tile_cols - 1)
            masks.append(jnp.where(inside, ice_mask[col, row], 0).astype(jnp.float32))
        for c in range(2):
            ice[MAIN[c] + first : MAIN[c] + first + count, :] = jnp.full((count, LANES), masks[1])
        side_ice.append(choose_side(lanes_of(HALO), masks[1], masks[2], masks[0], masks[1]))
    upper = lanes_of(HALO) < BAND
    for i in range(HALF // HALO):
        ice[SIDE + TOP + i * HALO : SIDE + TOP + (i + 1) * HALO, :] = side_ice[1]
    ice[SIDE + MARGIN : SIDE + TOP, :] = jnp.where(upper, side_ice[0], side_ice[1])
    ice[SIDE + TOP + HALF : SIDE + TOP + HALF + HALO, :] = jnp.where(upper, side_ice[1], side_ice[2])


def make_stages(ext, fr, ice, visc, vel_a, vel_b, coef):
    def load(ref, part, row, count, *lead):
        return [ref[(*lead, pl.ds(row + tile, count), slice(None))] for tile in part]

    def load_around(part, row, count, now):
        return [load(now, part, r, count, i) for i in range(2) for r in (row, row - 1, row + 1)]

    def load_right(part, row, count):
        return [load(ext, part, row, count, i) for i in (1, 2)]

    def read_thickness(part, row, count):
        return load(ext, part, row, count, 0)

    def keep_viscosity(q):
        return [(visc, (0,), q), (visc, (1,), shift_west(q)), (visc, (2,), shift_east(q))]

    def first_viscosity(part, thickness):
        factor = (4.0 * strain_floor) ** (-1.0 / 3.0)
        return keep_viscosity([factor * t for t in thickness])

    def read_viscosity(part, row, count):
        return read_thickness(part, row, count), load_around(part, row, count, vel_b)

    def viscosity(part, read):
        thickness, (u, u_n, u_s, v, v_n, v_s) = read
        u_e, u_w = shift_east(u), shift_west(u)
        v_e, v_w = shift_east(v), shift_west(v)
        result = []
        for c in range(len(part)):
            ux, vx = u_e[c] - u_w[c], v_e[c] - v_w[c]
            uy, vy = u_s[c] - u_n[c], v_s[c] - v_n[c]
            shear = uy + vx
            strain = (ux * (ux + vy) + vy * vy) + (0.25 * (shear * shear) + 4.0 * strain_floor)
            result.append(thickness[c] * jnp.exp(jnp.log(strain) * (-1.0 / 3.0)))
        return keep_viscosity(result)

    def inverse(x):
        near = pl.reciprocal(x, approx=True)
        return near * (2.0 - x * near)

    def read_coefficients(part, row, count):
        around = [load(visc, part, r, count, i) for i in range(3) for r in (row, row - 1, row + 1)]
        return around + [load(fr, part, row, count), load(ice, part, row, count)]

    def coefficients(part, read):
        tiles = range(len(part))
        q, q_n, q_s, q_w, q_nw, q_sw, q_e, q_ne, q_se, friction, mask = read
        w = [q[c] + q_w[c] for c in tiles]
        e = [q[c] + q_e[c] for c in tiles]
        s = [q[c] + q_s[c] for c in tiles]
        n = [q[c] + q_n[c] for c in tiles]
        scale_u, scale_v = [], []
        for c in tiles:
            across, along = e[c] + w[c], s[c] + n[c]
            scale_u.append(mask[c] * inverse(friction[c] + along + 4.0 * across))
            scale_v.append(mask[c] * inverse(friction[c] + across + 4.0 * along))
        corners = []
        half = [0.5 * q[c] for c in tiles]
        for shifted in (q_sw, q_nw, q_se, q_ne):
            corners.append([q[c] + 0.5 * shifted[c] for c in tiles])
            corners.append([half[c] + shifted[c] for c in tiles])
        return [e, w, s, n, scale_u, scale_v] + corners

    def relax(part, k, around, right):
        tiles = range(len(part))
        e, w, s, n, scale_u, scale_v, sw_u, sw_v, nw_u, nw_v, se_u, se_v, ne_u, ne_v = k
        u, u_n, u_s, v, v_n, v_s = around
        to_west_u, to_east_u, to_west_v, to_east_v = [], [], [], []
        for c in tiles:
            u4 = 4.0 * u[c]
            to_west_u.append(w[c] * u4 + (sw_u[c] * v_s[c] - nw_u[c] * v_n[c]))
            to_east_u.append(e[c] * u4 + (ne_u[c] * v_n[c] - se_u[c] * v_s[c]))
            to_west_v.append(w[c] * v[c] + (sw_v[c] * u_s[c] - nw_v[c] * u_n[c]))
            to_east_v.append(e[c] * v[c] + (ne_v[c] * u_n[c] - se_v[c] * u_s[c]))
        to_west_u, to_west_v = shift_east(to_west_u), shift_east(to_west_v)
        to_east_u, to_east_v = shift_west(to_east_u), shift_west(to_east_v)
        new_u, new_v = [], []
        for c in tiles:
            mid_u = s[c] * u_s[c] + n[c] * u_n[c]
            mid_v = 4.0 * (s[c] * v_s[c] + n[c] * v_n[c])
            new_u.append(scale_u[c] * (right[0][c] + mid_u + (to_west_u[c] + to_east_u[c])))
            new_v.append(scale_v[c] * (right[1][c] + mid_v + (to_west_v[c] + to_east_v[c])))
        return new_u, new_v

    def put(new, values):
        return [(new, (i,), values[i]) for i in range(2)]

    def keep(k):
        return [(coef, (i,), k[i]) for i in range(FACTORS)]

    def read_sweep(now):
        def read(part, row, count):
            k = [load(coef, part, row, count, i) for i in range(FACTORS)]
            return k, load_around(part, row, count, now), load_right(part, row, count)

        return read

    def sweep(new):
        return lambda part, read: put(new, relax(part, *read))

    def read_first(part, row, count):
        return read_coefficients(part, row, count), load_right(part, row, count)

    def first_start(part, read):
        k = coefficients(part, read[0])
        return keep(k) + put(vel_a, [[a * b for a, b in zip(k[4 + i], read[1][i])] for i in range(2)])

    def read_start(part, row, count):
        return (*read_first(part, row, count), load_around(part, row, count, vel_b))

    def start(part, read):
        k = coefficients(part, read[0])
        return keep(k) + put(vel_a, relax(part, k, read[2], read[1]))

    return SimpleNamespace(**locals())


def setup_kernel(
    fr, ice, woven, own_sides, first_col, second_col,
    ext, vel_b,
    visc, vel_a, coef,
):
    west, east = sides("gx", first_col[...], second_col[...])
    lane = lanes_of(HALF)
    for f, (first, count) in enumerate(STRIP):
        for c in range(2):
            ext[f, MAIN[c] + TOP : MAIN[c] + TOP + TILE, :] = woven[f, c]
        from_east = scale_of(f) * turn(east, first, HALO)
        from_west = scale_of(f) * turn(west, first, 3 * HALO - count)
        own = own_sides[f]
        ext[f, SIDE + TOP : SIDE + TOP + HALF, :] = choose_side(lane, own, from_east, from_west, own)
    step = make_stages(ext, fr, ice, visc, vel_a, vel_b, coef)
    over_rows("tile", step.read_thickness, step.first_viscosity)
    over_rows("tile", step.read_first, step.first_start)
    over_rows("tile", step.read_sweep(vel_a), step.sweep(vel_b))


def model_kernel(
    fr, ice, ext_in, vel_in, first_row, second_row,
    vel_b, sums,
    ext, visc, vel_a, vel_c, coef, small,
):
    half = ALL_ROWS // 2
    for target, source in ((ext, ext_in), (vel_b, vel_in)):
        for f in range(source.shape[0]):
            for row in (0, half):
                target[f, row : row + half, :] = source[f, row : row + half, :]
    north, south = sides("gy", first_row[...], second_row[...])
    here = SIDE + TOP
    ends = []
    for f, (first, count) in enumerate(STRIP):
        for c in range(2):
            rows = slice(64 * c + first, 64 * c + first + count)
            ends.append((f, MAIN[c] + TOP - count, north[rows]))
            ends.append((f, MAIN[c] + TOP + TILE, south[rows]))
        rows = slice(128 + first % 32, 128 + first % 32 + count)
        source = BAND if f >= 2 else 0
        upper = lanes_of(count) < BAND
        above = turn(ext_in[f, here + HALF - count : here + HALF, :], 0, BAND)
        below = turn(ext_in[f, here : here + count, :], 0, BAND)
        ends.append((f, here - count, jnp.where(upper, turn(north[rows], source, 0), above)))
        ends.append((f, here + HALF, jnp.where(upper, below, turn(south[rows], source, BAND))))
    for f, row, cells in ends:
        ext[f, row : row + cells.shape[0], :] = cells

    step = make_stages(ext, fr, ice, visc, vel_a, vel_b, coef)
    over_ends(32, step.read_thickness, step.first_viscosity)
    over_ends(32, step.read_first, step.first_start)
    over_ends(24, step.read_sweep(vel_a), step.sweep(vel_b))

    def iteration(i, carry):
        over_rows("frame", step.read_viscosity, step.viscosity)
        over_rows("frame", step.read_start, step.start)
        over_rows("frame", step.read_sweep(vel_a), step.sweep(vel_b))
        return carry

    lax.fori_loop(1, PIC - 1, iteration, 0)
    join_parts(vel_b, ((0,), (1,)), True)
    over_rows("inner", step.read_viscosity, step.viscosity)
    over_rows("inner", step.read_start, step.start)

    load = step.load

    def read_last(part, row, count):
        return (*step.read_sweep(vel_a)(part, row, count), [load(ext, part, row, count, 3 + i) for i in range(2)])

    def last_sweep(part, read):
        k, around, right, seen = read
        new = step.relax(part, k, around, right)
        misfit = [[0.5 * (a - b) for a, b in zip(new[i], seen[i])] for i in range(2)]
        first = [[a * b for a, b in zip(k[4 + i], misfit[i])] for i in range(2)]
        return step.put(vel_b, new) + step.put(vel_c, first) + [(ext, (1 + i,), misfit[i]) for i in range(2)]

    over_rows("inner", read_last, last_sweep)

    def two_sweeps(i, carry):
        over_rows("inner", step.read_sweep(vel_c), step.sweep(vel_a))
        over_rows("inner", step.read_sweep(vel_a), step.sweep(vel_c))
        return carry

    lax.fori_loop(0, (ADJ - 2) // 2, two_sweeps, 0)

    def read_gradient(part, row, count):
        others = [load(vel_b, part, row, count, i) for i in range(2)] + [load(fr, part, row, count)]
        return (*step.read_sweep(vel_c)(part, row, count), others)

    def gradient(part, read):
        k, around, right, (u, v, friction) = read
        lu, lv = step.relax(part, k, around, right)
        return [(visc, (0,), [-2.0 * friction[c] * (u[c] * lu[c] + v[c] * lv[c]) for c in range(len(part))])]

    over_rows("tile", read_gradient, gradient)
    join_parts(visc, ((0,),), False)
    down = sum(visc[0, pl.ds(tile + TOP + j, CT, stride=4), :] for tile in MAIN for j in range(4))
    k = lax.broadcasted_iota(jnp.int32, (LANES, LANES), 0)
    total = jnp.dot(
        down,
        (k // 2 == lanes_of(LANES) % CT).astype(jnp.float32),
        precision=lax.Precision.HIGHEST,
        preferred_element_type=jnp.float32,
    )
    small[...] = total
    packed = jnp.where(
        lanes_of(PACK) < CT, small[pl.ds(0, PACK, stride=2), :], small[pl.ds(1, PACK, stride=2), :]
    )
    for j in range(sums.shape[0]):
        sums[j] = packed


def unweave_kernel(vel, vel_u, vel_v, plain, sems):
    lane = lanes_of(HALF)
    edge = HALO // 2
    parts = [(i, band) for i in range(2) for band in range(2)]

    def read(i, band):
        row = TOP + HALF * band
        return [vel[i, tile + row : tile + row + HALF, :] for tile in MAIN] + [vel[i, SIDE + TOP : SIDE + TOP + HALF, :]]

    copies = []
    pending = read(*parts[0])
    for k, (i, band) in enumerate(parts):
        even, odd, mixed = pending
        if k + 1 < len(parts):
            pending = read(*parts[k + 1])
        cells = []
        for c in range(2):
            source = BAND * c + lane // 2
            cells.append(jnp.where(lane % 2 == 0, gather(even, source), gather(odd, source)))
        low = jnp.where(lane < edge, turn(mixed, BAND * band + 3 * HALO, 0), cells[0])
        high = jnp.where(lane >= LANES - edge, turn(mixed, BAND * band + edge, LANES - edge), cells[1])
        rows = slice(HALF * band, HALF * (band + 1))
        plain[i, rows, :LANES] = low
        plain[i, rows, LANES:] = high
        out = (vel_u, vel_v)[i]
        copies.append(pltpu.make_async_copy(plain.at[i, rows], out.at[rows], sems.at[2 * i + band]))
        copies[-1].start()
    for copy in copies:
        copy.wait()


def pick_kernel(owners, gathered, own, other):
    owned = own.shape[0]
    first = lax.axis_index("gy") % 2 == 0
    total = []
    for block in range(2 * owned):
        parts = [jnp.where(owners[t, block : block + 1, :] > 0, gathered[t], 0.0) for t in range(owners.shape[0])]
        while len(parts) > 1:
            parts = [sum(parts[i : i + 2]) for i in range(0, len(parts), 2)]
        total.append(parts[0])
    for block in range(owned):
        low, high = total[block], total[block + owned]
        for out, cells in ((own, jnp.where(first, low, high)), (other, jnp.where(first, high, low))):
            for j in range(PACK):
                out[block : block + 1, j * LANES : (j + 1) * LANES] = cells[j : j + 1]


def in_vmem(count):
    return [pl.BlockSpec(memory_space=pltpu.VMEM)] * count


def in_smem(count):
    return [pl.BlockSpec(memory_space=pltpu.SMEM)] * count


def per_device(thickness, driving, observed, control, ice_mask, tile_block):
    f32 = jnp.float32
    rows, cols = lax.axis_size("gy"), lax.axis_size("gx")
    tile_block, ice_mask = tile_block[:, :, 0].T, ice_mask.T
    params = pltpu.CompilerParams(vmem_limit_bytes=VMEM_LIMIT)

    def shape(*sizes):
        return jax.ShapeDtypeStruct(sizes, f32)

    def swap(axis, cells_first, cells_second):
        count = lax.axis_size(axis)
        received = []
        for cells, low in ((cells_second, 1), (cells_first, 0)):
            pairs = [(i, i + 1) for i in range(low, count - 1, 2)]
            received.append(lax.ppermute(cells, axis, pairs + [(j, i) for i, j in pairs]))
        return received[1], received[0]

    fields = thickness, driving, observed
    owned = control.shape[0]
    *edges, parcels = pl.pallas_call(
        pack_kernel,
        out_shape=[shape(HALF, LANES)] * 2 + [shape(rows, PARCEL, LANES)],
        in_specs=[pl.BlockSpec(memory_space=pltpu.HBM)] * 5,
        out_specs=[pl.BlockSpec(memory_space=pltpu.HBM)] * 3,
        scratch_shapes=[
            pltpu.SMEM(tile_block.shape, jnp.int32),
            pltpu.VMEM((5, TILE, TILE), f32),
            pltpu.VMEM(control.shape, f32),
            pltpu.VMEM((owned, PACK, LANES), f32),
            pltpu.VMEM((rows, PARCEL, LANES), f32),
            pltpu.VMEM((2, HALF, LANES), f32),
            pltpu.SemaphoreType.DMA((10,)),
        ],
        compiler_params=pltpu.CompilerParams(vmem_limit_bytes=PACK_VMEM_LIMIT),
        name="pack",
    )(tile_block, control, *fields)
    parcels = lax.all_to_all(parcels, "gy", 0, 0, tiled=True)
    columns_in = swap("gx", *edges)
    woven, own_sides, strips = pl.pallas_call(
        weave_kernel,
        out_shape=[shape(5, 2, TILE, LANES), shape(5, HALF, LANES), shape(2, 3, 64, LANES)],
        in_specs=in_vmem(3),
        out_specs=in_vmem(3),
        compiler_params=params,
        name="weave",
    )(*fields)
    strips = pl.pallas_call(
        rows_kernel,
        out_shape=[shape(160, LANES)] * 2,
        in_specs=in_vmem(3),
        out_specs=in_vmem(2),
        compiler_params=params,
        name="rows",
    )(strips, *columns_in)
    rows_in = swap("gy", *strips)
    *friction, owners = pl.pallas_call(
        friction_kernel,
        out_shape=[shape(ALL_ROWS, LANES)] * 2
        + [jax.ShapeDtypeStruct((cols * rows // 2, 2 * owned, LANES), jnp.int32)],
        in_specs=in_smem(2) + in_vmem(1),
        out_specs=in_vmem(3),
        scratch_shapes=[pltpu.VMEM((PATCH, LANES), f32)],
        compiler_params=params,
        name="friction",
    )(tile_block, ice_mask, parcels)
    prepared = pl.pallas_call(
        setup_kernel,
        out_shape=[shape(5, ALL_ROWS, LANES), shape(2, ALL_ROWS, LANES)],
        in_specs=in_vmem(6),
        out_specs=in_vmem(2),
        scratch_shapes=[
            pltpu.VMEM((3, ALL_ROWS, LANES), f32),
            pltpu.VMEM((2, ALL_ROWS, LANES), f32),
            pltpu.VMEM((FACTORS, ALL_ROWS, LANES), f32),
        ],
        compiler_params=params,
        name="setup",
    )(*friction, woven, own_sides, *columns_in)

    vel, sums = pl.pallas_call(
        model_kernel,
        out_shape=(shape(2, ALL_ROWS, LANES), shape(cols * rows // 2, PACK, LANES)),
        in_specs=in_vmem(6),
        out_specs=in_vmem(2),
        scratch_shapes=[
            pltpu.VMEM((5, ALL_ROWS, LANES), f32),
            pltpu.VMEM((3, ALL_ROWS, LANES), f32),
            pltpu.VMEM((2, ALL_ROWS, LANES), f32),
            pltpu.VMEM((2, ALL_ROWS, LANES), f32),
            pltpu.VMEM((FACTORS, ALL_ROWS, LANES), f32),
            pltpu.VMEM((CT, LANES), f32),
        ],
        compiler_params=params,
        name="model",
    )(*friction, *prepared, *rows_in)
    vel_u, vel_v = pl.pallas_call(
        unweave_kernel,
        out_shape=[shape(TILE, TILE)] * 2,
        in_specs=in_vmem(1),
        out_specs=[pl.BlockSpec(memory_space=pltpu.HBM)] * 2,
        scratch_shapes=[pltpu.VMEM((2, TILE, TILE), f32), pltpu.SemaphoreType.DMA((4,))],
        compiler_params=params,
        name="unweave",
    )(vel)

    same_core = [[i * rows + j for i in range(cols) for j in range(core, rows, 2)] for core in range(2)]
    sums = lax.all_to_all(sums, ("gx", "gy"), 0, 0, tiled=True, axis_index_groups=same_core)
    own, other = pl.pallas_call(
        pick_kernel,
        out_shape=[shape(*control.shape)] * 2,
        in_specs=in_vmem(2),
        out_specs=in_vmem(2),
        compiler_params=params,
        name="pick",
    )(owners, sums)
    gradient = own + lax.ppermute(other, "gy", [(j, j ^ 1) for j in range(rows)])
    return vel_u, vel_v, gradient


def solution(mesh):
    return jax.shard_map(
        per_device,
        mesh=mesh,
        in_specs=(P("gy", "gx"), P(None, "gy", "gx"), P(None, "gy", "gx"), P("gy", None), P(), P()),
        out_specs=(P("gy", "gx"), P("gy", "gx"), P("gy", None)),
        check_vma=False,
    )
```

```python
from types import SimpleNamespace

import jax
import jax.numpy as jnp
from jax import lax
from jax.experimental import pallas as pl
from jax.experimental.pallas import tpu as pltpu
from jax.sharding import PartitionSpec as P

TILE = 256
PIC = 4
SW = 2
ADJ = 6
CT = 64
COARSE = 4096

LANES = 128
HALO = 16
OBS = 8
MARGIN = 8
TOP = MARGIN + HALO
ROWS = TILE + 2 * TOP
HALF = TILE // 2
SIDE = 2 * ROWS
BAND = LANES // 2
ALL_ROWS = SIDE + HALF + 2 * TOP
MAIN = (0, ROWS)
SIDES = (SIDE,)
SPANS = {
    "frame": (MARGIN, 2, 144, MARGIN, 80, 0, 0),
    "inner": (MARGIN + 8, 2, 136, MARGIN + 8, 72, 0, 0),
    "tile": (TOP, 2, 128, TOP, 64, 0, 0),
}
FACTORS = 14
AHEAD = 8
PACK = COARSE // LANES
VMEM_LIMIT = 24 * 1024 * 1024
PACK_VMEM_LIMIT = 62 * 1024 * 1024

STRIP = ((0, HALO), (HALO, HALO), (2 * HALO, HALO), (3 * HALO, OBS), (3 * HALO + OBS, OBS))

CONTROL = ((0, 0, PACK, 0), (-1, PACK - 2, 2, PACK), (1, 0, 2, PACK + 2))
FOLDED = 40
PARCEL = 48
PATCH = CT + 8

visc_scale = 0.1
strain_floor = 0.05


def lanes_of(rows):
    return lax.broadcasted_iota(jnp.int32, (rows, LANES), 1)


def is_even(axis):
    return lax.axis_index(axis) % 2 == 0


def side_lanes(rows, ds, group):
    place = (lanes_of(rows) - 8 * group) % CT
    return place < 4 if ds > 0 else place >= CT - 4


def fill_parcels(tile_block, owned_blocks, parcels):
    tile_cols, tile_rows = tile_block.shape
    owned = owned_blocks.shape[0]
    mine = lax.axis_index("gy") * owned
    col_tile = lax.axis_index("gx")

    def spread(row, carry):
        for ds in (-1, 0, 1):
            col = col_tile + ds
            place = tile_block[jnp.clip(col, 0, tile_cols - 1), row] - mine

            @pl.when((col >= 0) & (col < tile_cols) & (place >= 0) & (place < owned))
            def _():
                for dr, first, count, at in CONTROL:
                    target = row - dr

                    @pl.when((target >= 0) & (target < tile_rows))
                    def _():
                        if ds == 0:
                            parcels[target, at : at + count, :] = owned_blocks[place, first : first + count, :]
                            return
                        start = FOLDED + at % 8
                        rows = min(count, 8)
                        folded = parcels[target, start : start + rows, :]
                        for i in range(count // rows):
                            group = at // 8 + i
                            cells = owned_blocks[place, first + 8 * i : first + 8 * i + rows, :]
                            folded = jnp.where(side_lanes(rows, ds, group), turn(cells, 0, 8 * group), folded)
                        parcels[target, start : start + rows, :] = folded

        return carry

    lax.fori_loop(0, tile_rows, spread, 0)


def pack_kernel(
    table, control, thick, drive, obs, first_col, second_col, parcels,
    tile_block, held, held_control, owned_blocks, packed_parcels, packed_cols, sems,
):
    table_copy = pltpu.make_async_copy(table, tile_block, sems.at[9])
    table_copy.start()
    copies = [pltpu.make_async_copy(control, held_control, sems.at[5])]
    for f, field in enumerate((thick, drive.at[0], drive.at[1], obs.at[0], obs.at[1])):
        copies.append(pltpu.make_async_copy(field, held.at[f], sems.at[f]))
    for copy in copies:
        copy.start()
    packed_parcels[...] = jnp.zeros_like(packed_parcels)
    copies[0].wait()
    shard = [held_control[:, j * LANES : (j + 1) * LANES] for j in range(PACK)]
    for j in range(PACK):
        owned_blocks[:, j, :] = shard[j]
    table_copy.wait()
    fill_parcels(tile_block, owned_blocks, packed_parcels)
    results = [pltpu.make_async_copy(packed_parcels, parcels, sems.at[6])]
    results[0].start()

    lane = lanes_of(HALF)
    left = jnp.zeros((HALF, LANES), jnp.float32)
    right = jnp.zeros((HALF, LANES), jnp.float32)
    for f, (first, count) in enumerate(STRIP):
        copies[1 + f].wait()
        for part in range(2):
            rows = slice(part * HALF, (part + 1) * HALF)
            start = part * BAND + first
            inside = (lane >= start) & (lane < start + count)
            left = jnp.where(inside, turn(held[f, rows, :LANES], 0, start), left)
            right = jnp.where(inside, turn(held[f, rows, LANES:], LANES - count, start), right)
    even = is_even("gx")
    packed_cols[0] = jnp.where(even, right, left)
    packed_cols[1] = jnp.where(even, left, right)
    for i, out in enumerate((first_col, second_col)):
        results.append(pltpu.make_async_copy(packed_cols.at[i], out, sems.at[7 + i]))
        results[-1].start()
    for copy in results:
        copy.wait()


def sides(axis, first_pair, second_pair):
    even = is_even(axis)
    return jnp.where(even, second_pair, first_pair), jnp.where(even, first_pair, second_pair)


def choose_side(lane, high, east, west, low):
    place = lane % BAND
    return jnp.where(
        place < HALO, high, jnp.where(place < 2 * HALO, east, jnp.where(place < 3 * HALO, west, low))
    )


def turn(cells, source, target):
    shift = (target - source) % LANES
    return pltpu.roll(cells, shift, 1) if shift else cells


def gather(cells, source):
    return jnp.take_along_axis(cells, source, axis=1)


def scale_of(f):
    return (0.25 * visc_scale * 4.0 ** (1.0 / 3.0), 0.5, 0.5, 1.0, 1.0)[f]


def weave_kernel(thick, drive, obs, woven, own_sides, edges):
    lane, half_lane = lanes_of(TILE), lanes_of(HALF)
    source = 2 * lane % LANES
    for f, (field, (first, count)) in enumerate(zip((thick, drive.at[0], drive.at[1], obs.at[0], obs.at[1]), STRIP)):
        low, high = scale_of(f) * field[:, :LANES], scale_of(f) * field[:, LANES:]
        tiles = [jnp.where(lane < BAND, gather(low, source + i), gather(high, source + i)) for i in range(2)]
        bands = []
        for band in (0, BAND):
            bands.append(
                jnp.where(lane % BAND < BAND // 2, turn(high, LANES - HALO, band), turn(low, 0, band + 3 * HALO))
            )
        own_sides[f] = jnp.where(half_lane < BAND, bands[0][:HALF], bands[1][HALF:])
        for c in range(2):
            woven[f, c] = tiles[c]
        for c, tile in enumerate(tiles + [bands[0]]):
            edges[0, c, first : first + count, :] = tile[:count]
            edges[1, c, first : first + count, :] = tile[TILE - count :]


def rows_kernel(edges, first_col, second_col, first_pair, second_pair):
    west, east = sides("gx", first_col[...], second_col[...])
    even = is_even("gy")
    for c in range(2):
        top, bottom = edges[0, c], edges[1, c]
        first_pair[64 * c : 64 * c + 64, :] = jnp.where(even, bottom, top)
        second_pair[64 * c : 64 * c + 64, :] = jnp.where(even, top, bottom)
    strips = []
    for i in range(2):
        fields = []
        for f, (first, count) in enumerate(STRIP):
            packed = slice(HALF - count, HALF) if i else slice(0, count)
            source = BAND * i + first
            target = BAND if f >= 2 else 0
            own = turn(edges[i, 2, first : first + count, :], 0, target)
            from_east = scale_of(f) * turn(east[packed], source, target + HALO)
            from_west = scale_of(f) * turn(west[packed], source, target + 3 * HALO - count)
            fields.append(choose_side(lanes_of(count), own, from_east, from_west, own))
        lane = lanes_of(HALO)
        lower = jnp.concatenate(fields[3:], axis=0)
        strips.append((jnp.where(lane < BAND, fields[0], fields[2]), jnp.where(lane < BAND, fields[1], lower)))
    for k in range(2):
        top, bottom = strips[0][k], strips[1][k]
        rows = slice(128 + HALO * k, 128 + HALO * (k + 1))
        first_pair[rows, :] = jnp.where(even, bottom, top)
        second_pair[rows, :] = jnp.where(even, top, bottom)


def shift_east(tiles):
    turned = pltpu.roll(tiles[0], LANES - 1, 1)
    return [turned] if len(tiles) == 1 else [tiles[1], turned]


def shift_west(tiles):
    turned = pltpu.roll(tiles[-1], 1, 1)
    return [turned] if len(tiles) == 1 else [turned, tiles[0]]


def run_groups(groups, read, work):
    pending = [read(*group) for group in groups[:AHEAD]]
    for k, (part, row, count) in enumerate(groups):
        if k + AHEAD < len(groups):
            pending.append(read(*groups[k + AHEAD]))
        for ref, lead, values in work(part, pending[k]):
            for tile, value in zip(part, values):
                ref[(*lead, pl.ds(row + tile, count), slice(None))] = value


def block_groups(row, main, side_row, side):
    step = 32 if main % 32 == 0 else 24
    first = side // 16 * 8 if side > 24 else side
    groups = [(MAIN, row + g, min(step, main - g)) for g in range(0, main, step)]
    groups[1:1] = [(SIDES, side_row, first)]
    if first < side:
        groups[3:3] = [(SIDES, side_row + first, side - first)]
    return groups


def over_rows(span, read, work):
    start, blocks, main, side_start, side, main_rest, side_rest = SPANS[span]

    def block(i, carry):
        row, side_row = pl.multiple_of(start + i * main, 8), pl.multiple_of(side_start + i * side, 8)
        run_groups(block_groups(row, main, side_row, side), read, work)
        return carry

    lax.fori_loop(0, blocks, block, 0)
    if main_rest:
        none = 8 * jnp.minimum(lax.axis_index("gx"), 0)
        row = pl.multiple_of(none + start + blocks * main, 8)
        side_row = pl.multiple_of(none + side_start + blocks * side, 8)
        run_groups(block_groups(row, main_rest, side_row, side_rest), read, work)


def over_ends(count, read, work):
    row = pl.multiple_of(MARGIN + 8 * jnp.minimum(lax.axis_index("gx"), 0), 8)
    far, side_far = TILE + 2 * HALO - count, HALF + 2 * HALO - count
    run_groups(
        [(MAIN, row, count), (SIDES, row, count), (MAIN, row + far, count), (SIDES, row + side_far, count)], read, work
    )


def join_parts(ref, leads, whole):
    edge = HALO // 2
    few = edge // 2
    frame = HALO if whole else 0
    first, count = TOP - frame, HALF + 2 * frame
    kept = HALF + frame
    lane = lanes_of(kept)
    outer = (lane < few) | (lane >= LANES - few)
    near = jnp.where(lane < few, 3 * HALO + 2 * lane, edge + 2 * (lane - LANES + few))
    near = jnp.clip(near, 0, LANES - 2 - BAND)
    side_lane = lanes_of(count)
    place = side_lane % BAND
    inner = jnp.clip(jnp.where(place < edge, LANES - edge + place // 2, place // 2 - 24), 0, LANES - 1)
    for lead in leads:
        def at(row, rows):
            return (*lead, slice(row, row + rows), slice(None))

        mixed = ref[at(SIDE + first, count)]
        halves = [[ref[at(tile + first + HALF * h, count)] for tile in MAIN] for h in range(2)]
        if whole:
            parts = [jnp.where(side_lane % 2 == 0, gather(even, inner), gather(odd, inner)) for even, odd in halves]
            wanted = (place < edge) | (place >= BAND - edge)
            ref[at(SIDE + first, count)] = jnp.where(wanted, jnp.where(side_lane < BAND, *parts), mixed)
        for h, skip in ((0, 0), (1, frame)):
            cells = mixed[skip : skip + kept]
            for c, tile in enumerate(MAIN):
                new = jnp.where(outer, gather(cells, near + (BAND * h + c)), halves[h][c][skip : skip + kept])
                ref[at(tile + first + HALF * h + skip, kept)] = new


def friction_kernel(tile_block, ice_mask, parcels, fr, ice, owners, patch):
    tile_cols, tile_rows = ice_mask.shape
    row_tile = lax.axis_index("gy")
    col_tile = lax.axis_index("gx")
    core = row_tile % 2
    place = lax.broadcasted_iota(jnp.int32, owners.shape[1:], 0)
    for t in range(owners.shape[0]):
        block = tile_block[t // (tile_rows // 2), t % (tile_rows // 2) * 2 + core]
        owners[t] = (place == block - (row_tile - core) * (owners.shape[1] // 2)).astype(jnp.int32)

    flat = sum(parcels[j] for j in range(tile_rows))
    folded = flat[FOLDED:]
    for dr, _, count, at in CONTROL:
        cells = flat[at : at + count]
        if dr == 0:
            side = jnp.concatenate([turn(folded, 8 * g, 0) for g in range(PACK // 8)], axis=0)
        else:
            side = turn(folded, PACK, 0)[at % 8 : at % 8 + count]
        inner = lanes_of(count) < CT
        row = 4 + {-1: -4, 0: 0, 1: CT}[dr]
        patch[pl.ds(row, count, stride=2), :] = jnp.where(inner, cells, turn(side, 0, CT))
        patch[pl.ds(row + 1, count, stride=2), :] = jnp.where(inner, turn(cells, 0, CT), side)

    cells = 0.5 * jnp.exp(patch[...])
    lane = lanes_of(PATCH)
    wide = gather(cells, lane // 2)
    for tile in MAIN:
        for j in range(4):
            fr[pl.ds(tile + MARGIN + j, PATCH, stride=4), :] = wide
    lane = lanes_of(40)
    place = lane % BAND // 4
    source = jnp.where(place < 8, 60 + place, (116 + place) % LANES)
    wide = jnp.where(
        lane < BAND,
        gather(cells[:40], source),
        gather(cells[PATCH - 40 :], source),
    )
    for j in range(4):
        fr[pl.ds(SIDE + MARGIN + j, 40, stride=4), :] = wide

    side_ice = []
    for dr, first, count in ((-1, MARGIN, HALO), (0, TOP, TILE), (1, TOP + TILE, HALO)):
        masks = []
        for ds in (-1, 0, 1):
            row, col = row_tile + dr, col_tile + ds
            inside = (row >= 0) & (row < tile_rows) & (col >= 0) & (col < tile_cols)
            row = jnp.clip(row, 0, tile_rows - 1)
            col = jnp.clip(col, 0, tile_cols - 1)
            masks.append(jnp.where(inside, ice_mask[col, row], 0).astype(jnp.float32))
        for c in range(2):
            ice[MAIN[c] + first : MAIN[c] + first + count, :] = jnp.full((count, LANES), masks[1])
        side_ice.append(choose_side(lanes_of(HALO), masks[1], masks[2], masks[0], masks[1]))
    upper = lanes_of(HALO) < BAND
    for i in range(HALF // HALO):
        ice[SIDE + TOP + i * HALO : SIDE + TOP + (i + 1) * HALO, :] = side_ice[1]
    ice[SIDE + MARGIN : SIDE + TOP, :] = jnp.where(upper, side_ice[0], side_ice[1])
    ice[SIDE + TOP + HALF : SIDE + TOP + HALF + HALO, :] = jnp.where(upper, side_ice[1], side_ice[2])


def make_stages(ext, fr, ice, visc, vel_a, vel_b, coef):
    def load(ref, part, row, count, *lead):
        return [ref[(*lead, pl.ds(row + tile, count), slice(None))] for tile in part]

    def load_around(part, row, count, now):
        return [load(now, part, r, count, i) for i in range(2) for r in (row, row - 1, row + 1)]

    def load_right(part, row, count):
        return [load(ext, part, row, count, i) for i in (1, 2)]

    def read_thickness(part, row, count):
        return load(ext, part, row, count, 0)

    def keep_viscosity(q):
        return [(visc, (0,), q), (visc, (1,), shift_west(q)), (visc, (2,), shift_east(q))]

    def first_viscosity(part, thickness):
        factor = (4.0 * strain_floor) ** (-1.0 / 3.0)
        return keep_viscosity([factor * t for t in thickness])

    def read_viscosity(part, row, count):
        return read_thickness(part, row, count), load_around(part, row, count, vel_b)

    def viscosity(part, read):
        thickness, (u, u_n, u_s, v, v_n, v_s) = read
        u_e, u_w = shift_east(u), shift_west(u)
        v_e, v_w = shift_east(v), shift_west(v)
        result = []
        for c in range(len(part)):
            ux, vx = u_e[c] - u_w[c], v_e[c] - v_w[c]
            uy, vy = u_s[c] - u_n[c], v_s[c] - v_n[c]
            shear = uy + vx
            strain = (ux * (ux + vy) + vy * vy) + (0.25 * (shear * shear) + 4.0 * strain_floor)
            result.append(thickness[c] * jnp.exp(jnp.log(strain) * (-1.0 / 3.0)))
        return keep_viscosity(result)

    def inverse(x):
        near = pl.reciprocal(x, approx=True)
        return near * (2.0 - x * near)

    def read_coefficients(part, row, count):
        around = [load(visc, part, r, count, i) for i in range(3) for r in (row, row - 1, row + 1)]
        return around + [load(fr, part, row, count), load(ice, part, row, count)]

    def coefficients(part, read):
        tiles = range(len(part))
        q, q_n, q_s, q_w, q_nw, q_sw, q_e, q_ne, q_se, friction, mask = read
        w = [q[c] + q_w[c] for c in tiles]
        e = [q[c] + q_e[c] for c in tiles]
        s = [q[c] + q_s[c] for c in tiles]
        n = [q[c] + q_n[c] for c in tiles]
        scale_u, scale_v = [], []
        for c in tiles:
            across, along = e[c] + w[c], s[c] + n[c]
            scale_u.append(mask[c] * inverse(friction[c] + along + 4.0 * across))
            scale_v.append(mask[c] * inverse(friction[c] + across + 4.0 * along))
        corners = []
        half = [0.5 * q[c] for c in tiles]
        for shifted in (q_sw, q_nw, q_se, q_ne):
            corners.append([q[c] + 0.5 * shifted[c] for c in tiles])
            corners.append([half[c] + shifted[c] for c in tiles])
        return [e, w, s, n, scale_u, scale_v] + corners

    def relax(part, k, around, right):
        tiles = range(len(part))
        e, w, s, n, scale_u, scale_v, sw_u, sw_v, nw_u, nw_v, se_u, se_v, ne_u, ne_v = k
        u, u_n, u_s, v, v_n, v_s = around
        to_west_u, to_east_u, to_west_v, to_east_v = [], [], [], []
        for c in tiles:
            u4 = 4.0 * u[c]
            to_west_u.append(w[c] * u4 + (sw_u[c] * v_s[c] - nw_u[c] * v_n[c]))
            to_east_u.append(e[c] * u4 + (ne_u[c] * v_n[c] - se_u[c] * v_s[c]))
            to_west_v.append(w[c] * v[c] + (sw_v[c] * u_s[c] - nw_v[c] * u_n[c]))
            to_east_v.append(e[c] * v[c] + (ne_v[c] * u_n[c] - se_v[c] * u_s[c]))
        to_west_u, to_west_v = shift_east(to_west_u), shift_east(to_west_v)
        to_east_u, to_east_v = shift_west(to_east_u), shift_west(to_east_v)
        new_u, new_v = [], []
        for c in tiles:
            mid_u = s[c] * u_s[c] + n[c] * u_n[c]
            mid_v = 4.0 * (s[c] * v_s[c] + n[c] * v_n[c])
            new_u.append(scale_u[c] * (right[0][c] + mid_u + (to_west_u[c] + to_east_u[c])))
            new_v.append(scale_v[c] * (right[1][c] + mid_v + (to_west_v[c] + to_east_v[c])))
        return new_u, new_v

    def put(new, values):
        return [(new, (i,), values[i]) for i in range(2)]

    def keep(k):
        return [(coef, (i,), k[i]) for i in range(FACTORS)]

    def read_sweep(now):
        def read(part, row, count):
            k = [load(coef, part, row, count, i) for i in range(FACTORS)]
            return k, load_around(part, row, count, now), load_right(part, row, count)

        return read

    def sweep(new):
        return lambda part, read: put(new, relax(part, *read))

    def read_first(part, row, count):
        return read_coefficients(part, row, count), load_right(part, row, count)

    def first_start(part, read):
        k = coefficients(part, read[0])
        return keep(k) + put(vel_a, [[a * b for a, b in zip(k[4 + i], read[1][i])] for i in range(2)])

    def read_start(part, row, count):
        return (*read_first(part, row, count), load_around(part, row, count, vel_b))

    def start(part, read):
        k = coefficients(part, read[0])
        return keep(k) + put(vel_a, relax(part, k, read[2], read[1]))

    return SimpleNamespace(**locals())


def setup_kernel(
    fr, ice, woven, own_sides, first_col, second_col,
    ext, vel_b,
    visc, vel_a, coef,
):
    west, east = sides("gx", first_col[...], second_col[...])
    lane = lanes_of(HALF)
    for f, (first, count) in enumerate(STRIP):
        for c in range(2):
            ext[f, MAIN[c] + TOP : MAIN[c] + TOP + TILE, :] = woven[f, c]
        from_east = scale_of(f) * turn(east, first, HALO)
        from_west = scale_of(f) * turn(west, first, 3 * HALO - count)
        own = own_sides[f]
        ext[f, SIDE + TOP : SIDE + TOP + HALF, :] = choose_side(lane, own, from_east, from_west, own)
    step = make_stages(ext, fr, ice, visc, vel_a, vel_b, coef)
    over_rows("tile", step.read_thickness, step.first_viscosity)
    over_rows("tile", step.read_first, step.first_start)
    over_rows("tile", step.read_sweep(vel_a), step.sweep(vel_b))


def model_kernel(
    fr, ice, ext_in, vel_in, first_row, second_row,
    vel_b, sums,
    ext, visc, vel_a, vel_c, coef, small,
):
    half = ALL_ROWS // 2
    for target, source in ((ext, ext_in), (vel_b, vel_in)):
        for f in range(source.shape[0]):
            for row in (0, half):
                target[f, row : row + half, :] = source[f, row : row + half, :]
    north, south = sides("gy", first_row[...], second_row[...])
    here = SIDE + TOP
    ends = []
    for f, (first, count) in enumerate(STRIP):
        for c in range(2):
            rows = slice(64 * c + first, 64 * c + first + count)
            ends.append((f, MAIN[c] + TOP - count, north[rows]))
            ends.append((f, MAIN[c] + TOP + TILE, south[rows]))
        rows = slice(128 + first % 32, 128 + first % 32 + count)
        source = BAND if f >= 2 else 0
        upper = lanes_of(count) < BAND
        above = turn(ext_in[f, here + HALF - count : here + HALF, :], 0, BAND)
        below = turn(ext_in[f, here : here + count, :], 0, BAND)
        ends.append((f, here - count, jnp.where(upper, turn(north[rows], source, 0), above)))
        ends.append((f, here + HALF, jnp.where(upper, below, turn(south[rows], source, BAND))))
    for f, row, cells in ends:
        ext[f, row : row + cells.shape[0], :] = cells

    step = make_stages(ext, fr, ice, visc, vel_a, vel_b, coef)
    over_ends(32, step.read_thickness, step.first_viscosity)
    over_ends(32, step.read_first, step.first_start)
    over_ends(24, step.read_sweep(vel_a), step.sweep(vel_b))

    def iteration(i, carry):
        over_rows("frame", step.read_viscosity, step.viscosity)
        over_rows("frame", step.read_start, step.start)
        over_rows("frame", step.read_sweep(vel_a), step.sweep(vel_b))
        return carry

    lax.fori_loop(1, PIC - 1, iteration, 0)
    join_parts(vel_b, ((0,), (1,)), True)
    over_rows("inner", step.read_viscosity, step.viscosity)
    over_rows("inner", step.read_start, step.start)

    load = step.load

    def read_last(part, row, count):
        return (*step.read_sweep(vel_a)(part, row, count), [load(ext, part, row, count, 3 + i) for i in range(2)])

    def last_sweep(part, read):
        k, around, right, seen = read
        new = step.relax(part, k, around, right)
        misfit = [[0.5 * (a - b) for a, b in zip(new[i], seen[i])] for i in range(2)]
        first = [[a * b for a, b in zip(k[4 + i], misfit[i])] for i in range(2)]
        return step.put(vel_b, new) + step.put(vel_c, first) + [(ext, (1 + i,), misfit[i]) for i in range(2)]

    over_rows("inner", read_last, last_sweep)

    def two_sweeps(i, carry):
        over_rows("inner", step.read_sweep(vel_c), step.sweep(vel_a))
        over_rows("inner", step.read_sweep(vel_a), step.sweep(vel_c))
        return carry

    lax.fori_loop(0, (ADJ - 2) // 2, two_sweeps, 0)

    def read_gradient(part, row, count):
        others = [load(vel_b, part, row, count, i) for i in range(2)] + [load(fr, part, row, count)]
        return (*step.read_sweep(vel_c)(part, row, count), others)

    def gradient(part, read):
        k, around, right, (u, v, friction) = read
        lu, lv = step.relax(part, k, around, right)
        return [(visc, (0,), [-2.0 * friction[c] * (u[c] * lu[c] + v[c] * lv[c]) for c in range(len(part))])]

    over_rows("tile", read_gradient, gradient)
    join_parts(visc, ((0,),), False)
    down = sum(visc[0, pl.ds(tile + TOP + j, CT, stride=4), :] for tile in MAIN for j in range(4))
    total = gather(down + turn(down, 1, 0), 2 * (lanes_of(CT) % CT))
    small[...] = total
    packed = jnp.where(
        lanes_of(PACK) < CT, small[pl.ds(0, PACK, stride=2), :], small[pl.ds(1, PACK, stride=2), :]
    )
    for j in range(sums.shape[0]):
        sums[j] = packed


def unweave_kernel(vel, vel_u, vel_v, plain, sems):
    lane = lanes_of(HALF)
    edge = HALO // 2
    parts = [(i, band) for i in range(2) for band in range(2)]

    def read(i, band):
        row = TOP + HALF * band
        return [vel[i, tile + row : tile + row + HALF, :] for tile in MAIN] + [vel[i, SIDE + TOP : SIDE + TOP + HALF, :]]

    copies = []
    pending = read(*parts[0])
    for k, (i, band) in enumerate(parts):
        even, odd, mixed = pending
        if k + 1 < len(parts):
            pending = read(*parts[k + 1])
        cells = []
        for c in range(2):
            source = BAND * c + lane // 2
            cells.append(jnp.where(lane % 2 == 0, gather(even, source), gather(odd, source)))
        low = jnp.where(lane < edge, turn(mixed, BAND * band + 3 * HALO, 0), cells[0])
        high = jnp.where(lane >= LANES - edge, turn(mixed, BAND * band + edge, LANES - edge), cells[1])
        rows = slice(HALF * band, HALF * (band + 1))
        plain[i, rows, :LANES] = low
        plain[i, rows, LANES:] = high
        out = (vel_u, vel_v)[i]
        copies.append(pltpu.make_async_copy(plain.at[i, rows], out.at[rows], sems.at[2 * i + band]))
        copies[-1].start()
    for copy in copies:
        copy.wait()


def pick_kernel(owners, gathered, own, other):
    owned = own.shape[0]
    first = lax.axis_index("gy") % 2 == 0
    total = []
    for block in range(2 * owned):
        parts = [jnp.where(owners[t, block : block + 1, :] > 0, gathered[t], 0.0) for t in range(owners.shape[0])]
        while len(parts) > 1:
            parts = [sum(parts[i : i + 2]) for i in range(0, len(parts), 2)]
        total.append(parts[0])
    for block in range(owned):
        low, high = total[block], total[block + owned]
        for out, cells in ((own, jnp.where(first, low, high)), (other, jnp.where(first, high, low))):
            for j in range(PACK):
                out[block : block + 1, j * LANES : (j + 1) * LANES] = cells[j : j + 1]


def in_vmem(count):
    return [pl.BlockSpec(memory_space=pltpu.VMEM)] * count


def in_smem(count):
    return [pl.BlockSpec(memory_space=pltpu.SMEM)] * count


def per_device(thickness, driving, observed, control, ice_mask, tile_block):
    f32 = jnp.float32
    rows, cols = lax.axis_size("gy"), lax.axis_size("gx")
    tile_block, ice_mask = tile_block[:, :, 0].T, ice_mask.T
    params = pltpu.CompilerParams(vmem_limit_bytes=VMEM_LIMIT)

    def shape(*sizes):
        return jax.ShapeDtypeStruct(sizes, f32)

    def swap(axis, cells_first, cells_second):
        count = lax.axis_size(axis)
        received = []
        for cells, low in ((cells_first, 0), (cells_second, 1)):
            pairs = [(i, i + 1) for i in range(low, count - 1, 2)]
            received.append(lax.ppermute(cells, axis, pairs + [(j, i) for i, j in pairs]))
        return received

    fields = thickness, driving, observed
    owned = control.shape[0]
    *edges, parcels = pl.pallas_call(
        pack_kernel,
        out_shape=[shape(HALF, LANES)] * 2 + [shape(rows, PARCEL, LANES)],
        in_specs=[pl.BlockSpec(memory_space=pltpu.HBM)] * 5,
        out_specs=[pl.BlockSpec(memory_space=pltpu.HBM)] * 3,
        scratch_shapes=[
            pltpu.SMEM(tile_block.shape, jnp.int32),
            pltpu.VMEM((5, TILE, TILE), f32),
            pltpu.VMEM(control.shape, f32),
            pltpu.VMEM((owned, PACK, LANES), f32),
            pltpu.VMEM((rows, PARCEL, LANES), f32),
            pltpu.VMEM((2, HALF, LANES), f32),
            pltpu.SemaphoreType.DMA((10,)),
        ],
        compiler_params=pltpu.CompilerParams(vmem_limit_bytes=PACK_VMEM_LIMIT),
        name="pack",
    )(tile_block, control, *fields)
    parcels = lax.all_to_all(parcels, "gy", 0, 0, tiled=True)
    columns_in = swap("gx", *edges)
    woven, own_sides, strips = pl.pallas_call(
        weave_kernel,
        out_shape=[shape(5, 2, TILE, LANES), shape(5, HALF, LANES), shape(2, 3, 64, LANES)],
        in_specs=in_vmem(3),
        out_specs=in_vmem(3),
        compiler_params=params,
        name="weave",
    )(*fields)
    strips = pl.pallas_call(
        rows_kernel,
        out_shape=[shape(160, LANES)] * 2,
        in_specs=in_vmem(3),
        out_specs=in_vmem(2),
        compiler_params=params,
        name="rows",
    )(strips, *columns_in)
    rows_in = swap("gy", *strips)
    *friction, owners = pl.pallas_call(
        friction_kernel,
        out_shape=[shape(ALL_ROWS, LANES)] * 2
        + [jax.ShapeDtypeStruct((cols * rows // 2, 2 * owned, LANES), jnp.int32)],
        in_specs=in_smem(2) + in_vmem(1),
        out_specs=in_vmem(3),
        scratch_shapes=[pltpu.VMEM((PATCH, LANES), f32)],
        compiler_params=params,
        name="friction",
    )(tile_block, ice_mask, parcels)
    prepared = pl.pallas_call(
        setup_kernel,
        out_shape=[shape(5, ALL_ROWS, LANES), shape(2, ALL_ROWS, LANES)],
        in_specs=in_vmem(6),
        out_specs=in_vmem(2),
        scratch_shapes=[
            pltpu.VMEM((3, ALL_ROWS, LANES), f32),
            pltpu.VMEM((2, ALL_ROWS, LANES), f32),
            pltpu.VMEM((FACTORS, ALL_ROWS, LANES), f32),
        ],
        compiler_params=params,
        name="setup",
    )(*friction, woven, own_sides, *columns_in)

    vel, sums = pl.pallas_call(
        model_kernel,
        out_shape=(shape(2, ALL_ROWS, LANES), shape(cols * rows // 2, PACK, LANES)),
        in_specs=in_vmem(6),
        out_specs=in_vmem(2),
        scratch_shapes=[
            pltpu.VMEM((5, ALL_ROWS, LANES), f32),
            pltpu.VMEM((3, ALL_ROWS, LANES), f32),
            pltpu.VMEM((2, ALL_ROWS, LANES), f32),
            pltpu.VMEM((2, ALL_ROWS, LANES), f32),
            pltpu.VMEM((FACTORS, ALL_ROWS, LANES), f32),
            pltpu.VMEM((CT, LANES), f32),
        ],
        compiler_params=params,
        name="model",
    )(*friction, *prepared, *rows_in)
    vel_u, vel_v = pl.pallas_call(
        unweave_kernel,
        out_shape=[shape(TILE, TILE)] * 2,
        in_specs=in_vmem(1),
        out_specs=[pl.BlockSpec(memory_space=pltpu.HBM)] * 2,
        scratch_shapes=[pltpu.VMEM((2, TILE, TILE), f32), pltpu.SemaphoreType.DMA((4,))],
        compiler_params=params,
        name="unweave",
    )(vel)

    same_core = [[i * rows + j for i in range(cols) for j in range(core, rows, 2)] for core in range(2)]
    sums = lax.all_to_all(sums, ("gx", "gy"), 0, 0, tiled=True, axis_index_groups=same_core)
    own, other = pl.pallas_call(
        pick_kernel,
        out_shape=[shape(*control.shape)] * 2,
        in_specs=in_vmem(2),
        out_specs=in_vmem(2),
        compiler_params=params,
        name="pick",
    )(owners, sums)
    gradient = own + lax.ppermute(other, "gy", [(j, j ^ 1) for j in range(rows)])
    return vel_u, vel_v, gradient


def solution(mesh):
    return jax.shard_map(
        per_device,
        mesh=mesh,
        in_specs=(P("gy", "gx"), P(None, "gy", "gx"), P(None, "gy", "gx"), P("gy", None), P(), P()),
        out_specs=(P("gy", "gx"), P("gy", "gx"), P("gy", None)),
        check_vma=False,
    )
```

```python
from types import SimpleNamespace

import jax
import jax.numpy as jnp
from jax import lax
from jax.experimental import pallas as pl
from jax.experimental.pallas import tpu as pltpu
from jax.sharding import PartitionSpec as P

TILE = 256
PIC = 4
SW = 2
ADJ = 6
CT = 64
COARSE = 4096

LANES = 128
HALO = 16
OBS = 8
MARGIN = 8
TOP = MARGIN + HALO
ROWS = TILE + 2 * TOP
HALF = TILE // 2
SIDE = 2 * ROWS
BAND = LANES // 2
ALL_ROWS = SIDE + HALF + 2 * TOP
MAIN = (0, ROWS)
SIDES = (SIDE,)
SPANS = {
    "frame": (MARGIN, 2, 144, MARGIN, 80, 0, 0),
    "inner": (MARGIN + 8, 2, 136, MARGIN + 8, 72, 0, 0),
    "tile": (TOP, 2, 128, TOP, 64, 0, 0),
}
FACTORS = 14
AHEAD = 8
PACK = COARSE // LANES
VMEM_LIMIT = 24 * 1024 * 1024
PACK_VMEM_LIMIT = 62 * 1024 * 1024

STRIP = ((0, HALO), (HALO, HALO), (2 * HALO, HALO), (3 * HALO, OBS), (3 * HALO + OBS, OBS))

CONTROL = ((0, 0, PACK, 0), (-1, PACK - 2, 2, PACK), (1, 0, 2, PACK + 2))
FOLDED = 40
PARCEL = 48
PATCH = CT + 8

visc_scale = 0.1
strain_floor = 0.05


def lanes_of(rows):
    return lax.broadcasted_iota(jnp.int32, (rows, LANES), 1)


def is_even(axis):
    return lax.axis_index(axis) % 2 == 0


def side_lanes(rows, ds, group):
    place = (lanes_of(rows) - 8 * group) % CT
    return place < 4 if ds > 0 else place >= CT - 4


def fill_parcels(tile_block, owned_blocks, parcels):
    tile_cols, tile_rows = tile_block.shape
    owned = owned_blocks.shape[0]
    mine = lax.axis_index("gy") * owned
    col_tile = lax.axis_index("gx")

    def spread(row, carry):
        for ds in (-1, 0, 1):
            col = col_tile + ds
            place = tile_block[jnp.clip(col, 0, tile_cols - 1), row] - mine

            @pl.when((col >= 0) & (col < tile_cols) & (place >= 0) & (place < owned))
            def _():
                for dr, first, count, at in CONTROL:
                    target = row - dr

                    @pl.when((target >= 0) & (target < tile_rows))
                    def _():
                        if ds == 0:
                            parcels[target, at : at + count, :] = owned_blocks[place, first : first + count, :]
                            return
                        start = FOLDED + at % 8
                        rows = min(count, 8)
                        folded = parcels[target, start : start + rows, :]
                        for i in range(count // rows):
                            group = at // 8 + i
                            cells = owned_blocks[place, first + 8 * i : first + 8 * i + rows, :]
                            folded = jnp.where(side_lanes(rows, ds, group), turn(cells, 0, 8 * group), folded)
                        parcels[target, start : start + rows, :] = folded

        return carry

    lax.fori_loop(0, tile_rows, spread, 0)


def pack_kernel(
    table, control, thick, drive, obs, first_col, second_col, parcels,
    tile_block, held, held_control, owned_blocks, packed_parcels, packed_cols, sems,
):
    table_copy = pltpu.make_async_copy(table, tile_block, sems.at[9])
    table_copy.start()
    copies = [pltpu.make_async_copy(control, held_control, sems.at[5])]
    for f, field in enumerate((thick, drive.at[0], drive.at[1], obs.at[0], obs.at[1])):
        copies.append(pltpu.make_async_copy(field, held.at[f], sems.at[f]))
    for copy in copies:
        copy.start()
    packed_parcels[...] = jnp.zeros_like(packed_parcels)
    copies[0].wait()
    shard = [held_control[:, j * LANES : (j + 1) * LANES] for j in range(PACK)]
    for j in range(PACK):
        owned_blocks[:, j, :] = shard[j]
    table_copy.wait()
    fill_parcels(tile_block, owned_blocks, packed_parcels)
    results = [pltpu.make_async_copy(packed_parcels, parcels, sems.at[6])]
    results[0].start()

    lane = lanes_of(HALF)
    left = jnp.zeros((HALF, LANES), jnp.float32)
    right = jnp.zeros((HALF, LANES), jnp.float32)
    for f, (first, count) in enumerate(STRIP):
        copies[1 + f].wait()
        for part in range(2):
            rows = slice(part * HALF, (part + 1) * HALF)
            start = part * BAND + first
            inside = (lane >= start) & (lane < start + count)
            left = jnp.where(inside, turn(held[f, rows, :LANES], 0, start), left)
            right = jnp.where(inside, turn(held[f, rows, LANES:], LANES - count, start), right)
    even = is_even("gx")
    packed_cols[0] = jnp.where(even, right, left)
    packed_cols[1] = jnp.where(even, left, right)
    for i, out in enumerate((first_col, second_col)):
        results.append(pltpu.make_async_copy(packed_cols.at[i], out, sems.at[7 + i]))
        results[-1].start()
    for copy in results:
        copy.wait()


def sides(axis, first_pair, second_pair):
    even = is_even(axis)
    return jnp.where(even, second_pair, first_pair), jnp.where(even, first_pair, second_pair)


def choose_side(lane, high, east, west, low):
    place = lane % BAND
    return jnp.where(
        place < HALO, high, jnp.where(place < 2 * HALO, east, jnp.where(place < 3 * HALO, west, low))
    )


def turn(cells, source, target):
    shift = (target - source) % LANES
    return pltpu.roll(cells, shift, 1) if shift else cells


def gather(cells, source):
    return jnp.take_along_axis(cells, source, axis=1)


def scale_of(f):
    return (0.25 * visc_scale * 4.0 ** (1.0 / 3.0), 0.5, 0.5, 1.0, 1.0)[f]


def weave_kernel(thick, drive, obs, woven, own_sides, edges):
    lane, half_lane = lanes_of(TILE), lanes_of(HALF)
    source = 2 * lane % LANES
    for f, (field, (first, count)) in enumerate(zip((thick, drive.at[0], drive.at[1], obs.at[0], obs.at[1]), STRIP)):
        low, high = scale_of(f) * field[:, :LANES], scale_of(f) * field[:, LANES:]
        tiles = [jnp.where(lane < BAND, gather(low, source + i), gather(high, source + i)) for i in range(2)]
        bands = []
        for band in (0, BAND):
            bands.append(
                jnp.where(lane % BAND < BAND // 2, turn(high, LANES - HALO, band), turn(low, 0, band + 3 * HALO))
            )
        own_sides[f] = jnp.where(half_lane < BAND, bands[0][:HALF], bands[1][HALF:])
        for c in range(2):
            woven[f, c] = tiles[c]
        for c, tile in enumerate(tiles + [bands[0]]):
            edges[0, c, first : first + count, :] = tile[:count]
            edges[1, c, first : first + count, :] = tile[TILE - count :]


def rows_kernel(edges, first_col, second_col, first_pair, second_pair):
    west, east = sides("gx", first_col[...], second_col[...])
    even = is_even("gy")
    for c in range(2):
        top, bottom = edges[0, c], edges[1, c]
        first_pair[64 * c : 64 * c + 64, :] = jnp.where(even, bottom, top)
        second_pair[64 * c : 64 * c + 64, :] = jnp.where(even, top, bottom)
    strips = []
    for i in range(2):
        fields = []
        for f, (first, count) in enumerate(STRIP):
            packed = slice(HALF - count, HALF) if i else slice(0, count)
            source = BAND * i + first
            target = BAND if f >= 2 else 0
            own = turn(edges[i, 2, first : first + count, :], 0, target)
            from_east = scale_of(f) * turn(east[packed], source, target + HALO)
            from_west = scale_of(f) * turn(west[packed], source, target + 3 * HALO - count)
            fields.append(choose_side(lanes_of(count), own, from_east, from_west, own))
        lane = lanes_of(HALO)
        lower = jnp.concatenate(fields[3:], axis=0)
        strips.append((jnp.where(lane < BAND, fields[0], fields[2]), jnp.where(lane < BAND, fields[1], lower)))
    for k in range(2):
        top, bottom = strips[0][k], strips[1][k]
        rows = slice(128 + HALO * k, 128 + HALO * (k + 1))
        first_pair[rows, :] = jnp.where(even, bottom, top)
        second_pair[rows, :] = jnp.where(even, top, bottom)


def shift_east(tiles):
    turned = pltpu.roll(tiles[0], LANES - 1, 1)
    return [turned] if len(tiles) == 1 else [tiles[1], turned]


def shift_west(tiles):
    turned = pltpu.roll(tiles[-1], 1, 1)
    return [turned] if len(tiles) == 1 else [turned, tiles[0]]


def run_groups(groups, read, work):
    pending = [read(*group) for group in groups[:AHEAD]]
    for k, (part, row, count) in enumerate(groups):
        if k + AHEAD < len(groups):
            pending.append(read(*groups[k + AHEAD]))
        for ref, lead, values in work(part, pending[k]):
            for tile, value in zip(part, values):
                ref[(*lead, pl.ds(row + tile, count), slice(None))] = value


def block_groups(row, main, side_row, side):
    step = 64 if main % 32 == 0 else 48
    first = side // 16 * 8 if side > 24 else side
    groups = [(MAIN, row + g, min(step, main - g)) for g in range(0, main, step)]
    groups[1:1] = [(SIDES, side_row, first)]
    if first < side:
        groups[3:3] = [(SIDES, side_row + first, side - first)]
    return groups


def over_rows(span, read, work):
    start, blocks, main, side_start, side, main_rest, side_rest = SPANS[span]

    def block(i, carry):
        row, side_row = pl.multiple_of(start + i * main, 8), pl.multiple_of(side_start + i * side, 8)
        run_groups(block_groups(row, main, side_row, side), read, work)
        return carry

    lax.fori_loop(0, blocks, block, 0)
    if main_rest:
        none = 8 * jnp.minimum(lax.axis_index("gx"), 0)
        row = pl.multiple_of(none + start + blocks * main, 8)
        side_row = pl.multiple_of(none + side_start + blocks * side, 8)
        run_groups(block_groups(row, main_rest, side_row, side_rest), read, work)


def over_ends(count, read, work):
    row = pl.multiple_of(MARGIN + 8 * jnp.minimum(lax.axis_index("gx"), 0), 8)
    far, side_far = TILE + 2 * HALO - count, HALF + 2 * HALO - count
    run_groups(
        [(MAIN, row, count), (SIDES, row, count), (MAIN, row + far, count), (SIDES, row + side_far, count)], read, work
    )


def join_parts(ref, leads, whole):
    edge = HALO // 2
    few = edge // 2
    frame = HALO if whole else 0
    first, count = TOP - frame, HALF + 2 * frame
    kept = HALF + frame
    lane = lanes_of(kept)
    outer = (lane < few) | (lane >= LANES - few)
    near = jnp.where(lane < few, 3 * HALO + 2 * lane, edge + 2 * (lane - LANES + few))
    near = jnp.clip(near, 0, LANES - 2 - BAND)
    side_lane = lanes_of(count)
    place = side_lane % BAND
    inner = jnp.clip(jnp.where(place < edge, LANES - edge + place // 2, place // 2 - 24), 0, LANES - 1)
    for lead in leads:
        def at(row, rows):
            return (*lead, slice(row, row + rows), slice(None))

        mixed = ref[at(SIDE + first, count)]
        halves = [[ref[at(tile + first + HALF * h, count)] for tile in MAIN] for h in range(2)]
        if whole:
            parts = [jnp.where(side_lane % 2 == 0, gather(even, inner), gather(odd, inner)) for even, odd in halves]
            wanted = (place < edge) | (place >= BAND - edge)
            ref[at(SIDE + first, count)] = jnp.where(wanted, jnp.where(side_lane < BAND, *parts), mixed)
        for h, skip in ((0, 0), (1, frame)):
            cells = mixed[skip : skip + kept]
            for c, tile in enumerate(MAIN):
                new = jnp.where(outer, gather(cells, near + (BAND * h + c)), halves[h][c][skip : skip + kept])
                ref[at(tile + first + HALF * h + skip, kept)] = new


def friction_kernel(tile_block, ice_mask, parcels, fr, ice, owners, patch):
    tile_cols, tile_rows = ice_mask.shape
    row_tile = lax.axis_index("gy")
    col_tile = lax.axis_index("gx")
    core = row_tile % 2
    place = lax.broadcasted_iota(jnp.int32, owners.shape[1:], 0)
    for t in range(owners.shape[0]):
        block = tile_block[t // (tile_rows // 2), t % (tile_rows // 2) * 2 + core]
        owners[t] = (place == block - (row_tile - core) * (owners.shape[1] // 2)).astype(jnp.int32)

    flat = sum(parcels[j] for j in range(tile_rows))
    folded = flat[FOLDED:]
    for dr, _, count, at in CONTROL:
        cells = flat[at : at + count]
        if dr == 0:
            side = jnp.concatenate([turn(folded, 8 * g, 0) for g in range(PACK // 8)], axis=0)
        else:
            side = turn(folded, PACK, 0)[at % 8 : at % 8 + count]
        inner = lanes_of(count) < CT
        row = 4 + {-1: -4, 0: 0, 1: CT}[dr]
        patch[pl.ds(row, count, stride=2), :] = jnp.where(inner, cells, turn(side, 0, CT))
        patch[pl.ds(row + 1, count, stride=2), :] = jnp.where(inner, turn(cells, 0, CT), side)

    cells = 0.5 * jnp.exp(patch[...])
    lane = lanes_of(PATCH)
    wide = gather(cells, lane // 2)
    for tile in MAIN:
        for j in range(4):
            fr[pl.ds(tile + MARGIN + j, PATCH, stride=4), :] = wide
    lane = lanes_of(40)
    place = lane % BAND // 4
    source = jnp.where(place < 8, 60 + place, (116 + place) % LANES)
    wide = jnp.where(
        lane < BAND,
        gather(cells[:40], source),
        gather(cells[PATCH - 40 :], source),
    )
    for j in range(4):
        fr[pl.ds(SIDE + MARGIN + j, 40, stride=4), :] = wide

    side_ice = []
    for dr, first, count in ((-1, MARGIN, HALO), (0, TOP, TILE), (1, TOP + TILE, HALO)):
        masks = []
        for ds in (-1, 0, 1):
            row, col = row_tile + dr, col_tile + ds
            inside = (row >= 0) & (row < tile_rows) & (col >= 0) & (col < tile_cols)
            row = jnp.clip(row, 0, tile_rows - 1)
            col = jnp.clip(col, 0, tile_cols - 1)
            masks.append(jnp.where(inside, ice_mask[col, row], 0).astype(jnp.float32))
        for c in range(2):
            ice[MAIN[c] + first : MAIN[c] + first + count, :] = jnp.full((count, LANES), masks[1])
        side_ice.append(choose_side(lanes_of(HALO), masks[1], masks[2], masks[0], masks[1]))
    upper = lanes_of(HALO) < BAND
    for i in range(HALF // HALO):
        ice[SIDE + TOP + i * HALO : SIDE + TOP + (i + 1) * HALO, :] = side_ice[1]
    ice[SIDE + MARGIN : SIDE + TOP, :] = jnp.where(upper, side_ice[0], side_ice[1])
    ice[SIDE + TOP + HALF : SIDE + TOP + HALF + HALO, :] = jnp.where(upper, side_ice[1], side_ice[2])


def make_stages(ext, fr, ice, visc, vel_a, vel_b, coef):
    def load(ref, part, row, count, *lead):
        return [ref[(*lead, pl.ds(row + tile, count), slice(None))] for tile in part]

    def load_around(part, row, count, now):
        return [load(now, part, r, count, i) for i in range(2) for r in (row, row - 1, row + 1)]

    def load_right(part, row, count):
        return [load(ext, part, row, count, i) for i in (1, 2)]

    def read_thickness(part, row, count):
        return load(ext, part, row, count, 0)

    def keep_viscosity(q):
        return [(visc, (0,), q), (visc, (1,), shift_west(q)), (visc, (2,), shift_east(q))]

    def first_viscosity(part, thickness):
        factor = (4.0 * strain_floor) ** (-1.0 / 3.0)
        return keep_viscosity([factor * t for t in thickness])

    def read_viscosity(part, row, count):
        return read_thickness(part, row, count), load_around(part, row, count, vel_b)

    def viscosity(part, read):
        thickness, (u, u_n, u_s, v, v_n, v_s) = read
        u_e, u_w = shift_east(u), shift_west(u)
        v_e, v_w = shift_east(v), shift_west(v)
        result = []
        for c in range(len(part)):
            ux, vx = u_e[c] - u_w[c], v_e[c] - v_w[c]
            uy, vy = u_s[c] - u_n[c], v_s[c] - v_n[c]
            shear = uy + vx
            strain = (ux * (ux + vy) + vy * vy) + (0.25 * (shear * shear) + 4.0 * strain_floor)
            result.append(thickness[c] * jnp.exp(jnp.log(strain) * (-1.0 / 3.0)))
        return keep_viscosity(result)

    def inverse(x):
        near = pl.reciprocal(x, approx=True)
        return near * (2.0 - x * near)

    def read_coefficients(part, row, count):
        around = [load(visc, part, r, count, i) for i in range(3) for r in (row, row - 1, row + 1)]
        return around + [load(fr, part, row, count), load(ice, part, row, count)]

    def coefficients(part, read):
        tiles = range(len(part))
        q, q_n, q_s, q_w, q_nw, q_sw, q_e, q_ne, q_se, friction, mask = read
        w = [q[c] + q_w[c] for c in tiles]
        e = [q[c] + q_e[c] for c in tiles]
        s = [q[c] + q_s[c] for c in tiles]
        n = [q[c] + q_n[c] for c in tiles]
        scale_u, scale_v = [], []
        for c in tiles:
            across, along = e[c] + w[c], s[c] + n[c]
            scale_u.append(mask[c] * inverse(friction[c] + along + 4.0 * across))
            scale_v.append(mask[c] * inverse(friction[c] + across + 4.0 * along))
        corners = []
        half = [0.5 * q[c] for c in tiles]
        for shifted in (q_sw, q_nw, q_se, q_ne):
            corners.append([q[c] + 0.5 * shifted[c] for c in tiles])
            corners.append([half[c] + shifted[c] for c in tiles])
        return [e, w, s, n, scale_u, scale_v] + corners

    def relax(part, k, around, right):
        tiles = range(len(part))
        e, w, s, n, scale_u, scale_v, sw_u, sw_v, nw_u, nw_v, se_u, se_v, ne_u, ne_v = k
        u, u_n, u_s, v, v_n, v_s = around
        to_west_u, to_east_u, to_west_v, to_east_v = [], [], [], []
        for c in tiles:
            u4 = 4.0 * u[c]
            to_west_u.append(w[c] * u4 + (sw_u[c] * v_s[c] - nw_u[c] * v_n[c]))
            to_east_u.append(e[c] * u4 + (ne_u[c] * v_n[c] - se_u[c] * v_s[c]))
            to_west_v.append(w[c] * v[c] + (sw_v[c] * u_s[c] - nw_v[c] * u_n[c]))
            to_east_v.append(e[c] * v[c] + (ne_v[c] * u_n[c] - se_v[c] * u_s[c]))
        to_west_u, to_west_v = shift_east(to_west_u), shift_east(to_west_v)
        to_east_u, to_east_v = shift_west(to_east_u), shift_west(to_east_v)
        new_u, new_v = [], []
        for c in tiles:
            mid_u = s[c] * u_s[c] + n[c] * u_n[c]
            mid_v = 4.0 * (s[c] * v_s[c] + n[c] * v_n[c])
            new_u.append(scale_u[c] * (right[0][c] + mid_u + (to_west_u[c] + to_east_u[c])))
            new_v.append(scale_v[c] * (right[1][c] + mid_v + (to_west_v[c] + to_east_v[c])))
        return new_u, new_v

    def put(new, values):
        return [(new, (i,), values[i]) for i in range(2)]

    def keep(k):
        return [(coef, (i,), k[i]) for i in range(FACTORS)]

    def read_sweep(now):
        def read(part, row, count):
            k = [load(coef, part, row, count, i) for i in range(FACTORS)]
            return k, load_around(part, row, count, now), load_right(part, row, count)

        return read

    def sweep(new):
        return lambda part, read: put(new, relax(part, *read))

    def read_first(part, row, count):
        return read_coefficients(part, row, count), load_right(part, row, count)

    def first_start(part, read):
        k = coefficients(part, read[0])
        return keep(k) + put(vel_a, [[a * b for a, b in zip(k[4 + i], read[1][i])] for i in range(2)])

    def read_start(part, row, count):
        return (*read_first(part, row, count), load_around(part, row, count, vel_b))

    def start(part, read):
        k = coefficients(part, read[0])
        return keep(k) + put(vel_a, relax(part, k, read[2], read[1]))

    return SimpleNamespace(**locals())


def setup_kernel(
    fr, ice, woven, own_sides, first_col, second_col,
    ext, vel_b,
    visc, vel_a, coef,
):
    west, east = sides("gx", first_col[...], second_col[...])
    lane = lanes_of(HALF)
    for f, (first, count) in enumerate(STRIP):
        for c in range(2):
            ext[f, MAIN[c] + TOP : MAIN[c] + TOP + TILE, :] = woven[f, c]
        from_east = scale_of(f) * turn(east, first, HALO)
        from_west = scale_of(f) * turn(west, first, 3 * HALO - count)
        own = own_sides[f]
        ext[f, SIDE + TOP : SIDE + TOP + HALF, :] = choose_side(lane, own, from_east, from_west, own)
    step = make_stages(ext, fr, ice, visc, vel_a, vel_b, coef)
    over_rows("tile", step.read_thickness, step.first_viscosity)
    over_rows("tile", step.read_first, step.first_start)
    over_rows("tile", step.read_sweep(vel_a), step.sweep(vel_b))


def model_kernel(
    fr, ice, ext_in, vel_in, first_row, second_row,
    vel_b, sums,
    ext, visc, vel_a, vel_c, coef, small,
):
    half = ALL_ROWS // 2
    for target, source in ((ext, ext_in), (vel_b, vel_in)):
        for f in range(source.shape[0]):
            for row in (0, half):
                target[f, row : row + half, :] = source[f, row : row + half, :]
    north, south = sides("gy", first_row[...], second_row[...])
    here = SIDE + TOP
    ends = []
    for f, (first, count) in enumerate(STRIP):
        for c in range(2):
            rows = slice(64 * c + first, 64 * c + first + count)
            ends.append((f, MAIN[c] + TOP - count, north[rows]))
            ends.append((f, MAIN[c] + TOP + TILE, south[rows]))
        rows = slice(128 + first % 32, 128 + first % 32 + count)
        source = BAND if f >= 2 else 0
        upper = lanes_of(count) < BAND
        above = turn(ext_in[f, here + HALF - count : here + HALF, :], 0, BAND)
        below = turn(ext_in[f, here : here + count, :], 0, BAND)
        ends.append((f, here - count, jnp.where(upper, turn(north[rows], source, 0), above)))
        ends.append((f, here + HALF, jnp.where(upper, below, turn(south[rows], source, BAND))))
    for f, row, cells in ends:
        ext[f, row : row + cells.shape[0], :] = cells

    step = make_stages(ext, fr, ice, visc, vel_a, vel_b, coef)
    over_ends(32, step.read_thickness, step.first_viscosity)
    over_ends(32, step.read_first, step.first_start)
    over_ends(24, step.read_sweep(vel_a), step.sweep(vel_b))

    def iteration(i, carry):
        over_rows("frame", step.read_viscosity, step.viscosity)
        over_rows("frame", step.read_start, step.start)
        over_rows("frame", step.read_sweep(vel_a), step.sweep(vel_b))
        return carry

    lax.fori_loop(1, PIC - 1, iteration, 0)
    join_parts(vel_b, ((0,), (1,)), True)
    over_rows("inner", step.read_viscosity, step.viscosity)
    over_rows("inner", step.read_start, step.start)

    load = step.load

    def read_last(part, row, count):
        return (*step.read_sweep(vel_a)(part, row, count), [load(ext, part, row, count, 3 + i) for i in range(2)])

    def last_sweep(part, read):
        k, around, right, seen = read
        new = step.relax(part, k, around, right)
        misfit = [[0.5 * (a - b) for a, b in zip(new[i], seen[i])] for i in range(2)]
        first = [[a * b for a, b in zip(k[4 + i], misfit[i])] for i in range(2)]
        return step.put(vel_b, new) + step.put(vel_c, first) + [(ext, (1 + i,), misfit[i]) for i in range(2)]

    over_rows("inner", read_last, last_sweep)

    def two_sweeps(i, carry):
        over_rows("inner", step.read_sweep(vel_c), step.sweep(vel_a))
        over_rows("inner", step.read_sweep(vel_a), step.sweep(vel_c))
        return carry

    lax.fori_loop(0, (ADJ - 2) // 2, two_sweeps, 0)

    def read_gradient(part, row, count):
        others = [load(vel_b, part, row, count, i) for i in range(2)] + [load(fr, part, row, count)]
        return (*step.read_sweep(vel_c)(part, row, count), others)

    def gradient(part, read):
        k, around, right, (u, v, friction) = read
        lu, lv = step.relax(part, k, around, right)
        return [(visc, (0,), [-2.0 * friction[c] * (u[c] * lu[c] + v[c] * lv[c]) for c in range(len(part))])]

    over_rows("tile", read_gradient, gradient)
    join_parts(visc, ((0,),), False)
    down = sum(visc[0, pl.ds(tile + TOP + j, CT, stride=4), :] for tile in MAIN for j in range(4))
    total = gather(down + turn(down, 1, 0), 2 * (lanes_of(CT) % CT))
    small[...] = total
    packed = jnp.where(
        lanes_of(PACK) < CT, small[pl.ds(0, PACK, stride=2), :], small[pl.ds(1, PACK, stride=2), :]
    )
    for j in range(sums.shape[0]):
        sums[j] = packed


def unweave_kernel(vel, vel_u, vel_v, plain, sems):
    lane = lanes_of(HALF)
    edge = HALO // 2
    parts = [(i, band) for i in range(2) for band in range(2)]

    def read(i, band):
        row = TOP + HALF * band
        return [vel[i, tile + row : tile + row + HALF, :] for tile in MAIN] + [vel[i, SIDE + TOP : SIDE + TOP + HALF, :]]

    copies = []
    pending = read(*parts[0])
    for k, (i, band) in enumerate(parts):
        even, odd, mixed = pending
        if k + 1 < len(parts):
            pending = read(*parts[k + 1])
        cells = []
        for c in range(2):
            source = BAND * c + lane // 2
            cells.append(jnp.where(lane % 2 == 0, gather(even, source), gather(odd, source)))
        low = jnp.where(lane < edge, turn(mixed, BAND * band + 3 * HALO, 0), cells[0])
        high = jnp.where(lane >= LANES - edge, turn(mixed, BAND * band + edge, LANES - edge), cells[1])
        rows = slice(HALF * band, HALF * (band + 1))
        plain[i, rows, :LANES] = low
        plain[i, rows, LANES:] = high
        out = (vel_u, vel_v)[i]
        copies.append(pltpu.make_async_copy(plain.at[i, rows], out.at[rows], sems.at[2 * i + band]))
        copies[-1].start()
    for copy in copies:
        copy.wait()


def pick_kernel(owners, gathered, own, other):
    owned = own.shape[0]
    first = lax.axis_index("gy") % 2 == 0
    total = []
    for block in range(2 * owned):
        parts = [jnp.where(owners[t, block : block + 1, :] > 0, gathered[t], 0.0) for t in range(owners.shape[0])]
        while len(parts) > 1:
            parts = [sum(parts[i : i + 2]) for i in range(0, len(parts), 2)]
        total.append(parts[0])
    for block in range(owned):
        low, high = total[block], total[block + owned]
        for out, cells in ((own, jnp.where(first, low, high)), (other, jnp.where(first, high, low))):
            for j in range(PACK):
                out[block : block + 1, j * LANES : (j + 1) * LANES] = cells[j : j + 1]


def in_vmem(count):
    return [pl.BlockSpec(memory_space=pltpu.VMEM)] * count


def in_smem(count):
    return [pl.BlockSpec(memory_space=pltpu.SMEM)] * count


def per_device(thickness, driving, observed, control, ice_mask, tile_block):
    f32 = jnp.float32
    rows, cols = lax.axis_size("gy"), lax.axis_size("gx")
    tile_block, ice_mask = tile_block[:, :, 0].T, ice_mask.T
    params = pltpu.CompilerParams(vmem_limit_bytes=VMEM_LIMIT)

    def shape(*sizes):
        return jax.ShapeDtypeStruct(sizes, f32)

    def swap(axis, cells_first, cells_second):
        count = lax.axis_size(axis)
        received = []
        for cells, low in ((cells_first, 0), (cells_second, 1)):
            pairs = [(i, i + 1) for i in range(low, count - 1, 2)]
            received.append(lax.ppermute(cells, axis, pairs + [(j, i) for i, j in pairs]))
        return received

    fields = thickness, driving, observed
    owned = control.shape[0]
    *edges, parcels = pl.pallas_call(
        pack_kernel,
        out_shape=[shape(HALF, LANES)] * 2 + [shape(rows, PARCEL, LANES)],
        in_specs=[pl.BlockSpec(memory_space=pltpu.HBM)] * 5,
        out_specs=[pl.BlockSpec(memory_space=pltpu.HBM)] * 3,
        scratch_shapes=[
            pltpu.SMEM(tile_block.shape, jnp.int32),
            pltpu.VMEM((5, TILE, TILE), f32),
            pltpu.VMEM(control.shape, f32),
            pltpu.VMEM((owned, PACK, LANES), f32),
            pltpu.VMEM((rows, PARCEL, LANES), f32),
            pltpu.VMEM((2, HALF, LANES), f32),
            pltpu.SemaphoreType.DMA((10,)),
        ],
        compiler_params=pltpu.CompilerParams(vmem_limit_bytes=PACK_VMEM_LIMIT),
        name="pack",
    )(tile_block, control, *fields)
    parcels = lax.all_to_all(parcels, "gy", 0, 0, tiled=True)
    columns_in = swap("gx", *edges)
    woven, own_sides, strips = pl.pallas_call(
        weave_kernel,
        out_shape=[shape(5, 2, TILE, LANES), shape(5, HALF, LANES), shape(2, 3, 64, LANES)],
        in_specs=in_vmem(3),
        out_specs=in_vmem(3),
        compiler_params=params,
        name="weave",
    )(*fields)
    strips = pl.pallas_call(
        rows_kernel,
        out_shape=[shape(160, LANES)] * 2,
        in_specs=in_vmem(3),
        out_specs=in_vmem(2),
        compiler_params=params,
        name="rows",
    )(strips, *columns_in)
    rows_in = swap("gy", *strips)
    *friction, owners = pl.pallas_call(
        friction_kernel,
        out_shape=[shape(ALL_ROWS, LANES)] * 2
        + [jax.ShapeDtypeStruct((cols * rows // 2, 2 * owned, LANES), jnp.int32)],
        in_specs=in_smem(2) + in_vmem(1),
        out_specs=in_vmem(3),
        scratch_shapes=[pltpu.VMEM((PATCH, LANES), f32)],
        compiler_params=params,
        name="friction",
    )(tile_block, ice_mask, parcels)
    prepared = pl.pallas_call(
        setup_kernel,
        out_shape=[shape(5, ALL_ROWS, LANES), shape(2, ALL_ROWS, LANES)],
        in_specs=in_vmem(6),
        out_specs=in_vmem(2),
        scratch_shapes=[
            pltpu.VMEM((3, ALL_ROWS, LANES), f32),
            pltpu.VMEM((2, ALL_ROWS, LANES), f32),
            pltpu.VMEM((FACTORS, ALL_ROWS, LANES), f32),
        ],
        compiler_params=params,
        name="setup",
    )(*friction, woven, own_sides, *columns_in)

    vel, sums = pl.pallas_call(
        model_kernel,
        out_shape=(shape(2, ALL_ROWS, LANES), shape(cols * rows // 2, PACK, LANES)),
        in_specs=in_vmem(6),
        out_specs=in_vmem(2),
        scratch_shapes=[
            pltpu.VMEM((5, ALL_ROWS, LANES), f32),
            pltpu.VMEM((3, ALL_ROWS, LANES), f32),
            pltpu.VMEM((2, ALL_ROWS, LANES), f32),
            pltpu.VMEM((2, ALL_ROWS, LANES), f32),
            pltpu.VMEM((FACTORS, ALL_ROWS, LANES), f32),
            pltpu.VMEM((CT, LANES), f32),
        ],
        compiler_params=params,
        name="model",
    )(*friction, *prepared, *rows_in)
    vel_u, vel_v = pl.pallas_call(
        unweave_kernel,
        out_shape=[shape(TILE, TILE)] * 2,
        in_specs=in_vmem(1),
        out_specs=[pl.BlockSpec(memory_space=pltpu.HBM)] * 2,
        scratch_shapes=[pltpu.VMEM((2, TILE, TILE), f32), pltpu.SemaphoreType.DMA((4,))],
        compiler_params=params,
        name="unweave",
    )(vel)

    same_core = [[i * rows + j for i in range(cols) for j in range(core, rows, 2)] for core in range(2)]
    sums = lax.all_to_all(sums, ("gx", "gy"), 0, 0, tiled=True, axis_index_groups=same_core)
    own, other = pl.pallas_call(
        pick_kernel,
        out_shape=[shape(*control.shape)] * 2,
        in_specs=in_vmem(2),
        out_specs=in_vmem(2),
        compiler_params=params,
        name="pick",
    )(owners, sums)
    gradient = own + lax.ppermute(other, "gy", [(j, j ^ 1) for j in range(rows)])
    return vel_u, vel_v, gradient


def solution(mesh):
    return jax.shard_map(
        per_device,
        mesh=mesh,
        in_specs=(P("gy", "gx"), P(None, "gy", "gx"), P(None, "gy", "gx"), P("gy", None), P(), P()),
        out_specs=(P("gy", "gx"), P("gy", "gx"), P("gy", None)),
        check_vma=False,
    )
```

```python
from types import SimpleNamespace

import jax
import jax.numpy as jnp
from jax import lax
from jax.experimental import pallas as pl
from jax.experimental.pallas import tpu as pltpu
from jax.sharding import PartitionSpec as P

TILE = 256
PIC = 4
SW = 2
ADJ = 6
CT = 64
COARSE = 4096

LANES = 128
HALO = 16
OBS = 8
MARGIN = 8
TOP = MARGIN + HALO
ROWS = TILE + 2 * TOP
HALF = TILE // 2
SIDE = 2 * ROWS
BAND = LANES // 2
ALL_ROWS = SIDE + HALF + 2 * TOP
MAIN = (0, ROWS)
SIDES = (SIDE,)
SPANS = {
    "frame": (MARGIN, 2, 144, MARGIN, 80, 0, 0),
    "inner": (MARGIN + 8, 2, 136, MARGIN + 8, 72, 0, 0),
    "tile": (TOP, 2, 128, TOP, 64, 0, 0),
}
FACTORS = 14
AHEAD = 16
PACK = COARSE // LANES
VMEM_LIMIT = 24 * 1024 * 1024
PACK_VMEM_LIMIT = 62 * 1024 * 1024

STRIP = ((0, HALO), (HALO, HALO), (2 * HALO, HALO), (3 * HALO, OBS), (3 * HALO + OBS, OBS))

CONTROL = ((0, 0, PACK, 0), (-1, PACK - 2, 2, PACK), (1, 0, 2, PACK + 2))
FOLDED = 40
PARCEL = 48
PATCH = CT + 8

visc_scale = 0.1
strain_floor = 0.05


def lanes_of(rows):
    return lax.broadcasted_iota(jnp.int32, (rows, LANES), 1)


def is_even(axis):
    return lax.axis_index(axis) % 2 == 0


def side_lanes(rows, ds, group):
    place = (lanes_of(rows) - 8 * group) % CT
    return place < 4 if ds > 0 else place >= CT - 4


def fill_parcels(tile_block, owned_blocks, parcels):
    tile_cols, tile_rows = tile_block.shape
    owned = owned_blocks.shape[0]
    mine = lax.axis_index("gy") * owned
    col_tile = lax.axis_index("gx")

    def spread(row, carry):
        for ds in (-1, 0, 1):
            col = col_tile + ds
            place = tile_block[jnp.clip(col, 0, tile_cols - 1), row] - mine

            @pl.when((col >= 0) & (col < tile_cols) & (place >= 0) & (place < owned))
            def _():
                for dr, first, count, at in CONTROL:
                    target = row - dr

                    @pl.when((target >= 0) & (target < tile_rows))
                    def _():
                        if ds == 0:
                            parcels[target, at : at + count, :] = owned_blocks[place, first : first + count, :]
                            return
                        start = FOLDED + at % 8
                        rows = min(count, 8)
                        folded = parcels[target, start : start + rows, :]
                        for i in range(count // rows):
                            group = at // 8 + i
                            cells = owned_blocks[place, first + 8 * i : first + 8 * i + rows, :]
                            folded = jnp.where(side_lanes(rows, ds, group), turn(cells, 0, 8 * group), folded)
                        parcels[target, start : start + rows, :] = folded

        return carry

    lax.fori_loop(0, tile_rows, spread, 0)


def pack_kernel(
    table, control, thick, drive, obs, first_col, second_col, parcels,
    tile_block, held, held_control, owned_blocks, packed_parcels, packed_cols, sems,
):
    table_copy = pltpu.make_async_copy(table, tile_block, sems.at[9])
    table_copy.start()
    copies = [pltpu.make_async_copy(control, held_control, sems.at[5])]
    for f, field in enumerate((thick, drive.at[0], drive.at[1], obs.at[0], obs.at[1])):
        copies.append(pltpu.make_async_copy(field, held.at[f], sems.at[f]))
    for copy in copies:
        copy.start()
    packed_parcels[...] = jnp.zeros_like(packed_parcels)
    copies[0].wait()
    shard = [held_control[:, j * LANES : (j + 1) * LANES] for j in range(PACK)]
    for j in range(PACK):
        owned_blocks[:, j, :] = shard[j]
    table_copy.wait()
    fill_parcels(tile_block, owned_blocks, packed_parcels)
    results = [pltpu.make_async_copy(packed_parcels, parcels, sems.at[6])]
    results[0].start()

    lane = lanes_of(HALF)
    left = jnp.zeros((HALF, LANES), jnp.float32)
    right = jnp.zeros((HALF, LANES), jnp.float32)
    for f, (first, count) in enumerate(STRIP):
        copies[1 + f].wait()
        for part in range(2):
            rows = slice(part * HALF, (part + 1) * HALF)
            start = part * BAND + first
            inside = (lane >= start) & (lane < start + count)
            left = jnp.where(inside, turn(held[f, rows, :LANES], 0, start), left)
            right = jnp.where(inside, turn(held[f, rows, LANES:], LANES - count, start), right)
    even = is_even("gx")
    packed_cols[0] = jnp.where(even, right, left)
    packed_cols[1] = jnp.where(even, left, right)
    for i, out in enumerate((first_col, second_col)):
        results.append(pltpu.make_async_copy(packed_cols.at[i], out, sems.at[7 + i]))
        results[-1].start()
    for copy in results:
        copy.wait()


def sides(axis, first_pair, second_pair):
    even = is_even(axis)
    return jnp.where(even, second_pair, first_pair), jnp.where(even, first_pair, second_pair)


def choose_side(lane, high, east, west, low):
    place = lane % BAND
    return jnp.where(
        place < HALO, high, jnp.where(place < 2 * HALO, east, jnp.where(place < 3 * HALO, west, low))
    )


def turn(cells, source, target):
    shift = (target - source) % LANES
    return pltpu.roll(cells, shift, 1) if shift else cells


def gather(cells, source):
    return jnp.take_along_axis(cells, source, axis=1)


def scale_of(f):
    return (0.25 * visc_scale * 4.0 ** (1.0 / 3.0), 0.5, 0.5, 1.0, 1.0)[f]


def weave_kernel(thick, drive, obs, woven, own_sides, edges):
    lane, half_lane = lanes_of(TILE), lanes_of(HALF)
    source = 2 * lane % LANES
    for f, (field, (first, count)) in enumerate(zip((thick, drive.at[0], drive.at[1], obs.at[0], obs.at[1]), STRIP)):
        low, high = scale_of(f) * field[:, :LANES], scale_of(f) * field[:, LANES:]
        tiles = [jnp.where(lane < BAND, gather(low, source + i), gather(high, source + i)) for i in range(2)]
        bands = []
        for band in (0, BAND):
            bands.append(
                jnp.where(lane % BAND < BAND // 2, turn(high, LANES - HALO, band), turn(low, 0, band + 3 * HALO))
            )
        own_sides[f] = jnp.where(half_lane < BAND, bands[0][:HALF], bands[1][HALF:])
        for c in range(2):
            woven[f, c] = tiles[c]
        for c, tile in enumerate(tiles + [bands[0]]):
            edges[0, c, first : first + count, :] = tile[:count]
            edges[1, c, first : first + count, :] = tile[TILE - count :]


def rows_kernel(edges, first_col, second_col, first_pair, second_pair):
    west, east = sides("gx", first_col[...], second_col[...])
    even = is_even("gy")
    for c in range(2):
        top, bottom = edges[0, c], edges[1, c]
        first_pair[64 * c : 64 * c + 64, :] = jnp.where(even, bottom, top)
        second_pair[64 * c : 64 * c + 64, :] = jnp.where(even, top, bottom)
    strips = []
    for i in range(2):
        fields = []
        for f, (first, count) in enumerate(STRIP):
            packed = slice(HALF - count, HALF) if i else slice(0, count)
            source = BAND * i + first
            target = BAND if f >= 2 else 0
            own = turn(edges[i, 2, first : first + count, :], 0, target)
            from_east = scale_of(f) * turn(east[packed], source, target + HALO)
            from_west = scale_of(f) * turn(west[packed], source, target + 3 * HALO - count)
            fields.append(choose_side(lanes_of(count), own, from_east, from_west, own))
        lane = lanes_of(HALO)
        lower = jnp.concatenate(fields[3:], axis=0)
        strips.append((jnp.where(lane < BAND, fields[0], fields[2]), jnp.where(lane < BAND, fields[1], lower)))
    for k in range(2):
        top, bottom = strips[0][k], strips[1][k]
        rows = slice(128 + HALO * k, 128 + HALO * (k + 1))
        first_pair[rows, :] = jnp.where(even, bottom, top)
        second_pair[rows, :] = jnp.where(even, top, bottom)


def shift_east(tiles):
    turned = pltpu.roll(tiles[0], LANES - 1, 1)
    return [turned] if len(tiles) == 1 else [tiles[1], turned]


def shift_west(tiles):
    turned = pltpu.roll(tiles[-1], 1, 1)
    return [turned] if len(tiles) == 1 else [turned, tiles[0]]


def run_groups(groups, read, work):
    pending = [read(*group) for group in groups[:AHEAD]]
    for k, (part, row, count) in enumerate(groups):
        if k + AHEAD < len(groups):
            pending.append(read(*groups[k + AHEAD]))
        for ref, lead, values in work(part, pending[k]):
            for tile, value in zip(part, values):
                ref[(*lead, pl.ds(row + tile, count), slice(None))] = value


def block_groups(row, main, side_row, side):
    step = 16
    groups = [(g / main, MAIN, row + g, min(step, main - g)) for g in range(0, main, step)]
    groups += [((g + 1) / side, SIDES, side_row + g, min(step, side - g)) for g in range(0, side, step)]
    return [group[1:] for group in sorted(groups, key=lambda group: group[0])]


def over_rows(span, read, work):
    start, blocks, main, side_start, side, main_rest, side_rest = SPANS[span]

    def block(i, carry):
        row, side_row = pl.multiple_of(start + i * main, 8), pl.multiple_of(side_start + i * side, 8)
        run_groups(block_groups(row, main, side_row, side), read, work)
        return carry

    lax.fori_loop(0, blocks, block, 0)
    if main_rest:
        none = 8 * jnp.minimum(lax.axis_index("gx"), 0)
        row = pl.multiple_of(none + start + blocks * main, 8)
        side_row = pl.multiple_of(none + side_start + blocks * side, 8)
        run_groups(block_groups(row, main_rest, side_row, side_rest), read, work)


def over_ends(count, read, work):
    row = pl.multiple_of(MARGIN + 8 * jnp.minimum(lax.axis_index("gx"), 0), 8)
    far, side_far = TILE + 2 * HALO - count, HALF + 2 * HALO - count
    run_groups(
        [(MAIN, row, count), (SIDES, row, count), (MAIN, row + far, count), (SIDES, row + side_far, count)], read, work
    )


def join_parts(ref, leads, whole):
    edge = HALO // 2
    few = edge // 2
    frame = HALO if whole else 0
    first, count = TOP - frame, HALF + 2 * frame
    kept = HALF + frame
    lane = lanes_of(kept)
    outer = (lane < few) | (lane >= LANES - few)
    near = jnp.where(lane < few, 3 * HALO + 2 * lane, edge + 2 * (lane - LANES + few))
    near = jnp.clip(near, 0, LANES - 2 - BAND)
    side_lane = lanes_of(count)
    place = side_lane % BAND
    inner = jnp.clip(jnp.where(place < edge, LANES - edge + place // 2, place // 2 - 24), 0, LANES - 1)
    for lead in leads:
        def at(row, rows):
            return (*lead, slice(row, row + rows), slice(None))

        mixed = ref[at(SIDE + first, count)]
        halves = [[ref[at(tile + first + HALF * h, count)] for tile in MAIN] for h in range(2)]
        if whole:
            parts = [jnp.where(side_lane % 2 == 0, gather(even, inner), gather(odd, inner)) for even, odd in halves]
            wanted = (place < edge) | (place >= BAND - edge)
            ref[at(SIDE + first, count)] = jnp.where(wanted, jnp.where(side_lane < BAND, *parts), mixed)
        for h, skip in ((0, 0), (1, frame)):
            cells = mixed[skip : skip + kept]
            for c, tile in enumerate(MAIN):
                new = jnp.where(outer, gather(cells, near + (BAND * h + c)), halves[h][c][skip : skip + kept])
                ref[at(tile + first + HALF * h + skip, kept)] = new


def friction_kernel(tile_block, ice_mask, parcels, fr, ice, owners, patch):
    tile_cols, tile_rows = ice_mask.shape
    row_tile = lax.axis_index("gy")
    col_tile = lax.axis_index("gx")
    core = row_tile % 2
    place = lax.broadcasted_iota(jnp.int32, owners.shape[1:], 0)
    for t in range(owners.shape[0]):
        block = tile_block[t // (tile_rows // 2), t % (tile_rows // 2) * 2 + core]
        owners[t] = (place == block - (row_tile - core) * (owners.shape[1] // 2)).astype(jnp.int32)

    flat = sum(parcels[j] for j in range(tile_rows))
    folded = flat[FOLDED:]
    for dr, _, count, at in CONTROL:
        cells = flat[at : at + count]
        if dr == 0:
            side = jnp.concatenate([turn(folded, 8 * g, 0) for g in range(PACK // 8)], axis=0)
        else:
            side = turn(folded, PACK, 0)[at % 8 : at % 8 + count]
        inner = lanes_of(count) < CT
        row = 4 + {-1: -4, 0: 0, 1: CT}[dr]
        patch[pl.ds(row, count, stride=2), :] = jnp.where(inner, cells, turn(side, 0, CT))
        patch[pl.ds(row + 1, count, stride=2), :] = jnp.where(inner, turn(cells, 0, CT), side)

    cells = 0.5 * jnp.exp(patch[...])
    lane = lanes_of(PATCH)
    wide = gather(cells, lane // 2)
    for tile in MAIN:
        for j in range(4):
            fr[pl.ds(tile + MARGIN + j, PATCH, stride=4), :] = wide
    lane = lanes_of(40)
    place = lane % BAND // 4
    source = jnp.where(place < 8, 60 + place, (116 + place) % LANES)
    wide = jnp.where(
        lane < BAND,
        gather(cells[:40], source),
        gather(cells[PATCH - 40 :], source),
    )
    for j in range(4):
        fr[pl.ds(SIDE + MARGIN + j, 40, stride=4), :] = wide

    side_ice = []
    for dr, first, count in ((-1, MARGIN, HALO), (0, TOP, TILE), (1, TOP + TILE, HALO)):
        masks = []
        for ds in (-1, 0, 1):
            row, col = row_tile + dr, col_tile + ds
            inside = (row >= 0) & (row < tile_rows) & (col >= 0) & (col < tile_cols)
            row = jnp.clip(row, 0, tile_rows - 1)
            col = jnp.clip(col, 0, tile_cols - 1)
            masks.append(jnp.where(inside, ice_mask[col, row], 0).astype(jnp.float32))
        for c in range(2):
            ice[MAIN[c] + first : MAIN[c] + first + count, :] = jnp.full((count, LANES), masks[1])
        side_ice.append(choose_side(lanes_of(HALO), masks[1], masks[2], masks[0], masks[1]))
    upper = lanes_of(HALO) < BAND
    for i in range(HALF // HALO):
        ice[SIDE + TOP + i * HALO : SIDE + TOP + (i + 1) * HALO, :] = side_ice[1]
    ice[SIDE + MARGIN : SIDE + TOP, :] = jnp.where(upper, side_ice[0], side_ice[1])
    ice[SIDE + TOP + HALF : SIDE + TOP + HALF + HALO, :] = jnp.where(upper, side_ice[1], side_ice[2])


def make_stages(ext, fr, ice, visc, vel_a, vel_b, coef):
    def load(ref, part, row, count, *lead):
        return [ref[(*lead, pl.ds(row + tile, count), slice(None))] for tile in part]

    def load_around(part, row, count, now):
        return [load(now, part, r, count, i) for i in range(2) for r in (row, row - 1, row + 1)]

    def load_right(part, row, count):
        return [load(ext, part, row, count, i) for i in (1, 2)]

    def read_thickness(part, row, count):
        return load(ext, part, row, count, 0)

    def keep_viscosity(q):
        return [(visc, (0,), q), (visc, (1,), shift_west(q)), (visc, (2,), shift_east(q))]

    def first_viscosity(part, thickness):
        factor = (4.0 * strain_floor) ** (-1.0 / 3.0)
        return keep_viscosity([factor * t for t in thickness])

    def read_viscosity(part, row, count):
        return read_thickness(part, row, count), load_around(part, row, count, vel_b)

    def viscosity(part, read):
        thickness, (u, u_n, u_s, v, v_n, v_s) = read
        u_e, u_w = shift_east(u), shift_west(u)
        v_e, v_w = shift_east(v), shift_west(v)
        result = []
        for c in range(len(part)):
            ux, vx = u_e[c] - u_w[c], v_e[c] - v_w[c]
            uy, vy = u_s[c] - u_n[c], v_s[c] - v_n[c]
            shear = uy + vx
            strain = (ux * (ux + vy) + vy * vy) + (0.25 * (shear * shear) + 4.0 * strain_floor)
            result.append(thickness[c] * jnp.exp(jnp.log(strain) * (-1.0 / 3.0)))
        return keep_viscosity(result)

    def inverse(x):
        near = pl.reciprocal(x, approx=True)
        return near * (2.0 - x * near)

    def read_coefficients(part, row, count):
        around = [load(visc, part, r, count, i) for i in range(3) for r in (row, row - 1, row + 1)]
        return around + [load(fr, part, row, count), load(ice, part, row, count)]

    def coefficients(part, read):
        tiles = range(len(part))
        q, q_n, q_s, q_w, q_nw, q_sw, q_e, q_ne, q_se, friction, mask = read
        w = [q[c] + q_w[c] for c in tiles]
        e = [q[c] + q_e[c] for c in tiles]
        s = [q[c] + q_s[c] for c in tiles]
        n = [q[c] + q_n[c] for c in tiles]
        scale_u, scale_v = [], []
        for c in tiles:
            across, along = e[c] + w[c], s[c] + n[c]
            scale_u.append(mask[c] * inverse(friction[c] + along + 4.0 * across))
            scale_v.append(mask[c] * inverse(friction[c] + across + 4.0 * along))
        corners = []
        half = [0.5 * q[c] for c in tiles]
        for shifted in (q_sw, q_nw, q_se, q_ne):
            corners.append([q[c] + 0.5 * shifted[c] for c in tiles])
            corners.append([half[c] + shifted[c] for c in tiles])
        return [e, w, s, n, scale_u, scale_v] + corners

    def relax(part, k, around, right):
        tiles = range(len(part))
        e, w, s, n, scale_u, scale_v, sw_u, sw_v, nw_u, nw_v, se_u, se_v, ne_u, ne_v = k
        u, u_n, u_s, v, v_n, v_s = around
        to_west_u, to_east_u, to_west_v, to_east_v = [], [], [], []
        for c in tiles:
            u4 = 4.0 * u[c]
            to_west_u.append(w[c] * u4 + (sw_u[c] * v_s[c] - nw_u[c] * v_n[c]))
            to_east_u.append(e[c] * u4 + (ne_u[c] * v_n[c] - se_u[c] * v_s[c]))
            to_west_v.append(w[c] * v[c] + (sw_v[c] * u_s[c] - nw_v[c] * u_n[c]))
            to_east_v.append(e[c] * v[c] + (ne_v[c] * u_n[c] - se_v[c] * u_s[c]))
        to_west_u, to_west_v = shift_east(to_west_u), shift_east(to_west_v)
        to_east_u, to_east_v = shift_west(to_east_u), shift_west(to_east_v)
        new_u, new_v = [], []
        for c in tiles:
            mid_u = s[c] * u_s[c] + n[c] * u_n[c]
            mid_v = 4.0 * (s[c] * v_s[c] + n[c] * v_n[c])
            new_u.append(scale_u[c] * (right[0][c] + mid_u + (to_west_u[c] + to_east_u[c])))
            new_v.append(scale_v[c] * (right[1][c] + mid_v + (to_west_v[c] + to_east_v[c])))
        return new_u, new_v

    def put(new, values):
        return [(new, (i,), values[i]) for i in range(2)]

    def keep(k):
        return [(coef, (i,), k[i]) for i in range(FACTORS)]

    def read_sweep(now):
        def read(part, row, count):
            k = [load(coef, part, row, count, i) for i in range(FACTORS)]
            return k, load_around(part, row, count, now), load_right(part, row, count)

        return read

    def sweep(new):
        return lambda part, read: put(new, relax(part, *read))

    def read_first(part, row, count):
        return read_coefficients(part, row, count), load_right(part, row, count)

    def first_start(part, read):
        k = coefficients(part, read[0])
        return keep(k) + put(vel_a, [[a * b for a, b in zip(k[4 + i], read[1][i])] for i in range(2)])

    def read_start(part, row, count):
        return (*read_first(part, row, count), load_around(part, row, count, vel_b))

    def start(part, read):
        k = coefficients(part, read[0])
        return keep(k) + put(vel_a, relax(part, k, read[2], read[1]))

    return SimpleNamespace(**locals())


def setup_kernel(
    fr, ice, woven, own_sides, first_col, second_col,
    ext, vel_b,
    visc, vel_a, coef,
):
    west, east = sides("gx", first_col[...], second_col[...])
    lane = lanes_of(HALF)
    for f, (first, count) in enumerate(STRIP):
        for c in range(2):
            ext[f, MAIN[c] + TOP : MAIN[c] + TOP + TILE, :] = woven[f, c]
        from_east = scale_of(f) * turn(east, first, HALO)
        from_west = scale_of(f) * turn(west, first, 3 * HALO - count)
        own = own_sides[f]
        ext[f, SIDE + TOP : SIDE + TOP + HALF, :] = choose_side(lane, own, from_east, from_west, own)
    step = make_stages(ext, fr, ice, visc, vel_a, vel_b, coef)
    over_rows("tile", step.read_thickness, step.first_viscosity)
    over_rows("tile", step.read_first, step.first_start)
    over_rows("tile", step.read_sweep(vel_a), step.sweep(vel_b))


def model_kernel(
    fr, ice, ext_in, vel_in, first_row, second_row,
    vel_b, sums,
    ext, visc, vel_a, vel_c, coef, small,
):
    half = ALL_ROWS // 2
    for target, source in ((ext, ext_in), (vel_b, vel_in)):
        for f in range(source.shape[0]):
            for row in (0, half):
                target[f, row : row + half, :] = source[f, row : row + half, :]
    north, south = sides("gy", first_row[...], second_row[...])
    here = SIDE + TOP
    ends = []
    for f, (first, count) in enumerate(STRIP):
        for c in range(2):
            rows = slice(64 * c + first, 64 * c + first + count)
            ends.append((f, MAIN[c] + TOP - count, north[rows]))
            ends.append((f, MAIN[c] + TOP + TILE, south[rows]))
        rows = slice(128 + first % 32, 128 + first % 32 + count)
        source = BAND if f >= 2 else 0
        upper = lanes_of(count) < BAND
        above = turn(ext_in[f, here + HALF - count : here + HALF, :], 0, BAND)
        below = turn(ext_in[f, here : here + count, :], 0, BAND)
        ends.append((f, here - count, jnp.where(upper, turn(north[rows], source, 0), above)))
        ends.append((f, here + HALF, jnp.where(upper, below, turn(south[rows], source, BAND))))
    for f, row, cells in ends:
        ext[f, row : row + cells.shape[0], :] = cells

    step = make_stages(ext, fr, ice, visc, vel_a, vel_b, coef)
    over_ends(32, step.read_thickness, step.first_viscosity)
    over_ends(32, step.read_first, step.first_start)
    over_ends(24, step.read_sweep(vel_a), step.sweep(vel_b))

    def iteration(i, carry):
        over_rows("frame", step.read_viscosity, step.viscosity)
        over_rows("frame", step.read_start, step.start)
        over_rows("frame", step.read_sweep(vel_a), step.sweep(vel_b))
        return carry

    lax.fori_loop(1, PIC - 1, iteration, 0)
    join_parts(vel_b, ((0,), (1,)), True)
    over_rows("inner", step.read_viscosity, step.viscosity)
    over_rows("inner", step.read_start, step.start)

    load = step.load

    def read_last(part, row, count):
        return (*step.read_sweep(vel_a)(part, row, count), [load(ext, part, row, count, 3 + i) for i in range(2)])

    def last_sweep(part, read):
        k, around, right, seen = read
        new = step.relax(part, k, around, right)
        misfit = [[0.5 * (a - b) for a, b in zip(new[i], seen[i])] for i in range(2)]
        first = [[a * b for a, b in zip(k[4 + i], misfit[i])] for i in range(2)]
        return step.put(vel_b, new) + step.put(vel_c, first) + [(ext, (1 + i,), misfit[i]) for i in range(2)]

    over_rows("inner", read_last, last_sweep)

    def two_sweeps(i, carry):
        over_rows("inner", step.read_sweep(vel_c), step.sweep(vel_a))
        over_rows("inner", step.read_sweep(vel_a), step.sweep(vel_c))
        return carry

    lax.fori_loop(0, (ADJ - 2) // 2, two_sweeps, 0)

    def read_gradient(part, row, count):
        others = [load(vel_b, part, row, count, i) for i in range(2)] + [load(fr, part, row, count)]
        return (*step.read_sweep(vel_c)(part, row, count), others)

    def gradient(part, read):
        k, around, right, (u, v, friction) = read
        lu, lv = step.relax(part, k, around, right)
        return [(visc, (0,), [-2.0 * friction[c] * (u[c] * lu[c] + v[c] * lv[c]) for c in range(len(part))])]

    over_rows("tile", read_gradient, gradient)
    join_parts(visc, ((0,),), False)
    down = sum(visc[0, pl.ds(tile + TOP + j, CT, stride=4), :] for tile in MAIN for j in range(4))
    total = gather(down + turn(down, 1, 0), 2 * (lanes_of(CT) % CT))
    small[...] = total
    packed = jnp.where(
        lanes_of(PACK) < CT, small[pl.ds(0, PACK, stride=2), :], small[pl.ds(1, PACK, stride=2), :]
    )
    for j in range(sums.shape[0]):
        sums[j] = packed


def unweave_kernel(vel, vel_u, vel_v, plain, sems):
    lane = lanes_of(HALF)
    edge = HALO // 2
    parts = [(i, band) for i in range(2) for band in range(2)]

    def read(i, band):
        row = TOP + HALF * band
        return [vel[i, tile + row : tile + row + HALF, :] for tile in MAIN] + [vel[i, SIDE + TOP : SIDE + TOP + HALF, :]]

    copies = []
    pending = read(*parts[0])
    for k, (i, band) in enumerate(parts):
        even, odd, mixed = pending
        if k + 1 < len(parts):
            pending = read(*parts[k + 1])
        cells = []
        for c in range(2):
            source = BAND * c + lane // 2
            cells.append(jnp.where(lane % 2 == 0, gather(even, source), gather(odd, source)))
        low = jnp.where(lane < edge, turn(mixed, BAND * band + 3 * HALO, 0), cells[0])
        high = jnp.where(lane >= LANES - edge, turn(mixed, BAND * band + edge, LANES - edge), cells[1])
        rows = slice(HALF * band, HALF * (band + 1))
        plain[i, rows, :LANES] = low
        plain[i, rows, LANES:] = high
        out = (vel_u, vel_v)[i]
        copies.append(pltpu.make_async_copy(plain.at[i, rows], out.at[rows], sems.at[2 * i + band]))
        copies[-1].start()
    for copy in copies:
        copy.wait()


def pick_kernel(owners, gathered, own, other):
    owned = own.shape[0]
    first = lax.axis_index("gy") % 2 == 0
    total = []
    for block in range(2 * owned):
        parts = [jnp.where(owners[t, block : block + 1, :] > 0, gathered[t], 0.0) for t in range(owners.shape[0])]
        while len(parts) > 1:
            parts = [sum(parts[i : i + 2]) for i in range(0, len(parts), 2)]
        total.append(parts[0])
    for block in range(owned):
        low, high = total[block], total[block + owned]
        for out, cells in ((own, jnp.where(first, low, high)), (other, jnp.where(first, high, low))):
            for j in range(PACK):
                out[block : block + 1, j * LANES : (j + 1) * LANES] = cells[j : j + 1]


def in_vmem(count):
    return [pl.BlockSpec(memory_space=pltpu.VMEM)] * count


def in_smem(count):
    return [pl.BlockSpec(memory_space=pltpu.SMEM)] * count


def per_device(thickness, driving, observed, control, ice_mask, tile_block):
    f32 = jnp.float32
    rows, cols = lax.axis_size("gy"), lax.axis_size("gx")
    tile_block, ice_mask = tile_block[:, :, 0].T, ice_mask.T
    params = pltpu.CompilerParams(vmem_limit_bytes=VMEM_LIMIT)

    def shape(*sizes):
        return jax.ShapeDtypeStruct(sizes, f32)

    def swap(axis, cells_first, cells_second):
        count = lax.axis_size(axis)
        received = []
        for cells, low in ((cells_first, 0), (cells_second, 1)):
            pairs = [(i, i + 1) for i in range(low, count - 1, 2)]
            received.append(lax.ppermute(cells, axis, pairs + [(j, i) for i, j in pairs]))
        return received

    fields = thickness, driving, observed
    owned = control.shape[0]
    *edges, parcels = pl.pallas_call(
        pack_kernel,
        out_shape=[shape(HALF, LANES)] * 2 + [shape(rows, PARCEL, LANES)],
        in_specs=[pl.BlockSpec(memory_space=pltpu.HBM)] * 5,
        out_specs=[pl.BlockSpec(memory_space=pltpu.HBM)] * 3,
        scratch_shapes=[
            pltpu.SMEM(tile_block.shape, jnp.int32),
            pltpu.VMEM((5, TILE, TILE), f32),
            pltpu.VMEM(control.shape, f32),
            pltpu.VMEM((owned, PACK, LANES), f32),
            pltpu.VMEM((rows, PARCEL, LANES), f32),
            pltpu.VMEM((2, HALF, LANES), f32),
            pltpu.SemaphoreType.DMA((10,)),
        ],
        compiler_params=pltpu.CompilerParams(vmem_limit_bytes=PACK_VMEM_LIMIT),
        name="pack",
    )(tile_block, control, *fields)
    parcels = lax.all_to_all(parcels, "gy", 0, 0, tiled=True)
    columns_in = swap("gx", *edges)
    woven, own_sides, strips = pl.pallas_call(
        weave_kernel,
        out_shape=[shape(5, 2, TILE, LANES), shape(5, HALF, LANES), shape(2, 3, 64, LANES)],
        in_specs=in_vmem(3),
        out_specs=in_vmem(3),
        compiler_params=params,
        name="weave",
    )(*fields)
    strips = pl.pallas_call(
        rows_kernel,
        out_shape=[shape(160, LANES)] * 2,
        in_specs=in_vmem(3),
        out_specs=in_vmem(2),
        compiler_params=params,
        name="rows",
    )(strips, *columns_in)
    rows_in = swap("gy", *strips)
    *friction, owners = pl.pallas_call(
        friction_kernel,
        out_shape=[shape(ALL_ROWS, LANES)] * 2
        + [jax.ShapeDtypeStruct((cols * rows // 2, 2 * owned, LANES), jnp.int32)],
        in_specs=in_smem(2) + in_vmem(1),
        out_specs=in_vmem(3),
        scratch_shapes=[pltpu.VMEM((PATCH, LANES), f32)],
        compiler_params=params,
        name="friction",
    )(tile_block, ice_mask, parcels)
    prepared = pl.pallas_call(
        setup_kernel,
        out_shape=[shape(5, ALL_ROWS, LANES), shape(2, ALL_ROWS, LANES)],
        in_specs=in_vmem(6),
        out_specs=in_vmem(2),
        scratch_shapes=[
            pltpu.VMEM((3, ALL_ROWS, LANES), f32),
            pltpu.VMEM((2, ALL_ROWS, LANES), f32),
            pltpu.VMEM((FACTORS, ALL_ROWS, LANES), f32),
        ],
        compiler_params=params,
        name="setup",
    )(*friction, woven, own_sides, *columns_in)

    vel, sums = pl.pallas_call(
        model_kernel,
        out_shape=(shape(2, ALL_ROWS, LANES), shape(cols * rows // 2, PACK, LANES)),
        in_specs=in_vmem(6),
        out_specs=in_vmem(2),
        scratch_shapes=[
            pltpu.VMEM((5, ALL_ROWS, LANES), f32),
            pltpu.VMEM((3, ALL_ROWS, LANES), f32),
            pltpu.VMEM((2, ALL_ROWS, LANES), f32),
            pltpu.VMEM((2, ALL_ROWS, LANES), f32),
            pltpu.VMEM((FACTORS, ALL_ROWS, LANES), f32),
            pltpu.VMEM((CT, LANES), f32),
        ],
        compiler_params=params,
        name="model",
    )(*friction, *prepared, *rows_in)
    vel_u, vel_v = pl.pallas_call(
        unweave_kernel,
        out_shape=[shape(TILE, TILE)] * 2,
        in_specs=in_vmem(1),
        out_specs=[pl.BlockSpec(memory_space=pltpu.HBM)] * 2,
        scratch_shapes=[pltpu.VMEM((2, TILE, TILE), f32), pltpu.SemaphoreType.DMA((4,))],
        compiler_params=params,
        name="unweave",
    )(vel)

    same_core = [[i * rows + j for i in range(cols) for j in range(core, rows, 2)] for core in range(2)]
    sums = lax.all_to_all(sums, ("gx", "gy"), 0, 0, tiled=True, axis_index_groups=same_core)
    own, other = pl.pallas_call(
        pick_kernel,
        out_shape=[shape(*control.shape)] * 2,
        in_specs=in_vmem(2),
        out_specs=in_vmem(2),
        compiler_params=params,
        name="pick",
    )(owners, sums)
    gradient = own + lax.ppermute(other, "gy", [(j, j ^ 1) for j in range(rows)])
    return vel_u, vel_v, gradient


def solution(mesh):
    return jax.shard_map(
        per_device,
        mesh=mesh,
        in_specs=(P("gy", "gx"), P(None, "gy", "gx"), P(None, "gy", "gx"), P("gy", None), P(), P()),
        out_specs=(P("gy", "gx"), P("gy", "gx"), P("gy", None)),
        check_vma=False,
    )
```
